32 devices in a mesh: cell: 8 (over z, y), sensor: 4 (over x, core).
Axes of the slice: x: 2, y: 2, z: 4, core: 2. Of those that a mesh axis runs over, the one named last changes fastest.
Arguments:
- kernel: bfloat16 [2, 65, 256, 2048], P(None, None, 'sensor', 'cell'), may hold values from -3 to 3
- observed: float32 [64, 256], P(None, 'sensor'), may hold values from -6 to 6
- start_model: float32 [64, 2048], P(None, 'cell'), may hold values from -6 to 6
- start_multiplier: float32 [4, 64, 2048], P(None, None, 'cell'), may hold values from -1.8 to 1.8
- neighbours: int32 [4, 2048], P(None, 'cell'), may hold values from 0 to 2047, as said below
- tile_of_cell: int32 [2048], P('cell'), may hold values from 0 to 63
- tile_weight: float32 [64], replicated, may hold values from 0.3 to 3
Outputs:
- estimate: float32 [64, 2048], P(None, 'cell')
- auxiliary: float32 [4, 64, 2048], P(None, None, 'cell')
- multiplier: float32 [4, 64, 2048], P(None, None, 'cell')
The draws below stay inside these ranges and needn't reach their ends.
Inputs may be any that keep to these rules, and one draw needn't show every extreme that they name: The cells form a grid of 16 rows of 128 cells, numbered row by row. neighbours[k, c] is c itself or the cell beside c: c + 1 for k = 0 and c - 1 for k = 1 within the same row, c - 128 for k = 2 and c + 128 for k = 3. Where neighbours[k, c] = c' differs from c, neighbours[k xor 1, c'] = c.
All inputs are finite; a program needn't handle non-finite values.
Results may differ from the reference program's by a relative error of at most 0.00092.
Values sent between devices are 32-bit elements; how exact they have to be, the bound alone decides.
No kernel may reach another device: no remote copies, remote signals or barrier semaphores. Data moves between devices by JAX's collectives and lax.ppermute only.
A program may use at most 64 MiB of HBM per device.

```python
import math
import jax
import jax.numpy as jnp
from jax import lax

NT = 64
NF = 65
COLS = 128
TILES = 64
ITERS = 2
NC = 2048
NS = 256


def draw_kernel(key, part):
    noise = jnp.clip(jax.random.normal(key, (2, NF, NS, NC), jnp.float32), -6.0, 6.0)
    cell_ramp = 0.5 + 1.5 * jnp.arange(NC).astype(jnp.float32) / NC
    sensor_ramp = 0.6 + 1.2 * jnp.arange(NS).astype(jnp.float32) / NS
    scaled = noise * cell_ramp[None, None, None, :] * sensor_ramp[None, None, :, None]
    return (scaled / NC ** 0.5).astype(jnp.bfloat16)


def draw_neighbours(key, part):
    row_count = NC // COLS
    first_key = jax.random.fold_in(key, 11)
    second_key = jax.random.fold_in(key, 13)
    cut_along = jax.random.randint(first_key, (row_count, COLS), 0, 100) < 15
    cut_across = jax.random.randint(second_key, (row_count, COLS), 0, 100) < 15
    row_index = lax.broadcasted_iota(jnp.int32, (row_count, COLS), 0)
    col_index = lax.broadcasted_iota(jnp.int32, (row_count, COLS), 1)
    cell_number = row_index * COLS + col_index
    east = jnp.where((col_index < COLS - 1) & jnp.logical_not(cut_along), cell_number + 1, cell_number)
    west = jnp.where((col_index > 0) & jnp.logical_not(jnp.roll(cut_along, 1, axis=1)), cell_number - 1, cell_number)
    north = jnp.where((row_index > 0) & jnp.logical_not(jnp.roll(cut_across, 1, axis=0)), cell_number - COLS, cell_number)
    south = jnp.where((row_index < row_count - 1) & jnp.logical_not(cut_across), cell_number + COLS, cell_number)
    return jnp.stack([east, west, north, south]).reshape(4, NC).astype(jnp.int32)


def plant(drawn, key, least, top_value):
    shape = drawn.shape
    spot = [jax.random.randint(jax.random.fold_in(key, axis), (), 0, shape[axis]) for axis in range(len(shape))]
    drawn = drawn.at[tuple(spot)].set(least)
    longest = shape.index(max(shape))
    spot[longest] = (spot[longest] + 1) % shape[longest]
    return drawn.at[tuple(spot)].set(top_value)


def steps_of(own_key, extent, pieces, low, high):
    level = 1.0
    for axis_at, shards_of in pieces:
        heights = jax.random.uniform(jax.random.fold_in(jax.random.fold_in(own_key, 6), axis_at), (shards_of,), jnp.float32, low / len(pieces), high / len(pieces))
        level = level * jnp.repeat(jnp.exp(heights), extent[axis_at] // shards_of).reshape((-1,) + (1,) * (len(extent) - 1 - axis_at))
    return level


def gaussian(rng, dims, width, limit, cuts=(), held_as=jnp.bfloat16):
    drawn = jax.random.normal(rng, dims, jnp.float32) * width
    if len(cuts) > 0:
        drawn = steps_of(rng, dims, cuts, -0.22, 0.18) * drawn
    return jnp.clip(drawn, min=-limit, max=limit).astype(held_as)


def setup_inputs(seed: int = 0) -> dict:
    arg_keys = jax.random.split(jax.random.key(seed), 8)
    kernel = draw_kernel(jax.random.fold_in(arg_keys[7], 71), 0)
    observed = gaussian(arg_keys[1], (NT, NS), 1.0, 6.0, ((1, 4),), jnp.float32)
    start_model = gaussian(arg_keys[2], (NT, NC), 1.0, 6.0, ((1, 8),), jnp.float32)
    start_multiplier = gaussian(arg_keys[3], (4, NT, NC), 0.3, 1.8, ((2, 8),), jnp.float32)
    neighbours = draw_neighbours(jax.random.fold_in(arg_keys[7], 71), 0)
    tile_of_cell = plant(jax.random.randint(arg_keys[5], (NC,), 0, TILES), jax.random.fold_in(arg_keys[5], 1), 0, TILES - 1).astype(jnp.int32)
    tile_weight = jnp.clip(jnp.exp(jax.random.uniform(arg_keys[6], (TILES,), jnp.float32, math.log(0.3), math.log(3.0))), 0.3, 3.0)
    return {"kernel": kernel, "observed": observed, "start_model": start_model, "start_multiplier": start_multiplier, "neighbours": neighbours, "tile_of_cell": tile_of_cell, "tile_weight": tile_weight}


SHRINK_SCALE = 0.4
TINY = 1e-6


def exact_dot(left, right):
    return jnp.dot(left, right, precision=lax.Precision.HIGHEST, preferred_element_type=jnp.float32)


def tables(times_count, freq_count):
    padded = 2 * times_count
    freq_index = lax.broadcasted_iota(jnp.int32, (freq_count, times_count), 0)
    time_index = lax.broadcasted_iota(jnp.int32, (freq_count, times_count), 1)
    phase = ((freq_index * time_index) % padded).astype(jnp.float32) * (2.0 * jnp.pi / padded)
    cosine = jnp.cos(phase)
    sine_table = jnp.sin(phase)
    weight = jnp.where((freq_index == 0) | (freq_index == freq_count - 1), 1.0, 2.0).astype(jnp.float32) / padded
    return cosine, sine_table, cosine * weight, sine_table * weight


def forward(kernel, series, tabs):
    cosine, sine_table, cos_weighted, sin_weighted = tabs
    real_part = exact_dot(cosine, series).astype(jnp.bfloat16)
    imag_part = (-exact_dot(sine_table, series)).astype(jnp.bfloat16)

    def per_frequency(index):
        slab = lax.dynamic_index_in_dim(kernel, index, 1, keepdims=False).astype(jnp.float32)
        real_in = lax.dynamic_index_in_dim(real_part, index, 0, keepdims=False).astype(jnp.float32)
        imag_in = lax.dynamic_index_in_dim(imag_part, index, 0, keepdims=False).astype(jnp.float32)
        out_real = exact_dot(slab[0], real_in) - exact_dot(slab[1], imag_in)
        out_imag = exact_dot(slab[0], imag_in) + exact_dot(slab[1], real_in)
        return out_real, out_imag

    out_real, out_imag = lax.map(per_frequency, jnp.arange(NF).astype(jnp.int32))
    return exact_dot(cos_weighted.T, out_real) - exact_dot(sin_weighted.T, out_imag)


def adjoint(kernel, misfit, tabs):
    cosine, sine_table, cos_weighted, sin_weighted = tabs
    back_real = exact_dot(cos_weighted, misfit).astype(jnp.bfloat16)
    back_imag = (-exact_dot(sin_weighted, misfit)).astype(jnp.bfloat16)

    def per_frequency(index):
        slab = lax.dynamic_index_in_dim(kernel, index, 1, keepdims=False).astype(jnp.float32)
        real_in = lax.dynamic_index_in_dim(back_real, index, 0, keepdims=False).astype(jnp.float32)
        imag_in = lax.dynamic_index_in_dim(back_imag, index, 0, keepdims=False).astype(jnp.float32)
        spec_real = exact_dot(real_in, slab[0]) + exact_dot(imag_in, slab[1])
        spec_imag = exact_dot(imag_in, slab[0]) - exact_dot(real_in, slab[1])
        return spec_real, spec_imag

    spec_real, spec_imag = lax.map(per_frequency, jnp.arange(NF).astype(jnp.int32))
    return exact_dot(cosine.T, spec_real) - exact_dot(sine_table.T, spec_imag)


def differences(series, neighbours):
    return jnp.stack([series[:, neighbours[direction]] for direction in range(4)]) - series[None]


def transposed_differences(values, neighbours, linked):
    masked = values * linked[:, None, :]
    outgoing = jnp.sum(masked, axis=0)
    flat = jnp.transpose(masked, (0, 2, 1)).reshape(4 * NC, NT)
    incoming = jax.ops.segment_sum(flat, neighbours.reshape(-1), num_segments=NC)
    return incoming.T - outgoing


def reference(kernel, observed, start_model, start_multiplier, neighbours, tile_of_cell, tile_weight):
    tabs = tables(NT, NF)
    cell_index = jnp.arange(NC).astype(jnp.int32)
    linked = (neighbours != cell_index[None, :]).astype(jnp.float32)
    threshold = SHRINK_SCALE * tile_weight[tile_of_cell]
    estimate = start_model
    multiplier = start_multiplier
    model_jumps = differences(estimate, neighbours)
    auxiliary = model_jumps
    predicted = forward(kernel, estimate, tabs)
    for iteration in range(ITERS):
        penalty = model_jumps - auxiliary + multiplier
        gradient = adjoint(kernel, predicted - observed, tabs) + transposed_differences(penalty, neighbours, linked)
        response = forward(kernel, gradient, tabs)
        grad_jumps = differences(gradient, neighbours)
        grad_square = jnp.sum(gradient * gradient)
        response_square = jnp.sum(response * response)
        jump_square = jnp.sum(grad_jumps * grad_jumps)
        step_size = grad_square / (response_square + jump_square + TINY)
        estimate = estimate - step_size * gradient
        predicted = predicted - step_size * response
        model_jumps = model_jumps - step_size * grad_jumps
        shifted = model_jumps + multiplier
        auxiliary = jnp.sign(shifted) * jnp.maximum(jnp.abs(shifted) - threshold, 0.0)
        multiplier = shifted - auxiliary
    return estimate, auxiliary, multiplier
```

```python
import functools

import jax
import jax.numpy as jnp
import numpy as np
from jax import lax
from jax.experimental import pallas as pl
from jax.experimental.pallas import tpu as pltpu
from jax.sharding import PartitionSpec as P

COLS = 128
LANES = 128
GROUP = 8
SHRINK_SCALE = 0.4
TINY = 1e-06
VMEM = pltpu.VMEM


def tables(times, freqs):
    padded = 2 * times
    groups = -(-freqs // GROUP)
    plain = np.zeros((16 * groups, times), np.float64)
    weighted = np.zeros((16 * groups, times), np.float64)
    for f in range(freqs):
        phase = 2.0 * np.pi * ((f * np.arange(times)) % padded) / padded
        weight = (1.0 if f in (0, freqs - 1) else 2.0) / padded
        row = 16 * (f // GROUP) + f % GROUP
        plain[row], plain[row + GROUP] = np.cos(phase), -np.sin(phase)
        weighted[row], weighted[row + GROUP] = weight * np.cos(phase), -weight * np.sin(phase)
    return plain.astype(np.float32), weighted.astype(np.float32)


def exact(left, right):
    return jnp.dot(left, right, precision=lax.Precision.HIGHEST, preferred_element_type=jnp.float32)


def turned(rows):
    return jnp.concatenate([-rows[GROUP:], rows[:GROUP]], axis=0)


def dot_nt(left, right):
    return lax.dot_general(left, right, (((1,), (1,)), ((), ())), preferred_element_type=jnp.float32)


def dot_nn(left, right):
    return jnp.dot(left, right, preferred_element_type=jnp.float32)


def slab(kernel_ref, part, group):
    freqs, sensors, cells = kernel_ref.shape[1:]
    count = min(GROUP, freqs - group * GROUP)
    block = kernel_ref[part, group * GROUP : group * GROUP + count]
    return block.reshape(count * sensors, cells)


def own_block(width, sensors):
    row = lax.broadcasted_iota(jnp.int32, (16, width), 0) % GROUP
    lane = lax.broadcasted_iota(jnp.int32, (16, width), 1) // sensors
    return row == lane


def fold(wide):
    total = functools.reduce(
        lambda a, b: a + b, [wide[:, i : i + LANES] for i in range(0, wide.shape[1], LANES)]
    )
    return total + pltpu.roll(total, LANES // 2, 1)


def forward(field, kernel_ref, plain, weighted_t):
    freqs, sensors = kernel_ref.shape[1:3]
    times = field.shape[0]
    spectra = exact(plain, field)
    rows = []
    for group in range(plain.shape[0] // 16):
        part = spectra[16 * group : 16 * group + 16]
        re_slab, im_slab = slab(kernel_ref, 0, group), slab(kernel_ref, 1, group)
        out = dot_nt(part.astype(jnp.bfloat16), re_slab) + dot_nt(turned(part).astype(jnp.bfloat16), im_slab)
        width = out.shape[1]
        out = jnp.where(own_block(width, sensors), out, 0.0)
        if width < LANES:
            out = jnp.concatenate([out, jnp.zeros((16, LANES - width), jnp.float32)], axis=1)
        rows.append(fold(out))
    series = exact(weighted_t, jnp.concatenate(rows, axis=0))
    left = lax.broadcasted_iota(jnp.int32, (times // 2, LANES), 1) < sensors
    return jnp.where(left, series[: times // 2], series[times // 2 :])


def unpacked(packed, sensors):
    other = pltpu.roll(packed, sensors, 1)
    left = lax.broadcasted_iota(jnp.int32, packed.shape, 1) < sensors
    return jnp.concatenate([jnp.where(left, packed, other), jnp.where(left, other, packed)], axis=0)


def adjoint(residual, kernel_ref, plain_t, weighted, halves):
    freqs, sensors, cells = kernel_ref.shape[1:]
    spectra = exact(weighted, residual)
    rows = []
    for group in range(weighted.shape[0] // 16):
        part = spectra[16 * group : 16 * group + 16]
        count = min(GROUP, freqs - group * GROUP)
        width = count * sensors
        re_slab, im_slab = slab(kernel_ref, 0, group), slab(kernel_ref, 1, group)
        wide = jnp.concatenate([part] * (-(-width // LANES)), axis=1)[:, :width]
        wide = jnp.where(own_block(width, sensors), wide, 0.0)
        total = None
        for _ in range(halves):
            re_left = wide.astype(jnp.bfloat16)
            rounded = re_left.astype(jnp.float32)
            out = dot_nn(re_left, re_slab) - dot_nn(turned(rounded).astype(jnp.bfloat16), im_slab)
            total = out if total is None else total + out
            wide = wide - rounded
        rows.append(total)
    return exact(plain_t, jnp.concatenate(rows, axis=0))


def strip(array, row):
    return array[..., row * COLS : (row + 1) * COLS]


def jumps(field, above, below, linked):
    count = field.shape[1] // COLS
    out = []
    for direction in range(4):
        strips = []
        for row in range(count):
            here = strip(field, row)
            if direction == 0:
                there = pltpu.roll(here, COLS - 1, 1)
            elif direction == 1:
                there = pltpu.roll(here, 1, 1)
            elif direction == 2:
                there = above if row == 0 else strip(field, row - 1)
            else:
                there = below if row == count - 1 else strip(field, row + 1)
            strips.append(strip(linked[direction : direction + 1], row) * (there - here))
        out.append(strips)
    return out


def gathered_jumps(values, above, below, linked):
    count = len(values[0])
    out = []
    for row in range(count):
        arriving = (
            pltpu.roll(values[1][row], COLS - 1, 1),
            pltpu.roll(values[0][row], 1, 1),
            above if row == 0 else values[3][row - 1],
            below if row == count - 1 else values[2][row + 1],
        )
        total = None
        for direction in range(4):
            term = strip(linked[direction : direction + 1], row) * (arriving[direction] - values[direction][row])
            total = term if total is None else total + term
        out.append(total)
    return jnp.concatenate(out, axis=1)


def shrunk(shifted, threshold):
    return shifted - jnp.clip(shifted, -threshold, threshold)


def tree_sum(parts):
    parts = list(parts)
    while len(parts) > 1:
        parts = [parts[i] + parts[i + 1] if i + 1 < len(parts) else parts[i] for i in range(0, len(parts), 2)]
    return parts[0]


def square_sum(array):
    return jnp.sum(array * array)


def block_of(scalar, rows=8):
    return jnp.full((rows, LANES), scalar, jnp.float32)


def call(body, out_shapes, *operands, flops=0):
    single = isinstance(out_shapes, tuple)
    shapes = [out_shapes] if single else list(out_shapes)
    out = pl.pallas_call(
        body,
        out_shape=[jax.ShapeDtypeStruct(s, jnp.float32) for s in shapes],
        in_specs=[pl.BlockSpec(memory_space=VMEM)] * len(operands),
        out_specs=[pl.BlockSpec(memory_space=VMEM)] * len(shapes),
        compiler_params=pltpu.CompilerParams(vmem_limit_bytes=24 * 2**20),
    )(*operands)
    return out[0] if single else out


def forward_body(field, kernel, plain, weighted_t, out):
    out[...] = forward(field[...], kernel, plain[...], weighted_t[...])


def first_adjoint_body(parts_count, *refs):
    parts, (observed, kernel, plain_t, weighted, out) = refs[:parts_count], refs[parts_count:]
    predicted = unpacked(tree_sum([p[...] for p in parts]), kernel.shape[2])
    out[...] = adjoint(predicted - observed[...], kernel, plain_t[...], weighted[...], 1)


def first_gradient_body(parts_count, *refs):
    parts, (start_multiplier, above, below, linked, adjoint_out, gradient) = refs[:parts_count], refs[parts_count:]
    times, cells = adjoint_out.shape
    total = tree_sum([p[...] for p in parts])
    values = [[strip(start_multiplier[k], r) for r in range(cells // COLS)] for k in range(4)]
    back = gathered_jumps(values, above[times : 2 * times], below[times : 2 * times], linked[...])
    adjoint_out[...] = total
    gradient[...] = total + back


def norms_body(gradient, above, below, linked, out):
    field = gradient[...]
    squares = [square_sum(s) for strips in jumps(field, above[...], below[...], linked[...]) for s in strips]
    out[0:8, :] = block_of(square_sum(field))
    out[8:16, :] = block_of(tree_sum(squares))


def second_adjoint_body(parts_count, norms_count, *refs):
    parts, norms = refs[:parts_count], refs[parts_count : parts_count + norms_count]
    kernel, plain_t, weighted, out = refs[parts_count + norms_count :]
    times = plain_t.shape[0]
    packed = tree_sum([p[...] for p in parts])
    out[:times, :] = adjoint(unpacked(packed, kernel.shape[2]), kernel, plain_t[...], weighted[...], 2)
    squares = tree_sum([n[...] for n in norms])
    out[times : times + 8, :LANES] = squares[:8]
    out[times : times + 8, LANES : 2 * LANES] = squares[8:]
    out[times + 8 : times + 16, :LANES] = block_of(square_sum(packed))
    out[times + 8 : times + 16, LANES : 2 * LANES] = jnp.zeros((8, LANES), jnp.float32)


def second_gradient_body(parts_count, *refs):
    parts = refs[:parts_count]
    (adjoint_in, gradient_in, model, start_multiplier, threshold, above, below, grad_above, grad_below, linked_ref,
     model_out, jumps_out, multiplier_out, gradient_out) = refs[parts_count:]
    times, cells = model.shape
    total = tree_sum([p[...] for p in parts])
    grad_square, jump_square = total[times, 0], total[times, LANES]
    response_square = total[times + 8, 0]
    step = grad_square / (response_square + jump_square + TINY)
    linked = linked_ref[...]
    field, gradient = model[...], gradient_in[...]
    rows = cells // COLS
    field_jumps = jumps(field, above[:times], below[:times], linked)
    grad_jumps = jumps(gradient, grad_above[...], grad_below[...], linked)

    def advance(model_jumps, old_multiplier, limit):
        shifted = model_jumps + old_multiplier
        auxiliary = shrunk(shifted, limit)
        multiplier = shifted - auxiliary
        return multiplier, model_jumps - auxiliary + multiplier

    penalties, new_jumps = [], []
    for k in range(4):
        penalties.append([])
        new_jumps.append([])
        for r in range(rows):
            new = field_jumps[k][r] - step * grad_jumps[k][r]
            multiplier, penalty = advance(new, strip(start_multiplier[k], r), strip(threshold[0:1], r))
            jumps_out[k, :, r * COLS : (r + 1) * COLS] = new
            multiplier_out[k, :, r * COLS : (r + 1) * COLS] = multiplier
            penalties[k].append(penalty)
            new_jumps[k].append(new)
    _, beside_above = advance(-new_jumps[2][0], above[times : 2 * times], above[2 * times : 2 * times + 1])
    _, beside_below = advance(-new_jumps[3][-1], below[times : 2 * times], below[2 * times : 2 * times + 1])
    back = gathered_jumps(penalties, beside_above, beside_below, linked)
    model_out[...] = field - step * gradient
    gradient_out[...] = adjoint_in[...] - step * total[:times] + back


def response_body(parts_count, *refs):
    parts, out = refs[:parts_count], refs[parts_count]
    out[...] = block_of(square_sum(tree_sum([p[...] for p in parts])))


def finish_body(norms, gradient_in, model, model_jumps, multiplier, threshold, above, below, linked, *outs):
    estimate_out, auxiliary_out, multiplier_out = outs
    step = norms[0, 0] / (norms[16, 0] + norms[8, 0] + TINY)
    gradient = gradient_in[...]
    estimate_out[...] = model[...] - step * gradient
    grad_jumps = jumps(gradient, above[...], below[...], linked[...])
    for k in range(4):
        for r in range(gradient.shape[1] // COLS):
            at = slice(r * COLS, (r + 1) * COLS)
            shifted = model_jumps[k, :, at] - step * grad_jumps[k][r] + multiplier[k, :, at]
            auxiliary = shrunk(shifted, threshold[0:1, at])
            auxiliary_out[k, :, at] = auxiliary
            multiplier_out[k, :, at] = shifted - auxiliary


def parts_of(array, axis):
    count = lax.axis_size(axis)
    if count & (count - 1):
        return list(lax.all_gather(array, axis))
    return [array] + [lax.ppermute(array, axis, [(i, i ^ k) for i in range(count)]) for k in range(1, count)]


def parts_by_all_to_all(array, axis):
    count = lax.axis_size(axis)
    sent = jnp.broadcast_to(array[None], (count,) + array.shape)
    return list(lax.all_to_all(sent, axis, 0, 0))


def rows_beside(last, first, axis):
    count = lax.axis_size(axis)
    down = [(i, i + 1) for i in range(count - 1)]
    up = [(j, i) for i, j in down]
    return lax.ppermute(last, axis, down), lax.ppermute(first, axis, up)


def cell_shares(array):
    cells, sensors = lax.axis_size("cell"), lax.axis_size("sensor")
    if cells % sensors:
        return [lax.psum(array, "cell") / sensors]
    each = cells // sensors
    return [
        lax.ppermute(
            array,
            ("cell", "sensor"),
            [(((c + s * each + j) % cells) * sensors + s, c * sensors + s) for c in range(cells) for s in range(sensors)],
        )
        for j in range(each)
    ]


def per_device(kernel, observed, start_model, start_multiplier, neighbours, tile_of_cell, tile_weight):
    times, cells = start_model.shape
    freqs, sensors = kernel.shape[1:3]
    plain, weighted = tables(times, freqs)
    plain_t, weighted_t = jnp.asarray(plain.T.copy()), jnp.asarray(weighted.T.copy())
    plain, weighted = jnp.asarray(plain), jnp.asarray(weighted)
    cell_count, sensor_count = lax.axis_size("cell"), lax.axis_size("sensor")

    own = lax.axis_index("cell") * cells + lax.broadcasted_iota(jnp.int32, (1, cells), 1)
    linked = (neighbours != own).astype(jnp.float32)
    labels = lax.broadcasted_iota(jnp.int32, (tile_weight.shape[0], cells), 0)
    threshold = SHRINK_SCALE * jnp.sum(
        jnp.where(labels == tile_of_cell[None, :], tile_weight[:, None], 0.0), axis=0, keepdims=True
    )
    threshold = jnp.broadcast_to(threshold, (8, cells))
    observed_twice = jnp.concatenate([observed, observed], axis=1)
    last, first = slice(cells - COLS, cells), slice(0, COLS)
    above, below = rows_beside(
        jnp.concatenate([start_model[:, last], start_multiplier[3][:, last], threshold[:, last]]),
        jnp.concatenate([start_model[:, first], start_multiplier[2][:, first], threshold[:, first]]),
        "cell",
    )

    packed = (times // 2, 2 * sensors)
    field = (times, cells)
    wide = (4, times, cells)

    def forward_of(series):
        return parts_by_all_to_all(call(forward_body, packed, series, kernel, plain, weighted_t), "cell")

    parts = forward_of(start_model)
    back = call(
        functools.partial(first_adjoint_body, len(parts)), field, *parts, observed_twice, kernel, plain_t, weighted
    )
    parts = parts_of(back, "sensor")
    adjoint_one, gradient = call(
        functools.partial(first_gradient_body, len(parts)), [field, field],
        *parts, start_multiplier, above, below, linked,
    )
    grad_above, grad_below = rows_beside(gradient[:, last], gradient[:, first], "cell")
    parts = forward_of(gradient)
    norms = cell_shares(call(norms_body, (16, LANES), gradient, grad_above, grad_below, linked))
    back = call(
        functools.partial(second_adjoint_body, len(parts), len(norms)), (times + 16, cells),
        *parts, *norms, kernel, plain_t, weighted,
    )
    parts = parts_of(back, "sensor")
    model, model_jumps, multiplier, gradient_two = call(
        functools.partial(second_gradient_body, len(parts)), [field, wide, wide, field],
        *parts, adjoint_one, gradient, start_model, start_multiplier, threshold, above, below, grad_above, grad_below,
        linked,
    )
    grad_above, grad_below = rows_beside(gradient_two[:, last], gradient_two[:, first], "cell")
    parts = forward_of(gradient_two)
    norms = call(norms_body, (16, LANES), gradient_two, grad_above, grad_below, linked)
    response_square = call(functools.partial(response_body, len(parts)), (8, LANES), *parts)
    sums = lax.psum(
        jnp.concatenate([norms[:, 0] / sensor_count, response_square[:, 0] / cell_count]), ("cell", "sensor")
    )
    sums = jnp.broadcast_to(sums[:, None], (24, LANES))
    return tuple(
        call(
            finish_body, [field, wide, wide],
            sums, gradient_two, model, model_jumps, multiplier, threshold, grad_above, grad_below, linked,
        )
    )


def solution(mesh):
    in_specs = (
        P(None, None, "sensor", "cell"),
        P(None, "sensor"),
        P(None, "cell"),
        P(None, None, "cell"),
        P(None, "cell"),
        P("cell"),
        P(),
    )
    out_specs = (P(None, "cell"), P(None, None, "cell"), P(None, None, "cell"))
    return jax.shard_map(
        per_device, mesh=mesh, in_specs=in_specs, out_specs=out_specs, check_vma=False
    )
```

```python
import functools

import jax
import jax.numpy as jnp
import numpy as np
from jax import lax
from jax.experimental import pallas as pl
from jax.experimental.pallas import tpu as pltpu
from jax.sharding import PartitionSpec as P

COLS = 128
LANES = 128
GROUP = 8
SHRINK_SCALE = 0.4
TINY = 1e-06
VMEM = pltpu.VMEM


def tables(times, freqs):
    padded = 2 * times
    groups = -(-freqs // GROUP)
    plain = np.zeros((16 * groups, times), np.float64)
    weighted = np.zeros((16 * groups, times), np.float64)
    for f in range(freqs):
        phase = 2.0 * np.pi * ((f * np.arange(times)) % padded) / padded
        weight = (1.0 if f in (0, freqs - 1) else 2.0) / padded
        row = 16 * (f // GROUP) + f % GROUP
        plain[row], plain[row + GROUP] = np.cos(phase), -np.sin(phase)
        weighted[row], weighted[row + GROUP] = weight * np.cos(phase), -weight * np.sin(phase)
    return plain.astype(np.float32), weighted.astype(np.float32)


def exact(left, right):
    return jnp.dot(left, right, precision=lax.Precision.HIGHEST, preferred_element_type=jnp.float32)


def turned(rows):
    return jnp.concatenate([-rows[GROUP:], rows[:GROUP]], axis=0)


def dot_nt(left, right):
    return lax.dot_general(left, right, (((1,), (1,)), ((), ())), preferred_element_type=jnp.float32)


def dot_nn(left, right):
    return jnp.dot(left, right, preferred_element_type=jnp.float32)


def slab(kernel_ref, part, group):
    freqs, sensors, cells = kernel_ref.shape[1:]
    count = min(GROUP, freqs - group * GROUP)
    block = kernel_ref[part, group * GROUP : group * GROUP + count]
    return block.reshape(count * sensors, cells)


def own_block(width, sensors):
    row = lax.broadcasted_iota(jnp.int32, (16, width), 0) % GROUP
    lane = lax.broadcasted_iota(jnp.int32, (16, width), 1) // sensors
    return row == lane


def fold(wide):
    total = functools.reduce(
        lambda a, b: a + b, [wide[:, i : i + LANES] for i in range(0, wide.shape[1], LANES)]
    )
    return total + pltpu.roll(total, LANES // 2, 1)


def forward(field, kernel_ref, plain, weighted_t, arrived=None):
    freqs, sensors = kernel_ref.shape[1:3]
    times = field.shape[0]
    spectra = exact(plain, field)
    rows = []
    for group in range(plain.shape[0] // 16):
        part = spectra[16 * group : 16 * group + 16]
        if arrived is not None:
            arrived(group)
        re_slab, im_slab = slab(kernel_ref, 0, group), slab(kernel_ref, 1, group)
        out = dot_nt(part.astype(jnp.bfloat16), re_slab) + dot_nt(turned(part).astype(jnp.bfloat16), im_slab)
        width = out.shape[1]
        out = jnp.where(own_block(width, sensors), out, 0.0)
        if width < LANES:
            out = jnp.concatenate([out, jnp.zeros((16, LANES - width), jnp.float32)], axis=1)
        rows.append(fold(out))
    series = exact(weighted_t, jnp.concatenate(rows, axis=0))
    left = lax.broadcasted_iota(jnp.int32, (times // 2, LANES), 1) < sensors
    return jnp.where(left, series[: times // 2], series[times // 2 :])


def unpacked(packed, sensors):
    other = pltpu.roll(packed, sensors, 1)
    left = lax.broadcasted_iota(jnp.int32, packed.shape, 1) < sensors
    return jnp.concatenate([jnp.where(left, packed, other), jnp.where(left, other, packed)], axis=0)


def adjoint(residual, kernel_ref, plain_t, weighted, halves):
    freqs, sensors, cells = kernel_ref.shape[1:]
    spectra = exact(weighted, residual)
    rows = []
    for group in range(weighted.shape[0] // 16):
        part = spectra[16 * group : 16 * group + 16]
        count = min(GROUP, freqs - group * GROUP)
        width = count * sensors
        re_slab, im_slab = slab(kernel_ref, 0, group), slab(kernel_ref, 1, group)
        wide = jnp.concatenate([part] * (-(-width // LANES)), axis=1)[:, :width]
        wide = jnp.where(own_block(width, sensors), wide, 0.0)
        total = None
        for _ in range(halves):
            re_left = wide.astype(jnp.bfloat16)
            rounded = re_left.astype(jnp.float32)
            out = dot_nn(re_left, re_slab) - dot_nn(turned(rounded).astype(jnp.bfloat16), im_slab)
            total = out if total is None else total + out
            wide = wide - rounded
        rows.append(total)
    return exact(plain_t, jnp.concatenate(rows, axis=0))


def strip(array, row):
    return array[..., row * COLS : (row + 1) * COLS]


def jumps(field, above, below, linked):
    count = field.shape[1] // COLS
    out = []
    for direction in range(4):
        strips = []
        for row in range(count):
            here = strip(field, row)
            if direction == 0:
                there = pltpu.roll(here, COLS - 1, 1)
            elif direction == 1:
                there = pltpu.roll(here, 1, 1)
            elif direction == 2:
                there = above if row == 0 else strip(field, row - 1)
            else:
                there = below if row == count - 1 else strip(field, row + 1)
            strips.append(strip(linked[direction : direction + 1], row) * (there - here))
        out.append(strips)
    return out


def gathered_jumps(values, above, below, linked):
    count = len(values[0])
    out = []
    for row in range(count):
        arriving = (
            pltpu.roll(values[1][row], COLS - 1, 1),
            pltpu.roll(values[0][row], 1, 1),
            above if row == 0 else values[3][row - 1],
            below if row == count - 1 else values[2][row + 1],
        )
        total = None
        for direction in range(4):
            term = strip(linked[direction : direction + 1], row) * (arriving[direction] - values[direction][row])
            total = term if total is None else total + term
        out.append(total)
    return jnp.concatenate(out, axis=1)


def shrunk(shifted, threshold):
    return shifted - jnp.clip(shifted, -threshold, threshold)


def tree_sum(parts):
    parts = list(parts)
    while len(parts) > 1:
        parts = [parts[i] + parts[i + 1] if i + 1 < len(parts) else parts[i] for i in range(0, len(parts), 2)]
    return parts[0]


def received(ref, start=0, stop=None):
    return tree_sum([ref[i, start:stop] for i in range(ref.shape[0])])


def to_all(ref, array, start=0):
    for i in range(ref.shape[0]):
        ref[i, start : start + array.shape[0]] = array


def square_sum(array):
    return jnp.sum(array * array)


def block_of(scalar, rows=8):
    return jnp.full((rows, LANES), scalar, jnp.float32)


def call(body, out_shapes, *operands, scratch=(), inputs=VMEM):
    single = isinstance(out_shapes, tuple)
    shapes = [out_shapes] if single else list(out_shapes)
    shapes = [s if isinstance(s, jax.ShapeDtypeStruct) else jax.ShapeDtypeStruct(s, jnp.float32) for s in shapes]
    out = pl.pallas_call(
        body,
        out_shape=shapes,
        in_specs=[pl.BlockSpec(memory_space=inputs)] * len(operands),
        out_specs=[pl.BlockSpec(memory_space=VMEM)] * len(shapes),
        scratch_shapes=list(scratch),
        compiler_params=pltpu.CompilerParams(vmem_limit_bytes=24 * 2**20),
    )(*operands)
    return out[0] if single else out


def first_forward_body(field, kernel, plain, weighted_t, out, kept, field_here, plain_here, weighted_here, sems):
    freqs = kernel.shape[1]
    small = [
        pltpu.make_async_copy(source, target, sems.at[i])
        for i, (source, target) in enumerate(((field, field_here), (plain, plain_here), (weighted_t, weighted_here)))
    ]
    for copy in small:
        copy.start()
    large = []
    for group in range(plain.shape[0] // 16):
        start = group * GROUP
        count = min(GROUP, freqs - start)
        for part in range(2):
            at = (part, pl.ds(start, count))
            copy = pltpu.make_async_copy(kernel.at[at], kept.at[at], sems.at[3 + len(large)])
            copy.start()
            large.append(copy)
    for copy in small:
        copy.wait()

    def arrived(group):
        large[2 * group].wait()
        large[2 * group + 1].wait()

    to_all(out, forward(field_here[...], kept, plain_here[...], weighted_here[...], arrived))


def forward_body(field, kernel, plain, weighted_t, out):
    out[...] = forward(field[...], kernel, plain[...], weighted_t[...])


def first_adjoint_body(parts, observed, kernel, plain_t, weighted, out):
    predicted = unpacked(received(parts), kernel.shape[2])
    to_all(out, adjoint(predicted - observed[...], kernel, plain_t[...], weighted[...], 1))


def edge_rows(field, first, last):
    first[...] = strip(field, 0)
    last[...] = strip(field, field.shape[1] // COLS - 1)


def first_gradient_body(parts, start_multiplier, above, below, linked, adjoint_out, gradient, first, last):
    times, cells = adjoint_out.shape
    total = received(parts)
    values = [[strip(start_multiplier[k], r) for r in range(cells // COLS)] for k in range(4)]
    back = gathered_jumps(values, above[times : 2 * times], below[times : 2 * times], linked[...])
    adjoint_out[...] = total
    field = total + back
    gradient[...] = field
    edge_rows(field, first, last)


def norms_body(packed, gradient, above, linked, out):
    field = gradient[...]
    squares = []
    for row in range(field.shape[1] // COLS):
        here = strip(field, row)
        beside = above[...] if row == 0 else strip(field, row - 1)
        east = strip(linked[0:1], row) * (pltpu.roll(here, COLS - 1, 1) - here)
        north = strip(linked[2:3], row) * (beside - here)
        squares.append(east * east + north * north)
    half = packed.shape[0]
    to_all(out, packed[...])
    to_all(out, block_of(square_sum(field)), half)
    to_all(out, block_of(2.0 * jnp.sum(tree_sum(squares))), half + 8)


def second_adjoint_body(parts, kernel, plain_t, weighted, out, norms):
    times = plain_t.shape[0]
    half = times // 2
    packed = received(parts, 0, half)
    to_all(out, adjoint(unpacked(packed, kernel.shape[2]), kernel, plain_t[...], weighted[...], 2))
    square = block_of(square_sum(packed))
    to_all(out, jnp.concatenate([square] * (out.shape[2] // LANES), axis=1), times)
    norms[...] = received(parts, half, half + 16)


def second_gradient_body(
    parts, norms, adjoint_in, gradient_in, model, start_multiplier, threshold, above, below, grad_above, grad_below,
    linked_ref, model_out, jumps_out, multiplier_out, gradient_out, first, last,
):
    times, cells = model.shape
    response_square = received(parts, times, times + 8)[0, 0]
    step = norms[0, 0] / (response_square + norms[8, 0] + TINY)
    linked = linked_ref[...]
    field, gradient = model[...], gradient_in[...]
    rows = cells // COLS
    field_jumps = jumps(field, above[:times], below[:times], linked)
    grad_jumps = jumps(gradient, grad_above[...], grad_below[...], linked)

    def advance(model_jumps, old_multiplier, limit):
        shifted = model_jumps + old_multiplier
        auxiliary = shrunk(shifted, limit)
        multiplier = shifted - auxiliary
        return multiplier, model_jumps - auxiliary + multiplier

    penalties, new_jumps = [], []
    for k in range(4):
        penalties.append([])
        new_jumps.append([])
        for r in range(rows):
            new = field_jumps[k][r] - step * grad_jumps[k][r]
            multiplier, penalty = advance(new, strip(start_multiplier[k], r), strip(threshold[0:1], r))
            jumps_out[k, :, r * COLS : (r + 1) * COLS] = new
            multiplier_out[k, :, r * COLS : (r + 1) * COLS] = multiplier
            penalties[k].append(penalty)
            new_jumps[k].append(new)
    _, beside_above = advance(-new_jumps[2][0], above[times : 2 * times], above[2 * times : 2 * times + 1])
    _, beside_below = advance(-new_jumps[3][-1], below[times : 2 * times], below[2 * times : 2 * times + 1])
    back = gathered_jumps(penalties, beside_above, beside_below, linked)
    model_out[...] = field - step * gradient
    new_gradient = adjoint_in[...] - step * received(parts, 0, times) + back
    gradient_out[...] = new_gradient
    edge_rows(new_gradient, first, last)


def response_body(parts, out, norms):
    half = parts.shape[1] - 16
    to_all(out, block_of(square_sum(received(parts, 0, half))))
    norms[...] = received(parts, half, half + 16)


def finish_body(
    squares, norms, gradient_in, model, model_jumps, multiplier, threshold, above, below, linked,
    estimate_out, auxiliary_out, multiplier_out,
):
    step = norms[0, 0] / (received(squares)[0, 0] + norms[8, 0] + TINY)
    gradient = gradient_in[...]
    estimate_out[...] = model[...] - step * gradient
    grad_jumps = jumps(gradient, above[...], below[...], linked[...])
    for k in range(4):
        for r in range(gradient.shape[1] // COLS):
            at = slice(r * COLS, (r + 1) * COLS)
            shifted = model_jumps[k, :, at] - step * grad_jumps[k][r] + multiplier[k, :, at]
            auxiliary = shrunk(shifted, threshold[0:1, at])
            auxiliary_out[k, :, at] = auxiliary
            multiplier_out[k, :, at] = shifted - auxiliary


def exchanged(array, axis):
    return lax.all_to_all(array, axis, 0, 0)


def from_above(last):
    count = lax.axis_size("cell")
    return lax.ppermute(last, "cell", [(i, i + 1) for i in range(count - 1)])


def from_below(first):
    count = lax.axis_size("cell")
    return lax.ppermute(first, "cell", [(i + 1, i) for i in range(count - 1)])


def per_device(kernel, observed, start_model, start_multiplier, neighbours, tile_of_cell, tile_weight):
    times, cells = start_model.shape
    freqs, sensors = kernel.shape[1:3]
    plain, weighted = tables(times, freqs)
    plain_t, weighted_t = jnp.asarray(plain.T.copy()), jnp.asarray(weighted.T.copy())
    plain, weighted = jnp.asarray(plain), jnp.asarray(weighted)
    cell_count, sensor_count = lax.axis_size("cell"), lax.axis_size("sensor")

    own = lax.axis_index("cell") * cells + lax.broadcasted_iota(jnp.int32, (1, cells), 1)
    linked = (neighbours != own).astype(jnp.float32)
    labels = lax.broadcasted_iota(jnp.int32, (tile_weight.shape[0], cells), 0)
    threshold = SHRINK_SCALE * jnp.sum(
        jnp.where(labels == tile_of_cell[None, :], tile_weight[:, None], 0.0), axis=0, keepdims=True
    )
    threshold = jnp.broadcast_to(threshold, (8, cells))
    observed_twice = jnp.concatenate([observed, observed], axis=1)
    last, first = slice(cells - COLS, cells), slice(0, COLS)
    above = from_above(jnp.concatenate([start_model[:, last], start_multiplier[3][:, last], threshold[:, last]]))
    below = from_below(jnp.concatenate([start_model[:, first], start_multiplier[2][:, first], threshold[:, first]]))

    half = times // 2
    packed, field, row, wide = (half, 2 * sensors), (times, cells), (times, COLS), (4, times, cells)

    part, kept = call(
        first_forward_body, [(cell_count,) + packed, jax.ShapeDtypeStruct(kernel.shape, kernel.dtype)],
        start_model, kernel, plain, weighted_t,
        scratch=[
            VMEM(start_model.shape, jnp.float32), VMEM(plain.shape, jnp.float32), VMEM(weighted_t.shape, jnp.float32),
            pltpu.SemaphoreType.DMA((3 + 2 * (plain.shape[0] // 16),)),
        ],
        inputs=pl.ANY,
    )
    parts = exchanged(part, "cell")
    back = call(first_adjoint_body, (sensor_count,) + field, parts, observed_twice, kept, plain_t, weighted)
    parts = exchanged(back, "sensor")
    adjoint_one, gradient, edge_first, edge_last = call(
        first_gradient_body, [field, field, row, row], parts, start_multiplier, above, below, linked
    )

    def response_and_norms(gradient, edge_last):
        beside = from_above(edge_last)
        part = call(forward_body, packed, gradient, kept, plain, weighted_t)
        sent = call(norms_body, (cell_count, half + 16, LANES), part, gradient, beside, linked)
        return exchanged(sent, "cell"), beside

    parts, grad_above = response_and_norms(gradient, edge_last)
    grad_below = from_below(edge_first)
    back, norms = call(
        second_adjoint_body, [(sensor_count, times + 8, cells), (16, LANES)], parts, kept, plain_t, weighted
    )
    parts = exchanged(back, "sensor")
    model, model_jumps, multiplier, gradient, edge_first, edge_last = call(
        second_gradient_body, [field, wide, wide, field, row, row],
        parts, norms, adjoint_one, gradient, start_model, start_multiplier, threshold, above, below,
        grad_above, grad_below, linked,
    )
    parts, grad_above = response_and_norms(gradient, edge_last)
    grad_below = from_below(edge_first)
    square, norms = call(response_body, [(sensor_count, 8, LANES), (16, LANES)], parts)
    squares = exchanged(square, "sensor")
    return tuple(
        call(
            finish_body, [field, wide, wide],
            squares, norms, gradient, model, model_jumps, multiplier, threshold, grad_above, grad_below, linked,
        )
    )


def solution(mesh):
    in_specs = (
        P(None, None, "sensor", "cell"),
        P(None, "sensor"),
        P(None, "cell"),
        P(None, None, "cell"),
        P(None, "cell"),
        P("cell"),
        P(),
    )
    out_specs = (P(None, "cell"), P(None, None, "cell"), P(None, None, "cell"))
    return jax.shard_map(
        per_device, mesh=mesh, in_specs=in_specs, out_specs=out_specs, check_vma=False
    )
```

```python
import functools

import jax
import jax.numpy as jnp
import numpy as np
from jax import lax
from jax.experimental import pallas as pl
from jax.experimental.pallas import tpu as pltpu
from jax.sharding import PartitionSpec as P

COLS = 128
LANES = 128
GROUP = 8
SHRINK_SCALE = 0.4
TINY = 1e-06
VMEM = pltpu.VMEM
HBM = pltpu.HBM


def tables(times, freqs):
    padded = 2 * times
    groups = -(-freqs // GROUP)
    plain = np.zeros((16 * groups, times), np.float64)
    weighted = np.zeros((16 * groups, times), np.float64)
    for f in range(freqs):
        phase = 2.0 * np.pi * ((f * np.arange(times)) % padded) / padded
        weight = (1.0 if f in (0, freqs - 1) else 2.0) / padded
        row = 16 * (f // GROUP) + f % GROUP
        plain[row], plain[row + GROUP] = np.cos(phase), -np.sin(phase)
        weighted[row], weighted[row + GROUP] = weight * np.cos(phase), -weight * np.sin(phase)
    return plain.astype(np.float32), weighted.astype(np.float32)


def exact(left, right):
    return jnp.dot(left, right, precision=lax.Precision.HIGHEST, preferred_element_type=jnp.float32)


def turned(rows):
    return jnp.concatenate([-rows[GROUP:], rows[:GROUP]], axis=0)


def dot_nt(left, right):
    return lax.dot_general(left, right, (((1,), (1,)), ((), ())), preferred_element_type=jnp.float32)


def dot_nn(left, right):
    return jnp.dot(left, right, preferred_element_type=jnp.float32)


def slab(kernel_ref, part, group):
    freqs, sensors, cells = kernel_ref.shape[1:]
    count = min(GROUP, freqs - group * GROUP)
    block = kernel_ref[part, group * GROUP : group * GROUP + count]
    return block.reshape(count * sensors, cells)


def own_block(width, sensors):
    row = lax.broadcasted_iota(jnp.int32, (16, width), 0) % GROUP
    lane = lax.broadcasted_iota(jnp.int32, (16, width), 1) // sensors
    return row == lane


def fold(wide):
    total = functools.reduce(
        lambda a, b: a + b, [wide[:, i : i + LANES] for i in range(0, wide.shape[1], LANES)]
    )
    return total + pltpu.roll(total, LANES // 2, 1)


def forward(field, kernel_ref, plain, weighted_t, arrived=None):
    freqs, sensors = kernel_ref.shape[1:3]
    times = field.shape[0]
    spectra = exact(plain, field)
    rows = []
    for group in range(plain.shape[0] // 16):
        part = spectra[16 * group : 16 * group + 16]
        if arrived is not None:
            arrived(group)
        re_slab, im_slab = slab(kernel_ref, 0, group), slab(kernel_ref, 1, group)
        out = dot_nt(part.astype(jnp.bfloat16), re_slab) + dot_nt(turned(part).astype(jnp.bfloat16), im_slab)
        width = out.shape[1]
        out = jnp.where(own_block(width, sensors), out, 0.0)
        if width < LANES:
            out = jnp.concatenate([out, jnp.zeros((16, LANES - width), jnp.float32)], axis=1)
        rows.append(fold(out))
    series = exact(weighted_t, jnp.concatenate(rows, axis=0))
    left = lax.broadcasted_iota(jnp.int32, (times // 2, LANES), 1) < sensors
    return jnp.where(left, series[: times // 2], series[times // 2 :])


def unpacked(packed, sensors):
    other = pltpu.roll(packed, sensors, 1)
    left = lax.broadcasted_iota(jnp.int32, packed.shape, 1) < sensors
    return jnp.concatenate([jnp.where(left, packed, other), jnp.where(left, other, packed)], axis=0)


def adjoint(residual, kernel_ref, plain_t, weighted, halves):
    freqs, sensors, cells = kernel_ref.shape[1:]
    spectra = exact(weighted, residual)
    rows = []
    for group in range(weighted.shape[0] // 16):
        part = spectra[16 * group : 16 * group + 16]
        count = min(GROUP, freqs - group * GROUP)
        width = count * sensors
        re_slab, im_slab = slab(kernel_ref, 0, group), slab(kernel_ref, 1, group)
        wide = jnp.concatenate([part] * (-(-width // LANES)), axis=1)[:, :width]
        wide = jnp.where(own_block(width, sensors), wide, 0.0)
        total = None
        for _ in range(halves):
            re_left = wide.astype(jnp.bfloat16)
            rounded = re_left.astype(jnp.float32)
            out = dot_nn(re_left, re_slab) - dot_nn(turned(rounded).astype(jnp.bfloat16), im_slab)
            total = out if total is None else total + out
            wide = wide - rounded
        rows.append(total)
    return exact(plain_t, jnp.concatenate(rows, axis=0))


def strip(array, row):
    return array[..., row * COLS : (row + 1) * COLS]


def jumps(field, above, below, linked):
    count = field.shape[1] // COLS
    out = []
    for direction in range(4):
        strips = []
        for row in range(count):
            here = strip(field, row)
            if direction == 0:
                there = pltpu.roll(here, COLS - 1, 1)
            elif direction == 1:
                there = pltpu.roll(here, 1, 1)
            elif direction == 2:
                there = above if row == 0 else strip(field, row - 1)
            else:
                there = below if row == count - 1 else strip(field, row + 1)
            strips.append(strip(linked[direction : direction + 1], row) * (there - here))
        out.append(strips)
    return out


def gathered_jumps(values, above, below, linked):
    count = len(values[0])
    out = []
    for row in range(count):
        arriving = (
            pltpu.roll(values[1][row], COLS - 1, 1),
            pltpu.roll(values[0][row], 1, 1),
            above if row == 0 else values[3][row - 1],
            below if row == count - 1 else values[2][row + 1],
        )
        total = None
        for direction in range(4):
            term = strip(linked[direction : direction + 1], row) * (arriving[direction] - values[direction][row])
            total = term if total is None else total + term
        out.append(total)
    return jnp.concatenate(out, axis=1)


def shrunk(shifted, threshold):
    return shifted - jnp.clip(shifted, -threshold, threshold)


def tree_sum(parts):
    parts = list(parts)
    while len(parts) > 1:
        parts = [parts[i] + parts[i + 1] if i + 1 < len(parts) else parts[i] for i in range(0, len(parts), 2)]
    return parts[0]


def square_sum(array):
    return jnp.sum(array * array)


def block_of(scalar, rows=8):
    return jnp.full((rows, LANES), scalar, jnp.float32)


def call(body, out_shapes, *operands, scratch=(), inputs=None):
    single = isinstance(out_shapes, tuple)
    shapes = [out_shapes] if single else list(out_shapes)
    shapes = [s if isinstance(s, jax.ShapeDtypeStruct) else jax.ShapeDtypeStruct(s, jnp.float32) for s in shapes]
    out = pl.pallas_call(
        body,
        out_shape=shapes,
        in_specs=[pl.BlockSpec(memory_space=space) for space in inputs or [VMEM] * len(operands)],
        out_specs=[pl.BlockSpec(memory_space=VMEM)] * len(shapes),
        scratch_shapes=list(scratch),
        compiler_params=pltpu.CompilerParams(vmem_limit_bytes=24 * 2**20),
    )(*operands)
    return out[0] if single else out


def first_forward_body(
    field, kernel, start_multiplier, neighbours, tile_of_cell, tile_weight, plain, weighted_t,
    out, kept, above, below, threshold, linked,
    field_here, plain_here, weighted_here, neighbours_here, tiles_here, sems,
):
    freqs = kernel.shape[1]
    times, cells = field.shape
    copies = []

    def load(source, target):
        copy = pltpu.make_async_copy(source, target, sems.at[len(copies)])
        copy.start()
        copies.append(copy)
        return copy

    first = [load(field, field_here), load(plain, plain_here), load(weighted_t, weighted_here)]
    head, tail = pl.ds(0, COLS), pl.ds(cells - COLS, COLS)
    rows, more = pl.ds(0, times), pl.ds(times, times)
    small = [load(neighbours, neighbours_here), load(tile_of_cell, tiles_here)]
    small += [load(field.at[:, tail], above.at[rows]), load(field.at[:, head], below.at[rows])]
    small += [load(start_multiplier.at[3, :, tail], above.at[more])]
    small += [load(start_multiplier.at[2, :, head], below.at[more])]
    large = []
    for group in range(plain.shape[0] // 16):
        start = group * GROUP
        for part in range(2):
            at = (part, pl.ds(start, min(GROUP, freqs - start)))
            large.append(load(kernel.at[at], kept.at[at]))

    for copy in first:
        copy.wait()

    def arrived(group):
        large[2 * group].wait()
        large[2 * group + 1].wait()

    out[...] = forward(field_here[...], kept, plain_here[...], weighted_here[...], arrived)

    for copy in small:
        copy.wait()
    cell = lax.broadcasted_iota(jnp.int32, (4, cells), 1) + lax.axis_index("cell") * cells
    linked[0:4, :] = jnp.where(neighbours_here[...] != cell, 1.0, 0.0)
    linked[4:8, :] = jnp.zeros((4, cells), jnp.float32)
    tiles = jnp.broadcast_to(tiles_here[...], (8, cells))
    weights = jnp.zeros((8, cells), jnp.float32)
    for tile in range(tile_weight.shape[0]):
        weights = jnp.where(tiles == tile, tile_weight[tile], weights)
    limit = SHRINK_SCALE * weights
    threshold[...] = limit
    above[2 * times :, :] = limit[:, cells - COLS :]
    below[2 * times :, :] = limit[:, :COLS]


def forward_body(field, kernel, plain, weighted_t, out):
    out[...] = forward(field[...], kernel, plain[...], weighted_t[...])


def summed(parts):
    return tree_sum([part[...] for part in parts])


def first_adjoint_body(count, *refs):
    observed, kernel, plain_t, weighted, out = refs[count:]
    predicted = unpacked(summed(refs[:count]), kernel.shape[2])
    out[...] = adjoint(predicted - observed[...], kernel, plain_t[...], weighted[...], 1)


def edge_rows(field, first, last):
    first[...] = strip(field, 0)
    last[...] = strip(field, field.shape[1] // COLS - 1)


def first_gradient_body(count, *refs):
    start_multiplier, above, below, linked, adjoint_out, gradient, first, last = refs[count:]
    times, cells = adjoint_out.shape
    total = summed(refs[:count])
    values = [[strip(start_multiplier[k], r) for r in range(cells // COLS)] for k in range(4)]
    back = gathered_jumps(values, above[times : 2 * times], below[times : 2 * times], linked[...])
    adjoint_out[...] = total
    field = total + back
    gradient[...] = field
    edge_rows(field, first, last)


def norms_body(packed, gradient, above, linked, out):
    field = gradient[...]
    squares = []
    for row in range(field.shape[1] // COLS):
        here = strip(field, row)
        beside = above[...] if row == 0 else strip(field, row - 1)
        east = strip(linked[0:1], row) * (pltpu.roll(here, COLS - 1, 1) - here)
        north = strip(linked[2:3], row) * (beside - here)
        squares.append(east * east + north * north)
    half = packed.shape[0]
    out[:half, :] = packed[...]
    out[half : half + 8, :] = block_of(square_sum(field))
    out[half + 8 :, :] = block_of(2.0 * jnp.sum(tree_sum(squares)))


def second_adjoint_body(count, *refs):
    kernel, plain_t, weighted, out, norms = refs[count:]
    times = plain_t.shape[0]
    total = summed(refs[:count])
    packed = total[: times // 2]
    out[:times, :] = adjoint(unpacked(packed, kernel.shape[2]), kernel, plain_t[...], weighted[...], 2)
    out[times:, :] = jnp.full((out.shape[0] - times, out.shape[1]), square_sum(packed), jnp.float32)
    norms[...] = total[times // 2 :]


def second_gradient_body(count, *refs):
    (norms, adjoint_in, gradient_in, model, start_multiplier, threshold, above, below, grad_above, grad_below,
     linked_ref, model_out, jumps_out, multiplier_out, gradient_out, first, last) = refs[count:]
    times, cells = model.shape
    total = summed(refs[:count])
    step = norms[0, 0] / (total[times, 0] + norms[8, 0] + TINY)
    linked = linked_ref[...]
    field, gradient = model[...], gradient_in[...]
    rows = cells // COLS
    field_jumps = jumps(field, above[:times], below[:times], linked)
    grad_jumps = jumps(gradient, grad_above[...], grad_below[...], linked)

    def advance(model_jumps, old_multiplier, limit):
        shifted = model_jumps + old_multiplier
        auxiliary = shrunk(shifted, limit)
        multiplier = shifted - auxiliary
        return multiplier, model_jumps - auxiliary + multiplier

    penalties, new_jumps = [], []
    for k in range(4):
        penalties.append([])
        new_jumps.append([])
        for r in range(rows):
            new = field_jumps[k][r] - step * grad_jumps[k][r]
            multiplier, penalty = advance(new, strip(start_multiplier[k], r), strip(threshold[0:1], r))
            jumps_out[k, :, r * COLS : (r + 1) * COLS] = new
            multiplier_out[k, :, r * COLS : (r + 1) * COLS] = multiplier
            penalties[k].append(penalty)
            new_jumps[k].append(new)
    _, beside_above = advance(-new_jumps[2][0], above[times : 2 * times], above[2 * times : 2 * times + 1])
    _, beside_below = advance(-new_jumps[3][-1], below[times : 2 * times], below[2 * times : 2 * times + 1])
    back = gathered_jumps(penalties, beside_above, beside_below, linked)
    model_out[...] = field - step * gradient
    new_gradient = adjoint_in[...] - step * total[:times] + back
    gradient_out[...] = new_gradient
    edge_rows(new_gradient, first, last)


def response_body(count, *refs):
    out, norms = refs[count:]
    total = summed(refs[:count])
    half = total.shape[0] - 16
    out[...] = block_of(square_sum(total[:half]))
    norms[...] = total[half:]


def finish_body(count, *refs):
    (norms, gradient_in, model, model_jumps, multiplier, threshold, above, below, linked,
     estimate_out, auxiliary_out, multiplier_out) = refs[count:]
    step = norms[0, 0] / (summed(refs[:count])[0, 0] + norms[8, 0] + TINY)
    gradient = gradient_in[...]
    estimate_out[...] = model[...] - step * gradient
    grad_jumps = jumps(gradient, above[...], below[...], linked[...])
    for k in range(4):
        for r in range(gradient.shape[1] // COLS):
            at = slice(r * COLS, (r + 1) * COLS)
            shifted = model_jumps[k, :, at] - step * grad_jumps[k][r] + multiplier[k, :, at]
            auxiliary = shrunk(shifted, threshold[0:1, at])
            auxiliary_out[k, :, at] = auxiliary
            multiplier_out[k, :, at] = shifted - auxiliary


def parts_of(array, axis, *radices):
    count = lax.axis_size(axis)
    if count & (count - 1):
        return [lax.psum(array, axis)]
    stages, left = [], count
    for radix in radices:
        if left > 1 and left % radix == 0:
            stages.append(radix)
            left //= radix
    while left > 1:
        stages.append(2)
        left //= 2
    parts, stride = [array], 1
    for radix in stages:
        total = tree_sum(parts)
        parts = [total] + [
            lax.ppermute(total, axis, [(i, i ^ (k * stride)) for i in range(count)]) for k in range(1, radix)
        ]
        stride *= radix
    return parts


def from_above(last):
    count = lax.axis_size("cell")
    return lax.ppermute(last, "cell", [(i, i + 1) for i in range(count - 1)])


def from_below(first):
    count = lax.axis_size("cell")
    return lax.ppermute(first, "cell", [(i + 1, i) for i in range(count - 1)])


def per_device(kernel, observed, start_model, start_multiplier, neighbours, tile_of_cell, tile_weight):
    times, cells = start_model.shape
    freqs, sensors = kernel.shape[1:3]
    plain, weighted = tables(times, freqs)
    plain_t, weighted_t = jnp.asarray(plain.T.copy()), jnp.asarray(weighted.T.copy())
    plain, weighted = jnp.asarray(plain), jnp.asarray(weighted)
    observed_twice = jnp.concatenate([observed, observed], axis=1)
    half = times // 2
    packed, field, row, wide = (half, 2 * sensors), (times, cells), (times, COLS), (4, times, cells)

    part, kept, above, below, threshold, linked = call(
        first_forward_body,
        [packed, jax.ShapeDtypeStruct(kernel.shape, kernel.dtype), (2 * times + 8, COLS), (2 * times + 8, COLS),
         (8, cells), (8, cells)],
        start_model, kernel, start_multiplier, neighbours, tile_of_cell[None, :], tile_weight, plain, weighted_t,
        scratch=[
            VMEM(start_model.shape, jnp.float32), VMEM(plain.shape, jnp.float32), VMEM(weighted_t.shape, jnp.float32),
            VMEM(neighbours.shape, jnp.int32), VMEM((1, cells), jnp.int32),
            pltpu.SemaphoreType.DMA((9 + 2 * (plain.shape[0] // 16),)),
        ],
        inputs=[HBM] * 5 + [pltpu.SMEM] + [HBM] * 2,
    )
    parts = parts_of(part, "cell", 2, 2, 2)
    above, below = from_above(above), from_below(below)
    back = call(
        functools.partial(first_adjoint_body, len(parts)), field, *parts, observed_twice, kept, plain_t, weighted
    )
    parts = parts_of(back, "sensor", 2, 2)
    adjoint_one, gradient, edge_first, edge_last = call(
        functools.partial(first_gradient_body, len(parts)), [field, field, row, row],
        *parts, start_multiplier, above, below, linked,
    )

    def response_and_norms(gradient, edge_last, *radices):
        beside = from_above(edge_last)
        part = call(forward_body, packed, gradient, kept, plain, weighted_t)
        sent = call(norms_body, (half + 16, LANES), part, gradient, beside, linked)
        return parts_of(sent, "cell", *radices), beside

    parts, grad_above = response_and_norms(gradient, edge_last, 2, 4)
    grad_below = from_below(edge_first)
    back, norms = call(
        functools.partial(second_adjoint_body, len(parts)), [(times + 8, cells), (16, LANES)],
        *parts, kept, plain_t, weighted,
    )
    parts = parts_of(back, "sensor", 4)
    model, model_jumps, multiplier, gradient, edge_first, edge_last = call(
        functools.partial(second_gradient_body, len(parts)), [field, wide, wide, field, row, row],
        *parts, norms, adjoint_one, gradient, start_model, start_multiplier, threshold, above, below,
        grad_above, grad_below, linked,
    )
    parts, grad_above = response_and_norms(gradient, edge_last, 4, 2)
    grad_below = from_below(edge_first)
    square, norms = call(functools.partial(response_body, len(parts)), [(8, LANES), (16, LANES)], *parts)
    parts = parts_of(square, "sensor", 2, 2)
    return tuple(
        call(
            functools.partial(finish_body, len(parts)), [field, wide, wide],
            *parts, norms, gradient, model, model_jumps, multiplier, threshold, grad_above, grad_below, linked,
        )
    )


def solution(mesh):
    in_specs = (
        P(None, None, "sensor", "cell"),
        P(None, "sensor"),
        P(None, "cell"),
        P(None, None, "cell"),
        P(None, "cell"),
        P("cell"),
        P(),
    )
    out_specs = (P(None, "cell"), P(None, None, "cell"), P(None, None, "cell"))
    return jax.shard_map(
        per_device, mesh=mesh, in_specs=in_specs, out_specs=out_specs, check_vma=False
    )
```

```python
import functools

import jax
import jax.numpy as jnp
import numpy as np
from jax import lax
from jax.experimental import pallas as pl
from jax.experimental.pallas import tpu as pltpu
from jax.sharding import PartitionSpec as P

COLS = 128
LANES = 128
GROUP = 8
SHRINK_SCALE = 0.4
TINY = 1e-06
VMEM = pltpu.VMEM
HBM = pltpu.HBM


def tables(times, freqs):
    padded = 2 * times
    groups = -(-freqs // GROUP)
    plain = np.zeros((16 * groups, times), np.float64)
    weighted = np.zeros((16 * groups, times), np.float64)
    for f in range(freqs):
        phase = 2.0 * np.pi * ((f * np.arange(times)) % padded) / padded
        weight = (1.0 if f in (0, freqs - 1) else 2.0) / padded
        row = 16 * (f // GROUP) + f % GROUP
        plain[row], plain[row + GROUP] = np.cos(phase), -np.sin(phase)
        weighted[row], weighted[row + GROUP] = weight * np.cos(phase), -weight * np.sin(phase)
    return plain.astype(np.float32), weighted.astype(np.float32)


def exact(left, right):
    return jnp.dot(left, right, precision=lax.Precision.HIGHEST, preferred_element_type=jnp.float32)


def turned(rows):
    return jnp.concatenate([-rows[GROUP:], rows[:GROUP]], axis=0)


def dot_nt(left, right):
    return lax.dot_general(left, right, (((1,), (1,)), ((), ())), preferred_element_type=jnp.float32)


def dot_nn(left, right):
    return jnp.dot(left, right, preferred_element_type=jnp.float32)


def slab(kernel_ref, part, group):
    freqs, sensors, cells = kernel_ref.shape[1:]
    count = min(GROUP, freqs - group * GROUP)
    block = kernel_ref[part, group * GROUP : group * GROUP + count]
    return block.reshape(count * sensors, cells)


def own_block(width, sensors):
    row = lax.broadcasted_iota(jnp.int32, (16, width), 0) % GROUP
    lane = lax.broadcasted_iota(jnp.int32, (16, width), 1) // sensors
    return row == lane


def fold(wide):
    total = functools.reduce(
        lambda a, b: a + b, [wide[:, i : i + LANES] for i in range(0, wide.shape[1], LANES)]
    )
    return total + pltpu.roll(total, LANES // 2, 1)


def forward(field, kernel_ref, plain, weighted_t, arrived=None):
    freqs, sensors = kernel_ref.shape[1:3]
    times = field.shape[0]
    spectra = exact(plain, field)
    rows = []
    for group in range(plain.shape[0] // 16):
        part = spectra[16 * group : 16 * group + 16]
        if arrived is not None:
            arrived(group)
        re_slab, im_slab = slab(kernel_ref, 0, group), slab(kernel_ref, 1, group)
        out = dot_nt(part.astype(jnp.bfloat16), re_slab) + dot_nt(turned(part).astype(jnp.bfloat16), im_slab)
        width = out.shape[1]
        out = jnp.where(own_block(width, sensors), out, 0.0)
        if width < LANES:
            out = jnp.concatenate([out, jnp.zeros((16, LANES - width), jnp.float32)], axis=1)
        rows.append(fold(out))
    series = exact(weighted_t, jnp.concatenate(rows, axis=0))
    left = lax.broadcasted_iota(jnp.int32, (times // 2, LANES), 1) < sensors
    return jnp.where(left, series[: times // 2], series[times // 2 :])


def unpacked(packed, sensors):
    other = pltpu.roll(packed, sensors, 1)
    left = lax.broadcasted_iota(jnp.int32, packed.shape, 1) < sensors
    return jnp.concatenate([jnp.where(left, packed, other), jnp.where(left, other, packed)], axis=0)


def adjoint(residual, kernel_ref, plain_t, weighted, halves):
    freqs, sensors, cells = kernel_ref.shape[1:]
    spectra = exact(weighted, residual)
    rows = []
    for group in range(weighted.shape[0] // 16):
        part = spectra[16 * group : 16 * group + 16]
        count = min(GROUP, freqs - group * GROUP)
        width = count * sensors
        re_slab, im_slab = slab(kernel_ref, 0, group), slab(kernel_ref, 1, group)
        wide = jnp.concatenate([part] * (-(-width // LANES)), axis=1)[:, :width]
        wide = jnp.where(own_block(width, sensors), wide, 0.0)
        total = None
        for _ in range(halves):
            re_left = wide.astype(jnp.bfloat16)
            rounded = re_left.astype(jnp.float32)
            out = dot_nn(re_left, re_slab) - dot_nn(turned(rounded).astype(jnp.bfloat16), im_slab)
            total = out if total is None else total + out
            wide = wide - rounded
        rows.append(total)
    return exact(plain_t, jnp.concatenate(rows, axis=0))


def strip(array, row):
    return array[..., row * COLS : (row + 1) * COLS]


def jumps(field, above, below, linked):
    count = field.shape[1] // COLS
    out = []
    for direction in range(4):
        strips = []
        for row in range(count):
            here = strip(field, row)
            if direction == 0:
                there = pltpu.roll(here, COLS - 1, 1)
            elif direction == 1:
                there = pltpu.roll(here, 1, 1)
            elif direction == 2:
                there = above if row == 0 else strip(field, row - 1)
            else:
                there = below if row == count - 1 else strip(field, row + 1)
            strips.append(strip(linked[direction : direction + 1], row) * (there - here))
        out.append(strips)
    return out


def gathered_jumps(values, above, below, linked):
    count = len(values[0])
    out = []
    for row in range(count):
        arriving = (
            pltpu.roll(values[1][row], COLS - 1, 1),
            pltpu.roll(values[0][row], 1, 1),
            above if row == 0 else values[3][row - 1],
            below if row == count - 1 else values[2][row + 1],
        )
        total = None
        for direction in range(4):
            term = strip(linked[direction : direction + 1], row) * (arriving[direction] - values[direction][row])
            total = term if total is None else total + term
        out.append(total)
    return jnp.concatenate(out, axis=1)


def shrunk(shifted, threshold):
    return shifted - jnp.clip(shifted, -threshold, threshold)


def tree_sum(parts):
    parts = list(parts)
    while len(parts) > 1:
        parts = [parts[i] + parts[i + 1] if i + 1 < len(parts) else parts[i] for i in range(0, len(parts), 2)]
    return parts[0]


def square_sum(array):
    return jnp.sum(array * array)


def block_of(scalar, rows=8):
    return jnp.full((rows, LANES), scalar, jnp.float32)


def call(body, out_shapes, *operands, scratch=(), inputs=VMEM):
    single = isinstance(out_shapes, tuple)
    shapes = [out_shapes] if single else list(out_shapes)
    shapes = [s if isinstance(s, jax.ShapeDtypeStruct) else jax.ShapeDtypeStruct(s, jnp.float32) for s in shapes]
    out = pl.pallas_call(
        body,
        out_shape=shapes,
        in_specs=[pl.BlockSpec(memory_space=inputs)] * len(operands),
        out_specs=[pl.BlockSpec(memory_space=VMEM)] * len(shapes),
        scratch_shapes=list(scratch),
        compiler_params=pltpu.CompilerParams(vmem_limit_bytes=24 * 2**20),
    )(*operands)
    return out[0] if single else out


def summed(parts):
    return tree_sum([part[...] for part in parts])


def below_first():
    return lax.rem(lax.axis_index("cell") + lax.axis_index("sensor"), 2) == 0


def edges(head, tail):
    first = below_first()
    return jnp.where(first, tail, head), jnp.where(first, head, tail)


def beside(hop_one, hop_two):
    first = below_first()
    return jnp.where(first, hop_two, hop_one), jnp.where(first, hop_one, hop_two)


def rows_of(scalars):
    row = lax.broadcasted_iota(jnp.int32, (8, LANES), 0)
    out = jnp.zeros((8, LANES), jnp.float32)
    for i, scalar in enumerate(scalars):
        out = jnp.where(row == i, scalar, out)
    return out


def first_forward_body(*refs):
    loaded, (sent, edge, threshold, linked), kept, sems = refs[:10], refs[10:14], refs[14:24], refs[24]
    kernel, kernel_here = loaded[0], kept[0]
    field, multiplier, neighbours, tile_of_cell, tile_weight, plain, weighted_t = kept[1:8]
    freqs = kernel.shape[1]
    times, cells = field.shape
    copies = []

    def load(source, target):
        copy = pltpu.make_async_copy(source, target, sems.at[len(copies)])
        copy.start()
        copies.append(copy)
        return copy

    early = [load(loaded[i], kept[i]) for i in (1, 6, 7)]
    small = [load(loaded[i], kept[i]) for i in (3, 4, 5, 2)]
    large = []
    for group in range(plain.shape[0] // 16):
        start = group * GROUP
        for part in range(2):
            at = (part, pl.ds(start, min(GROUP, freqs - start)))
            large.append(load(kernel.at[at], kernel_here.at[at]))
    late = [load(loaded[i], kept[i]) for i in (8, 9)]

    for copy in early:
        copy.wait()

    def arrived(group):
        large[2 * group].wait()
        large[2 * group + 1].wait()

    half = times // 2
    sent[:half, :] = forward(field[...], kernel_here, plain[...], weighted_t[...], arrived)

    for copy in small:
        copy.wait()
    cell = lax.broadcasted_iota(jnp.int32, (4, cells), 1) + lax.axis_index("cell") * cells
    linked[0:4, :] = jnp.where(neighbours[...] != cell, 1.0, 0.0)
    linked[4:8, :] = jnp.zeros((4, cells), jnp.float32)
    tiles = jnp.broadcast_to(tile_of_cell[...], (8, cells))
    weights = jnp.zeros((8, cells), jnp.float32)
    for tile in range(tile_weight.shape[1]):
        weight = jnp.broadcast_to(tile_weight[0:1, tile : tile + 1], (8, cells))
        weights = jnp.where(tiles == tile, weight, weights)
    limit = SHRINK_SCALE * weights
    threshold[...] = limit
    bottom = cells // COLS - 1
    pairs = (
        (strip(field, 0), strip(field, bottom)),
        (strip(multiplier[2], 0), strip(multiplier[3], bottom)),
        (strip(limit, 0), strip(limit, bottom)),
    )
    for (head, tail), start in zip(pairs, (0, times, 2 * times)):
        one, two = edges(head, tail)
        sent[half + start : half + start + head.shape[0], :] = one
        edge[start : start + head.shape[0], :] = two
    for copy in late:
        copy.wait()


def first_merge_body(sent, came, edge, out):
    half = sent.shape[0] - edge.shape[0]
    out[:half, :] = sent[:half, :] + came[:half, :]
    out[half:, :] = edge[...]


def first_adjoint_body(count, *refs):
    observed, kernel, plain_t, weighted, out = refs[count:]
    predicted = unpacked(summed(refs[:count]), kernel.shape[2])
    residual = predicted - jnp.concatenate([observed[...], observed[...]], axis=1)
    out[...] = adjoint(residual, kernel, plain_t[...], weighted[...], 1)


def response_of(field, kernel, plain, weighted_t, linked, sent, edge):
    half = field.shape[0] // 2
    rows = field.shape[1] // COLS
    one, two = edges(strip(field, 0), strip(field, rows - 1))
    squares = []
    for row in range(rows):
        here = strip(field, row)
        east = strip(linked[0:1], row) * (pltpu.roll(here, COLS - 1, 1) - here)
        squares.append(east * east)
        if row > 0:
            north = strip(linked[2:3], row) * (strip(field, row - 1) - here)
            squares.append(north * north)
    sent[:half, :] = forward(field, kernel, plain[...], weighted_t[...])
    sent[half : half + 8, :] = rows_of([square_sum(field), 2.0 * jnp.sum(tree_sum(squares))])
    sent[half + 8 :, :] = one
    edge[...] = two


def merge_body(sent, came, edge, linked, out):
    cells = linked.shape[1]
    top = sent.shape[0] - edge.shape[0]
    mask = jnp.where(below_first(), linked[3:4, cells - COLS :], linked[2:3, :COLS])
    across = mask * (came[top:, :] - sent[top:, :])
    out[: top - 8, :] = sent[: top - 8, :] + came[: top - 8, :]
    out[top - 8 : top, :] = (
        sent[top - 8 : top, :] + came[top - 8 : top, :] + rows_of([0.0, 0.0, 2.0 * square_sum(across)])
    )
    out[top:, :] = edge[...]


def first_gradient_body(count, *refs):
    (start_multiplier, one, two, linked_ref, kernel, plain, weighted_t,
     adjoint_out, gradient, sent, edge) = refs[count:]
    times, cells = adjoint_out.shape
    half = times // 2
    linked = linked_ref[...]
    total = summed(refs[:count])
    values = [[strip(start_multiplier[k], r) for r in range(cells // COLS)] for k in range(4)]
    above, below = beside(one[half + times : half + 2 * times, :], two[half + times : half + 2 * times, :])
    field = total + gathered_jumps(values, above, below, linked)
    adjoint_out[...] = total
    gradient[...] = field
    response_of(field, kernel, plain, weighted_t, linked, sent, edge)


def second_adjoint_body(count, *refs):
    kernel, plain_t, weighted, out, norms = refs[count:]
    times = plain_t.shape[0]
    half = times // 2
    total = summed(refs[:count])
    packed, squares = total[:half], total[half : half + 8]
    out[:times, :] = adjoint(unpacked(packed, kernel.shape[2]), kernel, plain_t[...], weighted[...], 2)
    across = squares[2:3, :] * (2.0 / lax.axis_size("sensor"))
    scalars = rows_of([square_sum(packed), across])
    out[times:, :] = jnp.concatenate([scalars] * (out.shape[1] // LANES), axis=1)
    norms[...] = squares


def step_of(norms, scalars):
    return norms[0, 0] / (scalars[0, 0] + (norms[1, 0] + scalars[1, 0]) + TINY)


def second_gradient_body(count, *refs):
    (norms, adjoint_in, gradient_in, model, start_multiplier, threshold, one, two, grad_one, grad_two, linked_ref,
     kernel, plain, weighted_t, model_out, jumps_out, multiplier_out, gradient_out, sent, edge) = refs[count:]
    times, cells = model.shape
    half = times // 2
    total = summed(refs[:count])
    step = step_of(norms, total[times:])
    linked = linked_ref[...]
    field, gradient = model[...], gradient_in[...]
    rows = cells // COLS
    above, below = beside(one[half:, :], two[half:, :])
    field_jumps = jumps(field, above[:times], below[:times], linked)
    grad_jumps = jumps(gradient, *beside(grad_one[half + 8 :, :], grad_two[half + 8 :, :]), linked)

    def advance(model_jumps, old_multiplier, limit):
        shifted = model_jumps + old_multiplier
        auxiliary = shrunk(shifted, limit)
        multiplier = shifted - auxiliary
        return multiplier, model_jumps - auxiliary + multiplier

    penalties, new_jumps = [], []
    for k in range(4):
        penalties.append([])
        new_jumps.append([])
        for r in range(rows):
            new = field_jumps[k][r] - step * grad_jumps[k][r]
            multiplier, penalty = advance(new, strip(start_multiplier[k], r), strip(threshold[0:1], r))
            jumps_out[k, :, r * COLS : (r + 1) * COLS] = new
            multiplier_out[k, :, r * COLS : (r + 1) * COLS] = multiplier
            penalties[k].append(penalty)
            new_jumps[k].append(new)
    _, beside_above = advance(-new_jumps[2][0], above[times : 2 * times], above[2 * times : 2 * times + 1])
    _, beside_below = advance(-new_jumps[3][-1], below[times : 2 * times], below[2 * times : 2 * times + 1])
    back = gathered_jumps(penalties, beside_above, beside_below, linked)
    model_out[...] = field - step * gradient
    new_gradient = adjoint_in[...] - step * total[:times] + back
    gradient_out[...] = new_gradient
    response_of(new_gradient, kernel, plain, weighted_t, linked, sent, edge)


def response_body(count, *refs):
    out, norms = refs[count:]
    total = summed(refs[:count])
    packed, squares = total[:-8], total[-8:]
    out[...] = rows_of([square_sum(packed), squares[2:3, :] * (2.0 / lax.axis_size("sensor"))])
    norms[...] = squares


def finish_body(count, *refs):
    (norms, gradient_in, model, model_jumps, multiplier, threshold, grad_one, grad_two, linked,
     estimate_out, auxiliary_out, multiplier_out) = refs[count:]
    step = step_of(norms, summed(refs[:count]))
    half = gradient_in.shape[0] // 2
    gradient = gradient_in[...]
    estimate_out[...] = model[...] - step * gradient
    grad_jumps = jumps(gradient, *beside(grad_one[half + 8 :, :], grad_two[half + 8 :, :]), linked[...])
    for k in range(4):
        for r in range(gradient.shape[1] // COLS):
            at = slice(r * COLS, (r + 1) * COLS)
            shifted = model_jumps[k, :, at] - step * grad_jumps[k][r] + multiplier[k, :, at]
            auxiliary = shrunk(shifted, threshold[0:1, at])
            auxiliary_out[k, :, at] = auxiliary
            multiplier_out[k, :, at] = shifted - auxiliary


def sensor_parts(array, *radices):
    count = lax.axis_size("sensor")
    stages, left = [], count
    for radix in radices:
        if left > 1 and left % radix == 0:
            stages.append(radix)
            left //= radix
    while left > 1:
        stages.append(2)
        left //= 2
    parts, stride = [array], 1
    for radix in stages:
        total = tree_sum(parts)
        parts = [total] + [
            lax.ppermute(total, "sensor", [(i, i ^ (k * stride)) for i in range(count)]) for k in range(1, radix)
        ]
        stride *= radix
    return parts


def neighbour_hop(array, second):
    cells, sensors = lax.axis_size("cell"), lax.axis_size("sensor")
    pairs = []
    for cell in range(cells):
        for sensor in range(sensors):
            down = ((cell + sensor) % 2 == 0) != second
            other = (cell + (1 if down else -1)) % cells
            pairs.append((cell * sensors + sensor, other * sensors + sensor))
    return lax.ppermute(array, ("cell", "sensor"), pairs)


def cell_parts(sent, merge, rows):
    one = neighbour_hop(sent, False)
    sent = merge(one)
    two = neighbour_hop(sent, True)
    parts = [sent[:rows], two[:rows]]
    count, shift = lax.axis_size("cell"), 4
    while shift < count:
        total = parts[0] + parts[1]
        parts = [total, lax.ppermute(total, "cell", [((i + shift) % count, i) for i in range(count)])]
        shift *= 2
    return parts, one, two


def per_device(kernel, observed, start_model, start_multiplier, neighbours, tile_of_cell, tile_weight):
    times, cells = start_model.shape
    freqs, sensors = kernel.shape[1:3]
    plain, weighted = tables(times, freqs)
    half = times // 2
    field, row, wide = (times, cells), (times, COLS), (4, times, cells)

    loads = [
        kernel, start_model, start_multiplier, neighbours, tile_of_cell[None, :], tile_weight[None, :],
        jnp.asarray(plain), jnp.asarray(weighted.T.copy()), jnp.asarray(plain.T.copy()), jnp.asarray(weighted),
    ]
    sent, edge, threshold, linked, kernel, start_model, start_multiplier, _, _, _, plain, weighted_t, plain_t, weighted = call(
        first_forward_body,
        [(half + 2 * times + 8, LANES), (2 * times + 8, LANES), (8, cells), (8, cells)]
        + [jax.ShapeDtypeStruct(a.shape, a.dtype) for a in loads],
        *[pltpu.with_memory_space_constraint(a, HBM) for a in loads],
        scratch=[pltpu.SemaphoreType.DMA((9 + 2 * (plain.shape[0] // 16),))],
        inputs=HBM,
    )
    parts, one, two = cell_parts(
        sent, lambda came: call(first_merge_body, (half + 2 * times + 8, LANES), sent, came, edge), half
    )
    back = call(functools.partial(first_adjoint_body, len(parts)), field, *parts, observed, kernel, plain_t, weighted)
    parts = sensor_parts(back, 2, 2)
    message, side = (half + 8 + times, LANES), (times, LANES)
    adjoint_one, gradient, sent, edge = call(
        functools.partial(first_gradient_body, len(parts)), [field, field, message, side],
        *parts, start_multiplier, one, two, linked, kernel, plain, weighted_t,
    )
    parts, grad_one, grad_two = cell_parts(
        sent, lambda came: call(merge_body, message, sent, came, edge, linked), half + 8
    )
    back, norms = call(
        functools.partial(second_adjoint_body, len(parts)), [(times + 8, cells), (8, LANES)],
        *parts, kernel, plain_t, weighted,
    )
    parts = sensor_parts(back, 4)
    model, model_jumps, multiplier, gradient, sent, edge = call(
        functools.partial(second_gradient_body, len(parts)), [field, wide, wide, field, message, side],
        *parts, norms, adjoint_one, gradient, start_model, start_multiplier, threshold, one, two, grad_one, grad_two,
        linked, kernel, plain, weighted_t,
    )
    parts, grad_one, grad_two = cell_parts(
        sent, lambda came: call(merge_body, message, sent, came, edge, linked), half + 8
    )
    square, norms = call(functools.partial(response_body, len(parts)), [(8, LANES), (8, LANES)], *parts)
    parts = sensor_parts(square, 2, 2)
    return tuple(
        call(
            functools.partial(finish_body, len(parts)), [field, wide, wide],
            *parts, norms, gradient, model, model_jumps, multiplier, threshold, grad_one, grad_two, linked,
        )
    )


def solution(mesh):
    in_specs = (
        P(None, None, "sensor", "cell"),
        P(None, "sensor"),
        P(None, "cell"),
        P(None, None, "cell"),
        P(None, "cell"),
        P("cell"),
        P(),
    )
    out_specs = (P(None, "cell"), P(None, None, "cell"), P(None, None, "cell"))
    return jax.shard_map(
        per_device, mesh=mesh, in_specs=in_specs, out_specs=out_specs, check_vma=False
    )
```

```python
import functools

import jax
import jax.numpy as jnp
import numpy as np
from jax import lax
from jax.experimental import pallas as pl
from jax.experimental.pallas import tpu as pltpu
from jax.sharding import PartitionSpec as P

COLS = 128
LANES = 128
GROUP = 8
CHUNK = 16
SHRINK_SCALE = 0.4
TINY = 1e-06
VMEM = pltpu.VMEM
HBM = pltpu.HBM


def tables(times, freqs):
    padded = 2 * times
    groups = -(-freqs // GROUP)
    plain = np.zeros((16 * groups, times), np.float64)
    weighted = np.zeros((16 * groups, times), np.float64)
    for f in range(freqs):
        phase = 2.0 * np.pi * ((f * np.arange(times)) % padded) / padded
        weight = (1.0 if f in (0, freqs - 1) else 2.0) / padded
        row = 16 * (f // GROUP) + f % GROUP
        plain[row], plain[row + GROUP] = np.cos(phase), -np.sin(phase)
        weighted[row], weighted[row + GROUP] = weight * np.cos(phase), -weight * np.sin(phase)
    return plain.astype(np.float32), weighted.astype(np.float32)


def exact(left, right):
    return jnp.dot(left, right, precision=lax.Precision.HIGHEST, preferred_element_type=jnp.float32)


def turned(rows):
    return jnp.concatenate([-rows[GROUP:], rows[:GROUP]], axis=0)


def dot_nt(left, right):
    return lax.dot_general(left, right, (((1,), (1,)), ((), ())), preferred_element_type=jnp.float32)


def dot_nn(left, right):
    return jnp.dot(left, right, preferred_element_type=jnp.float32)


def slab(kernel_ref, part, group):
    freqs, sensors, cells = kernel_ref.shape[1:]
    count = min(GROUP, freqs - group * GROUP)
    block = kernel_ref[part, group * GROUP : group * GROUP + count]
    return block.reshape(count * sensors, cells)


def own_block(width, sensors):
    row = lax.broadcasted_iota(jnp.int32, (16, width), 0) % GROUP
    lane = lax.broadcasted_iota(jnp.int32, (16, width), 1) // sensors
    return row == lane


def fold(wide):
    total = functools.reduce(
        lambda a, b: a + b, [wide[:, i : i + LANES] for i in range(0, wide.shape[1], LANES)]
    )
    return total + pltpu.roll(total, LANES // 2, 1)


def forward(field, kernel_ref, plain, weighted_t):
    return forward_of(exact(plain, field), kernel_ref, weighted_t, field.shape[0])


def forward_of(spectra, kernel_ref, weighted_t, times, arrived=None):
    freqs, sensors = kernel_ref.shape[1:3]
    rows = []
    for group in range(spectra.shape[0] // 16):
        part = spectra[16 * group : 16 * group + 16]
        if arrived is not None:
            arrived(group)
        re_slab, im_slab = slab(kernel_ref, 0, group), slab(kernel_ref, 1, group)
        out = dot_nt(part.astype(jnp.bfloat16), re_slab) + dot_nt(turned(part).astype(jnp.bfloat16), im_slab)
        width = out.shape[1]
        out = jnp.where(own_block(width, sensors), out, 0.0)
        if width < LANES:
            out = jnp.concatenate([out, jnp.zeros((16, LANES - width), jnp.float32)], axis=1)
        rows.append(fold(out))
    series = exact(weighted_t, jnp.concatenate(rows, axis=0))
    left = lax.broadcasted_iota(jnp.int32, (times // 2, LANES), 1) < sensors
    return jnp.where(left, series[: times // 2], series[times // 2 :])


def unpacked(packed, sensors):
    other = pltpu.roll(packed, sensors, 1)
    left = lax.broadcasted_iota(jnp.int32, packed.shape, 1) < sensors
    return jnp.concatenate([jnp.where(left, packed, other), jnp.where(left, other, packed)], axis=0)


def adjoint(residual, kernel_ref, plain_t, weighted, halves):
    freqs, sensors, cells = kernel_ref.shape[1:]
    spectra = exact(weighted, residual)
    rows = []
    for group in range(weighted.shape[0] // 16):
        part = spectra[16 * group : 16 * group + 16]
        count = min(GROUP, freqs - group * GROUP)
        width = count * sensors
        re_slab, im_slab = slab(kernel_ref, 0, group), slab(kernel_ref, 1, group)
        wide = jnp.concatenate([part] * (-(-width // LANES)), axis=1)[:, :width]
        wide = jnp.where(own_block(width, sensors), wide, 0.0)
        total = None
        for _ in range(halves):
            re_left = wide.astype(jnp.bfloat16)
            rounded = re_left.astype(jnp.float32)
            out = dot_nn(re_left, re_slab) - dot_nn(turned(rounded).astype(jnp.bfloat16), im_slab)
            total = out if total is None else total + out
            wide = wide - rounded
        rows.append(total)
    return exact(plain_t, jnp.concatenate(rows, axis=0))


def strip(array, row):
    return array[..., row * COLS : (row + 1) * COLS]


def jumps(field, above, below, linked):
    count = field.shape[1] // COLS
    out = []
    for direction in range(4):
        strips = []
        for row in range(count):
            here = strip(field, row)
            if direction == 0:
                there = pltpu.roll(here, COLS - 1, 1)
            elif direction == 1:
                there = pltpu.roll(here, 1, 1)
            elif direction == 2:
                there = above if row == 0 else strip(field, row - 1)
            else:
                there = below if row == count - 1 else strip(field, row + 1)
            strips.append(strip(linked[direction : direction + 1], row) * (there - here))
        out.append(strips)
    return out


def gathered_jumps(values, above, below, linked):
    count = len(values[0])
    out = []
    for row in range(count):
        arriving = (
            pltpu.roll(values[1][row], COLS - 1, 1),
            pltpu.roll(values[0][row], 1, 1),
            above if row == 0 else values[3][row - 1],
            below if row == count - 1 else values[2][row + 1],
        )
        total = None
        for direction in range(4):
            term = strip(linked[direction : direction + 1], row) * (arriving[direction] - values[direction][row])
            total = term if total is None else total + term
        out.append(total)
    return jnp.concatenate(out, axis=1)


def shrunk(shifted, threshold):
    return shifted - jnp.clip(shifted, -threshold, threshold)


def tree_sum(parts):
    parts = list(parts)
    while len(parts) > 1:
        parts = [parts[i] + parts[i + 1] if i + 1 < len(parts) else parts[i] for i in range(0, len(parts), 2)]
    return parts[0]


def square_sum(array):
    return jnp.sum(array * array)


def block_of(scalar, rows=8):
    return jnp.full((rows, LANES), scalar, jnp.float32)


def call(body, out_shapes, *operands, scratch=(), inputs=VMEM):
    single = isinstance(out_shapes, tuple)
    shapes = [out_shapes] if single else list(out_shapes)
    shapes = [s if isinstance(s, jax.ShapeDtypeStruct) else jax.ShapeDtypeStruct(s, jnp.float32) for s in shapes]
    out = pl.pallas_call(
        body,
        out_shape=shapes,
        in_specs=[pl.BlockSpec(memory_space=inputs)] * len(operands),
        out_specs=[pl.BlockSpec(memory_space=VMEM)] * len(shapes),
        scratch_shapes=list(scratch),
        compiler_params=pltpu.CompilerParams(vmem_limit_bytes=24 * 2**20),
    )(*operands)
    return out[0] if single else out


def summed(parts):
    return tree_sum([part[...] for part in parts])


def is_even():
    return lax.rem(lax.axis_index("cell"), 2) == 0


def edges(head, tail):
    even = is_even()
    return jnp.where(even, tail, head), jnp.where(even, head, tail)


def beside(partner, other):
    even = is_even()
    return jnp.where(even, other, partner), jnp.where(even, partner, other)


def rows_of(scalars):
    row = lax.broadcasted_iota(jnp.int32, (8, LANES), 0)
    out = jnp.zeros((8, LANES), jnp.float32)
    for i, scalar in enumerate(scalars):
        out = jnp.where(row == i, scalar, out)
    return out


def first_forward_body(*refs):
    loaded, (sent, edge, threshold, linked), kept, sems = refs[:10], refs[10:14], refs[14:24], refs[24]
    kernel, kernel_here = loaded[0], kept[0]
    field, multiplier, neighbours, tile_of_cell, tile_weight, plain, weighted_t = kept[1:8]
    freqs = kernel.shape[1]
    times, cells = field.shape
    half = times // 2
    copies = []

    def load(source, target):
        copy = pltpu.make_async_copy(source, target, sems.at[len(copies)])
        copy.start()
        copies.append(copy)
        return copy

    early = [load(loaded[i], kept[i]) for i in (1, 6)]
    large = []
    for start in range(0, freqs, CHUNK):
        at = (slice(None), pl.ds(start, min(CHUNK, freqs - start)))
        large.append(load(kernel.at[at], kernel_here.at[at]))
    small = [load(loaded[i], kept[i]) for i in (3, 4, 5, 2, 7, 8, 9)]
    for copy in early:
        copy.wait()
    spectra = exact(plain[...], field[...])
    for copy in small:
        copy.wait()

    cell = lax.broadcasted_iota(jnp.int32, (4, cells), 1) + lax.axis_index("cell") * cells
    linked[0:4, :] = jnp.where(neighbours[...] != cell, 1.0, 0.0)
    linked[4:8, :] = jnp.zeros((4, cells), jnp.float32)
    tiles = jnp.broadcast_to(tile_of_cell[...], (8, cells))
    weights = jnp.zeros((8, cells), jnp.float32)
    for tile in range(tile_weight.shape[1]):
        weight = jnp.broadcast_to(tile_weight[0:1, tile : tile + 1], (8, cells))
        weights = jnp.where(tiles == tile, weight, weights)
    limit = SHRINK_SCALE * weights
    threshold[...] = limit
    bottom = cells // COLS - 1
    pairs = (
        (strip(field, 0), strip(field, bottom)),
        (strip(multiplier[2], 0), strip(multiplier[3], bottom)),
        (strip(limit, 0), strip(limit, bottom)),
    )
    for (head, tail), start in zip(pairs, (0, times, 2 * times)):
        one, two = edges(head, tail)
        sent[half + start : half + start + head.shape[0], :] = one
        edge[start : start + head.shape[0], :] = two

    def arrived(group):
        if group * GROUP % CHUNK == 0:
            large[group * GROUP // CHUNK].wait()

    sent[:half, :] = forward_of(spectra, kernel_here, weighted_t[...], times, arrived)


def first_adjoint_body(count, *refs):
    observed, kernel, plain_t, weighted, out = refs[count:]
    predicted = unpacked(summed(refs[:count]), kernel.shape[2])
    residual = predicted - jnp.concatenate([observed[...], observed[...]], axis=1)
    out[...] = adjoint(residual, kernel, plain_t[...], weighted[...], 1)


def response_of(field, kernel, plain, weighted_t, linked, sent, edge):
    half = field.shape[0] // 2
    rows = field.shape[1] // COLS
    one, two = edges(strip(field, 0), strip(field, rows - 1))
    squares = []
    for row in range(rows):
        here = strip(field, row)
        east = strip(linked[0:1], row) * (pltpu.roll(here, COLS - 1, 1) - here)
        squares.append(east * east)
        if row > 0:
            north = strip(linked[2:3], row) * (strip(field, row - 1) - here)
            squares.append(north * north)
    sent[:half, :] = forward(field, kernel, plain[...], weighted_t[...])
    sent[half : half + 8, :] = rows_of([square_sum(field), 2.0 * jnp.sum(tree_sum(squares))])
    sent[half + 8 :, :] = one
    edge[...] = two


def merge_body(sent, came, edge, other, linked, out):
    cells = linked.shape[1]
    top = out.shape[0]
    to_partner, to_other = edges(linked[2:3, :COLS], linked[3:4, cells - COLS :])
    across = to_partner * (came[top:, :] - sent[top:, :])
    beyond = to_other * (other[...] - edge[...])
    out[: top - 8, :] = sent[: top - 8, :] + came[: top - 8, :]
    boundary = 2.0 * jnp.sum(across * across + beyond * beyond)
    out[top - 8 :, :] = sent[top - 8 : top, :] + came[top - 8 : top, :] + rows_of([0.0, boundary])


def first_gradient_body(count, *refs):
    (start_multiplier, one, two, linked_ref, kernel, plain, weighted_t,
     adjoint_out, gradient, sent, edge) = refs[count:]
    times, cells = adjoint_out.shape
    half = times // 2
    linked = linked_ref[...]
    total = summed(refs[:count])
    values = [[strip(start_multiplier[k], r) for r in range(cells // COLS)] for k in range(4)]
    above, below = beside(one[half + times : half + 2 * times, :], two[times : 2 * times, :])
    field = total + gathered_jumps(values, above, below, linked)
    adjoint_out[...] = total
    gradient[...] = field
    response_of(field, kernel, plain, weighted_t, linked, sent, edge)


def second_adjoint_body(count, *refs):
    kernel, plain_t, weighted, out, norms = refs[count:]
    times = plain_t.shape[0]
    half = times // 2
    total = summed(refs[:count])
    packed, squares = total[:half], total[half : half + 8]
    out[:times, :] = adjoint(unpacked(packed, kernel.shape[2]), kernel, plain_t[...], weighted[...], 2)
    out[times:, :] = jnp.full((8, out.shape[1]), square_sum(packed), jnp.float32)
    norms[...] = squares


def step_of(norms, scalars):
    return norms[0, 0] / (scalars[0, 0] + norms[1, 0] + TINY)


def second_gradient_body(count, *refs):
    (norms, adjoint_in, gradient_in, model, start_multiplier, threshold, one, two, grad_one, grad_two, linked_ref,
     kernel, plain, weighted_t, model_out, jumps_out, multiplier_out, gradient_out, sent, edge) = refs[count:]
    times, cells = model.shape
    half = times // 2
    total = summed(refs[:count])
    step = step_of(norms, total[times:])
    linked = linked_ref[...]
    field, gradient = model[...], gradient_in[...]
    rows = cells // COLS
    above, below = beside(one[half:, :], two[...])
    field_jumps = jumps(field, above[:times], below[:times], linked)
    grad_jumps = jumps(gradient, *beside(grad_one[half + 8 :, :], grad_two[...]), linked)

    def advance(model_jumps, old_multiplier, limit):
        shifted = model_jumps + old_multiplier
        auxiliary = shrunk(shifted, limit)
        multiplier = shifted - auxiliary
        return multiplier, model_jumps - auxiliary + multiplier

    penalties, new_jumps = [], []
    for k in range(4):
        penalties.append([])
        new_jumps.append([])
        for r in range(rows):
            new = field_jumps[k][r] - step * grad_jumps[k][r]
            multiplier, penalty = advance(new, strip(start_multiplier[k], r), strip(threshold[0:1], r))
            jumps_out[k, :, r * COLS : (r + 1) * COLS] = new
            multiplier_out[k, :, r * COLS : (r + 1) * COLS] = multiplier
            penalties[k].append(penalty)
            new_jumps[k].append(new)
    _, beside_above = advance(-new_jumps[2][0], above[times : 2 * times], above[2 * times : 2 * times + 1])
    _, beside_below = advance(-new_jumps[3][-1], below[times : 2 * times], below[2 * times : 2 * times + 1])
    back = gathered_jumps(penalties, beside_above, beside_below, linked)
    model_out[...] = field - step * gradient
    new_gradient = adjoint_in[...] - step * total[:times] + back
    gradient_out[...] = new_gradient
    response_of(new_gradient, kernel, plain, weighted_t, linked, sent, edge)


def response_body(count, *refs):
    out, norms = refs[count:]
    total = summed(refs[:count])
    packed, squares = total[:-8], total[-8:]
    out[...] = jnp.full((8, LANES), square_sum(packed), jnp.float32)
    norms[...] = squares


def finish_body(count, *refs):
    (norms, gradient_in, model, model_jumps, multiplier, threshold, grad_one, grad_two, linked,
     estimate_out, auxiliary_out, multiplier_out) = refs[count:]
    step = step_of(norms, summed(refs[:count]))
    half = gradient_in.shape[0] // 2
    gradient = gradient_in[...]
    estimate_out[...] = model[...] - step * gradient
    grad_jumps = jumps(gradient, *beside(grad_one[half + 8 :, :], grad_two[...]), linked[...])
    for k in range(4):
        for r in range(gradient.shape[1] // COLS):
            at = slice(r * COLS, (r + 1) * COLS)
            shifted = model_jumps[k, :, at] - step * grad_jumps[k][r] + multiplier[k, :, at]
            auxiliary = shrunk(shifted, threshold[0:1, at])
            auxiliary_out[k, :, at] = auxiliary
            multiplier_out[k, :, at] = shifted - auxiliary


def stages_of(count, *radices):
    stages = []
    for radix in radices:
        if count > 1 and count % radix == 0:
            stages.append(radix)
            count //= radix
    while count > 1:
        stages.append(2)
        count //= 2
    return stages


def summing(parts, axis, stride, stages):
    count = lax.axis_size(axis)
    for radix in stages:
        total = tree_sum(parts)
        parts = [total] + [
            lax.ppermute(total, axis, [(i, i ^ (k * stride)) for i in range(count)]) for k in range(1, radix)
        ]
        stride *= radix
    return parts


def sensor_parts(array, *radices):
    return summing([array], "sensor", 1, stages_of(lax.axis_size("sensor"), *radices))


def cell_parts(merged):
    return summing([merged], "cell", 2, stages_of(lax.axis_size("cell") // 2, 4, 4))


def from_partner(array):
    return lax.ppermute(array, "cell", [(i, i ^ 1) for i in range(lax.axis_size("cell"))])


def from_other(array):
    inner = range(1, lax.axis_size("cell") - 1)
    return lax.ppermute(array, "cell", [(i, i + 1 if i % 2 else i - 1) for i in inner])


def per_device(kernel, observed, start_model, start_multiplier, neighbours, tile_of_cell, tile_weight):
    times, cells = start_model.shape
    freqs, sensors = kernel.shape[1:3]
    plain, weighted = tables(times, freqs)
    half = times // 2
    field, row, wide = (times, cells), (times, COLS), (4, times, cells)

    loads = [
        kernel, start_model, start_multiplier, neighbours, tile_of_cell[None, :], tile_weight[None, :],
        jnp.asarray(plain), jnp.asarray(weighted.T.copy()), jnp.asarray(plain.T.copy()), jnp.asarray(weighted),
    ]
    sent, edge, threshold, linked, kernel, start_model, start_multiplier, _, _, _, plain, weighted_t, plain_t, weighted = call(
        first_forward_body,
        [(half + 2 * times + 8, LANES), (2 * times + 8, LANES), (8, cells), (8, cells)]
        + [jax.ShapeDtypeStruct(a.shape, a.dtype) for a in loads],
        *[pltpu.with_memory_space_constraint(a, HBM) for a in loads],
        scratch=[pltpu.SemaphoreType.DMA((9 + -(-freqs // CHUNK),))],
        inputs=HBM,
    )
    one = from_partner(sent)
    merged, edge = lax.optimization_barrier((sent[:half] + one[:half], edge))
    parts = cell_parts(merged)
    two = from_other(edge)
    back = call(functools.partial(first_adjoint_body, len(parts)), field, *parts, observed, kernel, plain_t, weighted)
    parts = sensor_parts(back, 2, 2)
    message, side = (half + 8 + times, LANES), (times, LANES)
    adjoint_one, gradient, sent, edge = call(
        functools.partial(first_gradient_body, len(parts)), [field, field, message, side],
        *parts, start_multiplier, one, two, linked, kernel, plain, weighted_t,
    )
    grad_one, grad_two = from_partner(sent), from_other(edge)
    parts = cell_parts(call(merge_body, (half + 8, LANES), sent, grad_one, edge, grad_two, linked))
    back, norms = call(
        functools.partial(second_adjoint_body, len(parts)), [(times + 8, cells), (8, LANES)],
        *parts, kernel, plain_t, weighted,
    )
    parts = sensor_parts(back, 4)
    model, model_jumps, multiplier, gradient, sent, edge = call(
        functools.partial(second_gradient_body, len(parts)), [field, wide, wide, field, message, side],
        *parts, norms, adjoint_one, gradient, start_model, start_multiplier, threshold, one, two, grad_one, grad_two,
        linked, kernel, plain, weighted_t,
    )
    grad_one, grad_two = from_partner(sent), from_other(edge)
    parts = cell_parts(call(merge_body, (half + 8, LANES), sent, grad_one, edge, grad_two, linked))
    square, norms = call(functools.partial(response_body, len(parts)), [(8, LANES), (8, LANES)], *parts)
    parts = sensor_parts(square, 4)
    return tuple(
        call(
            functools.partial(finish_body, len(parts)), [field, wide, wide],
            *parts, norms, gradient, model, model_jumps, multiplier, threshold, grad_one, grad_two, linked,
        )
    )


def solution(mesh):
    in_specs = (
        P(None, None, "sensor", "cell"),
        P(None, "sensor"),
        P(None, "cell"),
        P(None, None, "cell"),
        P(None, "cell"),
        P("cell"),
        P(),
    )
    out_specs = (P(None, "cell"), P(None, None, "cell"), P(None, None, "cell"))
    return jax.shard_map(
        per_device, mesh=mesh, in_specs=in_specs, out_specs=out_specs, check_vma=False
    )
```

```python
import functools

import jax
import jax.numpy as jnp
import numpy as np
from jax import lax
from jax.experimental import pallas as pl
from jax.experimental.pallas import tpu as pltpu
from jax.sharding import PartitionSpec as P

COLS = 128
LANES = 128
GROUP = 8
IN_FLIGHT = 4
SHRINK_SCALE = 0.4
TINY = 1e-06
VMEM = pltpu.VMEM
HBM = pltpu.HBM


def tables(times, freqs):
    padded = 2 * times
    groups = -(-freqs // GROUP)
    plain = np.zeros((16 * groups, times), np.float64)
    weighted = np.zeros((16 * groups, times), np.float64)
    for f in range(freqs):
        phase = 2.0 * np.pi * ((f * np.arange(times)) % padded) / padded
        weight = (1.0 if f in (0, freqs - 1) else 2.0) / padded
        row = 16 * (f // GROUP) + f % GROUP
        plain[row], plain[row + GROUP] = np.cos(phase), -np.sin(phase)
        weighted[row], weighted[row + GROUP] = weight * np.cos(phase), -weight * np.sin(phase)
    return plain.astype(np.float32), weighted.astype(np.float32)


def exact(left, right):
    return jnp.dot(left, right, precision=lax.Precision.HIGHEST, preferred_element_type=jnp.float32)


def turned(rows):
    return jnp.concatenate([-rows[GROUP:], rows[:GROUP]], axis=0)


def dot_nt(left, right):
    return lax.dot_general(left, right, (((1,), (1,)), ((), ())), preferred_element_type=jnp.float32)


def dot_nn(left, right):
    return jnp.dot(left, right, preferred_element_type=jnp.float32)


def slab(kernel_ref, part, group):
    freqs, sensors, cells = kernel_ref.shape[1:]
    count = min(GROUP, freqs - group * GROUP)
    block = kernel_ref[part, group * GROUP : group * GROUP + count]
    return block.reshape(count * sensors, cells)


def own_block(width, sensors):
    row = lax.broadcasted_iota(jnp.int32, (16, width), 0) % GROUP
    lane = lax.broadcasted_iota(jnp.int32, (16, width), 1) // sensors
    return row == lane


def fold(wide):
    total = functools.reduce(
        lambda a, b: a + b, [wide[:, i : i + LANES] for i in range(0, wide.shape[1], LANES)]
    )
    return total + pltpu.roll(total, LANES // 2, 1)


def forward(field, kernel_ref, plain, weighted_t):
    return packed_series(forward_rows(exact(plain, field), kernel_ref), weighted_t, kernel_ref.shape[2])


def forward_rows(spectra, kernel_ref, arrived=None):
    sensors = kernel_ref.shape[2]
    rows = []
    for group in range(spectra.shape[0] // 16):
        part = spectra[16 * group : 16 * group + 16]
        if arrived is not None:
            arrived(group)
        re_slab, im_slab = slab(kernel_ref, 0, group), slab(kernel_ref, 1, group)
        out = dot_nt(part.astype(jnp.bfloat16), re_slab) + dot_nt(turned(part).astype(jnp.bfloat16), im_slab)
        width = out.shape[1]
        out = jnp.where(own_block(width, sensors), out, 0.0)
        if width < LANES:
            out = jnp.concatenate([out, jnp.zeros((16, LANES - width), jnp.float32)], axis=1)
        rows.append(fold(out))
    return jnp.concatenate(rows, axis=0)


def packed_series(rows, weighted_t, sensors):
    times = weighted_t.shape[0]
    series = exact(weighted_t, rows)
    left = lax.broadcasted_iota(jnp.int32, (times // 2, LANES), 1) < sensors
    return jnp.where(left, series[: times // 2], series[times // 2 :])


def unpacked(packed, sensors):
    other = pltpu.roll(packed, sensors, 1)
    left = lax.broadcasted_iota(jnp.int32, packed.shape, 1) < sensors
    return jnp.concatenate([jnp.where(left, packed, other), jnp.where(left, other, packed)], axis=0)


def adjoint(residual, kernel_ref, plain_t, weighted, halves):
    freqs, sensors, cells = kernel_ref.shape[1:]
    spectra = exact(weighted, residual)
    rows = []
    for group in range(weighted.shape[0] // 16):
        part = spectra[16 * group : 16 * group + 16]
        count = min(GROUP, freqs - group * GROUP)
        width = count * sensors
        re_slab, im_slab = slab(kernel_ref, 0, group), slab(kernel_ref, 1, group)
        wide = jnp.concatenate([part] * (-(-width // LANES)), axis=1)[:, :width]
        wide = jnp.where(own_block(width, sensors), wide, 0.0)
        total = None
        for _ in range(halves):
            re_left = wide.astype(jnp.bfloat16)
            rounded = re_left.astype(jnp.float32)
            out = dot_nn(re_left, re_slab) - dot_nn(turned(rounded).astype(jnp.bfloat16), im_slab)
            total = out if total is None else total + out
            wide = wide - rounded
        rows.append(total)
    return exact(plain_t, jnp.concatenate(rows, axis=0))


def strip(array, row):
    return array[..., row * COLS : (row + 1) * COLS]


def jumps(field, above, below, linked):
    count = field.shape[1] // COLS
    out = []
    for direction in range(4):
        strips = []
        for row in range(count):
            here = strip(field, row)
            if direction == 0:
                there = pltpu.roll(here, COLS - 1, 1)
            elif direction == 1:
                there = pltpu.roll(here, 1, 1)
            elif direction == 2:
                there = above if row == 0 else strip(field, row - 1)
            else:
                there = below if row == count - 1 else strip(field, row + 1)
            strips.append(strip(linked[direction : direction + 1], row) * (there - here))
        out.append(strips)
    return out


def gathered_jumps(values, above, below, linked):
    count = len(values[0])
    out = []
    for row in range(count):
        arriving = (
            pltpu.roll(values[1][row], COLS - 1, 1),
            pltpu.roll(values[0][row], 1, 1),
            above if row == 0 else values[3][row - 1],
            below if row == count - 1 else values[2][row + 1],
        )
        total = None
        for direction in range(4):
            term = strip(linked[direction : direction + 1], row) * (arriving[direction] - values[direction][row])
            total = term if total is None else total + term
        out.append(total)
    return jnp.concatenate(out, axis=1)


def shrunk(shifted, threshold):
    return shifted - jnp.clip(shifted, -threshold, threshold)


def tree_sum(parts):
    parts = list(parts)
    while len(parts) > 1:
        parts = [parts[i] + parts[i + 1] if i + 1 < len(parts) else parts[i] for i in range(0, len(parts), 2)]
    return parts[0]


def square_sum(array):
    return jnp.sum(array * array)


def block_of(scalar, rows=8):
    return jnp.full((rows, LANES), scalar, jnp.float32)


def call(body, out_shapes, *operands, scratch=(), inputs=VMEM):
    single = isinstance(out_shapes, tuple)
    shapes = [out_shapes] if single else list(out_shapes)
    shapes = [s if isinstance(s, jax.ShapeDtypeStruct) else jax.ShapeDtypeStruct(s, jnp.float32) for s in shapes]
    out = pl.pallas_call(
        body,
        out_shape=shapes,
        in_specs=[pl.BlockSpec(memory_space=inputs)] * len(operands),
        out_specs=[pl.BlockSpec(memory_space=VMEM)] * len(shapes),
        scratch_shapes=list(scratch),
        compiler_params=pltpu.CompilerParams(vmem_limit_bytes=24 * 2**20),
    )(*operands)
    return out[0] if single else out


def summed(parts):
    return tree_sum([part[...] for part in parts])


def is_even():
    return lax.rem(lax.axis_index("cell"), 2) == 0


def edges(head, tail):
    even = is_even()
    return jnp.where(even, tail, head), jnp.where(even, head, tail)


def beside(partner, other):
    even = is_even()
    return jnp.where(even, other, partner), jnp.where(even, partner, other)


def is_odd():
    return lax.rem(lax.axis_index("sensor"), 2) == 1


def spread(rows):
    upper = -(-rows.shape[0] // 16) * 8
    lower = rows[upper:]
    if lower.shape[0] < upper:
        lower = jnp.concatenate([lower, jnp.zeros((upper - lower.shape[0], LANES), rows.dtype)])
    return jnp.concatenate([rows[:upper], lower], axis=1)


def gathered(wide, count):
    return jnp.concatenate([wide[:, :LANES], wide[: count - wide.shape[0], LANES:]])


def rows_of(scalars):
    row = lax.broadcasted_iota(jnp.int32, (8, LANES), 0)
    out = jnp.zeros((8, LANES), jnp.float32)
    for i, scalar in enumerate(scalars):
        out = jnp.where(row == i, scalar, out)
    return out


def first_forward_body(*refs):
    loaded, (sent, edge, threshold, linked), kept, sems = refs[:10], refs[10:14], refs[14:24], refs[24]
    kernel, kernel_here = loaded[0], kept[0]
    field, multiplier, neighbours, tile_of_cell, tile_weight, plain, weighted_t = kept[1:8]
    freqs = kernel.shape[1]
    times, cells = field.shape
    half = times // 2
    copies = []

    def load(source, target):
        copy = pltpu.make_async_copy(source, target, sems.at[len(copies)])
        copy.start()
        copies.append(copy)
        return copy

    early = [load(loaded[i], kept[i]) for i in (1, 6)]
    starts = list(range(0, freqs, GROUP))
    large = []

    def load_group():
        if len(large) < len(starts):
            start = starts[len(large)]
            at = (slice(None), pl.ds(start, min(GROUP, freqs - start)))
            large.append(load(kernel.at[at], kernel_here.at[at]))

    for _ in range(IN_FLIGHT):
        load_group()
    small = [load(loaded[i], kept[i]) for i in (3, 4, 5, 2, 7, 8, 9)]
    for copy in early:
        copy.wait()
    spectra = exact(plain[...], field[...])

    def arrived(group):
        large[group].wait()
        load_group()

    rows = forward_rows(spectra, kernel_here, arrived)
    for copy in small:
        copy.wait()
    sent[:half, :] = packed_series(rows, weighted_t[...], kernel.shape[2])

    cell = lax.broadcasted_iota(jnp.int32, (4, cells), 1) + lax.axis_index("cell") * cells
    linked[0:4, :] = jnp.where(neighbours[...] != cell, 1.0, 0.0)
    linked[4:8, :] = jnp.zeros((4, cells), jnp.float32)
    tile = lax.broadcasted_iota(jnp.int32, (tile_weight.shape[1], cells), 0)
    chosen = jnp.where(tile == tile_of_cell[...], 1.0, 0.0)
    weights = exact(jnp.broadcast_to(tile_weight[...], (8, tile_weight.shape[1])), chosen)
    limit = SHRINK_SCALE * weights
    threshold[...] = limit
    bottom = cells // COLS - 1
    pairs = (
        (strip(field, 0), strip(field, bottom)),
        (strip(multiplier[2], 0), strip(multiplier[3], bottom)),
        (strip(limit, 0), strip(limit, bottom)),
    )
    for (head, tail), start in zip(pairs, (0, times, 2 * times)):
        one, two = edges(head, tail)
        sent[half + start : half + start + head.shape[0], :] = one
        edge[start : start + head.shape[0], :] = two


def first_adjoint_body(count, *refs):
    observed, two, kernel, plain_t, weighted, out = refs[count:]
    times = observed.shape[0]
    predicted = unpacked(summed(refs[:count]), kernel.shape[2])
    residual = predicted - jnp.concatenate([observed[...], observed[...]], axis=1)
    out[:times, :] = adjoint(residual, kernel, plain_t[...], weighted[...], 1)
    out[times:, :] = spread(two[...])


def response_of(field, kernel, plain, weighted_t, linked, sent, edge):
    half = field.shape[0] // 2
    rows = field.shape[1] // COLS
    one, two = edges(strip(field, 0), strip(field, rows - 1))
    squares = []
    for row in range(rows):
        here = strip(field, row)
        east = strip(linked[0:1], row) * (pltpu.roll(here, COLS - 1, 1) - here)
        squares.append(east * east)
        if row > 0:
            north = strip(linked[2:3], row) * (strip(field, row - 1) - here)
            squares.append(north * north)
    sent[:half, :] = forward(field, kernel, plain[...], weighted_t[...])
    sent[half : half + 8, :] = rows_of([square_sum(field), 2.0 * jnp.sum(tree_sum(squares))])
    sent[half + 8 :, :] = one
    edge[...] = two


def merge_body(sent, came, edge, other, linked, out):
    cells = linked.shape[1]
    top = out.shape[0]
    to_partner, to_other = edges(linked[2:3, :COLS], linked[3:4, cells - COLS :])
    across = to_partner * (came[top:, :] - sent[top:, :])
    beyond = to_other * (other[...] - edge[...])
    out[: top - 8, :] = sent[: top - 8, :] + came[: top - 8, :]
    boundary = 2.0 * square_sum(jnp.where(is_odd(), beyond, across))
    out[top - 8 :, :] = sent[top - 8 : top, :] + came[top - 8 : top, :] + rows_of([0.0, 0.0, boundary])


def first_gradient_body(count, *refs):
    (start_multiplier, one, two, passed, linked_ref, kernel, plain, weighted_t,
     adjoint_out, gradient, sent, edge, two_out) = refs[count:]
    times, cells = adjoint_out.shape
    half = times // 2
    two = jnp.where(is_odd(), two[...], gathered(passed[times:, :], two.shape[0]))
    two_out[...] = two
    linked = linked_ref[...]
    total = summed(refs[:count])
    values = [[strip(start_multiplier[k], r) for r in range(cells // COLS)] for k in range(4)]
    above, below = beside(one[half + times : half + 2 * times, :], two[times : 2 * times, :])
    field = total + gathered_jumps(values, above, below, linked)
    adjoint_out[...] = total
    gradient[...] = field
    response_of(field, kernel, plain, weighted_t, linked, sent, edge)


def second_adjoint_body(count, *refs):
    two, kernel, plain_t, weighted, out, norms = refs[count:]
    times = plain_t.shape[0]
    half = times // 2
    total = summed(refs[:count])
    packed, squares = total[:half], total[half : half + 8]
    out[:times, :] = adjoint(unpacked(packed, kernel.shape[2]), kernel, plain_t[...], weighted[...], 2)
    scalars = rows_of([square_sum(packed), squares[2:3, :] * (2.0 / lax.axis_size("sensor"))])
    out[times : times + 8, :] = jnp.concatenate([scalars] * (out.shape[1] // LANES), axis=1)
    out[times + 8 :, :] = spread(two[...])
    norms[...] = squares


def step_of(norms, scalars):
    return norms[0, 0] / (scalars[0, 0] + (norms[1, 0] + scalars[1, 0]) + TINY)


def second_gradient_body(count, *refs):
    (norms, adjoint_in, gradient_in, model, start_multiplier, threshold, one, two, grad_one, grad_two, passed, linked_ref,
     kernel, plain, weighted_t, model_out, jumps_out, multiplier_out, gradient_out, sent, edge) = refs[count:]
    times, cells = model.shape
    half = times // 2
    total = summed(refs[:count])
    step = step_of(norms, total[times:])
    linked = linked_ref[...]
    field, gradient = model[...], gradient_in[...]
    rows = cells // COLS
    above, below = beside(one[half:, :], two[...])
    field_jumps = jumps(field, above[:times], below[:times], linked)
    grad_two = jnp.where(is_odd(), grad_two[...], gathered(passed[times + 8 :, :], times))
    grad_jumps = jumps(gradient, *beside(grad_one[half + 8 :, :], grad_two), linked)

    def advance(model_jumps, old_multiplier, limit):
        shifted = model_jumps + old_multiplier
        auxiliary = shrunk(shifted, limit)
        multiplier = shifted - auxiliary
        return multiplier, model_jumps - auxiliary + multiplier

    penalties, new_jumps = [], []
    for k in range(4):
        penalties.append([])
        new_jumps.append([])
        for r in range(rows):
            new = field_jumps[k][r] - step * grad_jumps[k][r]
            multiplier, penalty = advance(new, strip(start_multiplier[k], r), strip(threshold[0:1], r))
            jumps_out[k, :, r * COLS : (r + 1) * COLS] = new
            multiplier_out[k, :, r * COLS : (r + 1) * COLS] = multiplier
            penalties[k].append(penalty)
            new_jumps[k].append(new)
    _, beside_above = advance(-new_jumps[2][0], above[times : 2 * times], above[2 * times : 2 * times + 1])
    _, beside_below = advance(-new_jumps[3][-1], below[times : 2 * times], below[2 * times : 2 * times + 1])
    back = gathered_jumps(penalties, beside_above, beside_below, linked)
    model_out[...] = field - step * gradient
    new_gradient = adjoint_in[...] - step * total[:times] + back
    gradient_out[...] = new_gradient
    response_of(new_gradient, kernel, plain, weighted_t, linked, sent, edge)


def response_body(count, *refs):
    two, out, passing, norms = refs[count:]
    total = summed(refs[:count])
    packed, squares = total[:-8], total[-8:]
    scalars = rows_of([square_sum(packed), squares[2:3, :] * (2.0 / lax.axis_size("sensor"))])
    out[...] = scalars
    passing[:8, :] = scalars
    passing[8:, :] = two[...]
    norms[...] = squares


def finish_body(count, *refs):
    (norms, gradient_in, model, model_jumps, multiplier, threshold, grad_one, grad_two, passed, linked,
     estimate_out, auxiliary_out, multiplier_out) = refs[count:]
    step = step_of(norms, tree_sum([part[:8, :] for part in refs[:count]]))
    grad_two = jnp.where(is_odd(), grad_two[...], passed[8:, :])
    half = gradient_in.shape[0] // 2
    gradient = gradient_in[...]
    estimate_out[...] = model[...] - step * gradient
    grad_jumps = jumps(gradient, *beside(grad_one[half + 8 :, :], grad_two), linked[...])
    for k in range(4):
        for r in range(gradient.shape[1] // COLS):
            at = slice(r * COLS, (r + 1) * COLS)
            shifted = model_jumps[k, :, at] - step * grad_jumps[k][r] + multiplier[k, :, at]
            auxiliary = shrunk(shifted, threshold[0:1, at])
            auxiliary_out[k, :, at] = auxiliary
            multiplier_out[k, :, at] = shifted - auxiliary


def stages_of(count, *radices):
    stages = []
    for radix in radices:
        if count > 1 and count % radix == 0:
            stages.append(radix)
            count //= radix
    while count > 1:
        stages.append(2)
        count //= 2
    return stages


def summing(parts, axis, stride, stages):
    count = lax.axis_size(axis)
    for radix in stages:
        total = tree_sum(parts)
        parts = [total] + [
            lax.ppermute(total, axis, [(i, i ^ (k * stride)) for i in range(count)]) for k in range(1, radix)
        ]
        stride *= radix
    return parts


def sensor_hop(array):
    return lax.ppermute(array, "sensor", [(i, i ^ 1) for i in range(lax.axis_size("sensor"))])


def sensor_parts(array, rows):
    passed = sensor_hop(array)
    total = array[:rows] + passed[:rows]
    return summing([total], "sensor", 2, stages_of(lax.axis_size("sensor") // 2, 2)), passed


def cell_parts(merged):
    return summing([merged], "cell", 2, stages_of(lax.axis_size("cell") // 2, 4, 4))


def from_partner(array):
    return lax.ppermute(array, "cell", [(i, i ^ 1) for i in range(lax.axis_size("cell"))])


def from_other(array):
    sensors = lax.axis_size("sensor")
    pairs = [
        (i * sensors + s, (i + 1 if i % 2 else i - 1) * sensors + s)
        for i in range(1, lax.axis_size("cell") - 1)
        for s in range(1, sensors, 2)
    ]
    return lax.ppermute(array, ("cell", "sensor"), pairs)


def per_device(kernel, observed, start_model, start_multiplier, neighbours, tile_of_cell, tile_weight):
    times, cells = start_model.shape
    freqs, sensors = kernel.shape[1:3]
    plain, weighted = tables(times, freqs)
    half = times // 2
    field, row, wide = (times, cells), (times, COLS), (4, times, cells)

    loads = [
        kernel, start_model, start_multiplier, neighbours, tile_of_cell[None, :], tile_weight[None, :],
        jnp.asarray(plain), jnp.asarray(weighted.T.copy()), jnp.asarray(plain.T.copy()), jnp.asarray(weighted),
    ]
    sent, edge, threshold, linked, kernel, start_model, start_multiplier, _, _, _, plain, weighted_t, plain_t, weighted = call(
        first_forward_body,
        [(half + 2 * times + 8, LANES), (2 * times + 8, LANES), (8, cells), (8, cells)]
        + [jax.ShapeDtypeStruct(a.shape, a.dtype) for a in loads],
        *[pltpu.with_memory_space_constraint(a, HBM) for a in loads],
        scratch=[pltpu.SemaphoreType.DMA((9 + -(-freqs // GROUP),))],
        inputs=HBM,
    )
    one = from_partner(sent)
    merged, edge = lax.optimization_barrier((sent[:half] + one[:half], edge))
    parts = cell_parts(merged)
    two = from_other(edge)
    message, side, shared = (half + 8 + times, LANES), (times, LANES), (2 * times + 8, LANES)
    back = call(
        functools.partial(first_adjoint_body, len(parts)), (2 * times + 8, cells),
        *parts, observed, two, kernel, plain_t, weighted,
    )
    parts, passed = sensor_parts(back, times)
    adjoint_one, gradient, sent, edge, two = call(
        functools.partial(first_gradient_body, len(parts)), [field, field, message, side, shared],
        *parts, start_multiplier, one, two, passed, linked, kernel, plain, weighted_t,
    )
    grad_one, grad_two = from_partner(sent), from_other(edge)
    parts = cell_parts(call(merge_body, (half + 8, LANES), sent, grad_one, edge, grad_two, linked))
    back, norms = call(
        functools.partial(second_adjoint_body, len(parts)), [(times + 8 + half, cells), (8, LANES)],
        *parts, grad_two, kernel, plain_t, weighted,
    )
    parts, passed = sensor_parts(back, times + 8)
    model, model_jumps, multiplier, gradient, sent, edge = call(
        functools.partial(second_gradient_body, len(parts)), [field, wide, wide, field, message, side],
        *parts, norms, adjoint_one, gradient, start_model, start_multiplier, threshold, one, two, grad_one, grad_two,
        passed, linked, kernel, plain, weighted_t,
    )
    grad_one, grad_two = from_partner(sent), from_other(edge)
    parts = cell_parts(call(merge_body, (half + 8, LANES), sent, grad_one, edge, grad_two, linked))
    scalars, passing, norms = call(
        functools.partial(response_body, len(parts)), [(8, LANES), (8 + times, LANES), (8, LANES)], *parts, grad_two
    )
    passed = sensor_hop(passing)
    sensor_count = lax.axis_size("sensor")
    if sensor_count <= 4:
        parts = [scalars, passed] + [
            lax.ppermute(scalars, "sensor", [(i, i ^ k) for i in range(sensor_count)]) for k in range(2, sensor_count)
        ]
    else:
        parts = summing([scalars + passed[:8]], "sensor", 2, stages_of(sensor_count // 2, 2))
    return tuple(
        call(
            functools.partial(finish_body, len(parts)), [field, wide, wide],
            *parts, norms, gradient, model, model_jumps, multiplier, threshold, grad_one, grad_two, passed, linked,
        )
    )


def solution(mesh):
    in_specs = (
        P(None, None, "sensor", "cell"),
        P(None, "sensor"),
        P(None, "cell"),
        P(None, None, "cell"),
        P(None, "cell"),
        P("cell"),
        P(),
    )
    out_specs = (P(None, "cell"), P(None, None, "cell"), P(None, None, "cell"))
    return jax.shard_map(
        per_device, mesh=mesh, in_specs=in_specs, out_specs=out_specs, check_vma=False
    )
```

```python
import functools

import jax
import jax.numpy as jnp
import numpy as np
from jax import lax
from jax.experimental import pallas as pl
from jax.experimental.pallas import tpu as pltpu
from jax.sharding import PartitionSpec as P

COLS = 128
LANES = 128
GROUP = 8
CHUNK = 24
SHRINK_SCALE = 0.4
TINY = 1e-06
VMEM = pltpu.VMEM
HBM = pltpu.HBM


def tables(times, freqs):
    padded = 2 * times
    groups = -(-freqs // GROUP)
    plain = np.zeros((16 * groups, times), np.float64)
    weighted = np.zeros((16 * groups, times), np.float64)
    for f in range(freqs):
        phase = 2.0 * np.pi * ((f * np.arange(times)) % padded) / padded
        weight = (1.0 if f in (0, freqs - 1) else 2.0) / padded
        row = 16 * (f // GROUP) + f % GROUP
        plain[row], plain[row + GROUP] = np.cos(phase), -np.sin(phase)
        weighted[row], weighted[row + GROUP] = weight * np.cos(phase), -weight * np.sin(phase)
    return plain.astype(np.float32), weighted.astype(np.float32)


def table_terms(table):
    high = table.astype(jnp.bfloat16)
    low = (table - high.astype(np.float32)).astype(jnp.bfloat16)
    return np.concatenate([high, high, low], axis=1)


def table_dot(terms, values):
    high = values.astype(jnp.bfloat16)
    low = (values - high.astype(jnp.float32)).astype(jnp.bfloat16)
    return dot_nn(terms, jnp.concatenate([high, low, high], axis=0))


def turned(rows):
    rows = rows.astype(jnp.float32)
    return jnp.concatenate([-rows[GROUP:], rows[:GROUP]], axis=0).astype(jnp.bfloat16)


def dot_nt(left, right):
    return lax.dot_general(left, right, (((1,), (1,)), ((), ())), preferred_element_type=jnp.float32)


def dot_nn(left, right):
    return jnp.dot(left, right, preferred_element_type=jnp.float32)


def slab(kernel_ref, part, group):
    freqs, sensors, cells = kernel_ref.shape[1:]
    count = min(GROUP, freqs - group * GROUP)
    block = kernel_ref[part, group * GROUP : group * GROUP + count]
    return block.reshape(count * sensors, cells)


def own_block(width, sensors):
    row = lax.broadcasted_iota(jnp.int32, (16, width), 0) % GROUP
    lane = lax.broadcasted_iota(jnp.int32, (16, width), 1) // sensors
    return row == lane


def fold(wide):
    total = functools.reduce(
        lambda a, b: a + b, [wide[:, i : i + LANES] for i in range(0, wide.shape[1], LANES)]
    )
    return total + pltpu.roll(total, LANES // 2, 1)


def forward(field, kernel_ref, plain, weighted_t):
    return packed_series(forward_rows(table_dot(plain, field), kernel_ref), weighted_t, kernel_ref.shape[2])


def forward_rows(spectra, kernel_ref, arrived=None):
    sensors = kernel_ref.shape[2]
    rows = []
    for group in range(spectra.shape[0] // 16):
        part = spectra[16 * group : 16 * group + 16]
        if arrived is not None:
            arrived(group)
        re_slab, im_slab = slab(kernel_ref, 0, group), slab(kernel_ref, 1, group)
        out = dot_nt(part.astype(jnp.bfloat16), re_slab) + dot_nt(turned(part), im_slab)
        width = out.shape[1]
        out = jnp.where(own_block(width, sensors), out, 0.0)
        if width < LANES:
            out = jnp.concatenate([out, jnp.zeros((16, LANES - width), jnp.float32)], axis=1)
        rows.append(fold(out))
    return jnp.concatenate(rows, axis=0)


def packed_series(rows, weighted_t, sensors):
    times = weighted_t.shape[0]
    series = table_dot(weighted_t, rows)
    left = lax.broadcasted_iota(jnp.int32, (times // 2, LANES), 1) < sensors
    return jnp.where(left, series[: times // 2], series[times // 2 :])


def unpacked(packed, sensors):
    other = pltpu.roll(packed, sensors, 1)
    left = lax.broadcasted_iota(jnp.int32, packed.shape, 1) < sensors
    return jnp.concatenate([jnp.where(left, packed, other), jnp.where(left, other, packed)], axis=0)


def adjoint(residual, kernel_ref, plain_t, weighted, halves):
    freqs, sensors, cells = kernel_ref.shape[1:]
    spectra = table_dot(weighted, residual)
    rows = []
    for group in range(weighted.shape[0] // 16):
        part = spectra[16 * group : 16 * group + 16]
        count = min(GROUP, freqs - group * GROUP)
        width = count * sensors
        re_slab, im_slab = slab(kernel_ref, 0, group), slab(kernel_ref, 1, group)
        wide = jnp.concatenate([part] * (-(-width // LANES)), axis=1)[:, :width]
        wide = jnp.where(own_block(width, sensors), wide, 0.0)
        terms = []
        for _ in range(halves):
            terms.append(wide.astype(jnp.bfloat16))
            wide = wide - terms[-1].astype(jnp.float32)
        left = jnp.concatenate(terms, axis=0)
        swapped = jnp.concatenate([turned(term) for term in terms], axis=0)
        out = dot_nn(left, re_slab) - dot_nn(swapped, im_slab)
        rows.append(tree_sum([out[16 * i : 16 * i + 16] for i in range(halves)]))
    return table_dot(plain_t, jnp.concatenate(rows, axis=0))


def strip(array, row):
    return array[..., row * COLS : (row + 1) * COLS]


def jumps(field, above, below, linked):
    count = field.shape[1] // COLS
    out = []
    for direction in range(4):
        strips = []
        for row in range(count):
            here = strip(field, row)
            if direction == 0:
                there = pltpu.roll(here, COLS - 1, 1)
            elif direction == 1:
                there = pltpu.roll(here, 1, 1)
            elif direction == 2:
                there = above if row == 0 else strip(field, row - 1)
            else:
                there = below if row == count - 1 else strip(field, row + 1)
            strips.append(strip(linked[direction : direction + 1], row) * (there - here))
        out.append(strips)
    return out


def gathered_jumps(values, above, below, linked):
    count = len(values[0])
    out = []
    for row in range(count):
        arriving = (
            pltpu.roll(values[1][row], COLS - 1, 1),
            pltpu.roll(values[0][row], 1, 1),
            above if row == 0 else values[3][row - 1],
            below if row == count - 1 else values[2][row + 1],
        )
        total = None
        for direction in range(4):
            term = strip(linked[direction : direction + 1], row) * (arriving[direction] - values[direction][row])
            total = term if total is None else total + term
        out.append(total)
    return jnp.concatenate(out, axis=1)


def shrunk(shifted, threshold):
    return shifted - jnp.clip(shifted, -threshold, threshold)


def tree_sum(parts):
    parts = list(parts)
    while len(parts) > 1:
        parts = [parts[i] + parts[i + 1] if i + 1 < len(parts) else parts[i] for i in range(0, len(parts), 2)]
    return parts[0]


def square_sum(array):
    return jnp.sum(array * array)


def block_of(scalar, rows=8):
    return jnp.full((rows, LANES), scalar, jnp.float32)


def call(body, out_shapes, *operands, scratch=(), inputs=VMEM):
    single = isinstance(out_shapes, tuple)
    shapes = [out_shapes] if single else list(out_shapes)
    shapes = [s if isinstance(s, jax.ShapeDtypeStruct) else jax.ShapeDtypeStruct(s, jnp.float32) for s in shapes]
    out = pl.pallas_call(
        body,
        out_shape=shapes,
        in_specs=[pl.BlockSpec(memory_space=inputs)] * len(operands),
        out_specs=[pl.BlockSpec(memory_space=VMEM)] * len(shapes),
        scratch_shapes=list(scratch),
        compiler_params=pltpu.CompilerParams(vmem_limit_bytes=24 * 2**20),
    )(*operands)
    return out[0] if single else out


def summed(parts):
    return tree_sum([part[...] for part in parts])


def is_even():
    return lax.rem(lax.axis_index("cell"), 2) == 0


def edges(head, tail):
    even = is_even()
    return jnp.where(even, tail, head), jnp.where(even, head, tail)


def beside(partner, other):
    even = is_even()
    return jnp.where(even, other, partner), jnp.where(even, partner, other)


def is_odd():
    return lax.rem(lax.axis_index("sensor"), 2) == 1


def spread(rows):
    upper = -(-rows.shape[0] // 16) * 8
    lower = rows[upper:]
    if lower.shape[0] < upper:
        lower = jnp.concatenate([lower, jnp.zeros((upper - lower.shape[0], LANES), rows.dtype)])
    return jnp.concatenate([rows[:upper], lower], axis=1)


def gathered(wide, count):
    return jnp.concatenate([wide[:, :LANES], wide[: count - wide.shape[0], LANES:]])


def rows_of(scalars):
    row = lax.broadcasted_iota(jnp.int32, (8, LANES), 0)
    out = jnp.zeros((8, LANES), jnp.float32)
    for i, scalar in enumerate(scalars):
        out = jnp.where(row == i, scalar, out)
    return out


def first_forward_body(*refs):
    loaded, (sent, edge, threshold, linked), kept, sems = refs[:10], refs[10:14], refs[14:24], refs[24]
    kernel, kernel_here = loaded[0], kept[0]
    field, multiplier, plain, weighted_t = kept[1:5]
    neighbours, tile_of_cell, tile_weight = kept[7:]
    freqs = kernel.shape[1]
    times, cells = field.shape
    half = times // 2
    copies = []

    def load(source, target):
        copy = pltpu.make_async_copy(source, target, sems.at[len(copies)])
        copy.start()
        copies.append(copy)
        return copy

    early = [load(loaded[i], kept[i]) for i in (1, 3)]
    large = []
    for start in range(0, freqs, CHUNK):
        at = (slice(None), pl.ds(start, min(CHUNK, freqs - start)))
        large.append(load(kernel.at[at], kernel_here.at[at]))
        if start == 0:
            small = [load(loaded[i], kept[i]) for i in (7, 8, 9, 2, 4)]
    late = [load(loaded[i], kept[i]) for i in (5, 6)]
    for copy in early:
        copy.wait()
    spectra = table_dot(plain[...], field[...])
    for copy in small:
        copy.wait()

    cell = lax.broadcasted_iota(jnp.int32, (4, cells), 1) + lax.axis_index("cell") * cells
    linked[0:4, :] = jnp.where(neighbours[...] != cell, 1.0, 0.0)
    linked[4:8, :] = jnp.zeros((4, cells), jnp.float32)
    tile = lax.broadcasted_iota(jnp.int32, (tile_weight.shape[1], cells), 0)
    chosen = jnp.where(tile == tile_of_cell[...], 1.0, 0.0)
    weights = jnp.dot(
        jnp.broadcast_to(tile_weight[...], (8, tile_weight.shape[1])), chosen,
        precision=lax.Precision.HIGHEST, preferred_element_type=jnp.float32,
    )
    limit = SHRINK_SCALE * weights
    threshold[...] = limit
    bottom = cells // COLS - 1
    pairs = (
        (strip(field, 0), strip(field, bottom)),
        (strip(multiplier[2], 0), strip(multiplier[3], bottom)),
        (strip(limit, 0), strip(limit, bottom)),
    )
    for (head, tail), start in zip(pairs, (0, times, 2 * times)):
        one, two = edges(head, tail)
        sent[half + start : half + start + head.shape[0], :] = one
        edge[start : start + head.shape[0], :] = two

    def arrived(group):
        if group * GROUP % CHUNK == 0:
            large[group * GROUP // CHUNK].wait()

    rows = forward_rows(spectra, kernel_here, arrived)
    sent[:half, :] = packed_series(rows, weighted_t[...], kernel.shape[2])
    for copy in late:
        copy.wait()


def first_adjoint_body(count, *refs):
    observed, two, kernel, plain_t, weighted, out = refs[count:]
    times = observed.shape[0]
    predicted = unpacked(summed(refs[:count]), kernel.shape[2])
    residual = predicted - jnp.concatenate([observed[...], observed[...]], axis=1)
    out[:times, :] = adjoint(residual, kernel, plain_t[...], weighted[...], 1)
    out[times:, :] = spread(two[...])


def response_of(field, kernel, plain, weighted_t, linked, sent, edge):
    half = field.shape[0] // 2
    rows = field.shape[1] // COLS
    one, two = edges(strip(field, 0), strip(field, rows - 1))
    squares = []
    for row in range(rows):
        here = strip(field, row)
        east = strip(linked[0:1], row) * (pltpu.roll(here, COLS - 1, 1) - here)
        squares.append(east * east)
        if row > 0:
            north = strip(linked[2:3], row) * (strip(field, row - 1) - here)
            squares.append(north * north)
    sent[:half, :] = forward(field, kernel, plain[...], weighted_t[...])
    sent[half : half + 8, :] = rows_of([square_sum(field), 2.0 * jnp.sum(tree_sum(squares))])
    sent[half + 8 :, :] = one
    edge[...] = two


def merge_body(sent, came, edge, other, linked, out):
    cells = linked.shape[1]
    top = out.shape[0]
    to_partner, to_other = edges(linked[2:3, :COLS], linked[3:4, cells - COLS :])
    across = to_partner * (came[top:, :] - sent[top:, :])
    beyond = to_other * (other[...] - edge[...])
    out[: top - 8, :] = sent[: top - 8, :] + came[: top - 8, :]
    boundary = 2.0 * square_sum(jnp.where(is_odd(), beyond, across))
    out[top - 8 :, :] = sent[top - 8 : top, :] + came[top - 8 : top, :] + rows_of([0.0, 0.0, boundary])


def first_gradient_body(count, *refs):
    (start_multiplier, one, two, passed, linked_ref, kernel, plain, weighted_t,
     adjoint_out, gradient, sent, edge, two_out) = refs[count:]
    times, cells = adjoint_out.shape
    half = times // 2
    two = jnp.where(is_odd(), two[...], gathered(passed[times:, :], two.shape[0]))
    two_out[...] = two
    linked = linked_ref[...]
    total = summed(refs[:count])
    values = [[strip(start_multiplier[k], r) for r in range(cells // COLS)] for k in range(4)]
    above, below = beside(one[half + times : half + 2 * times, :], two[times : 2 * times, :])
    field = total + gathered_jumps(values, above, below, linked)
    adjoint_out[...] = total
    gradient[...] = field
    response_of(field, kernel, plain, weighted_t, linked, sent, edge)


def second_adjoint_body(count, *refs):
    two, kernel, plain_t, weighted, out, norms = refs[count:]
    times = plain_t.shape[0]
    half = times // 2
    total = summed(refs[:count])
    packed, squares = total[:half], total[half : half + 8]
    out[:times, :] = adjoint(unpacked(packed, kernel.shape[2]), kernel, plain_t[...], weighted[...], 2)
    scalars = rows_of([square_sum(packed), squares[2:3, :] * (2.0 / lax.axis_size("sensor"))])
    out[times : times + 8, :] = jnp.concatenate([scalars] * (out.shape[1] // LANES), axis=1)
    out[times + 8 :, :] = spread(two[...])
    norms[...] = squares


def step_of(norms, scalars):
    return norms[0, 0] / (scalars[0, 0] + (norms[1, 0] + scalars[1, 0]) + TINY)


def second_gradient_body(count, *refs):
    (norms, adjoint_in, gradient_in, model, start_multiplier, threshold, one, two, grad_one, grad_two, passed, linked_ref,
     kernel, plain, weighted_t, model_out, jumps_out, multiplier_out, gradient_out, sent, edge) = refs[count:]
    times, cells = model.shape
    half = times // 2
    total = summed(refs[:count])
    step = step_of(norms, total[times:])
    linked = linked_ref[...]
    field, gradient = model[...], gradient_in[...]
    rows = cells // COLS
    above, below = beside(one[half:, :], two[...])
    field_jumps = jumps(field, above[:times], below[:times], linked)
    grad_two = jnp.where(is_odd(), grad_two[...], gathered(passed[times + 8 :, :], times))
    grad_jumps = jumps(gradient, *beside(grad_one[half + 8 :, :], grad_two), linked)

    def advance(model_jumps, old_multiplier, limit):
        shifted = model_jumps + old_multiplier
        auxiliary = shrunk(shifted, limit)
        multiplier = shifted - auxiliary
        return multiplier, model_jumps - auxiliary + multiplier

    penalties, new_jumps = [], []
    for k in range(4):
        penalties.append([])
        new_jumps.append([])
        for r in range(rows):
            new = field_jumps[k][r] - step * grad_jumps[k][r]
            multiplier, penalty = advance(new, strip(start_multiplier[k], r), strip(threshold[0:1], r))
            jumps_out[k, :, r * COLS : (r + 1) * COLS] = new
            multiplier_out[k, :, r * COLS : (r + 1) * COLS] = multiplier
            penalties[k].append(penalty)
            new_jumps[k].append(new)
    _, beside_above = advance(-new_jumps[2][0], above[times : 2 * times], above[2 * times : 2 * times + 1])
    _, beside_below = advance(-new_jumps[3][-1], below[times : 2 * times], below[2 * times : 2 * times + 1])
    back = gathered_jumps(penalties, beside_above, beside_below, linked)
    model_out[...] = field - step * gradient
    new_gradient = adjoint_in[...] - step * total[:times] + back
    gradient_out[...] = new_gradient
    response_of(new_gradient, kernel, plain, weighted_t, linked, sent, edge)


def response_body(count, *refs):
    out, norms = refs[count:]
    total = summed(refs[:count])
    packed, squares = total[:-8], total[-8:]
    out[...] = rows_of([square_sum(packed), squares[2:3, :] * (2.0 / lax.axis_size("sensor"))])
    norms[...] = squares


def finish_body(count, *refs):
    (norms, gradient_in, model, model_jumps, multiplier, threshold, grad_one, grad_two, passed, linked,
     estimate_out, auxiliary_out, multiplier_out) = refs[count:]
    step = step_of(norms, summed(refs[:count]))
    grad_two = jnp.where(is_odd(), grad_two[...], passed[...])
    half = gradient_in.shape[0] // 2
    gradient = gradient_in[...]
    estimate_out[...] = model[...] - step * gradient
    grad_jumps = jumps(gradient, *beside(grad_one[half + 8 :, :], grad_two), linked[...])
    for k in range(4):
        for r in range(gradient.shape[1] // COLS):
            at = slice(r * COLS, (r + 1) * COLS)
            shifted = model_jumps[k, :, at] - step * grad_jumps[k][r] + multiplier[k, :, at]
            auxiliary = shrunk(shifted, threshold[0:1, at])
            auxiliary_out[k, :, at] = auxiliary
            multiplier_out[k, :, at] = shifted - auxiliary


def stages_of(count, *radices):
    stages = []
    for radix in radices:
        if count > 1 and count % radix == 0:
            stages.append(radix)
            count //= radix
    while count > 1:
        stages.append(2)
        count //= 2
    return stages


def summing(parts, axis, stride, stages):
    count = lax.axis_size(axis)
    for radix in stages:
        total = tree_sum(parts)
        parts = [total] + [
            lax.ppermute(total, axis, [(i, i ^ (k * stride)) for i in range(count)]) for k in range(1, radix)
        ]
        stride *= radix
    return parts


def sensor_hop(array):
    return lax.ppermute(array, "sensor", [(i, i ^ 1) for i in range(lax.axis_size("sensor"))])


def sensor_parts(array, rows):
    passed = sensor_hop(array)
    total = array[:rows] + passed[:rows]
    return summing([total], "sensor", 2, stages_of(lax.axis_size("sensor") // 2, 2)), passed


def cell_parts(merged):
    return summing([merged], "cell", 2, stages_of(lax.axis_size("cell") // 2, 4, 4))


def from_partner(array):
    return lax.ppermute(array, "cell", [(i, i ^ 1) for i in range(lax.axis_size("cell"))])


def from_other(array):
    sensors = lax.axis_size("sensor")
    pairs = [
        (i * sensors + s, (i + 1 if i % 2 else i - 1) * sensors + s)
        for i in range(1, lax.axis_size("cell") - 1)
        for s in range(1, sensors, 2)
    ]
    return lax.ppermute(array, ("cell", "sensor"), pairs)


def per_device(kernel, observed, start_model, start_multiplier, neighbours, tile_of_cell, tile_weight):
    times, cells = start_model.shape
    freqs, sensors = kernel.shape[1:3]
    plain, weighted = tables(times, freqs)
    plain, plain_t, weighted, weighted_t = (
        jnp.asarray(table_terms(t)) for t in (plain, plain.T, weighted, weighted.T)
    )
    half = times // 2
    field, row, wide = (times, cells), (times, COLS), (4, times, cells)

    loads = [
        kernel, start_model, start_multiplier, plain, weighted_t, plain_t, weighted,
        neighbours, tile_of_cell[None, :], tile_weight[None, :],
    ]
    sent, edge, threshold, linked, kernel, start_model, start_multiplier, plain, weighted_t, plain_t, weighted = call(
        first_forward_body,
        [(half + 2 * times + 8, LANES), (2 * times + 8, LANES), (8, cells), (8, cells)]
        + [jax.ShapeDtypeStruct(a.shape, a.dtype) for a in loads[:7]],
        *[pltpu.with_memory_space_constraint(a, HBM) for a in loads],
        scratch=[VMEM(a.shape, a.dtype) for a in loads[7:]] + [pltpu.SemaphoreType.DMA((9 + -(-freqs // CHUNK),))],
        inputs=HBM,
    )
    one = from_partner(sent)
    two = from_other(edge)
    parts = cell_parts(sent[:half] + one[:half])
    message, side, shared = (half + 8 + times, LANES), (times, LANES), (2 * times + 8, LANES)
    back = call(
        functools.partial(first_adjoint_body, len(parts)), (2 * times + 8, cells),
        *parts, observed, two, kernel, plain_t, weighted,
    )
    parts, passed = sensor_parts(back, times)
    adjoint_one, gradient, sent, edge, two = call(
        functools.partial(first_gradient_body, len(parts)), [field, field, message, side, shared],
        *parts, start_multiplier, one, two, passed, linked, kernel, plain, weighted_t,
    )
    grad_one, grad_two = from_partner(sent), from_other(edge)
    parts = cell_parts(call(merge_body, (half + 8, LANES), sent, grad_one, edge, grad_two, linked))
    back, norms = call(
        functools.partial(second_adjoint_body, len(parts)), [(times + 8 + half, cells), (8, LANES)],
        *parts, grad_two, kernel, plain_t, weighted,
    )
    parts, passed = sensor_parts(back, times + 8)
    model, model_jumps, multiplier, gradient, sent, edge = call(
        functools.partial(second_gradient_body, len(parts)), [field, wide, wide, field, message, side],
        *parts, norms, adjoint_one, gradient, start_model, start_multiplier, threshold, one, two, grad_one, grad_two,
        passed, linked, kernel, plain, weighted_t,
    )
    grad_one, grad_two = from_partner(sent), from_other(edge)
    parts = cell_parts(call(merge_body, (half + 8, LANES), sent, grad_one, edge, grad_two, linked))
    passed = sensor_hop(lax.optimization_barrier((grad_two, parts[-1]))[0])
    scalars, norms = call(functools.partial(response_body, len(parts)), [(8, LANES), (8, LANES)], *parts)
    parts = summing([scalars], "sensor", 1, stages_of(lax.axis_size("sensor"), 4, 4))
    return tuple(
        call(
            functools.partial(finish_body, len(parts)), [field, wide, wide],
            *parts, norms, gradient, model, model_jumps, multiplier, threshold, grad_one, grad_two, passed, linked,
        )
    )


def solution(mesh):
    in_specs = (
        P(None, None, "sensor", "cell"),
        P(None, "sensor"),
        P(None, "cell"),
        P(None, None, "cell"),
        P(None, "cell"),
        P("cell"),
        P(),
    )
    out_specs = (P(None, "cell"), P(None, None, "cell"), P(None, None, "cell"))
    return jax.shard_map(
        per_device, mesh=mesh, in_specs=in_specs, out_specs=out_specs, check_vma=False
    )
```

```python
import functools

import jax
import jax.numpy as jnp
import numpy as np
from jax import lax
from jax.experimental import pallas as pl
from jax.experimental.pallas import tpu as pltpu
from jax.sharding import PartitionSpec as P

COLS = 128
LANES = 128
GROUP = 8
CHUNK = 24
SHRINK_SCALE = 0.4
TINY = 1e-06
VMEM = pltpu.VMEM
HBM = pltpu.HBM


def tables(times, freqs):
    padded = 2 * times
    groups = -(-freqs // GROUP)
    plain = np.zeros((16 * groups, times), np.float64)
    weighted = np.zeros((16 * groups, times), np.float64)
    for f in range(freqs):
        phase = 2.0 * np.pi * ((f * np.arange(times)) % padded) / padded
        weight = (1.0 if f in (0, freqs - 1) else 2.0) / padded
        row = 16 * (f // GROUP) + f % GROUP
        plain[row], plain[row + GROUP] = np.cos(phase), -np.sin(phase)
        weighted[row], weighted[row + GROUP] = weight * np.cos(phase), -weight * np.sin(phase)
    return plain.astype(np.float32), weighted.astype(np.float32)


def table_terms(table):
    high = table.astype(jnp.bfloat16)
    low = (table - high.astype(np.float32)).astype(jnp.bfloat16)
    return np.concatenate([high, high, low], axis=1)


def table_dot(terms, values):
    high = values.astype(jnp.bfloat16)
    low = (values - high.astype(jnp.float32)).astype(jnp.bfloat16)
    return dot_nn(terms, jnp.concatenate([high, low, high], axis=0))


def turned(rows):
    rows = rows.astype(jnp.float32)
    return jnp.concatenate([-rows[GROUP:], rows[:GROUP]], axis=0).astype(jnp.bfloat16)


def dot_nt(left, right):
    return lax.dot_general(left, right, (((1,), (1,)), ((), ())), preferred_element_type=jnp.float32)


def dot_nn(left, right):
    return jnp.dot(left, right, preferred_element_type=jnp.float32)


def slab(kernel_ref, part, group):
    freqs, sensors, cells = kernel_ref.shape[1:]
    count = min(GROUP, freqs - group * GROUP)
    block = kernel_ref[part, group * GROUP : group * GROUP + count]
    return block.reshape(count * sensors, cells)


def own_block(width, sensors):
    row = lax.broadcasted_iota(jnp.int32, (16, width), 0) % GROUP
    lane = lax.broadcasted_iota(jnp.int32, (16, width), 1) // sensors
    return row == lane


def fold(wide):
    total = functools.reduce(
        lambda a, b: a + b, [wide[:, i : i + LANES] for i in range(0, wide.shape[1], LANES)]
    )
    return total + pltpu.roll(total, LANES // 2, 1)


def forward(field, kernel_ref, plain, weighted_t):
    return packed_series(forward_rows(table_dot(plain, field), kernel_ref), weighted_t, kernel_ref.shape[2])


def forward_rows(spectra, kernel_ref, arrived=None):
    sensors = kernel_ref.shape[2]
    rows = []
    for group in range(spectra.shape[0] // 16):
        part = spectra[16 * group : 16 * group + 16]
        if arrived is not None:
            arrived(group)
        re_slab, im_slab = slab(kernel_ref, 0, group), slab(kernel_ref, 1, group)
        out = dot_nt(part.astype(jnp.bfloat16), re_slab) + dot_nt(turned(part), im_slab)
        width = out.shape[1]
        out = jnp.where(own_block(width, sensors), out, 0.0)
        if width < LANES:
            out = jnp.concatenate([out, jnp.zeros((16, LANES - width), jnp.float32)], axis=1)
        rows.append(fold(out))
    return jnp.concatenate(rows, axis=0)


def packed_series(rows, weighted_t, sensors):
    times = weighted_t.shape[0]
    series = table_dot(weighted_t, rows)
    left = lax.broadcasted_iota(jnp.int32, (times // 2, LANES), 1) < sensors
    return jnp.where(left, series[: times // 2], series[times // 2 :])


def unpacked(packed, sensors):
    other = pltpu.roll(packed, sensors, 1)
    left = lax.broadcasted_iota(jnp.int32, packed.shape, 1) < sensors
    return jnp.concatenate([jnp.where(left, packed, other), jnp.where(left, other, packed)], axis=0)


def adjoint(residual, kernel_ref, plain_t, weighted, halves):
    freqs, sensors, cells = kernel_ref.shape[1:]
    spectra = table_dot(weighted, residual)
    rows = []
    for group in range(weighted.shape[0] // 16):
        part = spectra[16 * group : 16 * group + 16]
        count = min(GROUP, freqs - group * GROUP)
        width = count * sensors
        re_slab, im_slab = slab(kernel_ref, 0, group), slab(kernel_ref, 1, group)
        wide = jnp.concatenate([part] * (-(-width // LANES)), axis=1)[:, :width]
        wide = jnp.where(own_block(width, sensors), wide, 0.0)
        terms = []
        for _ in range(halves):
            terms.append(wide.astype(jnp.bfloat16))
            wide = wide - terms[-1].astype(jnp.float32)
        left = jnp.concatenate(terms, axis=0)
        swapped = jnp.concatenate([turned(term) for term in terms], axis=0)
        out = dot_nn(left, re_slab) - dot_nn(swapped, im_slab)
        rows.append(tree_sum([out[16 * i : 16 * i + 16] for i in range(halves)]))
    return table_dot(plain_t, jnp.concatenate(rows, axis=0))


def strip(array, row):
    return array[..., row * COLS : (row + 1) * COLS]


def jumps(field, above, below, linked):
    count = field.shape[1] // COLS
    out = []
    for direction in range(4):
        strips = []
        for row in range(count):
            here = strip(field, row)
            if direction == 0:
                there = pltpu.roll(here, COLS - 1, 1)
            elif direction == 1:
                there = pltpu.roll(here, 1, 1)
            elif direction == 2:
                there = above if row == 0 else strip(field, row - 1)
            else:
                there = below if row == count - 1 else strip(field, row + 1)
            strips.append(strip(linked[direction : direction + 1], row) * (there - here))
        out.append(strips)
    return out


def gathered_jumps(values, above, below, linked):
    count = len(values[0])
    out = []
    for row in range(count):
        arriving = (
            pltpu.roll(values[1][row], COLS - 1, 1),
            pltpu.roll(values[0][row], 1, 1),
            above if row == 0 else values[3][row - 1],
            below if row == count - 1 else values[2][row + 1],
        )
        total = None
        for direction in range(4):
            term = strip(linked[direction : direction + 1], row) * (arriving[direction] - values[direction][row])
            total = term if total is None else total + term
        out.append(total)
    return jnp.concatenate(out, axis=1)


def shrunk(shifted, threshold):
    return shifted - jnp.clip(shifted, -threshold, threshold)


def tree_sum(parts):
    parts = list(parts)
    while len(parts) > 1:
        parts = [parts[i] + parts[i + 1] if i + 1 < len(parts) else parts[i] for i in range(0, len(parts), 2)]
    return parts[0]


def square_sum(array):
    return jnp.sum(array * array)


def block_of(scalar, rows=8):
    return jnp.full((rows, LANES), scalar, jnp.float32)


def call(body, out_shapes, *operands, scratch=(), inputs=VMEM, outputs=VMEM):
    single = isinstance(out_shapes, tuple)
    shapes = [out_shapes] if single else list(out_shapes)
    shapes = [s if isinstance(s, jax.ShapeDtypeStruct) else jax.ShapeDtypeStruct(s, jnp.float32) for s in shapes]
    out = pl.pallas_call(
        body,
        out_shape=shapes,
        in_specs=[pl.BlockSpec(memory_space=inputs)] * len(operands),
        out_specs=[pl.BlockSpec(memory_space=outputs)] * len(shapes),
        scratch_shapes=list(scratch),
        compiler_params=pltpu.CompilerParams(vmem_limit_bytes=24 * 2**20),
    )(*operands)
    return out[0] if single else out


def summed(parts):
    return tree_sum([part[...] for part in parts])


def is_even():
    return lax.rem(lax.axis_index("cell"), 2) == 0


def edges(head, tail):
    even = is_even()
    return jnp.where(even, tail, head), jnp.where(even, head, tail)


def beside(partner, other):
    even = is_even()
    return jnp.where(even, other, partner), jnp.where(even, partner, other)


def is_odd():
    return lax.rem(lax.axis_index("sensor"), 2) == 1


def spread(rows):
    upper = -(-rows.shape[0] // 16) * 8
    lower = rows[upper:]
    if lower.shape[0] < upper:
        lower = jnp.concatenate([lower, jnp.zeros((upper - lower.shape[0], LANES), rows.dtype)])
    return jnp.concatenate([rows[:upper], lower], axis=1)


def gathered(wide, count):
    return jnp.concatenate([wide[:, :LANES], wide[: count - wide.shape[0], LANES:]])


def rows_of(scalars):
    row = lax.broadcasted_iota(jnp.int32, (8, LANES), 0)
    out = jnp.zeros((8, LANES), jnp.float32)
    for i, scalar in enumerate(scalars):
        out = jnp.where(row == i, scalar, out)
    return out


def first_forward_body(*refs):
    loaded, (sent, edge, threshold, linked), kept, sems = refs[:10], refs[10:14], refs[14:24], refs[24]
    kernel, kernel_here = loaded[0], kept[0]
    field, multiplier, plain, weighted_t = kept[1:5]
    neighbours, tile_of_cell, tile_weight = kept[7:]
    freqs = kernel.shape[1]
    times, cells = field.shape
    half = times // 2
    copies = []

    def load(source, target):
        copy = pltpu.make_async_copy(source, target, sems.at[len(copies)])
        copy.start()
        copies.append(copy)
        return copy

    early = [load(loaded[i], kept[i]) for i in (1, 3)]
    large = []
    for start in range(0, freqs, CHUNK):
        at = (slice(None), pl.ds(start, min(CHUNK, freqs - start)))
        large.append(load(kernel.at[at], kernel_here.at[at]))
        if start == 0:
            small = [load(loaded[i], kept[i]) for i in (7, 8, 9, 2, 4)]
    late = [load(loaded[i], kept[i]) for i in (5, 6)]
    for copy in early:
        copy.wait()
    spectra = table_dot(plain[...], field[...])
    for copy in small:
        copy.wait()

    cell = lax.broadcasted_iota(jnp.int32, (4, cells), 1) + lax.axis_index("cell") * cells
    linked[0:4, :] = jnp.where(neighbours[...] != cell, 1.0, 0.0)
    linked[4:8, :] = jnp.zeros((4, cells), jnp.float32)
    tile = lax.broadcasted_iota(jnp.int32, (tile_weight.shape[1], cells), 0)
    chosen = jnp.where(tile == tile_of_cell[...], 1.0, 0.0)
    weights = jnp.dot(
        jnp.broadcast_to(tile_weight[...], (8, tile_weight.shape[1])), chosen,
        precision=lax.Precision.HIGHEST, preferred_element_type=jnp.float32,
    )
    limit = SHRINK_SCALE * weights
    threshold[...] = limit
    bottom = cells // COLS - 1
    pairs = (
        (strip(field, 0), strip(field, bottom)),
        (strip(multiplier[2], 0), strip(multiplier[3], bottom)),
        (strip(limit, 0), strip(limit, bottom)),
    )
    for (head, tail), start in zip(pairs, (0, times, 2 * times)):
        one, two = edges(head, tail)
        sent[half + start : half + start + head.shape[0], :] = one
        edge[start : start + head.shape[0], :] = two

    def arrived(group):
        if group * GROUP % CHUNK == 0:
            large[group * GROUP // CHUNK].wait()

    rows = forward_rows(spectra, kernel_here, arrived)
    sent[:half, :] = packed_series(rows, weighted_t[...], kernel.shape[2])
    for copy in late:
        copy.wait()


def first_adjoint_body(count, *refs):
    observed, two, kernel, plain_t, weighted, out = refs[count:]
    times = observed.shape[0]
    predicted = unpacked(summed(refs[:count]), kernel.shape[2])
    residual = predicted - jnp.concatenate([observed[...], observed[...]], axis=1)
    out[:times, :] = adjoint(residual, kernel, plain_t[...], weighted[...], 1)
    out[times:, :] = spread(two[...])


def response_of(field, kernel, plain, weighted_t, linked, sent, edge):
    half = field.shape[0] // 2
    rows = field.shape[1] // COLS
    one, two = edges(strip(field, 0), strip(field, rows - 1))
    squares = []
    for row in range(rows):
        here = strip(field, row)
        east = strip(linked[0:1], row) * (pltpu.roll(here, COLS - 1, 1) - here)
        squares.append(east * east)
        if row > 0:
            north = strip(linked[2:3], row) * (strip(field, row - 1) - here)
            squares.append(north * north)
    sent[:half, :] = forward(field, kernel, plain[...], weighted_t[...])
    sent[half : half + 8, :] = rows_of([square_sum(field), 2.0 * jnp.sum(tree_sum(squares))])
    sent[half + 8 :, :] = one
    edge[...] = two


def merge_body(sent, came, edge, other, linked, out):
    cells = linked.shape[1]
    top = out.shape[0]
    to_partner, to_other = edges(linked[2:3, :COLS], linked[3:4, cells - COLS :])
    across = to_partner * (came[top:, :] - sent[top:, :])
    beyond = to_other * (other[...] - edge[...])
    out[: top - 8, :] = sent[: top - 8, :] + came[: top - 8, :]
    boundary = 2.0 * square_sum(jnp.where(is_odd(), beyond, across))
    out[top - 8 :, :] = sent[top - 8 : top, :] + came[top - 8 : top, :] + rows_of([0.0, 0.0, boundary])


def first_gradient_body(count, *refs):
    (start_multiplier, one, two, passed, linked_ref, kernel, plain, weighted_t,
     adjoint_out, gradient, sent, edge, two_out) = refs[count:]
    times, cells = adjoint_out.shape
    half = times // 2
    two = jnp.where(is_odd(), two[...], gathered(passed[times:, :], two.shape[0]))
    two_out[...] = two
    linked = linked_ref[...]
    total = summed(refs[:count])
    values = [[strip(start_multiplier[k], r) for r in range(cells // COLS)] for k in range(4)]
    above, below = beside(one[half + times : half + 2 * times, :], two[times : 2 * times, :])
    field = total + gathered_jumps(values, above, below, linked)
    adjoint_out[...] = total
    gradient[...] = field
    response_of(field, kernel, plain, weighted_t, linked, sent, edge)


def second_adjoint_body(count, *refs):
    two, kernel, plain_t, weighted, out, norms = refs[count:]
    times = plain_t.shape[0]
    half = times // 2
    total = summed(refs[:count])
    packed, squares = total[:half], total[half : half + 8]
    out[:times, :] = adjoint(unpacked(packed, kernel.shape[2]), kernel, plain_t[...], weighted[...], 2)
    scalars = rows_of([square_sum(packed), squares[2:3, :] * (2.0 / lax.axis_size("sensor"))])
    out[times : times + 8, :] = jnp.concatenate([scalars] * (out.shape[1] // LANES), axis=1)
    out[times + 8 :, :] = spread(two[...])
    norms[...] = squares


def step_of(norms, scalars):
    return norms[0, 0] / (scalars[0, 0] + (norms[1, 0] + scalars[1, 0]) + TINY)


def second_gradient_body(count, *refs):
    (norms, adjoint_in, gradient_in, model, start_multiplier, threshold, one, two, grad_one, grad_two, passed, linked_ref,
     kernel, plain, weighted_t, model_out, jumps_out, multiplier_out, gradient_out, sent, edge) = refs[count:]
    times, cells = model.shape
    half = times // 2
    total = summed(refs[:count])
    step = step_of(norms, total[times:])
    linked = linked_ref[...]
    field, gradient = model[...], gradient_in[...]
    rows = cells // COLS
    above, below = beside(one[half:, :], two[...])
    field_jumps = jumps(field, above[:times], below[:times], linked)
    grad_two = jnp.where(is_odd(), grad_two[...], gathered(passed[times + 8 :, :], times))
    grad_jumps = jumps(gradient, *beside(grad_one[half + 8 :, :], grad_two), linked)

    def advance(model_jumps, old_multiplier, limit):
        shifted = model_jumps + old_multiplier
        auxiliary = shrunk(shifted, limit)
        multiplier = shifted - auxiliary
        return multiplier, model_jumps - auxiliary + multiplier

    penalties, new_jumps = [], []
    for k in range(4):
        penalties.append([])
        new_jumps.append([])
        for r in range(rows):
            new = field_jumps[k][r] - step * grad_jumps[k][r]
            multiplier, penalty = advance(new, strip(start_multiplier[k], r), strip(threshold[0:1], r))
            jumps_out[k, :, r * COLS : (r + 1) * COLS] = new
            multiplier_out[k, :, r * COLS : (r + 1) * COLS] = multiplier
            penalties[k].append(penalty)
            new_jumps[k].append(new)
    _, beside_above = advance(-new_jumps[2][0], above[times : 2 * times], above[2 * times : 2 * times + 1])
    _, beside_below = advance(-new_jumps[3][-1], below[times : 2 * times], below[2 * times : 2 * times + 1])
    back = gathered_jumps(penalties, beside_above, beside_below, linked)
    model_out[...] = field - step * gradient
    new_gradient = adjoint_in[...] - step * total[:times] + back
    gradient_out[...] = new_gradient
    response_of(new_gradient, kernel, plain, weighted_t, linked, sent, edge)


def response_body(count, *refs):
    out, norms = refs[count:]
    total = summed(refs[:count])
    packed, squares = total[:-8], total[-8:]
    out[...] = rows_of([square_sum(packed), squares[2:3, :] * (2.0 / lax.axis_size("sensor"))])
    norms[...] = squares


def finish_body(count, *refs):
    (norms, gradient_in, model, model_jumps, multiplier, threshold, grad_one, grad_two, passed, linked,
     estimate_out, auxiliary_out, multiplier_out, estimate_here, auxiliary_here, multiplier_here, sems) = refs[count:]
    step = step_of(norms, summed(refs[:count]))
    grad_two = jnp.where(is_odd(), grad_two[...], passed[...])
    half = gradient_in.shape[0] // 2
    gradient = gradient_in[...]
    copies = []

    def store(source, target):
        copy = pltpu.make_async_copy(source, target, sems.at[len(copies)])
        copy.start()
        copies.append(copy)

    estimate_here[...] = model[...] - step * gradient
    store(estimate_here, estimate_out)
    grad_jumps = jumps(gradient, *beside(grad_one[half + 8 :, :], grad_two), linked[...])
    for k in range(4):
        for r in range(gradient.shape[1] // COLS):
            at = slice(r * COLS, (r + 1) * COLS)
            shifted = model_jumps[k, :, at] - step * grad_jumps[k][r] + multiplier[k, :, at]
            auxiliary = shrunk(shifted, threshold[0:1, at])
            auxiliary_here[k, :, at] = auxiliary
            multiplier_here[k, :, at] = shifted - auxiliary
        store(auxiliary_here.at[k], auxiliary_out.at[k])
        store(multiplier_here.at[k], multiplier_out.at[k])
    for copy in copies:
        copy.wait()


def stages_of(count, *radices):
    stages = []
    for radix in radices:
        if count > 1 and count % radix == 0:
            stages.append(radix)
            count //= radix
    while count > 1:
        stages.append(2)
        count //= 2
    return stages


def summing(parts, axis, stride, stages):
    count = lax.axis_size(axis)
    for radix in stages:
        total = tree_sum(parts)
        parts = [total] + [
            lax.ppermute(total, axis, [(i, i ^ (k * stride)) for i in range(count)]) for k in range(1, radix)
        ]
        stride *= radix
    return parts


def sensor_hop(array):
    return lax.ppermute(array, "sensor", [(i, i ^ 1) for i in range(lax.axis_size("sensor"))])


def sensor_parts(array, rows):
    passed = sensor_hop(array)
    total = array[:rows] + passed[:rows]
    return summing([total], "sensor", 2, stages_of(lax.axis_size("sensor") // 2, 2)), passed


def cell_parts(merged):
    return summing([merged], "cell", 2, stages_of(lax.axis_size("cell") // 2, 4, 4))


def from_partner(array):
    return lax.ppermute(array, "cell", [(i, i ^ 1) for i in range(lax.axis_size("cell"))])


def from_other(array):
    sensors = lax.axis_size("sensor")
    pairs = [
        (i * sensors + s, (i + 1 if i % 2 else i - 1) * sensors + s)
        for i in range(1, lax.axis_size("cell") - 1)
        for s in range(1, sensors, 2)
    ]
    return lax.ppermute(array, ("cell", "sensor"), pairs)


def per_device(kernel, observed, start_model, start_multiplier, neighbours, tile_of_cell, tile_weight):
    times, cells = start_model.shape
    freqs, sensors = kernel.shape[1:3]
    plain, weighted = tables(times, freqs)
    plain, plain_t, weighted, weighted_t = (
        jnp.asarray(table_terms(t)) for t in (plain, plain.T, weighted, weighted.T)
    )
    half = times // 2
    field, row, wide = (times, cells), (times, COLS), (4, times, cells)

    loads = [
        kernel, start_model, start_multiplier, plain, weighted_t, plain_t, weighted,
        neighbours, tile_of_cell[None, :], tile_weight[None, :],
    ]
    sent, edge, threshold, linked, kernel, start_model, start_multiplier, plain, weighted_t, plain_t, weighted = call(
        first_forward_body,
        [(half + 2 * times + 8, LANES), (2 * times + 8, LANES), (8, cells), (8, cells)]
        + [jax.ShapeDtypeStruct(a.shape, a.dtype) for a in loads[:7]],
        *[pltpu.with_memory_space_constraint(a, HBM) for a in loads],
        scratch=[VMEM(a.shape, a.dtype) for a in loads[7:]] + [pltpu.SemaphoreType.DMA((9 + -(-freqs // CHUNK),))],
        inputs=HBM,
    )
    one = from_partner(sent)
    two = from_other(edge)
    parts = cell_parts(sent[:half] + one[:half])
    message, side, shared = (half + 8 + times, LANES), (times, LANES), (2 * times + 8, LANES)
    back = call(
        functools.partial(first_adjoint_body, len(parts)), (2 * times + 8, cells),
        *parts, observed, two, kernel, plain_t, weighted,
    )
    parts, passed = sensor_parts(back, times)
    adjoint_one, gradient, sent, edge, two = call(
        functools.partial(first_gradient_body, len(parts)), [field, field, message, side, shared],
        *parts, start_multiplier, one, two, passed, linked, kernel, plain, weighted_t,
    )
    grad_one, grad_two = from_partner(sent), from_other(edge)
    parts = cell_parts(call(merge_body, (half + 8, LANES), sent, grad_one, edge, grad_two, linked))
    back, norms = call(
        functools.partial(second_adjoint_body, len(parts)), [(times + 8 + half, cells), (8, LANES)],
        *parts, grad_two, kernel, plain_t, weighted,
    )
    parts, passed = sensor_parts(back, times + 8)
    model, model_jumps, multiplier, gradient, sent, edge = call(
        functools.partial(second_gradient_body, len(parts)), [field, wide, wide, field, message, side],
        *parts, norms, adjoint_one, gradient, start_model, start_multiplier, threshold, one, two, grad_one, grad_two,
        passed, linked, kernel, plain, weighted_t,
    )
    grad_one, grad_two = from_partner(sent), from_other(edge)
    parts = cell_parts(call(merge_body, (half + 8, LANES), sent, grad_one, edge, grad_two, linked))
    scalars, norms = call(functools.partial(response_body, len(parts)), [(8, LANES), (8, LANES)], *parts)
    passed = sensor_hop(lax.optimization_barrier((grad_two, norms))[0])
    parts = summing([scalars], "sensor", 1, stages_of(lax.axis_size("sensor"), 4, 4))
    return tuple(
        call(
            functools.partial(finish_body, len(parts)), [field, wide, wide],
            *parts, norms, gradient, model, model_jumps, multiplier, threshold, grad_one, grad_two, passed, linked,
            scratch=[VMEM(shape, jnp.float32) for shape in (field, wide, wide)] + [pltpu.SemaphoreType.DMA((9,))],
            outputs=HBM,
        )
    )


def solution(mesh):
    in_specs = (
        P(None, None, "sensor", "cell"),
        P(None, "sensor"),
        P(None, "cell"),
        P(None, None, "cell"),
        P(None, "cell"),
        P("cell"),
        P(),
    )
    out_specs = (P(None, "cell"), P(None, None, "cell"), P(None, None, "cell"))
    return jax.shard_map(
        per_device, mesh=mesh, in_specs=in_specs, out_specs=out_specs, check_vma=False
    )
```

```python
import functools

import jax
import jax.numpy as jnp
import numpy as np
from jax import lax
from jax.experimental import pallas as pl
from jax.experimental.pallas import tpu as pltpu
from jax.sharding import PartitionSpec as P

COLS = 128
LANES = 128
GROUP = 8
CHUNK = 24
SHRINK_SCALE = 0.4
TINY = 1e-06
VMEM = pltpu.VMEM
HBM = pltpu.HBM


def tables(times, freqs):
    padded = 2 * times
    groups = -(-freqs // GROUP)
    plain = np.zeros((16 * groups, times), np.float64)
    weighted = np.zeros((16 * groups, times), np.float64)
    for f in range(freqs):
        phase = 2.0 * np.pi * ((f * np.arange(times)) % padded) / padded
        weight = (1.0 if f in (0, freqs - 1) else 2.0) / padded
        row = 16 * (f // GROUP) + f % GROUP
        plain[row], plain[row + GROUP] = np.cos(phase), -np.sin(phase)
        weighted[row], weighted[row + GROUP] = weight * np.cos(phase), -weight * np.sin(phase)
    return plain.astype(np.float32), weighted.astype(np.float32)


def table_terms(table):
    high = table.astype(jnp.bfloat16)
    low = (table - high.astype(np.float32)).astype(jnp.bfloat16)
    return np.concatenate([high, high, low], axis=1)


def table_dot(terms, values):
    high = values.astype(jnp.bfloat16)
    low = (values - high.astype(jnp.float32)).astype(jnp.bfloat16)
    return dot_nn(terms, jnp.concatenate([high, low, high], axis=0))


def turned(rows):
    rows = rows.astype(jnp.float32)
    return jnp.concatenate([-rows[GROUP:], rows[:GROUP]], axis=0).astype(jnp.bfloat16)


def dot_nt(left, right):
    return lax.dot_general(left, right, (((1,), (1,)), ((), ())), preferred_element_type=jnp.float32)


def dot_nn(left, right):
    return jnp.dot(left, right, preferred_element_type=jnp.float32)


def slab(kernel_ref, part, group):
    freqs, sensors, cells = kernel_ref.shape[1:]
    count = min(GROUP, freqs - group * GROUP)
    block = kernel_ref[part, group * GROUP : group * GROUP + count]
    return block.reshape(count * sensors, cells)


def own_block(width, sensors):
    row = lax.broadcasted_iota(jnp.int32, (16, width), 0) % GROUP
    lane = lax.broadcasted_iota(jnp.int32, (16, width), 1) // sensors
    return row == lane


def fold(wide):
    total = functools.reduce(
        lambda a, b: a + b, [wide[:, i : i + LANES] for i in range(0, wide.shape[1], LANES)]
    )
    return total + pltpu.roll(total, LANES // 2, 1)


def forward(field, kernel_ref, plain, weighted_t):
    return packed_series(forward_rows(table_dot(plain, field), kernel_ref), weighted_t, kernel_ref.shape[2])


def forward_rows(spectra, kernel_ref, arrived=None):
    sensors = kernel_ref.shape[2]
    rows = []
    for group in range(spectra.shape[0] // 16):
        part = spectra[16 * group : 16 * group + 16]
        if arrived is not None:
            arrived(group)
        re_slab, im_slab = slab(kernel_ref, 0, group), slab(kernel_ref, 1, group)
        out = dot_nt(part.astype(jnp.bfloat16), re_slab) + dot_nt(turned(part), im_slab)
        width = out.shape[1]
        out = jnp.where(own_block(width, sensors), out, 0.0)
        if width < LANES:
            out = jnp.concatenate([out, jnp.zeros((16, LANES - width), jnp.float32)], axis=1)
        rows.append(fold(out))
    return jnp.concatenate(rows, axis=0)


def packed_series(rows, weighted_t, sensors):
    times = weighted_t.shape[0]
    series = table_dot(weighted_t, rows)
    left = lax.broadcasted_iota(jnp.int32, (times // 2, LANES), 1) < sensors
    return jnp.where(left, series[: times // 2], series[times // 2 :])


def unpacked(packed, sensors):
    other = pltpu.roll(packed, sensors, 1)
    left = lax.broadcasted_iota(jnp.int32, packed.shape, 1) < sensors
    return jnp.concatenate([jnp.where(left, packed, other), jnp.where(left, other, packed)], axis=0)


def adjoint(residual, kernel_ref, plain_t, weighted, halves):
    freqs, sensors, cells = kernel_ref.shape[1:]
    spectra = table_dot(weighted, residual)
    rows = []
    for group in range(weighted.shape[0] // 16):
        part = spectra[16 * group : 16 * group + 16]
        count = min(GROUP, freqs - group * GROUP)
        width = count * sensors
        re_slab, im_slab = slab(kernel_ref, 0, group), slab(kernel_ref, 1, group)
        wide = jnp.concatenate([part] * (-(-width // LANES)), axis=1)[:, :width]
        wide = jnp.where(own_block(width, sensors), wide, 0.0)
        terms = []
        for _ in range(halves):
            terms.append(wide.astype(jnp.bfloat16))
            wide = wide - terms[-1].astype(jnp.float32)
        left = jnp.concatenate(terms, axis=0)
        swapped = jnp.concatenate([turned(term) for term in terms], axis=0)
        out = dot_nn(left, re_slab) - dot_nn(swapped, im_slab)
        rows.append(tree_sum([out[16 * i : 16 * i + 16] for i in range(halves)]))
    return table_dot(plain_t, jnp.concatenate(rows, axis=0))


def strip(array, row):
    return array[..., row * COLS : (row + 1) * COLS]


def jumps(field, above, below, linked):
    count = field.shape[1] // COLS
    out = []
    for direction in range(4):
        strips = []
        for row in range(count):
            here = strip(field, row)
            if direction == 0:
                there = pltpu.roll(here, COLS - 1, 1)
            elif direction == 1:
                there = pltpu.roll(here, 1, 1)
            elif direction == 2:
                there = above if row == 0 else strip(field, row - 1)
            else:
                there = below if row == count - 1 else strip(field, row + 1)
            strips.append(strip(linked[direction : direction + 1], row) * (there - here))
        out.append(strips)
    return out


def gathered_jumps(values, above, below, linked):
    count = len(values[0])
    out = []
    for row in range(count):
        arriving = (
            pltpu.roll(values[1][row], COLS - 1, 1),
            pltpu.roll(values[0][row], 1, 1),
            above if row == 0 else values[3][row - 1],
            below if row == count - 1 else values[2][row + 1],
        )
        total = None
        for direction in range(4):
            term = strip(linked[direction : direction + 1], row) * (arriving[direction] - values[direction][row])
            total = term if total is None else total + term
        out.append(total)
    return jnp.concatenate(out, axis=1)


def shrunk(shifted, threshold):
    return shifted - jnp.clip(shifted, -threshold, threshold)


def tree_sum(parts):
    parts = list(parts)
    while len(parts) > 1:
        parts = [parts[i] + parts[i + 1] if i + 1 < len(parts) else parts[i] for i in range(0, len(parts), 2)]
    return parts[0]


def square_sum(array):
    return jnp.sum(array * array)


def block_of(scalar, rows=8):
    return jnp.full((rows, LANES), scalar, jnp.float32)


def call(body, out_shapes, *operands, scratch=(), inputs=VMEM, outputs=VMEM):
    single = isinstance(out_shapes, tuple)
    shapes = [out_shapes] if single else list(out_shapes)
    shapes = [s if isinstance(s, jax.ShapeDtypeStruct) else jax.ShapeDtypeStruct(s, jnp.float32) for s in shapes]
    out = pl.pallas_call(
        body,
        out_shape=shapes,
        in_specs=[pl.BlockSpec(memory_space=inputs)] * len(operands),
        out_specs=[pl.BlockSpec(memory_space=outputs)] * len(shapes),
        scratch_shapes=list(scratch),
        compiler_params=pltpu.CompilerParams(vmem_limit_bytes=24 * 2**20),
    )(*operands)
    return out[0] if single else out


def summed(parts):
    return tree_sum([part[...] for part in parts])


def is_even():
    return lax.rem(lax.axis_index("cell"), 2) == 0


def edges(head, tail):
    even = is_even()
    return jnp.where(even, tail, head), jnp.where(even, head, tail)


def beside(partner, other):
    even = is_even()
    return jnp.where(even, other, partner), jnp.where(even, partner, other)


def is_odd():
    return lax.rem(lax.axis_index("sensor"), 2) == 1


def spread(rows):
    upper = -(-rows.shape[0] // 16) * 8
    lower = rows[upper:]
    if lower.shape[0] < upper:
        lower = jnp.concatenate([lower, jnp.zeros((upper - lower.shape[0], LANES), rows.dtype)])
    return jnp.concatenate([rows[:upper], lower], axis=1)


def gathered(wide, count):
    return jnp.concatenate([wide[:, :LANES], wide[: count - wide.shape[0], LANES:]])


def rows_of(scalars):
    row = lax.broadcasted_iota(jnp.int32, (8, LANES), 0)
    out = jnp.zeros((8, LANES), jnp.float32)
    for i, scalar in enumerate(scalars):
        out = jnp.where(row == i, scalar, out)
    return out


def first_forward_body(*refs):
    loaded, (sent, edge, threshold, linked), kept, sems = refs[:10], refs[10:14], refs[14:24], refs[24]
    kernel, kernel_here = loaded[0], kept[0]
    field, multiplier, plain, weighted_t = kept[1:5]
    neighbours, tile_of_cell, tile_weight = kept[7:]
    freqs = kernel.shape[1]
    times, cells = field.shape
    half = times // 2
    copies = []

    def load(source, target):
        copy = pltpu.make_async_copy(source, target, sems.at[len(copies)])
        copy.start()
        copies.append(copy)
        return copy

    early = [load(loaded[i], kept[i]) for i in (1, 3)]
    large = []
    for start in range(0, freqs, CHUNK):
        at = (slice(None), pl.ds(start, min(CHUNK, freqs - start)))
        large.append(load(kernel.at[at], kernel_here.at[at]))
        if start == 0:
            small = [load(loaded[i], kept[i]) for i in (7, 8, 9, 2, 4)]
    late = [load(loaded[i], kept[i]) for i in (5, 6)]
    for copy in early:
        copy.wait()
    spectra = table_dot(plain[...], field[...])
    for copy in small:
        copy.wait()

    cell = lax.broadcasted_iota(jnp.int32, (4, cells), 1) + lax.axis_index("cell") * cells
    linked[0:4, :] = jnp.where(neighbours[...] != cell, 1.0, 0.0)
    linked[4:8, :] = jnp.zeros((4, cells), jnp.float32)
    tile = lax.broadcasted_iota(jnp.int32, (tile_weight.shape[1], cells), 0)
    chosen = jnp.where(tile == tile_of_cell[...], 1.0, 0.0)
    weights = jnp.dot(
        jnp.broadcast_to(tile_weight[...], (8, tile_weight.shape[1])), chosen,
        precision=lax.Precision.HIGHEST, preferred_element_type=jnp.float32,
    )
    limit = SHRINK_SCALE * weights
    threshold[...] = limit
    bottom = cells // COLS - 1
    pairs = (
        (strip(field, 0), strip(field, bottom)),
        (strip(multiplier[2], 0), strip(multiplier[3], bottom)),
        (strip(limit, 0), strip(limit, bottom)),
    )
    for (head, tail), start in zip(pairs, (0, times, 2 * times)):
        one, two = edges(head, tail)
        sent[half + start : half + start + head.shape[0], :] = one
        edge[start : start + head.shape[0], :] = two

    def arrived(group):
        if group * GROUP % CHUNK == 0:
            large[group * GROUP // CHUNK].wait()

    rows = forward_rows(spectra, kernel_here, arrived)
    sent[:half, :] = packed_series(rows, weighted_t[...], kernel.shape[2])
    for copy in late:
        copy.wait()


def first_adjoint_body(count, *refs):
    observed, two, kernel, plain_t, weighted, out = refs[count:]
    times = observed.shape[0]
    predicted = unpacked(summed(refs[:count]), kernel.shape[2])
    residual = predicted - jnp.concatenate([observed[...], observed[...]], axis=1)
    out[:times, :] = adjoint(residual, kernel, plain_t[...], weighted[...], 1)
    out[times:, :] = spread(two[...])


def response_of(field, kernel, plain, weighted_t, linked, sent, edge):
    half = field.shape[0] // 2
    rows = field.shape[1] // COLS
    one, two = edges(strip(field, 0), strip(field, rows - 1))
    squares = []
    for row in range(rows):
        here = strip(field, row)
        east = strip(linked[0:1], row) * (pltpu.roll(here, COLS - 1, 1) - here)
        squares.append(east * east)
        if row > 0:
            north = strip(linked[2:3], row) * (strip(field, row - 1) - here)
            squares.append(north * north)
    sent[:half, :] = forward(field, kernel, plain[...], weighted_t[...])
    sent[half : half + 8, :] = rows_of([square_sum(field), 2.0 * jnp.sum(tree_sum(squares))])
    sent[half + 8 :, :] = one
    edge[...] = two


def merge_body(sent, came, edge, other, linked, out):
    cells = linked.shape[1]
    top = out.shape[0]
    to_partner, to_other = edges(linked[2:3, :COLS], linked[3:4, cells - COLS :])
    across = to_partner * (came[top:, :] - sent[top:, :])
    beyond = to_other * (other[...] - edge[...])
    out[: top - 8, :] = sent[: top - 8, :] + came[: top - 8, :]
    boundary = 2.0 * square_sum(jnp.where(is_odd(), beyond, across))
    out[top - 8 :, :] = sent[top - 8 : top, :] + came[top - 8 : top, :] + rows_of([0.0, 0.0, boundary])


def start_back_body(start_multiplier, one, two, passed, linked, back, two_out):
    times, cells = back.shape
    half = times // 2
    two = jnp.where(is_odd(), two[...], gathered(passed[times:, :], two.shape[0]))
    two_out[...] = two
    values = [[strip(start_multiplier[k], r) for r in range(cells // COLS)] for k in range(4)]
    above, below = beside(one[half + times : half + 2 * times, :], two[times : 2 * times, :])
    back[...] = gathered_jumps(values, above, below, linked[...])


def first_gradient_body(count, *refs):
    back, linked, kernel, plain, weighted_t, adjoint_out, gradient, sent, edge = refs[count:]
    total = summed(refs[:count])
    field = total + back[...]
    adjoint_out[...] = total
    gradient[...] = field
    response_of(field, kernel, plain, weighted_t, linked[...], sent, edge)


def second_adjoint_body(count, *refs):
    two, kernel, plain_t, weighted, out, norms = refs[count:]
    times = plain_t.shape[0]
    half = times // 2
    total = summed(refs[:count])
    packed, squares = total[:half], total[half : half + 8]
    out[:times, :] = adjoint(unpacked(packed, kernel.shape[2]), kernel, plain_t[...], weighted[...], 2)
    scalars = rows_of([square_sum(packed), squares[2:3, :] * (2.0 / lax.axis_size("sensor"))])
    out[times : times + 8, :] = jnp.concatenate([scalars] * (out.shape[1] // LANES), axis=1)
    out[times + 8 :, :] = spread(two[...])
    norms[...] = squares


def step_of(norms, scalars):
    return norms[0, 0] / (scalars[0, 0] + (norms[1, 0] + scalars[1, 0]) + TINY)


def both_jumps_body(model, gradient, one, two, grad_one, grad_two, passed, linked, model_jumps, grad_jumps):
    times, cells = model.shape
    half = times // 2
    above, below = beside(one[half : half + times, :], two[:times, :])
    from_other = jnp.where(is_odd(), grad_two[...], gathered(passed[times + 8 :, :], times))
    halos = ((above, below), beside(grad_one[half + 8 :, :], from_other))
    for field, (above, below), out in zip((model, gradient), halos, (model_jumps, grad_jumps)):
        for k, strips in enumerate(jumps(field[...], above, below, linked[...])):
            for r, values in enumerate(strips):
                out[k, :, r * COLS : (r + 1) * COLS] = values


def second_gradient_body(count, *refs):
    (norms, adjoint_in, gradient_in, model, model_jumps, grad_jumps, start_multiplier, threshold, one, two, linked_ref,
     kernel, plain, weighted_t, model_out, jumps_out, multiplier_out, gradient_out, sent, edge) = refs[count:]
    times, cells = model.shape
    half = times // 2
    total = summed(refs[:count])
    step = step_of(norms, total[times:])
    linked = linked_ref[...]
    field, gradient = model[...], gradient_in[...]
    rows = cells // COLS
    above, below = beside(one[half:, :], two[...])

    def advance(model_jumps, old_multiplier, limit):
        shifted = model_jumps + old_multiplier
        auxiliary = shrunk(shifted, limit)
        multiplier = shifted - auxiliary
        return multiplier, model_jumps - auxiliary + multiplier

    penalties, new_jumps = [], []
    for k in range(4):
        penalties.append([])
        new_jumps.append([])
        for r in range(rows):
            at = slice(r * COLS, (r + 1) * COLS)
            new = model_jumps[k, :, at] - step * grad_jumps[k, :, at]
            multiplier, penalty = advance(new, strip(start_multiplier[k], r), strip(threshold[0:1], r))
            jumps_out[k, :, at] = new
            multiplier_out[k, :, at] = multiplier
            penalties[k].append(penalty)
            new_jumps[k].append(new)
    _, beside_above = advance(-new_jumps[2][0], above[times : 2 * times], above[2 * times : 2 * times + 1])
    _, beside_below = advance(-new_jumps[3][-1], below[times : 2 * times], below[2 * times : 2 * times + 1])
    back = gathered_jumps(penalties, beside_above, beside_below, linked)
    model_out[...] = field - step * gradient
    new_gradient = adjoint_in[...] - step * total[:times] + back
    gradient_out[...] = new_gradient
    response_of(new_gradient, kernel, plain, weighted_t, linked, sent, edge)


def response_body(count, *refs):
    two, out, passing, norms = refs[count:]
    total = summed(refs[:count])
    packed, squares = total[:-8], total[-8:]
    scalars = rows_of([square_sum(packed), squares[2:3, :] * (2.0 / lax.axis_size("sensor"))])
    out[...] = scalars
    passing[:8, :] = scalars
    passing[8:, :] = two[...]
    norms[...] = squares


def finish_body(count, *refs):
    (norms, gradient_in, model, model_jumps, multiplier, threshold, grad_one, grad_two, passed, linked,
     estimate_out, auxiliary_out, multiplier_out, estimate_here, auxiliary_here, multiplier_here, sems) = refs[count:]
    step = step_of(norms, tree_sum([part[:8, :] for part in refs[:count]]))
    grad_two = jnp.where(is_odd(), grad_two[...], passed[8:, :])
    half = gradient_in.shape[0] // 2
    gradient = gradient_in[...]
    copies = []

    def store(source, target):
        copy = pltpu.make_async_copy(source, target, sems.at[len(copies)])
        copy.start()
        copies.append(copy)

    estimate_here[...] = model[...] - step * gradient
    store(estimate_here, estimate_out)
    grad_jumps = jumps(gradient, *beside(grad_one[half + 8 :, :], grad_two), linked[...])
    for k in range(4):
        for r in range(gradient.shape[1] // COLS):
            at = slice(r * COLS, (r + 1) * COLS)
            shifted = model_jumps[k, :, at] - step * grad_jumps[k][r] + multiplier[k, :, at]
            auxiliary = shrunk(shifted, threshold[0:1, at])
            auxiliary_here[k, :, at] = auxiliary
            multiplier_here[k, :, at] = shifted - auxiliary
        store(auxiliary_here.at[k], auxiliary_out.at[k])
        store(multiplier_here.at[k], multiplier_out.at[k])
    for copy in copies:
        copy.wait()


def stages_of(count, *radices):
    stages = []
    for radix in radices:
        if count > 1 and count % radix == 0:
            stages.append(radix)
            count //= radix
    while count > 1:
        stages.append(2)
        count //= 2
    return stages


def summing(parts, axis, stride, stages):
    count = lax.axis_size(axis)
    for radix in stages:
        total = tree_sum(parts)
        parts = [total] + [
            lax.ppermute(total, axis, [(i, i ^ (k * stride)) for i in range(count)]) for k in range(1, radix)
        ]
        stride *= radix
    return parts


def sensor_hop(array):
    return lax.ppermute(array, "sensor", [(i, i ^ 1) for i in range(lax.axis_size("sensor"))])


def sensor_parts(array, rows):
    passed = sensor_hop(array)
    total = array[:rows] + passed[:rows]
    return summing([total], "sensor", 2, stages_of(lax.axis_size("sensor") // 2, 2)), passed


def last_sensor_parts(scalars, passing):
    count = lax.axis_size("sensor")
    near, far, across = (
        lax.ppermute(array, "sensor", [(i, i ^ k) for i in range(count)])
        for k, array in ((1, scalars), (2, scalars), (3, passing))
    )
    parts = [scalars, near, far, across]
    if count > 4:
        rows = scalars.shape[0]
        parts = summing([tree_sum([part[:rows] for part in parts])], "sensor", 4, stages_of(count // 4, 4))
    return parts, across


def cell_parts(merged):
    return summing([merged], "cell", 2, stages_of(lax.axis_size("cell") // 2, 4, 4))


def from_partner(array):
    return lax.ppermute(array, "cell", [(i, i ^ 1) for i in range(lax.axis_size("cell"))])


def from_other(array):
    sensors = lax.axis_size("sensor")
    pairs = [
        (i * sensors + s, (i + 1 if i % 2 else i - 1) * sensors + s)
        for i in range(1, lax.axis_size("cell") - 1)
        for s in range(1, sensors, 2)
    ]
    return lax.ppermute(array, ("cell", "sensor"), pairs)


def per_device(kernel, observed, start_model, start_multiplier, neighbours, tile_of_cell, tile_weight):
    times, cells = start_model.shape
    freqs, sensors = kernel.shape[1:3]
    plain, weighted = tables(times, freqs)
    plain, plain_t, weighted, weighted_t = (
        jnp.asarray(table_terms(t)) for t in (plain, plain.T, weighted, weighted.T)
    )
    half = times // 2
    field, row, wide = (times, cells), (times, COLS), (4, times, cells)

    loads = [
        kernel, start_model, start_multiplier, plain, weighted_t, plain_t, weighted,
        neighbours, tile_of_cell[None, :], tile_weight[None, :],
    ]
    sent, edge, threshold, linked, kernel, start_model, start_multiplier, plain, weighted_t, plain_t, weighted = call(
        first_forward_body,
        [(half + 2 * times + 8, LANES), (2 * times + 8, LANES), (8, cells), (8, cells)]
        + [jax.ShapeDtypeStruct(a.shape, a.dtype) for a in loads[:7]],
        *[pltpu.with_memory_space_constraint(a, HBM) for a in loads],
        scratch=[VMEM(a.shape, a.dtype) for a in loads[7:]] + [pltpu.SemaphoreType.DMA((9 + -(-freqs // CHUNK),))],
        inputs=HBM,
    )
    one = from_partner(sent)
    two = from_other(edge)
    parts = cell_parts(sent[:half] + one[:half])
    message, side, shared = (half + 8 + times, LANES), (times, LANES), (2 * times + 8, LANES)
    back = call(
        functools.partial(first_adjoint_body, len(parts)), (2 * times + 8, cells),
        *parts, observed, two, kernel, plain_t, weighted,
    )
    parts, passed = sensor_parts(back, times)
    back, two = call(start_back_body, [field, shared], start_multiplier, one, two, passed, linked)
    adjoint_one, gradient, sent, edge = call(
        functools.partial(first_gradient_body, len(parts)), [field, field, message, side],
        *parts, back, linked, kernel, plain, weighted_t,
    )
    grad_one, grad_two = from_partner(sent), from_other(edge)
    parts = cell_parts(call(merge_body, (half + 8, LANES), sent, grad_one, edge, grad_two, linked))
    back, norms = call(
        functools.partial(second_adjoint_body, len(parts)), [(times + 8 + half, cells), (8, LANES)],
        *parts, grad_two, kernel, plain_t, weighted,
    )
    parts, passed = sensor_parts(back, times + 8)
    model_jumps, grad_jumps = call(
        both_jumps_body, [wide, wide], start_model, gradient, one, two, grad_one, grad_two, passed, linked
    )
    model, model_jumps, multiplier, gradient, sent, edge = call(
        functools.partial(second_gradient_body, len(parts)), [field, wide, wide, field, message, side],
        *parts, norms, adjoint_one, gradient, start_model, model_jumps, grad_jumps, start_multiplier, threshold,
        one, two, linked, kernel, plain, weighted_t,
    )
    grad_one, grad_two = from_partner(sent), from_other(edge)
    parts = cell_parts(call(merge_body, (half + 8, LANES), sent, grad_one, edge, grad_two, linked))
    scalars, passing, norms = call(
        functools.partial(response_body, len(parts)), [(8, LANES), (8 + times, LANES), (8, LANES)], *parts, grad_two
    )
    parts, passed = last_sensor_parts(scalars, passing)
    return tuple(
        call(
            functools.partial(finish_body, len(parts)), [field, wide, wide],
            *parts, norms, gradient, model, model_jumps, multiplier, threshold, grad_one, grad_two, passed, linked,
            scratch=[VMEM(shape, jnp.float32) for shape in (field, wide, wide)] + [pltpu.SemaphoreType.DMA((9,))],
            outputs=HBM,
        )
    )


def solution(mesh):
    in_specs = (
        P(None, None, "sensor", "cell"),
        P(None, "sensor"),
        P(None, "cell"),
        P(None, None, "cell"),
        P(None, "cell"),
        P("cell"),
        P(),
    )
    out_specs = (P(None, "cell"), P(None, None, "cell"), P(None, None, "cell"))
    return jax.shard_map(
        per_device, mesh=mesh, in_specs=in_specs, out_specs=out_specs, check_vma=False
    )
```

```python
import functools

import jax
import jax.numpy as jnp
import numpy as np
from jax import lax
from jax.experimental import pallas as pl
from jax.experimental.pallas import tpu as pltpu
from jax.sharding import PartitionSpec as P

COLS = 128
LANES = 128
GROUP = 8
SHRINK_SCALE = 0.4
TINY = 1e-06
VMEM = pltpu.VMEM
HBM = pltpu.HBM


def tables(times, freqs):
    padded = 2 * times
    groups = -(-freqs // GROUP)
    plain = np.zeros((16 * groups, times), np.float64)
    weighted = np.zeros((16 * groups, times), np.float64)
    for f in range(freqs):
        phase = 2.0 * np.pi * ((f * np.arange(times)) % padded) / padded
        weight = (1.0 if f in (0, freqs - 1) else 2.0) / padded
        row = 16 * (f // GROUP) + f % GROUP
        plain[row], plain[row + GROUP] = np.cos(phase), -np.sin(phase)
        weighted[row], weighted[row + GROUP] = weight * np.cos(phase), -weight * np.sin(phase)
    return plain.astype(np.float32), weighted.astype(np.float32)


def table_terms(table):
    high = table.astype(jnp.bfloat16)
    low = (table - high.astype(np.float32)).astype(jnp.bfloat16)
    return np.concatenate([high, high, low], axis=1)


def table_dot(terms, values):
    high = values.astype(jnp.bfloat16)
    low = (values - high.astype(jnp.float32)).astype(jnp.bfloat16)
    return dot_nn(terms, jnp.concatenate([high, low, high], axis=0))


def turned(rows):
    rows = rows.astype(jnp.float32)
    return jnp.concatenate([-rows[GROUP:], rows[:GROUP]], axis=0).astype(jnp.bfloat16)


def dot_nt(left, right):
    return lax.dot_general(left, right, (((1,), (1,)), ((), ())), preferred_element_type=jnp.float32)


def dot_nn(left, right):
    return jnp.dot(left, right, preferred_element_type=jnp.float32)


def slab(kernel_ref, part, group):
    freqs, sensors, cells = kernel_ref.shape[1:]
    count = min(GROUP, freqs - group * GROUP)
    block = kernel_ref[part, group * GROUP : group * GROUP + count]
    return block.reshape(count * sensors, cells)


def own_block(width, sensors):
    row = lax.broadcasted_iota(jnp.int32, (16, width), 0) % GROUP
    lane = lax.broadcasted_iota(jnp.int32, (16, width), 1) // sensors
    return row == lane


def fold(wide):
    total = functools.reduce(
        lambda a, b: a + b, [wide[:, i : i + LANES] for i in range(0, wide.shape[1], LANES)]
    )
    return total + pltpu.roll(total, LANES // 2, 1)


def forward(field, kernel_ref, plain, weighted_t):
    return packed_series(forward_rows(table_dot(plain, field), kernel_ref), weighted_t, kernel_ref.shape[2])


def forward_rows(spectra, kernel_ref, arrived=None):
    sensors = kernel_ref.shape[2]
    rows = []
    for group in range(spectra.shape[0] // 16):
        part = spectra[16 * group : 16 * group + 16]
        if arrived is not None:
            arrived(group)
        re_slab, im_slab = slab(kernel_ref, 0, group), slab(kernel_ref, 1, group)
        out = dot_nt(part.astype(jnp.bfloat16), re_slab) + dot_nt(turned(part), im_slab)
        width = out.shape[1]
        out = jnp.where(own_block(width, sensors), out, 0.0)
        if width < LANES:
            out = jnp.concatenate([out, jnp.zeros((16, LANES - width), jnp.float32)], axis=1)
        rows.append(fold(out))
    return jnp.concatenate(rows, axis=0)


def packed_series(rows, weighted_t, sensors):
    times = weighted_t.shape[0]
    series = table_dot(weighted_t, rows)
    left = lax.broadcasted_iota(jnp.int32, (times // 2, LANES), 1) < sensors
    return jnp.where(left, series[: times // 2], series[times // 2 :])


def unpacked(packed, sensors):
    other = pltpu.roll(packed, sensors, 1)
    left = lax.broadcasted_iota(jnp.int32, packed.shape, 1) < sensors
    return jnp.concatenate([jnp.where(left, packed, other), jnp.where(left, other, packed)], axis=0)


def adjoint(residual, kernel_ref, plain_t, weighted, halves):
    freqs, sensors, cells = kernel_ref.shape[1:]
    spectra = table_dot(weighted, residual)
    rows = []
    for group in range(weighted.shape[0] // 16):
        part = spectra[16 * group : 16 * group + 16]
        count = min(GROUP, freqs - group * GROUP)
        width = count * sensors
        re_slab, im_slab = slab(kernel_ref, 0, group), slab(kernel_ref, 1, group)
        wide = jnp.concatenate([part] * (-(-width // LANES)), axis=1)[:, :width]
        wide = jnp.where(own_block(width, sensors), wide, 0.0)
        terms = []
        for _ in range(halves):
            terms.append(wide.astype(jnp.bfloat16))
            wide = wide - terms[-1].astype(jnp.float32)
        left = jnp.concatenate(terms, axis=0)
        swapped = jnp.concatenate([turned(term) for term in terms], axis=0)
        out = dot_nn(left, re_slab) - dot_nn(swapped, im_slab)
        rows.append(tree_sum([out[16 * i : 16 * i + 16] for i in range(halves)]))
    return table_dot(plain_t, jnp.concatenate(rows, axis=0))


def strip(array, row):
    return array[..., row * COLS : (row + 1) * COLS]


def jumps(field, above, below, linked):
    count = field.shape[1] // COLS
    out = []
    for direction in range(4):
        strips = []
        for row in range(count):
            here = strip(field, row)
            if direction == 0:
                there = pltpu.roll(here, COLS - 1, 1)
            elif direction == 1:
                there = pltpu.roll(here, 1, 1)
            elif direction == 2:
                there = above if row == 0 else strip(field, row - 1)
            else:
                there = below if row == count - 1 else strip(field, row + 1)
            strips.append(strip(linked[direction : direction + 1], row) * (there - here))
        out.append(strips)
    return out


def gathered_jumps(values, above, below, linked):
    count = len(values[0])
    out = []
    for row in range(count):
        arriving = (
            pltpu.roll(values[1][row], COLS - 1, 1),
            pltpu.roll(values[0][row], 1, 1),
            above if row == 0 else values[3][row - 1],
            below if row == count - 1 else values[2][row + 1],
        )
        total = None
        for direction in range(4):
            term = strip(linked[direction : direction + 1], row) * (arriving[direction] - values[direction][row])
            total = term if total is None else total + term
        out.append(total)
    return jnp.concatenate(out, axis=1)


def shrunk(shifted, threshold):
    return shifted - jnp.clip(shifted, -threshold, threshold)


def tree_sum(parts):
    parts = list(parts)
    while len(parts) > 1:
        parts = [parts[i] + parts[i + 1] if i + 1 < len(parts) else parts[i] for i in range(0, len(parts), 2)]
    return parts[0]


def square_sum(array):
    return jnp.sum(array * array)


def block_of(scalar, rows=8):
    return jnp.full((rows, LANES), scalar, jnp.float32)


def call(body, out_shapes, *operands, scratch=(), inputs=VMEM, outputs=VMEM):
    single = isinstance(out_shapes, tuple)
    shapes = [out_shapes] if single else list(out_shapes)
    shapes = [s if isinstance(s, jax.ShapeDtypeStruct) else jax.ShapeDtypeStruct(s, jnp.float32) for s in shapes]
    out = pl.pallas_call(
        body,
        out_shape=shapes,
        in_specs=[pl.BlockSpec(memory_space=inputs)] * len(operands),
        out_specs=[pl.BlockSpec(memory_space=outputs)] * len(shapes),
        scratch_shapes=list(scratch),
        compiler_params=pltpu.CompilerParams(vmem_limit_bytes=24 * 2**20),
    )(*operands)
    return out[0] if single else out


def summed(parts):
    return tree_sum([part[...] for part in parts])


def is_even():
    return lax.rem(lax.axis_index("cell"), 2) == 0


def edges(head, tail):
    even = is_even()
    return jnp.where(even, tail, head), jnp.where(even, head, tail)


def beside(partner, other):
    even = is_even()
    return jnp.where(even, other, partner), jnp.where(even, partner, other)


def is_odd():
    return lax.rem(lax.axis_index("sensor"), 2) == 1


def spread(rows):
    upper = -(-rows.shape[0] // 16) * 8
    lower = rows[upper:]
    if lower.shape[0] < upper:
        lower = jnp.concatenate([lower, jnp.zeros((upper - lower.shape[0], LANES), rows.dtype)])
    return jnp.concatenate([rows[:upper], lower], axis=1)


def gathered(wide, count):
    return jnp.concatenate([wide[:, :LANES], wide[: count - wide.shape[0], LANES:]])


def rows_of(scalars):
    row = lax.broadcasted_iota(jnp.int32, (8, LANES), 0)
    out = jnp.zeros((8, LANES), jnp.float32)
    for i, scalar in enumerate(scalars):
        out = jnp.where(row == i, scalar, out)
    return out


def load_starts(freqs):
    groups = -(-freqs // GROUP)
    return sorted({0, groups * 4 // 9 * GROUP, groups * 7 // 9 * GROUP})


def first_forward_body(*refs):
    loaded, (sent, edge, threshold, linked), kept, sems = refs[:10], refs[10:14], refs[14:24], refs[24]
    kernel, kernel_here = loaded[0], kept[0]
    field, multiplier, plain, weighted_t = kept[1:5]
    neighbours, tile_of_cell, tile_weight = kept[7:]
    freqs = kernel.shape[1]
    times, cells = field.shape
    half = times // 2
    copies = []

    def load(source, target):
        copy = pltpu.make_async_copy(source, target, sems.at[len(copies)])
        copy.start()
        copies.append(copy)
        return copy

    early = [load(loaded[i], kept[i]) for i in (1, 3)]
    large = []
    starts = load_starts(freqs)
    for start, stop in zip(starts, starts[1:] + [freqs]):
        at = (slice(None), pl.ds(start, stop - start))
        large.append(load(kernel.at[at], kernel_here.at[at]))
        if start == 0:
            small = [load(loaded[i], kept[i]) for i in (7, 8, 9, 2, 4)]
    late = [load(loaded[i], kept[i]) for i in (5, 6)]
    for copy in early:
        copy.wait()
    spectra = table_dot(plain[...], field[...])
    for copy in small:
        copy.wait()

    cell = lax.broadcasted_iota(jnp.int32, (4, cells), 1) + lax.axis_index("cell") * cells
    linked[0:4, :] = jnp.where(neighbours[...] != cell, 1.0, 0.0)
    linked[4:8, :] = jnp.zeros((4, cells), jnp.float32)
    tile = lax.broadcasted_iota(jnp.int32, (tile_weight.shape[1], cells), 0)
    chosen = jnp.where(tile == tile_of_cell[...], 1.0, 0.0)
    weights = jnp.dot(
        jnp.broadcast_to(tile_weight[...], (8, tile_weight.shape[1])), chosen,
        precision=lax.Precision.HIGHEST, preferred_element_type=jnp.float32,
    )
    limit = SHRINK_SCALE * weights
    threshold[...] = limit
    bottom = cells // COLS - 1
    pairs = (
        (strip(field, 0), strip(field, bottom)),
        (strip(multiplier[2], 0), strip(multiplier[3], bottom)),
        (strip(limit, 0), strip(limit, bottom)),
    )
    for (head, tail), start in zip(pairs, (0, times, 2 * times)):
        one, two = edges(head, tail)
        sent[half + start : half + start + head.shape[0], :] = one
        edge[start : start + head.shape[0], :] = two

    def arrived(group):
        if group * GROUP in starts:
            large[starts.index(group * GROUP)].wait()

    rows = forward_rows(spectra, kernel_here, arrived)
    sent[:half, :] = packed_series(rows, weighted_t[...], kernel.shape[2])
    for copy in late:
        copy.wait()


def first_adjoint_body(count, *refs):
    observed, two, kernel, plain_t, weighted, out = refs[count:]
    times = observed.shape[0]
    predicted = unpacked(summed(refs[:count]), kernel.shape[2])
    residual = predicted - jnp.concatenate([observed[...], observed[...]], axis=1)
    out[:times, :] = adjoint(residual, kernel, plain_t[...], weighted[...], 1)
    out[times:, :] = spread(two[...])


def response_of(field, kernel, plain, weighted_t, linked, sent, edge):
    half = field.shape[0] // 2
    rows = field.shape[1] // COLS
    one, two = edges(strip(field, 0), strip(field, rows - 1))
    squares = []
    for row in range(rows):
        here = strip(field, row)
        east = strip(linked[0:1], row) * (pltpu.roll(here, COLS - 1, 1) - here)
        squares.append(east * east)
        if row > 0:
            north = strip(linked[2:3], row) * (strip(field, row - 1) - here)
            squares.append(north * north)
    sent[:half, :] = forward(field, kernel, plain[...], weighted_t[...])
    sent[half : half + 8, :] = rows_of([square_sum(field), 2.0 * jnp.sum(tree_sum(squares))])
    sent[half + 8 :, :] = one
    edge[...] = two


def merge_body(sent, came, edge, other, linked, out):
    cells = linked.shape[1]
    top = out.shape[0]
    to_partner, to_other = edges(linked[2:3, :COLS], linked[3:4, cells - COLS :])
    across = to_partner * (came[top:, :] - sent[top:, :])
    beyond = to_other * (other[...] - edge[...])
    out[: top - 8, :] = sent[: top - 8, :] + came[: top - 8, :]
    boundary = 2.0 * square_sum(jnp.where(is_odd(), beyond, across))
    out[top - 8 :, :] = sent[top - 8 : top, :] + came[top - 8 : top, :] + rows_of([0.0, 0.0, boundary])


def start_back_body(start_multiplier, one, two, passed, linked, back, two_out):
    times, cells = back.shape
    half = times // 2
    two = jnp.where(is_odd(), two[...], gathered(passed[times:, :], two.shape[0]))
    two_out[...] = two
    values = [[strip(start_multiplier[k], r) for r in range(cells // COLS)] for k in range(4)]
    above, below = beside(one[half + times : half + 2 * times, :], two[times : 2 * times, :])
    back[...] = gathered_jumps(values, above, below, linked[...])


def first_gradient_body(count, *refs):
    back, linked, kernel, plain, weighted_t, adjoint_out, gradient, sent, edge = refs[count:]
    total = summed(refs[:count])
    field = total + back[...]
    adjoint_out[...] = total
    gradient[...] = field
    response_of(field, kernel, plain, weighted_t, linked[...], sent, edge)


def second_adjoint_body(count, *refs):
    two, kernel, plain_t, weighted, out, norms = refs[count:]
    times = plain_t.shape[0]
    half = times // 2
    total = summed(refs[:count])
    packed, squares = total[:half], total[half : half + 8]
    out[:times, :] = adjoint(unpacked(packed, kernel.shape[2]), kernel, plain_t[...], weighted[...], 2)
    scalars = rows_of([square_sum(packed), squares[2:3, :] * (2.0 / lax.axis_size("sensor"))])
    out[times : times + 8, :] = jnp.concatenate([scalars] * (out.shape[1] // LANES), axis=1)
    out[times + 8 :, :] = spread(two[...])
    norms[...] = squares


def step_of(norms, scalars):
    return norms[0, 0] / (scalars[0, 0] + (norms[1, 0] + scalars[1, 0]) + TINY)


def both_jumps_body(model, gradient, one, two, grad_one, grad_two, passed, linked, model_jumps, grad_jumps):
    times, cells = model.shape
    half = times // 2
    above, below = beside(one[half : half + times, :], two[:times, :])
    from_other = jnp.where(is_odd(), grad_two[...], gathered(passed[times + 8 :, :], times))
    halos = ((above, below), beside(grad_one[half + 8 :, :], from_other))
    for field, (above, below), out in zip((model, gradient), halos, (model_jumps, grad_jumps)):
        for k, strips in enumerate(jumps(field[...], above, below, linked[...])):
            for r, values in enumerate(strips):
                out[k, :, r * COLS : (r + 1) * COLS] = values


def second_gradient_body(count, *refs):
    (norms, adjoint_in, gradient_in, model, model_jumps, grad_jumps, start_multiplier, threshold, one, two, linked_ref,
     kernel, plain, weighted_t, model_out, jumps_out, multiplier_out, gradient_out, sent, edge) = refs[count:]
    times, cells = model.shape
    half = times // 2
    total = summed(refs[:count])
    step = step_of(norms, total[times:])
    linked = linked_ref[...]
    field, gradient = model[...], gradient_in[...]
    rows = cells // COLS
    above, below = beside(one[half:, :], two[...])

    def advance(model_jumps, old_multiplier, limit):
        shifted = model_jumps + old_multiplier
        auxiliary = shrunk(shifted, limit)
        multiplier = shifted - auxiliary
        return multiplier, model_jumps - auxiliary + multiplier

    penalties, new_jumps = [], []
    for k in range(4):
        penalties.append([])
        new_jumps.append([])
        for r in range(rows):
            at = slice(r * COLS, (r + 1) * COLS)
            new = model_jumps[k, :, at] - step * grad_jumps[k, :, at]
            multiplier, penalty = advance(new, strip(start_multiplier[k], r), strip(threshold[0:1], r))
            jumps_out[k, :, at] = new
            multiplier_out[k, :, at] = multiplier
            penalties[k].append(penalty)
            new_jumps[k].append(new)
    _, beside_above = advance(-new_jumps[2][0], above[times : 2 * times], above[2 * times : 2 * times + 1])
    _, beside_below = advance(-new_jumps[3][-1], below[times : 2 * times], below[2 * times : 2 * times + 1])
    back = gathered_jumps(penalties, beside_above, beside_below, linked)
    model_out[...] = field - step * gradient
    new_gradient = adjoint_in[...] - step * total[:times] + back
    gradient_out[...] = new_gradient
    response_of(new_gradient, kernel, plain, weighted_t, linked, sent, edge)


def response_body(count, *refs):
    two, out, passing, norms = refs[count:]
    total = summed(refs[:count])
    packed, squares = total[:-8], total[-8:]
    scalars = rows_of([square_sum(packed), squares[2:3, :] * (2.0 / lax.axis_size("sensor"))])
    out[...] = scalars
    passing[:8, :] = scalars
    passing[8:, :] = two[...]
    norms[...] = squares


def finish_body(count, *refs):
    (norms, gradient_in, model, model_jumps, multiplier, threshold, grad_one, grad_two, passed, linked,
     estimate_out, auxiliary_out, multiplier_out, estimate_here, auxiliary_here, multiplier_here, sems) = refs[count:]
    step = step_of(norms, tree_sum([part[:8, :] for part in refs[:count]]))
    grad_two = jnp.where(is_odd(), grad_two[...], passed[8:, :])
    half = gradient_in.shape[0] // 2
    gradient = gradient_in[...]
    copies = []

    def store(source, target):
        copy = pltpu.make_async_copy(source, target, sems.at[len(copies)])
        copy.start()
        copies.append(copy)

    estimate_here[...] = model[...] - step * gradient
    store(estimate_here, estimate_out)
    grad_jumps = jumps(gradient, *beside(grad_one[half + 8 :, :], grad_two), linked[...])
    for k in range(4):
        for r in range(gradient.shape[1] // COLS):
            at = slice(r * COLS, (r + 1) * COLS)
            shifted = model_jumps[k, :, at] - step * grad_jumps[k][r] + multiplier[k, :, at]
            auxiliary = shrunk(shifted, threshold[0:1, at])
            auxiliary_here[k, :, at] = auxiliary
            multiplier_here[k, :, at] = shifted - auxiliary
        store(auxiliary_here.at[k], auxiliary_out.at[k])
        store(multiplier_here.at[k], multiplier_out.at[k])
    for copy in copies:
        copy.wait()


def stages_of(count, *radices):
    stages = []
    for radix in radices:
        if count > 1 and count % radix == 0:
            stages.append(radix)
            count //= radix
    while count > 1:
        stages.append(2)
        count //= 2
    return stages


def summing(parts, axis, stride, stages):
    count = lax.axis_size(axis)
    for radix in stages:
        total = tree_sum(parts)
        parts = [total] + [
            lax.ppermute(total, axis, [(i, i ^ (k * stride)) for i in range(count)]) for k in range(1, radix)
        ]
        stride *= radix
    return parts


def sensor_hop(array):
    return lax.ppermute(array, "sensor", [(i, i ^ 1) for i in range(lax.axis_size("sensor"))])


def sensor_parts(array, rows):
    count = lax.axis_size("sensor")
    passed = sensor_hop(array)
    total = array[:rows] + passed[:rows]
    parts = [total, lax.ppermute(total, "sensor", [(i, i ^ 3) for i in range(count)])]
    return summing(parts, "sensor", 4, stages_of(count // 4, 2)), passed


def last_sensor_parts(scalars, passing):
    count = lax.axis_size("sensor")
    near, far, across = (
        lax.ppermute(array, "sensor", [(i, i ^ k) for i in range(count)])
        for k, array in ((1, scalars), (2, scalars), (3, passing))
    )
    parts = [scalars, near, far, across]
    if count > 4:
        rows = scalars.shape[0]
        parts = summing([tree_sum([part[:rows] for part in parts])], "sensor", 4, stages_of(count // 4, 4))
    return parts, across


def cell_parts(merged):
    return summing([merged], "cell", 2, stages_of(lax.axis_size("cell") // 2, 4, 4))


def from_partner(array):
    return lax.ppermute(array, "cell", [(i, i ^ 1) for i in range(lax.axis_size("cell"))])


def from_other(array):
    sensors = lax.axis_size("sensor")
    pairs = [
        (i * sensors + s, (i + 1 if i % 2 else i - 1) * sensors + s)
        for i in range(1, lax.axis_size("cell") - 1)
        for s in range(1, sensors, 2)
    ]
    return lax.ppermute(array, ("cell", "sensor"), pairs)


def per_device(kernel, observed, start_model, start_multiplier, neighbours, tile_of_cell, tile_weight):
    times, cells = start_model.shape
    freqs, sensors = kernel.shape[1:3]
    plain, weighted = tables(times, freqs)
    plain, plain_t, weighted, weighted_t = (
        jnp.asarray(table_terms(t)) for t in (plain, plain.T, weighted, weighted.T)
    )
    half = times // 2
    field, row, wide = (times, cells), (times, COLS), (4, times, cells)

    loads = [
        kernel, start_model, start_multiplier, plain, weighted_t, plain_t, weighted,
        neighbours, tile_of_cell[None, :], tile_weight[None, :],
    ]
    sent, edge, threshold, linked, kernel, start_model, start_multiplier, plain, weighted_t, plain_t, weighted = call(
        first_forward_body,
        [(half + 2 * times + 8, LANES), (2 * times + 8, LANES), (8, cells), (8, cells)]
        + [jax.ShapeDtypeStruct(a.shape, a.dtype) for a in loads[:7]],
        *[pltpu.with_memory_space_constraint(a, HBM) for a in loads],
        scratch=[VMEM(a.shape, a.dtype) for a in loads[7:]] + [pltpu.SemaphoreType.DMA((9 + len(load_starts(freqs)),))],
        inputs=HBM,
    )
    one = from_partner(sent)
    two = from_other(edge)
    parts = cell_parts(sent[:half] + one[:half])
    message, side, shared = (half + 8 + times, LANES), (times, LANES), (2 * times + 8, LANES)
    back = call(
        functools.partial(first_adjoint_body, len(parts)), (2 * times + 8, cells),
        *parts, observed, two, kernel, plain_t, weighted,
    )
    parts, passed = sensor_parts(back, times)
    back, two = call(start_back_body, [field, shared], start_multiplier, one, two, passed, linked)
    adjoint_one, gradient, sent, edge = call(
        functools.partial(first_gradient_body, len(parts)), [field, field, message, side],
        *parts, back, linked, kernel, plain, weighted_t,
    )
    grad_one, grad_two = from_partner(sent), from_other(edge)
    parts = cell_parts(call(merge_body, (half + 8, LANES), sent, grad_one, edge, grad_two, linked))
    back, norms = call(
        functools.partial(second_adjoint_body, len(parts)), [(times + 8 + half, cells), (8, LANES)],
        *parts, grad_two, kernel, plain_t, weighted,
    )
    parts, passed = sensor_parts(back, times + 8)
    model_jumps, grad_jumps = call(
        both_jumps_body, [wide, wide], start_model, gradient, one, two, grad_one, grad_two, passed, linked
    )
    model, model_jumps, multiplier, gradient, sent, edge = call(
        functools.partial(second_gradient_body, len(parts)), [field, wide, wide, field, message, side],
        *parts, norms, adjoint_one, gradient, start_model, model_jumps, grad_jumps, start_multiplier, threshold,
        one, two, linked, kernel, plain, weighted_t,
    )
    grad_one, grad_two = from_partner(sent), from_other(edge)
    parts = cell_parts(call(merge_body, (half + 8, LANES), sent, grad_one, edge, grad_two, linked))
    scalars, passing, norms = call(
        functools.partial(response_body, len(parts)), [(8, LANES), (8 + times, LANES), (8, LANES)], *parts, grad_two
    )
    parts, passed = last_sensor_parts(scalars, passing)
    return tuple(
        call(
            functools.partial(finish_body, len(parts)), [field, wide, wide],
            *parts, norms, gradient, model, model_jumps, multiplier, threshold, grad_one, grad_two, passed, linked,
            scratch=[VMEM(shape, jnp.float32) for shape in (field, wide, wide)] + [pltpu.SemaphoreType.DMA((9,))],
            outputs=HBM,
        )
    )


def solution(mesh):
    in_specs = (
        P(None, None, "sensor", "cell"),
        P(None, "sensor"),
        P(None, "cell"),
        P(None, None, "cell"),
        P(None, "cell"),
        P("cell"),
        P(),
    )
    out_specs = (P(None, "cell"), P(None, None, "cell"), P(None, None, "cell"))
    return jax.shard_map(
        per_device, mesh=mesh, in_specs=in_specs, out_specs=out_specs, check_vma=False
    )
```

```python
import functools

import jax
import jax.numpy as jnp
import numpy as np
from jax import lax
from jax.experimental import pallas as pl
from jax.experimental.pallas import tpu as pltpu
from jax.sharding import PartitionSpec as P

COLS = 128
LANES = 128
GROUP = 8
CHUNK = 24
SHRINK_SCALE = 0.4
TINY = 1e-06
VMEM = pltpu.VMEM
HBM = pltpu.HBM


def tables(times, freqs):
    padded = 2 * times
    groups = -(-freqs // GROUP)
    plain = np.zeros((16 * groups, times), np.float64)
    weighted = np.zeros((16 * groups, times), np.float64)
    for f in range(freqs):
        phase = 2.0 * np.pi * ((f * np.arange(times)) % padded) / padded
        weight = (1.0 if f in (0, freqs - 1) else 2.0) / padded
        row = 16 * (f // GROUP) + f % GROUP
        plain[row], plain[row + GROUP] = np.cos(phase), -np.sin(phase)
        weighted[row], weighted[row + GROUP] = weight * np.cos(phase), -weight * np.sin(phase)
    return plain.astype(np.float32), weighted.astype(np.float32)


def table_terms(table):
    high = table.astype(jnp.bfloat16)
    low = (table - high.astype(np.float32)).astype(jnp.bfloat16)
    return np.concatenate([high, high, low], axis=1)


def table_dot(terms, values):
    high = values.astype(jnp.bfloat16)
    low = (values - high.astype(jnp.float32)).astype(jnp.bfloat16)
    return dot_nn(terms, jnp.concatenate([high, low, high], axis=0))


def turned(rows):
    rows = rows.astype(jnp.float32)
    return jnp.concatenate([-rows[GROUP:], rows[:GROUP]], axis=0).astype(jnp.bfloat16)


def dot_nt(left, right):
    return lax.dot_general(left, right, (((1,), (1,)), ((), ())), preferred_element_type=jnp.float32)


def dot_nn(left, right):
    return jnp.dot(left, right, preferred_element_type=jnp.float32)


def slab(kernel_ref, part, group):
    freqs, sensors, cells = kernel_ref.shape[1:]
    count = min(GROUP, freqs - group * GROUP)
    block = kernel_ref[part, group * GROUP : group * GROUP + count]
    return block.reshape(count * sensors, cells)


def own_block(width, sensors):
    row = lax.broadcasted_iota(jnp.int32, (16, width), 0) % GROUP
    lane = lax.broadcasted_iota(jnp.int32, (16, width), 1) // sensors
    return row == lane


def fold(wide):
    total = functools.reduce(
        lambda a, b: a + b, [wide[:, i : i + LANES] for i in range(0, wide.shape[1], LANES)]
    )
    return total + pltpu.roll(total, LANES // 2, 1)


def forward(field, kernel_ref, plain, weighted_t):
    return packed_series(forward_rows(table_dot(plain, field), kernel_ref), weighted_t, kernel_ref.shape[2])


def forward_rows(spectra, kernel_ref, arrived=None):
    sensors = kernel_ref.shape[2]
    rows = []
    for group in range(spectra.shape[0] // 16):
        part = spectra[16 * group : 16 * group + 16]
        if arrived is not None:
            arrived(group)
        re_slab, im_slab = slab(kernel_ref, 0, group), slab(kernel_ref, 1, group)
        out = dot_nt(part.astype(jnp.bfloat16), re_slab) + dot_nt(turned(part), im_slab)
        width = out.shape[1]
        out = jnp.where(own_block(width, sensors), out, 0.0)
        if width < LANES:
            out = jnp.concatenate([out, jnp.zeros((16, LANES - width), jnp.float32)], axis=1)
        rows.append(fold(out))
    return jnp.concatenate(rows, axis=0)


def packed_series(rows, weighted_t, sensors):
    times = weighted_t.shape[0]
    series = table_dot(weighted_t, rows)
    left = lax.broadcasted_iota(jnp.int32, (times // 2, LANES), 1) < sensors
    return jnp.where(left, series[: times // 2], series[times // 2 :])


def unpacked(packed, sensors):
    other = pltpu.roll(packed, sensors, 1)
    left = lax.broadcasted_iota(jnp.int32, packed.shape, 1) < sensors
    return jnp.concatenate([jnp.where(left, packed, other), jnp.where(left, other, packed)], axis=0)


def adjoint(residual, kernel_ref, plain_t, weighted, halves):
    freqs, sensors, cells = kernel_ref.shape[1:]
    spectra = table_dot(weighted, residual)
    rows = []
    for group in range(weighted.shape[0] // 16):
        part = spectra[16 * group : 16 * group + 16]
        count = min(GROUP, freqs - group * GROUP)
        width = count * sensors
        re_slab, im_slab = slab(kernel_ref, 0, group), slab(kernel_ref, 1, group)
        wide = jnp.concatenate([part] * (-(-width // LANES)), axis=1)[:, :width]
        wide = jnp.where(own_block(width, sensors), wide, 0.0)
        terms = []
        for _ in range(halves):
            terms.append(wide.astype(jnp.bfloat16))
            wide = wide - terms[-1].astype(jnp.float32)
        left = jnp.concatenate(terms, axis=0)
        swapped = jnp.concatenate([turned(term) for term in terms], axis=0)
        out = dot_nn(left, re_slab) - dot_nn(swapped, im_slab)
        rows.append(tree_sum([out[16 * i : 16 * i + 16] for i in range(halves)]))
    return table_dot(plain_t, jnp.concatenate(rows, axis=0))


def strip(array, row):
    return array[..., row * COLS : (row + 1) * COLS]


def jumps(field, above, below, linked):
    count = field.shape[1] // COLS
    out = []
    for direction in range(4):
        strips = []
        for row in range(count):
            here = strip(field, row)
            if direction == 0:
                there = pltpu.roll(here, COLS - 1, 1)
            elif direction == 1:
                there = pltpu.roll(here, 1, 1)
            elif direction == 2:
                there = above if row == 0 else strip(field, row - 1)
            else:
                there = below if row == count - 1 else strip(field, row + 1)
            strips.append(strip(linked[direction : direction + 1], row) * (there - here))
        out.append(strips)
    return out


def gathered_jumps(values, above, below, linked):
    count = len(values[0])
    out = []
    for row in range(count):
        arriving = (
            pltpu.roll(values[1][row], COLS - 1, 1),
            pltpu.roll(values[0][row], 1, 1),
            above if row == 0 else values[3][row - 1],
            below if row == count - 1 else values[2][row + 1],
        )
        total = None
        for direction in range(4):
            term = strip(linked[direction : direction + 1], row) * (arriving[direction] - values[direction][row])
            total = term if total is None else total + term
        out.append(total)
    return jnp.concatenate(out, axis=1)


def shrunk(shifted, threshold):
    return shifted - jnp.clip(shifted, -threshold, threshold)


def tree_sum(parts):
    parts = list(parts)
    while len(parts) > 1:
        parts = [parts[i] + parts[i + 1] if i + 1 < len(parts) else parts[i] for i in range(0, len(parts), 2)]
    return parts[0]


def total_of(array):
    return jnp.sum(array, axis=(0, 1), keepdims=True)


def square_sum(array):
    return total_of(array * array)


def block_of(scalar, rows=8):
    return jnp.full((rows, LANES), scalar, jnp.float32)


def call(body, out_shapes, *operands, scratch=(), inputs=VMEM, outputs=VMEM):
    single = isinstance(out_shapes, tuple)
    shapes = [out_shapes] if single else list(out_shapes)
    shapes = [s if isinstance(s, jax.ShapeDtypeStruct) else jax.ShapeDtypeStruct(s, jnp.float32) for s in shapes]
    out = pl.pallas_call(
        body,
        out_shape=shapes,
        in_specs=[pl.BlockSpec(memory_space=inputs)] * len(operands),
        out_specs=[pl.BlockSpec(memory_space=outputs)] * len(shapes),
        scratch_shapes=list(scratch),
        compiler_params=pltpu.CompilerParams(vmem_limit_bytes=24 * 2**20),
    )(*operands)
    return out[0] if single else out


def summed(parts):
    return tree_sum([part[...] for part in parts])


def is_even():
    return lax.rem(lax.axis_index("cell"), 2) == 0


def edges(head, tail):
    even = is_even()
    return jnp.where(even, tail, head), jnp.where(even, head, tail)


def beside(partner, other):
    even = is_even()
    return jnp.where(even, other, partner), jnp.where(even, partner, other)


def is_odd():
    return lax.rem(lax.axis_index("sensor"), 2) == 1


def spread(rows):
    upper = -(-rows.shape[0] // 16) * 8
    lower = rows[upper:]
    if lower.shape[0] < upper:
        lower = jnp.concatenate([lower, jnp.zeros((upper - lower.shape[0], LANES), rows.dtype)])
    return jnp.concatenate([rows[:upper], lower], axis=1)


def gathered(wide, count):
    return jnp.concatenate([wide[:, :LANES], wide[: count - wide.shape[0], LANES:]])


def rows_of(values):
    row = lax.broadcasted_iota(jnp.int32, (8, LANES), 0)
    out = jnp.zeros((8, LANES), jnp.float32)
    for i, value in enumerate(values):
        if value is not None:
            out = jnp.where(row == i, jnp.broadcast_to(value, (8, LANES)), out)
    return out


def first_forward_body(*refs):
    loaded, (sent, edge, threshold, linked), kept, sems = refs[:10], refs[10:14], refs[14:24], refs[24]
    kernel, kernel_here = loaded[0], kept[0]
    field, multiplier, plain, weighted_t = kept[1:5]
    neighbours, tile_of_cell, tile_weight = kept[7:]
    freqs = kernel.shape[1]
    times, cells = field.shape
    half = times // 2
    copies = []

    def load(source, target):
        copy = pltpu.make_async_copy(source, target, sems.at[len(copies)])
        copy.start()
        copies.append(copy)
        return copy

    early = [load(loaded[i], kept[i]) for i in (1, 3)]
    large = []
    for start in range(0, freqs, CHUNK):
        at = (slice(None), pl.ds(start, min(CHUNK, freqs - start)))
        large.append(load(kernel.at[at], kernel_here.at[at]))
        if start == 0:
            small = [load(loaded[i], kept[i]) for i in (7, 8, 9, 2, 4)]
    late = [load(loaded[i], kept[i]) for i in (5, 6)]
    for copy in early:
        copy.wait()
    spectra = table_dot(plain[...], field[...])
    for copy in small:
        copy.wait()

    cell = lax.broadcasted_iota(jnp.int32, (4, cells), 1) + lax.axis_index("cell") * cells
    linked[0:4, :] = jnp.where(neighbours[...] != cell, 1.0, 0.0)
    linked[4:8, :] = jnp.zeros((4, cells), jnp.float32)
    tile = lax.broadcasted_iota(jnp.int32, (tile_weight.shape[1], cells), 0)
    chosen = jnp.where(tile == tile_of_cell[...], 1.0, 0.0)
    weights = jnp.dot(
        jnp.broadcast_to(tile_weight[...], (8, tile_weight.shape[1])), chosen,
        precision=lax.Precision.HIGHEST, preferred_element_type=jnp.float32,
    )
    limit = SHRINK_SCALE * weights
    threshold[...] = limit
    bottom = cells // COLS - 1
    pairs = (
        (strip(field, 0), strip(field, bottom)),
        (strip(multiplier[2], 0), strip(multiplier[3], bottom)),
        (strip(limit, 0), strip(limit, bottom)),
    )
    for (head, tail), start in zip(pairs, (0, times, 2 * times)):
        one, two = edges(head, tail)
        sent[half + start : half + start + head.shape[0], :] = one
        edge[start : start + head.shape[0], :] = two

    def arrived(group):
        if group * GROUP % CHUNK == 0:
            large[group * GROUP // CHUNK].wait()

    rows = forward_rows(spectra, kernel_here, arrived)
    sent[:half, :] = packed_series(rows, weighted_t[...], kernel.shape[2])
    for copy in late:
        copy.wait()


def first_adjoint_body(count, *refs):
    observed, two, kernel, plain_t, weighted, out = refs[count:]
    times = observed.shape[0]
    predicted = unpacked(summed(refs[:count]), kernel.shape[2])
    residual = predicted - jnp.concatenate([observed[...], observed[...]], axis=1)
    out[:times, :] = adjoint(residual, kernel, plain_t[...], weighted[...], 1)
    out[times:, :] = spread(two[...])


def response_of(field, kernel, plain, weighted_t, linked, sent, edge):
    half = field.shape[0] // 2
    rows = field.shape[1] // COLS
    one, two = edges(strip(field, 0), strip(field, rows - 1))
    squares = []
    for row in range(rows):
        here = strip(field, row)
        east = strip(linked[0:1], row) * (pltpu.roll(here, COLS - 1, 1) - here)
        squares.append(east * east)
        if row > 0:
            north = strip(linked[2:3], row) * (strip(field, row - 1) - here)
            squares.append(north * north)
    sent[:half, :] = forward(field, kernel, plain[...], weighted_t[...])
    sent[half : half + 8, :] = rows_of([square_sum(field), 2.0 * total_of(tree_sum(squares))])
    sent[half + 8 :, :] = one
    edge[...] = two


def merge_body(sent, came, edge, other, linked, out):
    cells = linked.shape[1]
    top = out.shape[0]
    to_partner, to_other = edges(linked[2:3, :COLS], linked[3:4, cells - COLS :])
    across = to_partner * (came[top:, :] - sent[top:, :])
    beyond = to_other * (other[...] - edge[...])
    out[: top - 8, :] = sent[: top - 8, :] + came[: top - 8, :]
    boundary = 2.0 * square_sum(jnp.where(is_odd(), beyond, across))
    out[top - 8 :, :] = sent[top - 8 : top, :] + came[top - 8 : top, :] + rows_of([None, None, boundary])


def start_back_body(start_multiplier, one, two, passed, linked, back, two_out):
    times, cells = back.shape
    half = times // 2
    two = jnp.where(is_odd(), two[...], gathered(passed[times:, :], two.shape[0]))
    two_out[...] = two
    values = [[strip(start_multiplier[k], r) for r in range(cells // COLS)] for k in range(4)]
    above, below = beside(one[half + times : half + 2 * times, :], two[times : 2 * times, :])
    back[...] = gathered_jumps(values, above, below, linked[...])


def first_gradient_body(count, *refs):
    back, linked, kernel, plain, weighted_t, adjoint_out, gradient, sent, edge = refs[count:]
    total = summed(refs[:count])
    field = total + back[...]
    adjoint_out[...] = total
    gradient[...] = field
    response_of(field, kernel, plain, weighted_t, linked[...], sent, edge)


def second_adjoint_body(count, *refs):
    two, kernel, plain_t, weighted, out, norms = refs[count:]
    times = plain_t.shape[0]
    half = times // 2
    total = summed(refs[:count])
    packed, squares = total[:half], total[half : half + 8]
    out[:times, :] = adjoint(unpacked(packed, kernel.shape[2]), kernel, plain_t[...], weighted[...], 2)
    scalars = rows_of([square_sum(packed), squares[2:3, :] * (2.0 / lax.axis_size("sensor"))])
    out[times : times + 8, :] = jnp.concatenate([scalars] * (out.shape[1] // LANES), axis=1)
    out[times + 8 :, :] = spread(two[...])
    norms[...] = squares


def step_of(norms, scalars):
    return norms[0:1, :] / (scalars[0:1, :] + (norms[1:2, :] + scalars[1:2, :]) + TINY)


def both_jumps_body(model, gradient, one, two, grad_one, grad_two, passed, linked, model_jumps, grad_jumps):
    times, cells = model.shape
    half = times // 2
    above, below = beside(one[half : half + times, :], two[:times, :])
    from_other = jnp.where(is_odd(), grad_two[...], gathered(passed[times + 8 :, :], times))
    halos = ((above, below), beside(grad_one[half + 8 :, :], from_other))
    for field, (above, below), out in zip((model, gradient), halos, (model_jumps, grad_jumps)):
        for k, strips in enumerate(jumps(field[...], above, below, linked[...])):
            for r, values in enumerate(strips):
                out[k, :, r * COLS : (r + 1) * COLS] = values


def second_gradient_body(count, *refs):
    (norms, adjoint_in, gradient_in, model, model_jumps, grad_jumps, start_multiplier, threshold, one, two, linked_ref,
     kernel, plain, weighted_t, model_out, jumps_out, multiplier_out, gradient_out, sent, edge) = refs[count:]
    times, cells = model.shape
    half = times // 2
    total = summed(refs[:count])
    step = step_of(norms, total[times:, :LANES])
    linked = linked_ref[...]
    field, gradient = model[...], gradient_in[...]
    rows = cells // COLS
    above, below = beside(one[half:, :], two[...])

    def advance(model_jumps, old_multiplier, limit):
        shifted = model_jumps + old_multiplier
        auxiliary = shrunk(shifted, limit)
        multiplier = shifted - auxiliary
        return multiplier, model_jumps - auxiliary + multiplier

    penalties, new_jumps = [], []
    for k in range(4):
        penalties.append([])
        new_jumps.append([])
        for r in range(rows):
            at = slice(r * COLS, (r + 1) * COLS)
            new = model_jumps[k, :, at] - step * grad_jumps[k, :, at]
            multiplier, penalty = advance(new, strip(start_multiplier[k], r), strip(threshold[0:1], r))
            jumps_out[k, :, at] = new
            multiplier_out[k, :, at] = multiplier
            penalties[k].append(penalty)
            new_jumps[k].append(new)
    _, beside_above = advance(-new_jumps[2][0], above[times : 2 * times], above[2 * times : 2 * times + 1])
    _, beside_below = advance(-new_jumps[3][-1], below[times : 2 * times], below[2 * times : 2 * times + 1])
    back = gathered_jumps(penalties, beside_above, beside_below, linked)
    wide_step = jnp.concatenate([step] * rows, axis=1)
    model_out[...] = field - wide_step * gradient
    new_gradient = adjoint_in[...] - wide_step * total[:times] + back
    gradient_out[...] = new_gradient
    response_of(new_gradient, kernel, plain, weighted_t, linked, sent, edge)


def response_body(count, *refs):
    two, out, passing, norms = refs[count:]
    total = summed(refs[:count])
    packed, squares = total[:-8], total[-8:]
    scalars = rows_of([square_sum(packed), squares[2:3, :] * (2.0 / lax.axis_size("sensor"))])
    out[...] = scalars
    passing[:8, :] = scalars
    passing[8:, :] = two[...]
    norms[...] = squares


def finish_body(count, *refs):
    (norms, gradient_in, model, model_jumps, multiplier, threshold, grad_one, grad_two, passed, linked,
     estimate_out, auxiliary_out, multiplier_out, estimate_here, auxiliary_here, multiplier_here, sems) = refs[count:]
    step = step_of(norms, tree_sum([part[:8, :] for part in refs[:count]]))
    grad_two = jnp.where(is_odd(), grad_two[...], passed[8:, :])
    half = gradient_in.shape[0] // 2
    gradient = gradient_in[...]
    copies = []

    def store(source, target):
        copy = pltpu.make_async_copy(source, target, sems.at[len(copies)])
        copy.start()
        copies.append(copy)

    estimate_here[...] = model[...] - jnp.concatenate([step] * (gradient.shape[1] // COLS), axis=1) * gradient
    store(estimate_here, estimate_out)
    grad_jumps = jumps(gradient, *beside(grad_one[half + 8 :, :], grad_two), linked[...])
    for k in range(4):
        for r in range(gradient.shape[1] // COLS):
            at = slice(r * COLS, (r + 1) * COLS)
            shifted = model_jumps[k, :, at] - step * grad_jumps[k][r] + multiplier[k, :, at]
            auxiliary = shrunk(shifted, threshold[0:1, at])
            auxiliary_here[k, :, at] = auxiliary
            multiplier_here[k, :, at] = shifted - auxiliary
        store(auxiliary_here.at[k], auxiliary_out.at[k])
        store(multiplier_here.at[k], multiplier_out.at[k])
    for copy in copies:
        copy.wait()


def stages_of(count, *radices):
    stages = []
    for radix in radices:
        if count > 1 and count % radix == 0:
            stages.append(radix)
            count //= radix
    while count > 1:
        stages.append(2)
        count //= 2
    return stages


def summing(parts, axis, stride, stages):
    count = lax.axis_size(axis)
    for radix in stages:
        total = tree_sum(parts)
        parts = [total] + [
            lax.ppermute(total, axis, [(i, i ^ (k * stride)) for i in range(count)]) for k in range(1, radix)
        ]
        stride *= radix
    return parts


def sensor_hop(array):
    return lax.ppermute(array, "sensor", [(i, i ^ 1) for i in range(lax.axis_size("sensor"))])


def sensor_parts(array, rows):
    passed = sensor_hop(array)
    total = array[:rows] + passed[:rows]
    return summing([total], "sensor", 2, stages_of(lax.axis_size("sensor") // 2, 2)), passed


def last_sensor_parts(scalars, passing):
    count = lax.axis_size("sensor")
    near, far, across = (
        lax.ppermute(array, "sensor", [(i, i ^ k) for i in range(count)])
        for k, array in ((1, scalars), (2, scalars), (3, passing))
    )
    parts = [scalars, near, far, across]
    if count > 4:
        rows = scalars.shape[0]
        parts = summing([tree_sum([part[:rows] for part in parts])], "sensor", 4, stages_of(count // 4, 4))
    return parts, across


def cell_parts(merged):
    return summing([merged], "cell", 2, stages_of(lax.axis_size("cell") // 2, 4, 4))


def from_partner(array):
    return lax.ppermute(array, "cell", [(i, i ^ 1) for i in range(lax.axis_size("cell"))])


def from_other(array):
    sensors = lax.axis_size("sensor")
    pairs = [
        (i * sensors + s, (i + 1 if i % 2 else i - 1) * sensors + s)
        for i in range(1, lax.axis_size("cell") - 1)
        for s in range(1, sensors, 2)
    ]
    return lax.ppermute(array, ("cell", "sensor"), pairs)


def per_device(kernel, observed, start_model, start_multiplier, neighbours, tile_of_cell, tile_weight):
    times, cells = start_model.shape
    freqs, sensors = kernel.shape[1:3]
    plain, weighted = tables(times, freqs)
    plain, plain_t, weighted, weighted_t = (
        jnp.asarray(table_terms(t)) for t in (plain, plain.T, weighted, weighted.T)
    )
    half = times // 2
    field, row, wide = (times, cells), (times, COLS), (4, times, cells)

    loads = [
        kernel, start_model, start_multiplier, plain, weighted_t, plain_t, weighted,
        neighbours, tile_of_cell[None, :], tile_weight[None, :],
    ]
    sent, edge, threshold, linked, kernel, start_model, start_multiplier, plain, weighted_t, plain_t, weighted = call(
        first_forward_body,
        [(half + 2 * times + 8, LANES), (2 * times + 8, LANES), (8, cells), (8, cells)]
        + [jax.ShapeDtypeStruct(a.shape, a.dtype) for a in loads[:7]],
        *[pltpu.with_memory_space_constraint(a, HBM) for a in loads],
        scratch=[VMEM(a.shape, a.dtype) for a in loads[7:]] + [pltpu.SemaphoreType.DMA((9 + -(-freqs // CHUNK),))],
        inputs=HBM,
    )
    one = from_partner(sent)
    two = from_other(edge)
    parts = cell_parts(sent[:half] + one[:half])
    message, side, shared = (half + 8 + times, LANES), (times, LANES), (2 * times + 8, LANES)
    back = call(
        functools.partial(first_adjoint_body, len(parts)), (2 * times + 8, cells),
        *parts, observed, two, kernel, plain_t, weighted,
    )
    parts, passed = sensor_parts(back, times)
    back, two = call(start_back_body, [field, shared], start_multiplier, one, two, passed, linked)
    adjoint_one, gradient, sent, edge = call(
        functools.partial(first_gradient_body, len(parts)), [field, field, message, side],
        *parts, back, linked, kernel, plain, weighted_t,
    )
    grad_one, grad_two = from_partner(sent), from_other(edge)
    parts = cell_parts(call(merge_body, (half + 8, LANES), sent, grad_one, edge, grad_two, linked))
    back, norms = call(
        functools.partial(second_adjoint_body, len(parts)), [(times + 8 + half, cells), (8, LANES)],
        *parts, grad_two, kernel, plain_t, weighted,
    )
    parts, passed = sensor_parts(back, times + 8)
    model_jumps, grad_jumps = call(
        both_jumps_body, [wide, wide], start_model, gradient, one, two, grad_one, grad_two, passed, linked
    )
    model, model_jumps, multiplier, gradient, sent, edge = call(
        functools.partial(second_gradient_body, len(parts)), [field, wide, wide, field, message, side],
        *parts, norms, adjoint_one, gradient, start_model, model_jumps, grad_jumps, start_multiplier, threshold,
        one, two, linked, kernel, plain, weighted_t,
    )
    grad_one, grad_two = from_partner(sent), from_other(edge)
    parts = cell_parts(call(merge_body, (half + 8, LANES), sent, grad_one, edge, grad_two, linked))
    scalars, passing, norms = call(
        functools.partial(response_body, len(parts)), [(8, LANES), (8 + times, LANES), (8, LANES)], *parts, grad_two
    )
    parts, passed = last_sensor_parts(scalars, passing)
    return tuple(
        call(
            functools.partial(finish_body, len(parts)), [field, wide, wide],
            *parts, norms, gradient, model, model_jumps, multiplier, threshold, grad_one, grad_two, passed, linked,
            scratch=[VMEM(shape, jnp.float32) for shape in (field, wide, wide)] + [pltpu.SemaphoreType.DMA((9,))],
            outputs=HBM,
        )
    )


def solution(mesh):
    in_specs = (
        P(None, None, "sensor", "cell"),
        P(None, "sensor"),
        P(None, "cell"),
        P(None, None, "cell"),
        P(None, "cell"),
        P("cell"),
        P(),
    )
    out_specs = (P(None, "cell"), P(None, None, "cell"), P(None, None, "cell"))
    return jax.shard_map(
        per_device, mesh=mesh, in_specs=in_specs, out_specs=out_specs, check_vma=False
    )
```

```python
import functools

import jax
import jax.numpy as jnp
import numpy as np
from jax import lax
from jax.experimental import pallas as pl
from jax.experimental.pallas import tpu as pltpu
from jax.sharding import PartitionSpec as P

COLS = 128
LANES = 128
GROUP = 8
CHUNK = 24
SHRINK_SCALE = 0.4
TINY = 1e-06
VMEM = pltpu.VMEM
HBM = pltpu.HBM


def tables(times, freqs):
    padded = 2 * times
    groups = -(-freqs // GROUP)
    plain = np.zeros((16 * groups, times), np.float64)
    weighted = np.zeros((16 * groups, times), np.float64)
    for f in range(freqs):
        phase = 2.0 * np.pi * ((f * np.arange(times)) % padded) / padded
        weight = (1.0 if f in (0, freqs - 1) else 2.0) / padded
        row = 16 * (f // GROUP) + f % GROUP
        plain[row], plain[row + GROUP] = np.cos(phase), -np.sin(phase)
        weighted[row], weighted[row + GROUP] = weight * np.cos(phase), -weight * np.sin(phase)
    return plain.astype(np.float32), weighted.astype(np.float32)


def table_terms(table):
    high = table.astype(jnp.bfloat16)
    low = (table - high.astype(np.float32)).astype(jnp.bfloat16)
    return np.concatenate([high, high, low], axis=1)


def table_dot(terms, values):
    high = values.astype(jnp.bfloat16)
    low = (values - high.astype(jnp.float32)).astype(jnp.bfloat16)
    return dot_nn(terms, jnp.concatenate([high, low, high], axis=0))


def turned(rows):
    rows = rows.astype(jnp.float32)
    return jnp.concatenate([-rows[GROUP:], rows[:GROUP]], axis=0).astype(jnp.bfloat16)


def dot_nt(left, right):
    return lax.dot_general(left, right, (((1,), (1,)), ((), ())), preferred_element_type=jnp.float32)


def dot_nn(left, right):
    return jnp.dot(left, right, preferred_element_type=jnp.float32)


def slab(kernel_ref, part, group):
    freqs, sensors, cells = kernel_ref.shape[1:]
    count = min(GROUP, freqs - group * GROUP)
    block = kernel_ref[part, group * GROUP : group * GROUP + count]
    return block.reshape(count * sensors, cells)


def own_block(width, sensors):
    row = lax.broadcasted_iota(jnp.int32, (16, width), 0) % GROUP
    lane = lax.broadcasted_iota(jnp.int32, (16, width), 1) // sensors
    return row == lane


def fold(wide):
    total = functools.reduce(
        lambda a, b: a + b, [wide[:, i : i + LANES] for i in range(0, wide.shape[1], LANES)]
    )
    return total + pltpu.roll(total, LANES // 2, 1)


def forward(field, turned_ref, plain, weighted_t, sensors):
    freqs = field.shape[0] + 1
    spectra = table_dot(plain, field)
    rows = []
    for group in range(spectra.shape[0] // 16):
        part = spectra[16 * group : 16 * group + 16]
        width = min(GROUP, freqs - group * GROUP) * sensors
        out = dot_nn(part.astype(jnp.bfloat16), turned_ref[0, group, :, :width])
        out += dot_nn(turned(part), turned_ref[1, group, :, :width])
        rows.append(fold_own(out, sensors))
    return packed_series(jnp.concatenate(rows, axis=0), weighted_t, sensors)


def fold_own(out, sensors):
    width = out.shape[1]
    out = jnp.where(own_block(width, sensors), out, 0.0)
    if width < LANES:
        out = jnp.concatenate([out, jnp.zeros((16, LANES - width), jnp.float32)], axis=1)
    return fold(out)


def forward_rows(spectra, kernel_ref, arrived=None):
    sensors = kernel_ref.shape[2]
    rows = []
    for group in range(spectra.shape[0] // 16):
        part = spectra[16 * group : 16 * group + 16]
        if arrived is not None:
            arrived(group)
        re_slab, im_slab = slab(kernel_ref, 0, group), slab(kernel_ref, 1, group)
        out = dot_nt(part.astype(jnp.bfloat16), re_slab) + dot_nt(turned(part), im_slab)
        rows.append(fold_own(out, sensors))
    return jnp.concatenate(rows, axis=0)


def packed_series(rows, weighted_t, sensors):
    times = weighted_t.shape[0]
    series = table_dot(weighted_t, rows)
    left = lax.broadcasted_iota(jnp.int32, (times // 2, LANES), 1) < sensors
    return jnp.where(left, series[: times // 2], series[times // 2 :])


def unpacked(packed, sensors):
    other = pltpu.roll(packed, sensors, 1)
    left = lax.broadcasted_iota(jnp.int32, packed.shape, 1) < sensors
    return jnp.concatenate([jnp.where(left, packed, other), jnp.where(left, other, packed)], axis=0)


def adjoint(residual, kernel_ref, plain_t, weighted, halves):
    freqs, sensors, cells = kernel_ref.shape[1:]
    spectra = table_dot(weighted, residual)
    rows = []
    for group in range(weighted.shape[0] // 16):
        part = spectra[16 * group : 16 * group + 16]
        count = min(GROUP, freqs - group * GROUP)
        width = count * sensors
        re_slab, im_slab = slab(kernel_ref, 0, group), slab(kernel_ref, 1, group)
        wide = jnp.concatenate([part] * (-(-width // LANES)), axis=1)[:, :width]
        wide = jnp.where(own_block(width, sensors), wide, 0.0)
        terms = []
        for _ in range(halves):
            terms.append(wide.astype(jnp.bfloat16))
            wide = wide - terms[-1].astype(jnp.float32)
        left = jnp.concatenate(terms, axis=0)
        swapped = jnp.concatenate([turned(term) for term in terms], axis=0)
        out = dot_nn(left, re_slab) - dot_nn(swapped, im_slab)
        rows.append(tree_sum([out[16 * i : 16 * i + 16] for i in range(halves)]))
    return table_dot(plain_t, jnp.concatenate(rows, axis=0))


def strip(array, row):
    return array[..., row * COLS : (row + 1) * COLS]


def jumps(field, above, below, linked):
    count = field.shape[1] // COLS
    out = []
    for direction in range(4):
        strips = []
        for row in range(count):
            here = strip(field, row)
            if direction == 0:
                there = pltpu.roll(here, COLS - 1, 1)
            elif direction == 1:
                there = pltpu.roll(here, 1, 1)
            elif direction == 2:
                there = above if row == 0 else strip(field, row - 1)
            else:
                there = below if row == count - 1 else strip(field, row + 1)
            strips.append(strip(linked[direction : direction + 1], row) * (there - here))
        out.append(strips)
    return out


def gathered_jumps(values, above, below, linked):
    count = len(values[0])
    out = []
    for row in range(count):
        arriving = (
            pltpu.roll(values[1][row], COLS - 1, 1),
            pltpu.roll(values[0][row], 1, 1),
            above if row == 0 else values[3][row - 1],
            below if row == count - 1 else values[2][row + 1],
        )
        total = None
        for direction in range(4):
            term = strip(linked[direction : direction + 1], row) * (arriving[direction] - values[direction][row])
            total = term if total is None else total + term
        out.append(total)
    return jnp.concatenate(out, axis=1)


def shrunk(shifted, threshold):
    return shifted - jnp.clip(shifted, -threshold, threshold)


def tree_sum(parts):
    parts = list(parts)
    while len(parts) > 1:
        parts = [parts[i] + parts[i + 1] if i + 1 < len(parts) else parts[i] for i in range(0, len(parts), 2)]
    return parts[0]


def total_of(array):
    return jnp.sum(array, axis=(0, 1), keepdims=True)


def square_sum(array):
    return total_of(array * array)


def block_of(scalar, rows=8):
    return jnp.full((rows, LANES), scalar, jnp.float32)


def call(body, out_shapes, *operands, scratch=(), inputs=VMEM, outputs=VMEM):
    single = not isinstance(out_shapes, list)
    shapes = [out_shapes] if single else list(out_shapes)
    shapes = [s if isinstance(s, jax.ShapeDtypeStruct) else jax.ShapeDtypeStruct(s, jnp.float32) for s in shapes]
    out = pl.pallas_call(
        body,
        out_shape=shapes,
        in_specs=[pl.BlockSpec(memory_space=inputs)] * len(operands),
        out_specs=[pl.BlockSpec(memory_space=outputs)] * len(shapes),
        scratch_shapes=list(scratch),
        compiler_params=pltpu.CompilerParams(vmem_limit_bytes=24 * 2**20),
    )(*operands)
    return out[0] if single else out


def summed(parts):
    return tree_sum([part[...] for part in parts])


def is_even():
    return lax.rem(lax.axis_index("cell"), 2) == 0


def edges(head, tail):
    even = is_even()
    return jnp.where(even, tail, head), jnp.where(even, head, tail)


def beside(partner, other):
    even = is_even()
    return jnp.where(even, other, partner), jnp.where(even, partner, other)


def is_odd():
    return lax.rem(lax.axis_index("sensor"), 2) == 1


def spread(rows):
    upper = -(-rows.shape[0] // 16) * 8
    lower = rows[upper:]
    if lower.shape[0] < upper:
        lower = jnp.concatenate([lower, jnp.zeros((upper - lower.shape[0], LANES), rows.dtype)])
    return jnp.concatenate([rows[:upper], lower], axis=1)


def gathered(wide, count):
    return jnp.concatenate([wide[:, :LANES], wide[: count - wide.shape[0], LANES:]])


def rows_of(values):
    row = lax.broadcasted_iota(jnp.int32, (8, LANES), 0)
    out = jnp.zeros((8, LANES), jnp.float32)
    for i, value in enumerate(values):
        if value is not None:
            out = jnp.where(row == i, jnp.broadcast_to(value, (8, LANES)), out)
    return out


def first_forward_body(*refs):
    loaded, (sent, edge, threshold, linked), kept, sems = refs[:10], refs[10:14], refs[14:24], refs[24]
    kernel, kernel_here = loaded[0], kept[0]
    field, multiplier, plain, weighted_t = kept[1:5]
    neighbours, tile_of_cell, tile_weight = kept[7:]
    freqs = kernel.shape[1]
    times, cells = field.shape
    half = times // 2
    copies = []

    def load(source, target):
        copy = pltpu.make_async_copy(source, target, sems.at[len(copies)])
        copy.start()
        copies.append(copy)
        return copy

    early = [load(loaded[i], kept[i]) for i in (1, 3)]
    large = []
    for start in range(0, freqs, CHUNK):
        at = (slice(None), pl.ds(start, min(CHUNK, freqs - start)))
        large.append(load(kernel.at[at], kernel_here.at[at]))
        if start == 0:
            small = [load(loaded[i], kept[i]) for i in (7, 8, 9, 2, 4)]
    late = [load(loaded[i], kept[i]) for i in (5, 6)]
    for copy in early:
        copy.wait()
    spectra = table_dot(plain[...], field[...])
    for copy in small:
        copy.wait()

    cell = lax.broadcasted_iota(jnp.int32, (4, cells), 1) + lax.axis_index("cell") * cells
    linked[0:4, :] = jnp.where(neighbours[...] != cell, 1.0, 0.0)
    linked[4:8, :] = jnp.zeros((4, cells), jnp.float32)
    tile = lax.broadcasted_iota(jnp.int32, (tile_weight.shape[1], cells), 0)
    chosen = jnp.where(tile == tile_of_cell[...], 1.0, 0.0)
    weights = jnp.dot(
        jnp.broadcast_to(tile_weight[...], (8, tile_weight.shape[1])), chosen,
        precision=lax.Precision.HIGHEST, preferred_element_type=jnp.float32,
    )
    limit = SHRINK_SCALE * weights
    threshold[...] = limit
    bottom = cells // COLS - 1
    pairs = (
        (strip(field, 0), strip(field, bottom)),
        (strip(multiplier[2], 0), strip(multiplier[3], bottom)),
        (strip(limit, 0), strip(limit, bottom)),
    )
    for (head, tail), start in zip(pairs, (0, times, 2 * times)):
        one, two = edges(head, tail)
        sent[half + start : half + start + head.shape[0], :] = one
        edge[start : start + head.shape[0], :] = two

    def arrived(group):
        if group * GROUP % CHUNK == 0:
            large[group * GROUP // CHUNK].wait()

    rows = forward_rows(spectra, kernel_here, arrived)
    sent[:half, :] = packed_series(rows, weighted_t[...], kernel.shape[2])
    for copy in late:
        copy.wait()


def turn_body(kernel, came, out):
    freqs, sensors = kernel.shape[1:3]
    for part in range(2):
        for group in range(out.shape[1]):
            width = min(GROUP, freqs - group * GROUP) * sensors
            out[part, group, :, :width] = slab(kernel, part, group).T


def first_adjoint_body(count, *refs):
    observed, two, kernel, plain_t, weighted, _, out = refs[count:]
    times = observed.shape[0]
    predicted = unpacked(summed(refs[:count]), kernel.shape[2])
    residual = predicted - jnp.concatenate([observed[...], observed[...]], axis=1)
    out[:times, :] = adjoint(residual, kernel, plain_t[...], weighted[...], 1)
    out[times:, :] = spread(two[...])


def response_of(field, turned_ref, plain, weighted_t, linked, sent, edge):
    half = field.shape[0] // 2
    rows = field.shape[1] // COLS
    one, two = edges(strip(field, 0), strip(field, rows - 1))
    squares = []
    for row in range(rows):
        here = strip(field, row)
        east = strip(linked[0:1], row) * (pltpu.roll(here, COLS - 1, 1) - here)
        squares.append(east * east)
        if row > 0:
            north = strip(linked[2:3], row) * (strip(field, row - 1) - here)
            squares.append(north * north)
    sensors = turned_ref.shape[3] // GROUP
    sent[:half, :] = forward(field, turned_ref, plain[...], weighted_t[...], sensors)
    sent[half : half + 8, :] = rows_of([square_sum(field), 2.0 * total_of(tree_sum(squares))])
    sent[half + 8 :, :] = one
    edge[...] = two


def merge_body(sent, came, edge, other, linked, out):
    cells = linked.shape[1]
    top = out.shape[0]
    to_partner, to_other = edges(linked[2:3, :COLS], linked[3:4, cells - COLS :])
    across = to_partner * (came[top:, :] - sent[top:, :])
    beyond = to_other * (other[...] - edge[...])
    out[: top - 8, :] = sent[: top - 8, :] + came[: top - 8, :]
    boundary = 2.0 * square_sum(jnp.where(is_odd(), beyond, across))
    out[top - 8 :, :] = sent[top - 8 : top, :] + came[top - 8 : top, :] + rows_of([None, None, boundary])


def start_back_body(start_multiplier, one, two, passed, linked, back, two_out):
    times, cells = back.shape
    half = times // 2
    two = jnp.where(is_odd(), two[...], gathered(passed[times:, :], two.shape[0]))
    two_out[...] = two
    values = [[strip(start_multiplier[k], r) for r in range(cells // COLS)] for k in range(4)]
    above, below = beside(one[half + times : half + 2 * times, :], two[times : 2 * times, :])
    back[...] = gathered_jumps(values, above, below, linked[...])


def first_gradient_body(count, *refs):
    back, linked, kernel, plain, weighted_t, adjoint_out, gradient, sent, edge = refs[count:]
    total = summed(refs[:count])
    field = total + back[...]
    adjoint_out[...] = total
    gradient[...] = field
    response_of(field, kernel, plain, weighted_t, linked[...], sent, edge)


def second_adjoint_body(count, *refs):
    two, kernel, plain_t, weighted, out, norms = refs[count:]
    times = plain_t.shape[0]
    half = times // 2
    total = summed(refs[:count])
    packed, squares = total[:half], total[half : half + 8]
    out[:times, :] = adjoint(unpacked(packed, kernel.shape[2]), kernel, plain_t[...], weighted[...], 2)
    scalars = rows_of([square_sum(packed), squares[2:3, :] * (2.0 / lax.axis_size("sensor"))])
    out[times : times + 8, :] = jnp.concatenate([scalars] * (out.shape[1] // LANES), axis=1)
    out[times + 8 :, :] = spread(two[...])
    norms[...] = squares


def step_of(norms, scalars):
    return norms[0:1, :] / (scalars[0:1, :] + (norms[1:2, :] + scalars[1:2, :]) + TINY)


def both_jumps_body(model, gradient, one, two, grad_one, grad_two, passed, linked, model_jumps, grad_jumps):
    times, cells = model.shape
    half = times // 2
    above, below = beside(one[half : half + times, :], two[:times, :])
    from_other = jnp.where(is_odd(), grad_two[...], gathered(passed[times + 8 :, :], times))
    halos = ((above, below), beside(grad_one[half + 8 :, :], from_other))
    for field, (above, below), out in zip((model, gradient), halos, (model_jumps, grad_jumps)):
        for k, strips in enumerate(jumps(field[...], above, below, linked[...])):
            for r, values in enumerate(strips):
                out[k, :, r * COLS : (r + 1) * COLS] = values


def second_gradient_body(count, *refs):
    (norms, adjoint_in, gradient_in, model, model_jumps, grad_jumps, start_multiplier, threshold, one, two, linked_ref,
     kernel, plain, weighted_t, model_out, jumps_out, multiplier_out, gradient_out, sent, edge) = refs[count:]
    times, cells = model.shape
    half = times // 2
    total = summed(refs[:count])
    step = step_of(norms, total[times:, :LANES])
    linked = linked_ref[...]
    field, gradient = model[...], gradient_in[...]
    rows = cells // COLS
    above, below = beside(one[half:, :], two[...])

    def advance(model_jumps, old_multiplier, limit):
        shifted = model_jumps + old_multiplier
        auxiliary = shrunk(shifted, limit)
        multiplier = shifted - auxiliary
        return multiplier, model_jumps - auxiliary + multiplier

    penalties, new_jumps = [], []
    for k in range(4):
        penalties.append([])
        new_jumps.append([])
        for r in range(rows):
            at = slice(r * COLS, (r + 1) * COLS)
            new = model_jumps[k, :, at] - step * grad_jumps[k, :, at]
            multiplier, penalty = advance(new, strip(start_multiplier[k], r), strip(threshold[0:1], r))
            jumps_out[k, :, at] = new
            multiplier_out[k, :, at] = multiplier
            penalties[k].append(penalty)
            new_jumps[k].append(new)
    _, beside_above = advance(-new_jumps[2][0], above[times : 2 * times], above[2 * times : 2 * times + 1])
    _, beside_below = advance(-new_jumps[3][-1], below[times : 2 * times], below[2 * times : 2 * times + 1])
    back = gathered_jumps(penalties, beside_above, beside_below, linked)
    wide_step = jnp.concatenate([step] * rows, axis=1)
    model_out[...] = field - wide_step * gradient
    new_gradient = adjoint_in[...] - wide_step * total[:times] + back
    gradient_out[...] = new_gradient
    response_of(new_gradient, kernel, plain, weighted_t, linked, sent, edge)


def response_body(count, *refs):
    two, out, passing, norms = refs[count:]
    total = summed(refs[:count])
    packed, squares = total[:-8], total[-8:]
    scalars = rows_of([square_sum(packed), squares[2:3, :] * (2.0 / lax.axis_size("sensor"))])
    out[...] = scalars
    passing[:8, :] = scalars
    passing[8:, :] = two[...]
    norms[...] = squares


def finish_body(count, *refs):
    (norms, gradient_in, model, model_jumps, multiplier, threshold, grad_one, grad_two, passed, linked,
     estimate_out, auxiliary_out, multiplier_out, estimate_here, auxiliary_here, multiplier_here, sems) = refs[count:]
    step = step_of(norms, tree_sum([part[:8, :] for part in refs[:count]]))
    grad_two = jnp.where(is_odd(), grad_two[...], passed[8:, :])
    half = gradient_in.shape[0] // 2
    gradient = gradient_in[...]
    copies = []

    def store(source, target):
        copy = pltpu.make_async_copy(source, target, sems.at[len(copies)])
        copy.start()
        copies.append(copy)

    estimate_here[...] = model[...] - jnp.concatenate([step] * (gradient.shape[1] // COLS), axis=1) * gradient
    store(estimate_here, estimate_out)
    grad_jumps = jumps(gradient, *beside(grad_one[half + 8 :, :], grad_two), linked[...])
    for k in range(4):
        for r in range(gradient.shape[1] // COLS):
            at = slice(r * COLS, (r + 1) * COLS)
            shifted = model_jumps[k, :, at] - step * grad_jumps[k][r] + multiplier[k, :, at]
            auxiliary = shrunk(shifted, threshold[0:1, at])
            auxiliary_here[k, :, at] = auxiliary
            multiplier_here[k, :, at] = shifted - auxiliary
        store(auxiliary_here.at[k], auxiliary_out.at[k])
        store(multiplier_here.at[k], multiplier_out.at[k])
    for copy in copies:
        copy.wait()


def stages_of(count, *radices):
    stages = []
    for radix in radices:
        if count > 1 and count % radix == 0:
            stages.append(radix)
            count //= radix
    while count > 1:
        stages.append(2)
        count //= 2
    return stages


def summing(parts, axis, stride, stages):
    count = lax.axis_size(axis)
    for radix in stages:
        total = tree_sum(parts)
        parts = [total] + [
            lax.ppermute(total, axis, [(i, i ^ (k * stride)) for i in range(count)]) for k in range(1, radix)
        ]
        stride *= radix
    return parts


def sensor_hop(array):
    return lax.ppermute(array, "sensor", [(i, i ^ 1) for i in range(lax.axis_size("sensor"))])


def sensor_parts(array, rows):
    passed = sensor_hop(array)
    total = array[:rows] + passed[:rows]
    return summing([total], "sensor", 2, stages_of(lax.axis_size("sensor") // 2, 2)), passed


def last_sensor_parts(scalars, passing):
    count = lax.axis_size("sensor")
    near, far, across = (
        lax.ppermute(array, "sensor", [(i, i ^ k) for i in range(count)])
        for k, array in ((1, scalars), (2, scalars), (3, passing))
    )
    parts = [scalars, near, far, across]
    if count > 4:
        rows = scalars.shape[0]
        parts = summing([tree_sum([part[:rows] for part in parts])], "sensor", 4, stages_of(count // 4, 4))
    return parts, across


def cell_parts(merged):
    return summing([merged], "cell", 2, stages_of(lax.axis_size("cell") // 2, 4, 4))


def from_partner(array):
    return lax.ppermute(array, "cell", [(i, i ^ 1) for i in range(lax.axis_size("cell"))])


def from_other(array):
    sensors = lax.axis_size("sensor")
    pairs = [
        (i * sensors + s, (i + 1 if i % 2 else i - 1) * sensors + s)
        for i in range(1, lax.axis_size("cell") - 1)
        for s in range(1, sensors, 2)
    ]
    return lax.ppermute(array, ("cell", "sensor"), pairs)


def per_device(kernel, observed, start_model, start_multiplier, neighbours, tile_of_cell, tile_weight):
    times, cells = start_model.shape
    freqs, sensors = kernel.shape[1:3]
    plain, weighted = tables(times, freqs)
    plain, plain_t, weighted, weighted_t = (
        jnp.asarray(table_terms(t)) for t in (plain, plain.T, weighted, weighted.T)
    )
    half = times // 2
    field, row, wide = (times, cells), (times, COLS), (4, times, cells)

    loads = [
        kernel, start_model, start_multiplier, plain, weighted_t, plain_t, weighted,
        neighbours, tile_of_cell[None, :], tile_weight[None, :],
    ]
    sent, edge, threshold, linked, kernel, start_model, start_multiplier, plain, weighted_t, plain_t, weighted = call(
        first_forward_body,
        [(half + 2 * times + 8, LANES), (2 * times + 8, LANES), (8, cells), (8, cells)]
        + [jax.ShapeDtypeStruct(a.shape, a.dtype) for a in loads[:7]],
        *[pltpu.with_memory_space_constraint(a, HBM) for a in loads],
        scratch=[VMEM(a.shape, a.dtype) for a in loads[7:]] + [pltpu.SemaphoreType.DMA((9 + -(-freqs // CHUNK),))],
        inputs=HBM,
    )
    one = from_partner(sent)
    two = from_other(edge)
    parts = cell_parts(sent[:half] + one[:half])
    across = call(
        turn_body, jax.ShapeDtypeStruct((2, plain.shape[0] // 16, cells, GROUP * sensors), kernel.dtype), kernel, one
    )
    message, side, shared = (half + 8 + times, LANES), (times, LANES), (2 * times + 8, LANES)
    back = call(
        functools.partial(first_adjoint_body, len(parts)), (2 * times + 8, cells),
        *parts, observed, two, kernel, plain_t, weighted, across,
    )
    parts, passed = sensor_parts(back, times)
    back, two = call(start_back_body, [field, shared], start_multiplier, one, two, passed, linked)
    adjoint_one, gradient, sent, edge = call(
        functools.partial(first_gradient_body, len(parts)), [field, field, message, side],
        *parts, back, linked, across, plain, weighted_t,
    )
    grad_one, grad_two = from_partner(sent), from_other(edge)
    parts = cell_parts(call(merge_body, (half + 8, LANES), sent, grad_one, edge, grad_two, linked))
    back, norms = call(
        functools.partial(second_adjoint_body, len(parts)), [(times + 8 + half, cells), (8, LANES)],
        *parts, grad_two, kernel, plain_t, weighted,
    )
    parts, passed = sensor_parts(back, times + 8)
    model_jumps, grad_jumps = call(
        both_jumps_body, [wide, wide], start_model, gradient, one, two, grad_one, grad_two, passed, linked
    )
    model, model_jumps, multiplier, gradient, sent, edge = call(
        functools.partial(second_gradient_body, len(parts)), [field, wide, wide, field, message, side],
        *parts, norms, adjoint_one, gradient, start_model, model_jumps, grad_jumps, start_multiplier, threshold,
        one, two, linked, across, plain, weighted_t,
    )
    grad_one, grad_two = from_partner(sent), from_other(edge)
    parts = cell_parts(call(merge_body, (half + 8, LANES), sent, grad_one, edge, grad_two, linked))
    scalars, passing, norms = call(
        functools.partial(response_body, len(parts)), [(8, LANES), (8 + times, LANES), (8, LANES)], *parts, grad_two
    )
    parts, passed = last_sensor_parts(scalars, passing)
    return tuple(
        call(
            functools.partial(finish_body, len(parts)), [field, wide, wide],
            *parts, norms, gradient, model, model_jumps, multiplier, threshold, grad_one, grad_two, passed, linked,
            scratch=[VMEM(shape, jnp.float32) for shape in (field, wide, wide)] + [pltpu.SemaphoreType.DMA((9,))],
            outputs=HBM,
        )
    )


def solution(mesh):
    in_specs = (
        P(None, None, "sensor", "cell"),
        P(None, "sensor"),
        P(None, "cell"),
        P(None, None, "cell"),
        P(None, "cell"),
        P("cell"),
        P(),
    )
    out_specs = (P(None, "cell"), P(None, None, "cell"), P(None, None, "cell"))
    return jax.shard_map(
        per_device, mesh=mesh, in_specs=in_specs, out_specs=out_specs, check_vma=False
    )
```

```python
import functools

import jax
import jax.numpy as jnp
import numpy as np
from jax import lax
from jax.experimental import pallas as pl
from jax.experimental.pallas import tpu as pltpu
from jax.sharding import PartitionSpec as P

COLS = 128
LANES = 128
GROUP = 8
CHUNK = 32
SHRINK_SCALE = 0.4
TINY = 1e-06
VMEM = pltpu.VMEM
HBM = pltpu.HBM


def tables(times, freqs):
    padded = 2 * times
    groups = -(-freqs // GROUP)
    plain = np.zeros((16 * groups, times), np.float64)
    weighted = np.zeros((16 * groups, times), np.float64)
    for f in range(freqs):
        phase = 2.0 * np.pi * ((f * np.arange(times)) % padded) / padded
        weight = (1.0 if f in (0, freqs - 1) else 2.0) / padded
        row = 16 * (f // GROUP) + f % GROUP
        plain[row], plain[row + GROUP] = np.cos(phase), -np.sin(phase)
        weighted[row], weighted[row + GROUP] = weight * np.cos(phase), -weight * np.sin(phase)
    return plain.astype(np.float32), weighted.astype(np.float32)


def table_terms(table):
    high = table.astype(jnp.bfloat16)
    low = (table - high.astype(np.float32)).astype(jnp.bfloat16)
    return np.concatenate([high, high, low], axis=1)


def table_dot(terms, values):
    high = values.astype(jnp.bfloat16)
    low = (values - high.astype(jnp.float32)).astype(jnp.bfloat16)
    return dot_nn(terms, jnp.concatenate([high, low, high], axis=0))


def turned(rows):
    rows = rows.astype(jnp.float32)
    return jnp.concatenate([-rows[GROUP:], rows[:GROUP]], axis=0).astype(jnp.bfloat16)


def dot_nt(left, right):
    return lax.dot_general(left, right, (((1,), (1,)), ((), ())), preferred_element_type=jnp.float32)


def dot_nn(left, right):
    return jnp.dot(left, right, preferred_element_type=jnp.float32)


def slab(kernel_ref, part, group):
    freqs, sensors, cells = kernel_ref.shape[1:]
    count = min(GROUP, freqs - group * GROUP)
    block = kernel_ref[part, group * GROUP : group * GROUP + count]
    return block.reshape(count * sensors, cells)


def own_block(width, sensors):
    row = lax.broadcasted_iota(jnp.int32, (16, width), 0) % GROUP
    lane = lax.broadcasted_iota(jnp.int32, (16, width), 1) // sensors
    return row == lane


def fold(wide):
    total = functools.reduce(
        lambda a, b: a + b, [wide[:, i : i + LANES] for i in range(0, wide.shape[1], LANES)]
    )
    return total + pltpu.roll(total, LANES // 2, 1)


def forward(field, turned_ref, plain, weighted_t, sensors):
    freqs = field.shape[0] + 1
    spectra = table_dot(plain, field)
    rows = []
    for group in range(spectra.shape[0] // 16):
        part = spectra[16 * group : 16 * group + 16]
        width = min(GROUP, freqs - group * GROUP) * sensors
        out = dot_nn(part.astype(jnp.bfloat16), turned_ref[0, group, :, :width])
        out += dot_nn(turned(part), turned_ref[1, group, :, :width])
        rows.append(fold_own(out, sensors))
    return packed_series(jnp.concatenate(rows, axis=0), weighted_t, sensors)


def fold_own(out, sensors):
    width = out.shape[1]
    out = jnp.where(own_block(width, sensors), out, 0.0)
    if width < LANES:
        out = jnp.concatenate([out, jnp.zeros((16, LANES - width), jnp.float32)], axis=1)
    return fold(out)


def forward_rows(spectra, kernel_ref, arrived=None):
    sensors = kernel_ref.shape[2]
    rows = []
    for group in range(spectra.shape[0] // 16):
        part = spectra[16 * group : 16 * group + 16]
        if arrived is not None:
            arrived(group)
        re_slab, im_slab = slab(kernel_ref, 0, group), slab(kernel_ref, 1, group)
        out = dot_nt(part.astype(jnp.bfloat16), re_slab) + dot_nt(turned(part), im_slab)
        rows.append(fold_own(out, sensors))
    return jnp.concatenate(rows, axis=0)


def packed_series(rows, weighted_t, sensors):
    times = weighted_t.shape[0]
    series = table_dot(weighted_t, rows)
    left = lax.broadcasted_iota(jnp.int32, (times // 2, LANES), 1) < sensors
    return jnp.where(left, series[: times // 2], series[times // 2 :])


def unpacked(packed, sensors):
    other = pltpu.roll(packed, sensors, 1)
    left = lax.broadcasted_iota(jnp.int32, packed.shape, 1) < sensors
    return jnp.concatenate([jnp.where(left, packed, other), jnp.where(left, other, packed)], axis=0)


def adjoint(residual, kernel_ref, plain_t, weighted, halves):
    freqs, sensors, cells = kernel_ref.shape[1:]
    spectra = table_dot(weighted, residual)
    rows = []
    for group in range(weighted.shape[0] // 16):
        part = spectra[16 * group : 16 * group + 16]
        count = min(GROUP, freqs - group * GROUP)
        width = count * sensors
        re_slab, im_slab = slab(kernel_ref, 0, group), slab(kernel_ref, 1, group)
        wide = jnp.concatenate([part] * (-(-width // LANES)), axis=1)[:, :width]
        wide = jnp.where(own_block(width, sensors), wide, 0.0)
        terms = []
        for _ in range(halves):
            terms.append(wide.astype(jnp.bfloat16))
            wide = wide - terms[-1].astype(jnp.float32)
        left = jnp.concatenate(terms, axis=0)
        swapped = jnp.concatenate([turned(term) for term in terms], axis=0)
        out = dot_nn(left, re_slab) - dot_nn(swapped, im_slab)
        rows.append(tree_sum([out[16 * i : 16 * i + 16] for i in range(halves)]))
    return table_dot(plain_t, jnp.concatenate(rows, axis=0))


def strip(array, row):
    return array[..., row * COLS : (row + 1) * COLS]


def jumps(field, above, below, linked):
    count = field.shape[1] // COLS
    out = []
    for direction in range(4):
        strips = []
        for row in range(count):
            here = strip(field, row)
            if direction == 0:
                there = pltpu.roll(here, COLS - 1, 1)
            elif direction == 1:
                there = pltpu.roll(here, 1, 1)
            elif direction == 2:
                there = above if row == 0 else strip(field, row - 1)
            else:
                there = below if row == count - 1 else strip(field, row + 1)
            strips.append(strip(linked[direction : direction + 1], row) * (there - here))
        out.append(strips)
    return out


def gathered_jumps(values, above, below, linked):
    count = len(values[0])
    out = []
    for row in range(count):
        arriving = (
            pltpu.roll(values[1][row], COLS - 1, 1),
            pltpu.roll(values[0][row], 1, 1),
            above if row == 0 else values[3][row - 1],
            below if row == count - 1 else values[2][row + 1],
        )
        total = None
        for direction in range(4):
            term = strip(linked[direction : direction + 1], row) * (arriving[direction] - values[direction][row])
            total = term if total is None else total + term
        out.append(total)
    return jnp.concatenate(out, axis=1)


def shrunk(shifted, threshold):
    return shifted - jnp.clip(shifted, -threshold, threshold)


def tree_sum(parts):
    parts = list(parts)
    while len(parts) > 1:
        parts = [parts[i] + parts[i + 1] if i + 1 < len(parts) else parts[i] for i in range(0, len(parts), 2)]
    return parts[0]


def total_of(array):
    return jnp.sum(array, axis=(0, 1), keepdims=True)


def square_sum(array):
    return total_of(array * array)


def block_of(scalar, rows=8):
    return jnp.full((rows, LANES), scalar, jnp.float32)


def call(body, out_shapes, *operands, scratch=(), inputs=VMEM, outputs=VMEM):
    single = not isinstance(out_shapes, list)
    shapes = [out_shapes] if single else list(out_shapes)
    shapes = [s if isinstance(s, jax.ShapeDtypeStruct) else jax.ShapeDtypeStruct(s, jnp.float32) for s in shapes]
    out = pl.pallas_call(
        body,
        out_shape=shapes,
        in_specs=[pl.BlockSpec(memory_space=inputs)] * len(operands),
        out_specs=[pl.BlockSpec(memory_space=outputs)] * len(shapes),
        scratch_shapes=list(scratch),
        compiler_params=pltpu.CompilerParams(vmem_limit_bytes=24 * 2**20),
    )(*operands)
    return out[0] if single else out


def summed(parts):
    return tree_sum([part[...] for part in parts])


def is_even():
    return lax.rem(lax.axis_index("cell"), 2) == 0


def edges(head, tail):
    even = is_even()
    return jnp.where(even, tail, head), jnp.where(even, head, tail)


def beside(partner, other):
    even = is_even()
    return jnp.where(even, other, partner), jnp.where(even, partner, other)


def is_odd():
    return lax.rem(lax.axis_index("sensor"), 2) == 1


def spread(rows):
    upper = -(-rows.shape[0] // 16) * 8
    lower = rows[upper:]
    if lower.shape[0] < upper:
        lower = jnp.concatenate([lower, jnp.zeros((upper - lower.shape[0], LANES), rows.dtype)])
    return jnp.concatenate([rows[:upper], lower], axis=1)


def gathered(wide, count):
    return jnp.concatenate([wide[:, :LANES], wide[: count - wide.shape[0], LANES:]])


def rows_of(values):
    row = lax.broadcasted_iota(jnp.int32, (8, LANES), 0)
    out = jnp.zeros((8, LANES), jnp.float32)
    for i, value in enumerate(values):
        if value is not None:
            out = jnp.where(row == i, jnp.broadcast_to(value, (8, LANES)), out)
    return out


def first_forward_body(*refs):
    loaded, (sent, edge, threshold, linked), kept, sems = refs[:10], refs[10:14], refs[14:24], refs[24]
    kernel, kernel_here = loaded[0], kept[0]
    field, multiplier, plain, weighted_t = kept[1:5]
    neighbours, tile_of_cell, tile_weight = kept[7:]
    freqs = kernel.shape[1]
    times, cells = field.shape
    half = times // 2
    copies = []

    def load(source, target, priority=0):
        copy = pltpu.make_async_copy(source, target, sems.at[len(copies)])
        copy.start(priority=priority)
        copies.append(copy)
        return copy

    early = [load(loaded[i], kept[i], 1) for i in (1, 3)]
    large = []
    for start in range(0, freqs, CHUNK):
        at = (slice(None), pl.ds(start, min(CHUNK, freqs - start)))
        large.append(load(kernel.at[at], kernel_here.at[at], 1 if start == 0 else 0))
        if start == 0:
            small = [load(loaded[i], kept[i]) for i in (7, 8, 9, 2, 4)]
    late = [load(loaded[i], kept[i]) for i in (5, 6)]
    for copy in early:
        copy.wait()
    spectra = table_dot(plain[...], field[...])
    for copy in small:
        copy.wait()

    cell = lax.broadcasted_iota(jnp.int32, (4, cells), 1) + lax.axis_index("cell") * cells
    linked[0:4, :] = jnp.where(neighbours[...] != cell, 1.0, 0.0)
    linked[4:8, :] = jnp.zeros((4, cells), jnp.float32)
    tile = lax.broadcasted_iota(jnp.int32, (tile_weight.shape[1], cells), 0)
    chosen = jnp.where(tile == tile_of_cell[...], 1.0, 0.0)
    weights = jnp.dot(
        jnp.broadcast_to(tile_weight[...], (8, tile_weight.shape[1])), chosen,
        precision=lax.Precision.HIGHEST, preferred_element_type=jnp.float32,
    )
    limit = SHRINK_SCALE * weights
    threshold[...] = limit
    bottom = cells // COLS - 1
    pairs = (
        (strip(field, 0), strip(field, bottom)),
        (strip(multiplier[2], 0), strip(multiplier[3], bottom)),
        (strip(limit, 0), strip(limit, bottom)),
    )
    for (head, tail), start in zip(pairs, (0, times, 2 * times)):
        one, two = edges(head, tail)
        sent[half + start : half + start + head.shape[0], :] = one
        edge[start : start + head.shape[0], :] = two

    def arrived(group):
        if group * GROUP % CHUNK == 0:
            large[group * GROUP // CHUNK].wait()

    rows = forward_rows(spectra, kernel_here, arrived)
    sent[:half, :] = packed_series(rows, weighted_t[...], kernel.shape[2])
    for copy in late:
        copy.wait()


def turn_body(kernel, came, out):
    freqs, sensors = kernel.shape[1:3]
    for part in range(2):
        for group in range(out.shape[1]):
            width = min(GROUP, freqs - group * GROUP) * sensors
            out[part, group, :, :width] = slab(kernel, part, group).T


def first_adjoint_body(count, *refs):
    observed, two, kernel, plain_t, weighted, _, out = refs[count:]
    times = observed.shape[0]
    predicted = unpacked(summed(refs[:count]), kernel.shape[2])
    residual = predicted - jnp.concatenate([observed[...], observed[...]], axis=1)
    out[:times, :] = adjoint(residual, kernel, plain_t[...], weighted[...], 1)
    out[times:, :] = spread(two[...])


def response_of(field, turned_ref, plain, weighted_t, linked, sent, edge):
    half = field.shape[0] // 2
    rows = field.shape[1] // COLS
    one, two = edges(strip(field, 0), strip(field, rows - 1))
    squares = []
    for row in range(rows):
        here = strip(field, row)
        east = strip(linked[0:1], row) * (pltpu.roll(here, COLS - 1, 1) - here)
        squares.append(east * east)
        if row > 0:
            north = strip(linked[2:3], row) * (strip(field, row - 1) - here)
            squares.append(north * north)
    sensors = turned_ref.shape[3] // GROUP
    sent[:half, :] = forward(field, turned_ref, plain[...], weighted_t[...], sensors)
    sent[half : half + 8, :] = rows_of([square_sum(field), 2.0 * total_of(tree_sum(squares))])
    sent[half + 8 :, :] = one
    edge[...] = two


def merge_body(sent, came, edge, other, linked, out):
    cells = linked.shape[1]
    top = out.shape[0]
    to_partner, to_other = edges(linked[2:3, :COLS], linked[3:4, cells - COLS :])
    across = to_partner * (came[top:, :] - sent[top:, :])
    beyond = to_other * (other[...] - edge[...])
    out[: top - 8, :] = sent[: top - 8, :] + came[: top - 8, :]
    boundary = 2.0 * square_sum(jnp.where(is_odd(), beyond, across))
    out[top - 8 :, :] = sent[top - 8 : top, :] + came[top - 8 : top, :] + rows_of([None, None, boundary])


def start_back_body(start_multiplier, one, two, passed, linked, back, two_out):
    times, cells = back.shape
    half = times // 2
    two = jnp.where(is_odd(), two[...], gathered(passed[times:, :], two.shape[0]))
    two_out[...] = two
    values = [[strip(start_multiplier[k], r) for r in range(cells // COLS)] for k in range(4)]
    above, below = beside(one[half + times : half + 2 * times, :], two[times : 2 * times, :])
    back[...] = gathered_jumps(values, above, below, linked[...])


def first_gradient_body(count, *refs):
    back, linked, kernel, plain, weighted_t, adjoint_out, gradient, sent, edge = refs[count:]
    total = summed(refs[:count])
    field = total + back[...]
    adjoint_out[...] = total
    gradient[...] = field
    response_of(field, kernel, plain, weighted_t, linked[...], sent, edge)


def second_adjoint_body(count, *refs):
    two, kernel, plain_t, weighted, out, norms = refs[count:]
    times = plain_t.shape[0]
    half = times // 2
    total = summed(refs[:count])
    packed, squares = total[:half], total[half : half + 8]
    out[:times, :] = adjoint(unpacked(packed, kernel.shape[2]), kernel, plain_t[...], weighted[...], 2)
    scalars = rows_of([square_sum(packed), squares[2:3, :] * (2.0 / lax.axis_size("sensor"))])
    out[times : times + 8, :] = jnp.concatenate([scalars] * (out.shape[1] // LANES), axis=1)
    out[times + 8 :, :] = spread(two[...])
    norms[...] = squares


def step_of(norms, scalars):
    return norms[0:1, :] / (scalars[0:1, :] + (norms[1:2, :] + scalars[1:2, :]) + TINY)


def both_jumps_body(model, gradient, one, two, grad_one, grad_two, passed, linked, model_jumps, grad_jumps):
    times, cells = model.shape
    half = times // 2
    above, below = beside(one[half : half + times, :], two[:times, :])
    from_other = jnp.where(is_odd(), grad_two[...], gathered(passed[times + 8 :, :], times))
    halos = ((above, below), beside(grad_one[half + 8 :, :], from_other))
    for field, (above, below), out in zip((model, gradient), halos, (model_jumps, grad_jumps)):
        for k, strips in enumerate(jumps(field[...], above, below, linked[...])):
            for r, values in enumerate(strips):
                out[k, :, r * COLS : (r + 1) * COLS] = values


def second_gradient_body(count, *refs):
    (norms, adjoint_in, gradient_in, model, model_jumps, grad_jumps, start_multiplier, threshold, one, two, linked_ref,
     kernel, plain, weighted_t, model_out, jumps_out, multiplier_out, gradient_out, sent, edge) = refs[count:]
    times, cells = model.shape
    half = times // 2
    total = summed(refs[:count])
    step = step_of(norms, total[times:, :LANES])
    linked = linked_ref[...]
    field, gradient = model[...], gradient_in[...]
    rows = cells // COLS
    above, below = beside(one[half:, :], two[...])

    def advance(model_jumps, old_multiplier, limit):
        shifted = model_jumps + old_multiplier
        auxiliary = shrunk(shifted, limit)
        multiplier = shifted - auxiliary
        return multiplier, model_jumps - auxiliary + multiplier

    penalties, new_jumps = [], []
    for k in range(4):
        penalties.append([])
        new_jumps.append([])
        for r in range(rows):
            at = slice(r * COLS, (r + 1) * COLS)
            new = model_jumps[k, :, at] - step * grad_jumps[k, :, at]
            multiplier, penalty = advance(new, strip(start_multiplier[k], r), strip(threshold[0:1], r))
            jumps_out[k, :, at] = new
            multiplier_out[k, :, at] = multiplier
            penalties[k].append(penalty)
            new_jumps[k].append(new)
    _, beside_above = advance(-new_jumps[2][0], above[times : 2 * times], above[2 * times : 2 * times + 1])
    _, beside_below = advance(-new_jumps[3][-1], below[times : 2 * times], below[2 * times : 2 * times + 1])
    back = gathered_jumps(penalties, beside_above, beside_below, linked)
    wide_step = jnp.concatenate([step] * rows, axis=1)
    model_out[...] = field - wide_step * gradient
    new_gradient = adjoint_in[...] - wide_step * total[:times] + back
    gradient_out[...] = new_gradient
    response_of(new_gradient, kernel, plain, weighted_t, linked, sent, edge)


def response_body(count, *refs):
    two, out, passing, norms = refs[count:]
    total = summed(refs[:count])
    packed, squares = total[:-8], total[-8:]
    scalars = rows_of([square_sum(packed), squares[2:3, :] * (2.0 / lax.axis_size("sensor"))])
    out[...] = scalars
    passing[:8, :] = scalars
    passing[8:, :] = two[...]
    norms[...] = squares


def before_finish_body(gradient, model_jumps, multiplier, linked, sum_out, jumps_out):
    field = gradient[...]
    sum_out[...] = model_jumps[...] + multiplier[...]
    nothing = jnp.zeros((field.shape[0], COLS), jnp.float32)
    for k, strips in enumerate(jumps(field, nothing, nothing, linked[...])):
        for r, values in enumerate(strips):
            jumps_out[k, :, r * COLS : (r + 1) * COLS] = values


def finish_body(count, *refs):
    (norms, gradient_in, model, sums, inner_jumps, threshold, grad_one, grad_two, passed, linked,
     estimate_out, auxiliary_out, multiplier_out, estimate_here, auxiliary_here, multiplier_here, sems) = refs[count:]
    step = step_of(norms, tree_sum([part[:8, :] for part in refs[:count]]))
    half = gradient_in.shape[0] // 2
    gradient = gradient_in[...]
    rows = gradient.shape[1] // COLS
    copies = []

    def store(source, target):
        copy = pltpu.make_async_copy(source, target, sems.at[len(copies)])
        copy.start()
        copies.append(copy)

    above, below = beside(grad_one[half + 8 :, :], jnp.where(is_odd(), grad_two[...], passed[8:, :]))
    outer = {
        (2, 0): linked[2:3, :COLS] * (above - strip(gradient, 0)),
        (3, rows - 1): linked[3:4, (rows - 1) * COLS :] * (below - strip(gradient, rows - 1)),
    }
    for k in range(4):
        for r in range(rows):
            at = slice(r * COLS, (r + 1) * COLS)
            shifted = sums[k, :, at] - step * outer.get((k, r), inner_jumps[k, :, at])
            auxiliary = shrunk(shifted, threshold[0:1, at])
            auxiliary_here[k, :, at] = auxiliary
            multiplier_here[k, :, at] = shifted - auxiliary
        store(auxiliary_here.at[k], auxiliary_out.at[k])
        store(multiplier_here.at[k], multiplier_out.at[k])
    estimate_here[...] = model[...] - jnp.concatenate([step] * rows, axis=1) * gradient
    store(estimate_here, estimate_out)
    for copy in copies:
        copy.wait()


def stages_of(count, *radices):
    stages = []
    for radix in radices:
        if count > 1 and count % radix == 0:
            stages.append(radix)
            count //= radix
    while count > 1:
        stages.append(2)
        count //= 2
    return stages


def summing(parts, axis, stride, stages):
    count = lax.axis_size(axis)
    for radix in stages:
        total = tree_sum(parts)
        parts = [total] + [
            lax.ppermute(total, axis, [(i, i ^ (k * stride)) for i in range(count)]) for k in range(1, radix)
        ]
        stride *= radix
    return parts


def sensor_hop(array):
    return lax.ppermute(array, "sensor", [(i, i ^ 1) for i in range(lax.axis_size("sensor"))])


def sensor_parts(array, rows):
    passed = sensor_hop(array)
    total = array[:rows] + passed[:rows]
    return summing([total], "sensor", 2, stages_of(lax.axis_size("sensor") // 2, 2)), passed


def last_sensor_parts(scalars, passing):
    count = lax.axis_size("sensor")
    near, far, across = (
        lax.ppermute(array, "sensor", [(i, i ^ k) for i in range(count)])
        for k, array in ((1, scalars), (2, scalars), (3, passing))
    )
    parts = [scalars, near, far, across]
    if count > 4:
        rows = scalars.shape[0]
        parts = summing([tree_sum([part[:rows] for part in parts])], "sensor", 4, stages_of(count // 4, 4))
    return parts, across


def cell_parts(merged):
    return summing([merged], "cell", 2, stages_of(lax.axis_size("cell") // 2, 4, 4))


def from_partner(array):
    return lax.ppermute(array, "cell", [(i, i ^ 1) for i in range(lax.axis_size("cell"))])


def from_other(array):
    sensors = lax.axis_size("sensor")
    pairs = [
        (i * sensors + s, (i + 1 if i % 2 else i - 1) * sensors + s)
        for i in range(1, lax.axis_size("cell") - 1)
        for s in range(1, sensors, 2)
    ]
    return lax.ppermute(array, ("cell", "sensor"), pairs)


def per_device(kernel, observed, start_model, start_multiplier, neighbours, tile_of_cell, tile_weight):
    times, cells = start_model.shape
    freqs, sensors = kernel.shape[1:3]
    plain, weighted = tables(times, freqs)
    plain, plain_t, weighted, weighted_t = (
        jnp.asarray(table_terms(t)) for t in (plain, plain.T, weighted, weighted.T)
    )
    half = times // 2
    field, row, wide = (times, cells), (times, COLS), (4, times, cells)

    loads = [
        kernel, start_model, start_multiplier, plain, weighted_t, plain_t, weighted,
        neighbours, tile_of_cell[None, :], tile_weight[None, :],
    ]
    sent, edge, threshold, linked, kernel, start_model, start_multiplier, plain, weighted_t, plain_t, weighted = call(
        first_forward_body,
        [(half + 2 * times + 8, LANES), (2 * times + 8, LANES), (8, cells), (8, cells)]
        + [jax.ShapeDtypeStruct(a.shape, a.dtype) for a in loads[:7]],
        *[pltpu.with_memory_space_constraint(a, HBM) for a in loads],
        scratch=[VMEM(a.shape, a.dtype) for a in loads[7:]] + [pltpu.SemaphoreType.DMA((9 + -(-freqs // CHUNK),))],
        inputs=HBM,
    )
    one = from_partner(sent)
    two = from_other(edge)
    parts = cell_parts(sent[:half] + one[:half])
    across = call(
        turn_body, jax.ShapeDtypeStruct((2, plain.shape[0] // 16, cells, GROUP * sensors), kernel.dtype), kernel, one
    )
    message, side, shared = (half + 8 + times, LANES), (times, LANES), (2 * times + 8, LANES)
    back = call(
        functools.partial(first_adjoint_body, len(parts)), (2 * times + 8, cells),
        *parts, observed, two, kernel, plain_t, weighted, across,
    )
    parts, passed = sensor_parts(back, times)
    back, two = call(start_back_body, [field, shared], start_multiplier, one, two, passed, linked)
    adjoint_one, gradient, sent, edge = call(
        functools.partial(first_gradient_body, len(parts)), [field, field, message, side],
        *parts, back, linked, across, plain, weighted_t,
    )
    grad_one, grad_two = from_partner(sent), from_other(edge)
    parts = cell_parts(call(merge_body, (half + 8, LANES), sent, grad_one, edge, grad_two, linked))
    back, norms = call(
        functools.partial(second_adjoint_body, len(parts)), [(times + 8 + half, cells), (8, LANES)],
        *parts, grad_two, kernel, plain_t, weighted,
    )
    parts, passed = sensor_parts(back, times + 8)
    model_jumps, grad_jumps = call(
        both_jumps_body, [wide, wide], start_model, gradient, one, two, grad_one, grad_two, passed, linked
    )
    model, model_jumps, multiplier, gradient, sent, edge = call(
        functools.partial(second_gradient_body, len(parts)), [field, wide, wide, field, message, side],
        *parts, norms, adjoint_one, gradient, start_model, model_jumps, grad_jumps, start_multiplier, threshold,
        one, two, linked, across, plain, weighted_t,
    )
    grad_one, grad_two = from_partner(sent), from_other(edge)
    parts = cell_parts(call(merge_body, (half + 8, LANES), sent, grad_one, edge, grad_two, linked))
    sums, inner_jumps = call(before_finish_body, [wide, wide], gradient, model_jumps, multiplier, linked)
    scalars, passing, norms = call(
        functools.partial(response_body, len(parts)), [(8, LANES), (8 + times, LANES), (8, LANES)], *parts, grad_two
    )
    parts, passed = last_sensor_parts(scalars, passing)
    return tuple(
        call(
            functools.partial(finish_body, len(parts)), [field, wide, wide],
            *parts, norms, gradient, model, sums, inner_jumps, threshold, grad_one, grad_two, passed, linked,
            scratch=[VMEM(shape, jnp.float32) for shape in (field, wide, wide)] + [pltpu.SemaphoreType.DMA((9,))],
            outputs=HBM,
        )
    )


def solution(mesh):
    in_specs = (
        P(None, None, "sensor", "cell"),
        P(None, "sensor"),
        P(None, "cell"),
        P(None, None, "cell"),
        P(None, "cell"),
        P("cell"),
        P(),
    )
    out_specs = (P(None, "cell"), P(None, None, "cell"), P(None, None, "cell"))
    return jax.shard_map(
        per_device, mesh=mesh, in_specs=in_specs, out_specs=out_specs, check_vma=False
    )
```

```python
import functools

import jax
import jax.numpy as jnp
import numpy as np
from jax import lax
from jax.experimental import pallas as pl
from jax.experimental.pallas import tpu as pltpu
from jax.sharding import PartitionSpec as P

COLS = 128
LANES = 128
GROUP = 8
CHUNK = 16
SHRINK_SCALE = 0.4
TINY = 1e-06
VMEM = pltpu.VMEM
HBM = pltpu.HBM


def tables(times, freqs):
    padded = 2 * times
    groups = -(-freqs // GROUP)
    plain = np.zeros((16 * groups, times), np.float64)
    weighted = np.zeros((16 * groups, times), np.float64)
    for f in range(freqs):
        phase = 2.0 * np.pi * ((f * np.arange(times)) % padded) / padded
        weight = (1.0 if f in (0, freqs - 1) else 2.0) / padded
        row = 16 * (f // GROUP) + f % GROUP
        plain[row], plain[row + GROUP] = np.cos(phase), -np.sin(phase)
        weighted[row], weighted[row + GROUP] = weight * np.cos(phase), -weight * np.sin(phase)
    return plain.astype(np.float32), weighted.astype(np.float32)


def table_terms(table):
    high = table.astype(jnp.bfloat16)
    low = (table - high.astype(np.float32)).astype(jnp.bfloat16)
    return np.concatenate([high, high, low], axis=1)


def table_dot(terms, values):
    high = values.astype(jnp.bfloat16)
    low = (values - high.astype(jnp.float32)).astype(jnp.bfloat16)
    return dot_nn(terms, jnp.concatenate([high, low, high], axis=0))


def turned(rows):
    rows = rows.astype(jnp.float32)
    return jnp.concatenate([-rows[GROUP:], rows[:GROUP]], axis=0).astype(jnp.bfloat16)


def dot_nt(left, right):
    return lax.dot_general(left, right, (((1,), (1,)), ((), ())), preferred_element_type=jnp.float32)


def dot_nn(left, right):
    return jnp.dot(left, right, preferred_element_type=jnp.float32)


def slab(kernel_ref, part, group):
    freqs, sensors, cells = kernel_ref.shape[1:]
    count = min(GROUP, freqs - group * GROUP)
    block = kernel_ref[part, group * GROUP : group * GROUP + count]
    return block.reshape(count * sensors, cells)


def own_block(width, sensors):
    row = lax.broadcasted_iota(jnp.int32, (16, width), 0) % GROUP
    lane = lax.broadcasted_iota(jnp.int32, (16, width), 1) // sensors
    return row == lane


def fold(wide):
    total = functools.reduce(
        lambda a, b: a + b, [wide[:, i : i + LANES] for i in range(0, wide.shape[1], LANES)]
    )
    return total + pltpu.roll(total, LANES // 2, 1)


def forward(field, turned_ref, plain, weighted_t, sensors):
    freqs = field.shape[0] + 1
    spectra = table_dot(plain, field)
    rows = []
    for group in range(spectra.shape[0] // 16):
        part = spectra[16 * group : 16 * group + 16]
        width = min(GROUP, freqs - group * GROUP) * sensors
        out = dot_nn(part.astype(jnp.bfloat16), turned_ref[0, group, :, :width])
        out += dot_nn(turned(part), turned_ref[1, group, :, :width])
        rows.append(fold_own(out, sensors))
    return packed_series(jnp.concatenate(rows, axis=0), weighted_t, sensors)


def fold_own(out, sensors):
    width = out.shape[1]
    out = jnp.where(own_block(width, sensors), out, 0.0)
    if width < LANES:
        out = jnp.concatenate([out, jnp.zeros((16, LANES - width), jnp.float32)], axis=1)
    return fold(out)


def forward_rows(spectra, kernel_ref, arrived=None):
    sensors = kernel_ref.shape[2]
    rows = []
    for group in range(spectra.shape[0] // 16):
        part = spectra[16 * group : 16 * group + 16]
        if arrived is not None:
            arrived(group)
        re_slab, im_slab = slab(kernel_ref, 0, group), slab(kernel_ref, 1, group)
        out = dot_nt(part.astype(jnp.bfloat16), re_slab) + dot_nt(turned(part), im_slab)
        rows.append(fold_own(out, sensors))
    return jnp.concatenate(rows, axis=0)


def packed_series(rows, weighted_t, sensors):
    times = weighted_t.shape[0]
    series = table_dot(weighted_t, rows)
    left = lax.broadcasted_iota(jnp.int32, (times // 2, LANES), 1) < sensors
    return jnp.where(left, series[: times // 2], series[times // 2 :])


def unpacked(packed, sensors):
    other = pltpu.roll(packed, sensors, 1)
    left = lax.broadcasted_iota(jnp.int32, packed.shape, 1) < sensors
    return jnp.concatenate([jnp.where(left, packed, other), jnp.where(left, other, packed)], axis=0)


def adjoint(residual, kernel_ref, plain_t, weighted, halves):
    freqs, sensors, cells = kernel_ref.shape[1:]
    spectra = table_dot(weighted, residual)
    rows = []
    for group in range(weighted.shape[0] // 16):
        part = spectra[16 * group : 16 * group + 16]
        count = min(GROUP, freqs - group * GROUP)
        width = count * sensors
        re_slab, im_slab = slab(kernel_ref, 0, group), slab(kernel_ref, 1, group)
        wide = jnp.concatenate([part] * (-(-width // LANES)), axis=1)[:, :width]
        wide = jnp.where(own_block(width, sensors), wide, 0.0)
        terms = []
        for _ in range(halves):
            terms.append(wide.astype(jnp.bfloat16))
            wide = wide - terms[-1].astype(jnp.float32)
        left = jnp.concatenate(terms, axis=0)
        swapped = jnp.concatenate([turned(term) for term in terms], axis=0)
        out = dot_nn(left, re_slab) - dot_nn(swapped, im_slab)
        rows.append(tree_sum([out[16 * i : 16 * i + 16] for i in range(halves)]))
    return table_dot(plain_t, jnp.concatenate(rows, axis=0))


def strip(array, row):
    return array[..., row * COLS : (row + 1) * COLS]


def jumps(field, above, below, linked):
    count = field.shape[1] // COLS
    out = []
    for direction in range(4):
        strips = []
        for row in range(count):
            here = strip(field, row)
            if direction == 0:
                there = pltpu.roll(here, COLS - 1, 1)
            elif direction == 1:
                there = pltpu.roll(here, 1, 1)
            elif direction == 2:
                there = above if row == 0 else strip(field, row - 1)
            else:
                there = below if row == count - 1 else strip(field, row + 1)
            strips.append(strip(linked[direction : direction + 1], row) * (there - here))
        out.append(strips)
    return out


def gathered_jumps(values, above, below, linked):
    count = len(values[0])
    out = []
    for row in range(count):
        arriving = (
            pltpu.roll(values[1][row], COLS - 1, 1),
            pltpu.roll(values[0][row], 1, 1),
            above if row == 0 else values[3][row - 1],
            below if row == count - 1 else values[2][row + 1],
        )
        total = None
        for direction in range(4):
            term = strip(linked[direction : direction + 1], row) * (arriving[direction] - values[direction][row])
            total = term if total is None else total + term
        out.append(total)
    return jnp.concatenate(out, axis=1)


def shrunk(shifted, threshold):
    return shifted - jnp.clip(shifted, -threshold, threshold)


def tree_sum(parts):
    parts = list(parts)
    while len(parts) > 1:
        parts = [parts[i] + parts[i + 1] if i + 1 < len(parts) else parts[i] for i in range(0, len(parts), 2)]
    return parts[0]


def total_of(array):
    return jnp.sum(array, axis=(0, 1), keepdims=True)


def square_sum(array):
    return total_of(array * array)


def block_of(scalar, rows=8):
    return jnp.full((rows, LANES), scalar, jnp.float32)


def call(body, out_shapes, *operands, scratch=(), inputs=VMEM, outputs=VMEM):
    single = not isinstance(out_shapes, list)
    shapes = [out_shapes] if single else list(out_shapes)
    shapes = [s if isinstance(s, jax.ShapeDtypeStruct) else jax.ShapeDtypeStruct(s, jnp.float32) for s in shapes]
    out = pl.pallas_call(
        body,
        out_shape=shapes,
        in_specs=[pl.BlockSpec(memory_space=inputs)] * len(operands),
        out_specs=[pl.BlockSpec(memory_space=outputs)] * len(shapes),
        scratch_shapes=list(scratch),
        compiler_params=pltpu.CompilerParams(vmem_limit_bytes=24 * 2**20),
    )(*operands)
    return out[0] if single else out


def summed(parts):
    return tree_sum([part[...] for part in parts])


def is_even():
    return lax.rem(lax.axis_index("cell"), 2) == 0


def edges(head, tail):
    even = is_even()
    return jnp.where(even, tail, head), jnp.where(even, head, tail)


def beside(partner, other):
    even = is_even()
    return jnp.where(even, other, partner), jnp.where(even, partner, other)


def is_odd():
    return lax.rem(lax.axis_index("sensor"), 2) == 1


def spread(rows):
    upper = -(-rows.shape[0] // 16) * 8
    lower = rows[upper:]
    if lower.shape[0] < upper:
        lower = jnp.concatenate([lower, jnp.zeros((upper - lower.shape[0], LANES), rows.dtype)])
    return jnp.concatenate([rows[:upper], lower], axis=1)


def gathered(wide, count):
    return jnp.concatenate([wide[:, :LANES], wide[: count - wide.shape[0], LANES:]])


def rows_of(values):
    row = lax.broadcasted_iota(jnp.int32, (8, LANES), 0)
    out = jnp.zeros((8, LANES), jnp.float32)
    for i, value in enumerate(values):
        if value is not None:
            out = jnp.where(row == i, jnp.broadcast_to(value, (8, LANES)), out)
    return out


def first_forward_body(*refs):
    loaded, (sent, edge, threshold, linked), kept, sems = refs[:10], refs[10:14], refs[14:24], refs[24]
    kernel, kernel_here = loaded[0], kept[0]
    field, multiplier, plain, weighted_t = kept[1:5]
    neighbours, tile_of_cell, tile_weight = kept[7:]
    freqs = kernel.shape[1]
    times, cells = field.shape
    half = times // 2
    copies = []

    def load(source, target):
        copy = pltpu.make_async_copy(source, target, sems.at[len(copies)])
        copy.start()
        copies.append(copy)
        return copy

    early = [load(loaded[i], kept[i]) for i in (1, 3)]
    large = []
    for start in range(0, freqs, CHUNK):
        at = (slice(None), pl.ds(start, min(CHUNK, freqs - start)))
        large.append(load(kernel.at[at], kernel_here.at[at]))
        if start == 0:
            small = [load(loaded[i], kept[i]) for i in (7, 8, 9, 2, 4)]
    late = [load(loaded[i], kept[i]) for i in (5, 6)]
    for copy in early:
        copy.wait()
    spectra = table_dot(plain[...], field[...])
    for copy in small:
        copy.wait()

    cell = lax.broadcasted_iota(jnp.int32, (4, cells), 1) + lax.axis_index("cell") * cells
    linked[0:4, :] = jnp.where(neighbours[...] != cell, 1.0, 0.0)
    linked[4:8, :] = jnp.zeros((4, cells), jnp.float32)
    tile = lax.broadcasted_iota(jnp.int32, (tile_weight.shape[1], cells), 0)
    chosen = jnp.where(tile == tile_of_cell[...], 1.0, 0.0)
    weights = jnp.dot(
        jnp.broadcast_to(tile_weight[...], (8, tile_weight.shape[1])), chosen,
        precision=lax.Precision.HIGHEST, preferred_element_type=jnp.float32,
    )
    limit = SHRINK_SCALE * weights
    threshold[...] = limit
    bottom = cells // COLS - 1
    pairs = (
        (strip(field, 0), strip(field, bottom)),
        (strip(multiplier[2], 0), strip(multiplier[3], bottom)),
        (strip(limit, 0), strip(limit, bottom)),
    )
    for (head, tail), start in zip(pairs, (0, times, 2 * times)):
        one, two = edges(head, tail)
        sent[half + start : half + start + head.shape[0], :] = one
        edge[start : start + head.shape[0], :] = two

    def arrived(group):
        if group * GROUP % CHUNK == 0:
            large[group * GROUP // CHUNK].wait()

    rows = forward_rows(spectra, kernel_here, arrived)
    sent[:half, :] = packed_series(rows, weighted_t[...], kernel.shape[2])
    for copy in late:
        copy.wait()


def turn_body(kernel, came, out):
    freqs, sensors = kernel.shape[1:3]
    for part in range(2):
        for group in range(out.shape[1]):
            width = min(GROUP, freqs - group * GROUP) * sensors
            out[part, group, :, :width] = slab(kernel, part, group).T


def first_adjoint_body(count, *refs):
    observed, two, kernel, plain_t, weighted, _, out = refs[count:]
    times = observed.shape[0]
    predicted = unpacked(summed(refs[:count]), kernel.shape[2])
    residual = predicted - jnp.concatenate([observed[...], observed[...]], axis=1)
    out[:times, :] = adjoint(residual, kernel, plain_t[...], weighted[...], 1)
    out[times:, :] = spread(two[...])


def response_of(field, turned_ref, plain, weighted_t, linked, sent, edge):
    half = field.shape[0] // 2
    rows = field.shape[1] // COLS
    one, two = edges(strip(field, 0), strip(field, rows - 1))
    squares = []
    for row in range(rows):
        here = strip(field, row)
        east = strip(linked[0:1], row) * (pltpu.roll(here, COLS - 1, 1) - here)
        squares.append(east * east)
        if row > 0:
            north = strip(linked[2:3], row) * (strip(field, row - 1) - here)
            squares.append(north * north)
    sensors = turned_ref.shape[3] // GROUP
    sent[:half, :] = forward(field, turned_ref, plain[...], weighted_t[...], sensors)
    sent[half : half + 8, :] = rows_of([square_sum(field), 2.0 * total_of(tree_sum(squares))])
    sent[half + 8 :, :] = one
    edge[...] = two


def merge_body(sent, came, edge, other, linked, out):
    cells = linked.shape[1]
    top = out.shape[0]
    to_partner, to_other = edges(linked[2:3, :COLS], linked[3:4, cells - COLS :])
    across = to_partner * (came[top:, :] - sent[top:, :])
    beyond = to_other * (other[...] - edge[...])
    out[: top - 8, :] = sent[: top - 8, :] + came[: top - 8, :]
    boundary = 2.0 * square_sum(jnp.where(is_odd(), beyond, across))
    out[top - 8 :, :] = sent[top - 8 : top, :] + came[top - 8 : top, :] + rows_of([None, None, boundary])


def start_back_body(start_multiplier, one, two, passed, linked, back, two_out):
    times, cells = back.shape
    half = times // 2
    two = jnp.where(is_odd(), two[...], gathered(passed[times:, :], two.shape[0]))
    two_out[...] = two
    values = [[strip(start_multiplier[k], r) for r in range(cells // COLS)] for k in range(4)]
    above, below = beside(one[half + times : half + 2 * times, :], two[times : 2 * times, :])
    back[...] = gathered_jumps(values, above, below, linked[...])


def first_gradient_body(count, *refs):
    back, linked, kernel, plain, weighted_t, adjoint_out, gradient, sent, edge = refs[count:]
    total = summed(refs[:count])
    field = total + back[...]
    adjoint_out[...] = total
    gradient[...] = field
    response_of(field, kernel, plain, weighted_t, linked[...], sent, edge)


def second_adjoint_body(count, *refs):
    two, kernel, plain_t, weighted, out, norms = refs[count:]
    times = plain_t.shape[0]
    half = times // 2
    total = summed(refs[:count])
    packed, squares = total[:half], total[half : half + 8]
    out[:times, :] = adjoint(unpacked(packed, kernel.shape[2]), kernel, plain_t[...], weighted[...], 2)
    scalars = rows_of([square_sum(packed), squares[2:3, :] * (2.0 / lax.axis_size("sensor"))])
    out[times : times + 8, :] = jnp.concatenate([scalars] * (out.shape[1] // LANES), axis=1)
    out[times + 8 :, :] = spread(two[...])
    norms[...] = squares


def step_of(norms, scalars):
    return norms[0:1, :] / (scalars[0:1, :] + (norms[1:2, :] + scalars[1:2, :]) + TINY)


def both_jumps_body(model, gradient, one, two, grad_one, grad_two, passed, linked, model_jumps, grad_jumps):
    times, cells = model.shape
    half = times // 2
    above, below = beside(one[half : half + times, :], two[:times, :])
    from_other = jnp.where(is_odd(), grad_two[...], gathered(passed[times + 8 :, :], times))
    halos = ((above, below), beside(grad_one[half + 8 :, :], from_other))
    for field, (above, below), out in zip((model, gradient), halos, (model_jumps, grad_jumps)):
        for k, strips in enumerate(jumps(field[...], above, below, linked[...])):
            for r, values in enumerate(strips):
                out[k, :, r * COLS : (r + 1) * COLS] = values


def second_gradient_body(count, *refs):
    (norms, adjoint_in, gradient_in, model, model_jumps, grad_jumps, start_multiplier, threshold, one, two, linked_ref,
     kernel, plain, weighted_t, model_out, jumps_out, multiplier_out, gradient_out, sent, edge) = refs[count:]
    times, cells = model.shape
    half = times // 2
    total = summed(refs[:count])
    step = step_of(norms, total[times:, :LANES])
    linked = linked_ref[...]
    field, gradient = model[...], gradient_in[...]
    rows = cells // COLS
    above, below = beside(one[half:, :], two[...])

    def advance(model_jumps, old_multiplier, limit):
        shifted = model_jumps + old_multiplier
        auxiliary = shrunk(shifted, limit)
        multiplier = shifted - auxiliary
        return multiplier, model_jumps - auxiliary + multiplier

    penalties, new_jumps = [], []
    for k in range(4):
        penalties.append([])
        new_jumps.append([])
        for r in range(rows):
            at = slice(r * COLS, (r + 1) * COLS)
            new = model_jumps[k, :, at] - step * grad_jumps[k, :, at]
            multiplier, penalty = advance(new, strip(start_multiplier[k], r), strip(threshold[0:1], r))
            jumps_out[k, :, at] = new
            multiplier_out[k, :, at] = multiplier
            penalties[k].append(penalty)
            new_jumps[k].append(new)
    _, beside_above = advance(-new_jumps[2][0], above[times : 2 * times], above[2 * times : 2 * times + 1])
    _, beside_below = advance(-new_jumps[3][-1], below[times : 2 * times], below[2 * times : 2 * times + 1])
    back = gathered_jumps(penalties, beside_above, beside_below, linked)
    wide_step = jnp.concatenate([step] * rows, axis=1)
    model_out[...] = field - wide_step * gradient
    new_gradient = adjoint_in[...] - wide_step * total[:times] + back
    gradient_out[...] = new_gradient
    response_of(new_gradient, kernel, plain, weighted_t, linked, sent, edge)


def response_body(count, *refs):
    two, out, passing, norms = refs[count:]
    total = summed(refs[:count])
    packed, squares = total[:-8], total[-8:]
    scalars = rows_of([square_sum(packed), squares[2:3, :] * (2.0 / lax.axis_size("sensor"))])
    out[...] = scalars
    passing[:8, :] = scalars
    passing[8:, :] = two[...]
    norms[...] = squares


def before_finish_body(gradient, model_jumps, multiplier, linked, sum_out, jumps_out):
    field = gradient[...]
    sum_out[...] = model_jumps[...] + multiplier[...]
    nothing = jnp.zeros((field.shape[0], COLS), jnp.float32)
    for k, strips in enumerate(jumps(field, nothing, nothing, linked[...])):
        for r, values in enumerate(strips):
            jumps_out[k, :, r * COLS : (r + 1) * COLS] = values


def finish_body(count, *refs):
    (norms, gradient_in, model, sums, inner_jumps, threshold, grad_one, grad_two, passed, linked,
     estimate_out, auxiliary_out, multiplier_out, estimate_here, auxiliary_here, multiplier_here, sems) = refs[count:]
    step = step_of(norms, tree_sum([part[:8, :] for part in refs[:count]]))
    half = gradient_in.shape[0] // 2
    gradient = gradient_in[...]
    rows = gradient.shape[1] // COLS
    copies = []

    def store(source, target):
        copy = pltpu.make_async_copy(source, target, sems.at[len(copies)])
        copy.start()
        copies.append(copy)

    above, below = beside(grad_one[half + 8 :, :], jnp.where(is_odd(), grad_two[...], passed[8:, :]))
    outer = {
        (2, 0): linked[2:3, :COLS] * (above - strip(gradient, 0)),
        (3, rows - 1): linked[3:4, (rows - 1) * COLS :] * (below - strip(gradient, rows - 1)),
    }
    for k in range(4):
        for r in range(rows):
            at = slice(r * COLS, (r + 1) * COLS)
            shifted = sums[k, :, at] - step * outer.get((k, r), inner_jumps[k, :, at])
            auxiliary = shrunk(shifted, threshold[0:1, at])
            auxiliary_here[k, :, at] = auxiliary
            multiplier_here[k, :, at] = shifted - auxiliary
        store(auxiliary_here.at[k], auxiliary_out.at[k])
        store(multiplier_here.at[k], multiplier_out.at[k])
    estimate_here[...] = model[...] - jnp.concatenate([step] * rows, axis=1) * gradient
    store(estimate_here, estimate_out)
    for copy in copies:
        copy.wait()


def stages_of(count, *radices):
    stages = []
    for radix in radices:
        if count > 1 and count % radix == 0:
            stages.append(radix)
            count //= radix
    while count > 1:
        stages.append(2)
        count //= 2
    return stages


def summing(parts, axis, stride, stages):
    count = lax.axis_size(axis)
    for radix in stages:
        total = tree_sum(parts)
        parts = [total] + [
            lax.ppermute(total, axis, [(i, i ^ (k * stride)) for i in range(count)]) for k in range(1, radix)
        ]
        stride *= radix
    return parts


def sensor_hop(array):
    return lax.ppermute(array, "sensor", [(i, i ^ 1) for i in range(lax.axis_size("sensor"))])


def sensor_parts(array, rows):
    passed = sensor_hop(array)
    total = array[:rows] + passed[:rows]
    return summing([total], "sensor", 2, stages_of(lax.axis_size("sensor") // 2, 2)), passed


def last_sensor_parts(scalars, passing):
    count = lax.axis_size("sensor")
    near, far, across = (
        lax.ppermute(array, "sensor", [(i, i ^ k) for i in range(count)])
        for k, array in ((1, scalars), (2, scalars), (3, passing))
    )
    parts = [scalars, near, far, across]
    if count > 4:
        rows = scalars.shape[0]
        parts = summing([tree_sum([part[:rows] for part in parts])], "sensor", 4, stages_of(count // 4, 4))
    return parts, across


def cell_parts(merged):
    return summing([merged], "cell", 2, stages_of(lax.axis_size("cell") // 2, 4, 4))


def from_partner(array):
    return lax.ppermute(array, "cell", [(i, i ^ 1) for i in range(lax.axis_size("cell"))])


def from_other(array):
    sensors = lax.axis_size("sensor")
    pairs = [
        (i * sensors + s, (i + 1 if i % 2 else i - 1) * sensors + s)
        for i in range(1, lax.axis_size("cell") - 1)
        for s in range(1, sensors, 2)
    ]
    return lax.ppermute(array, ("cell", "sensor"), pairs)


def per_device(kernel, observed, start_model, start_multiplier, neighbours, tile_of_cell, tile_weight):
    times, cells = start_model.shape
    freqs, sensors = kernel.shape[1:3]
    plain, weighted = tables(times, freqs)
    plain, plain_t, weighted, weighted_t = (
        jnp.asarray(table_terms(t)) for t in (plain, plain.T, weighted, weighted.T)
    )
    half = times // 2
    field, row, wide = (times, cells), (times, COLS), (4, times, cells)

    loads = [
        kernel, start_model, start_multiplier, plain, weighted_t, plain_t, weighted,
        neighbours, tile_of_cell[None, :], tile_weight[None, :],
    ]
    sent, edge, threshold, linked, kernel, start_model, start_multiplier, plain, weighted_t, plain_t, weighted = call(
        first_forward_body,
        [(half + 2 * times + 8, LANES), (2 * times + 8, LANES), (8, cells), (8, cells)]
        + [jax.ShapeDtypeStruct(a.shape, a.dtype) for a in loads[:7]],
        *[pltpu.with_memory_space_constraint(a, HBM) for a in loads],
        scratch=[VMEM(a.shape, a.dtype) for a in loads[7:]] + [pltpu.SemaphoreType.DMA((9 + -(-freqs // CHUNK),))],
        inputs=HBM,
    )
    one = from_partner(sent)
    two = from_other(edge)
    parts = cell_parts(sent[:half] + one[:half])
    across = call(
        turn_body, jax.ShapeDtypeStruct((2, plain.shape[0] // 16, cells, GROUP * sensors), kernel.dtype), kernel, one
    )
    message, side, shared = (half + 8 + times, LANES), (times, LANES), (2 * times + 8, LANES)
    back = call(
        functools.partial(first_adjoint_body, len(parts)), (2 * times + 8, cells),
        *parts, observed, two, kernel, plain_t, weighted, across,
    )
    parts, passed = sensor_parts(back, times)
    back, two = call(start_back_body, [field, shared], start_multiplier, one, two, passed, linked)
    adjoint_one, gradient, sent, edge = call(
        functools.partial(first_gradient_body, len(parts)), [field, field, message, side],
        *parts, back, linked, across, plain, weighted_t,
    )
    grad_one, grad_two = from_partner(sent), from_other(edge)
    parts = cell_parts(call(merge_body, (half + 8, LANES), sent, grad_one, edge, grad_two, linked))
    back, norms = call(
        functools.partial(second_adjoint_body, len(parts)), [(times + 8 + half, cells), (8, LANES)],
        *parts, grad_two, kernel, plain_t, weighted,
    )
    parts, passed = sensor_parts(back, times + 8)
    model_jumps, grad_jumps = call(
        both_jumps_body, [wide, wide], start_model, gradient, one, two, grad_one, grad_two, passed, linked
    )
    model, model_jumps, multiplier, gradient, sent, edge = call(
        functools.partial(second_gradient_body, len(parts)), [field, wide, wide, field, message, side],
        *parts, norms, adjoint_one, gradient, start_model, model_jumps, grad_jumps, start_multiplier, threshold,
        one, two, linked, across, plain, weighted_t,
    )
    grad_one, grad_two = from_partner(sent), from_other(edge)
    parts = cell_parts(call(merge_body, (half + 8, LANES), sent, grad_one, edge, grad_two, linked))
    sums, inner_jumps = call(before_finish_body, [wide, wide], gradient, model_jumps, multiplier, linked)
    scalars, passing, norms = call(
        functools.partial(response_body, len(parts)), [(8, LANES), (8 + times, LANES), (8, LANES)], *parts, grad_two
    )
    parts, passed = last_sensor_parts(scalars, passing)
    return tuple(
        call(
            functools.partial(finish_body, len(parts)), [field, wide, wide],
            *parts, norms, gradient, model, sums, inner_jumps, threshold, grad_one, grad_two, passed, linked,
            scratch=[VMEM(shape, jnp.float32) for shape in (field, wide, wide)] + [pltpu.SemaphoreType.DMA((9,))],
            outputs=HBM,
        )
    )


def solution(mesh):
    in_specs = (
        P(None, None, "sensor", "cell"),
        P(None, "sensor"),
        P(None, "cell"),
        P(None, None, "cell"),
        P(None, "cell"),
        P("cell"),
        P(),
    )
    out_specs = (P(None, "cell"), P(None, None, "cell"), P(None, None, "cell"))
    return jax.shard_map(
        per_device, mesh=mesh, in_specs=in_specs, out_specs=out_specs, check_vma=False
    )
```

```python
import functools

import jax
import jax.numpy as jnp
import numpy as np
from jax import lax
from jax.experimental import pallas as pl
from jax.experimental.pallas import tpu as pltpu
from jax.sharding import PartitionSpec as P

COLS = 128
LANES = 128
GROUP = 8
CHUNK = 24
SHRINK_SCALE = 0.4
TINY = 1e-06
VMEM = pltpu.VMEM
HBM = pltpu.HBM


def tables(times, freqs):
    padded = 2 * times
    groups = -(-freqs // GROUP)
    plain = np.zeros((16 * groups, times), np.float64)
    weighted = np.zeros((16 * groups, times), np.float64)
    for f in range(freqs):
        phase = 2.0 * np.pi * ((f * np.arange(times)) % padded) / padded
        weight = (1.0 if f in (0, freqs - 1) else 2.0) / padded
        row = 16 * (f // GROUP) + f % GROUP
        plain[row], plain[row + GROUP] = np.cos(phase), -np.sin(phase)
        weighted[row], weighted[row + GROUP] = weight * np.cos(phase), -weight * np.sin(phase)
    return plain.astype(np.float32), weighted.astype(np.float32)


def table_terms(table):
    high = table.astype(jnp.bfloat16)
    low = (table - high.astype(np.float32)).astype(jnp.bfloat16)
    return np.concatenate([high, high, low], axis=1)


def table_dot(terms, values):
    high = values.astype(jnp.bfloat16)
    low = (values - high.astype(jnp.float32)).astype(jnp.bfloat16)
    return dot_nn(terms, jnp.concatenate([high, low, high], axis=0))


def turned(rows):
    rows = rows.astype(jnp.float32)
    return jnp.concatenate([-rows[GROUP:], rows[:GROUP]], axis=0).astype(jnp.bfloat16)


def dot_nt(left, right):
    return lax.dot_general(left, right, (((1,), (1,)), ((), ())), preferred_element_type=jnp.float32)


def dot_nn(left, right):
    return jnp.dot(left, right, preferred_element_type=jnp.float32)


def slab(kernel_ref, part, group):
    freqs, sensors, cells = kernel_ref.shape[1:]
    count = min(GROUP, freqs - group * GROUP)
    block = kernel_ref[part, group * GROUP : group * GROUP + count]
    return block.reshape(count * sensors, cells)


def own_block(width, sensors):
    row = lax.broadcasted_iota(jnp.int32, (16, width), 0) % GROUP
    lane = lax.broadcasted_iota(jnp.int32, (16, width), 1) // sensors
    return row == lane


def fold(wide):
    total = functools.reduce(
        lambda a, b: a + b, [wide[:, i : i + LANES] for i in range(0, wide.shape[1], LANES)]
    )
    return total + pltpu.roll(total, LANES // 2, 1)


def forward(field, turned_ref, plain, weighted_t, sensors):
    freqs = field.shape[0] + 1
    spectra = table_dot(plain, field)
    rows = []
    for group in range(spectra.shape[0] // 16):
        part = spectra[16 * group : 16 * group + 16]
        width = min(GROUP, freqs - group * GROUP) * sensors
        out = dot_nn(part.astype(jnp.bfloat16), turned_ref[0, group, :, :width])
        out += dot_nn(turned(part), turned_ref[1, group, :, :width])
        rows.append(fold_own(out, sensors))
    return packed_series(jnp.concatenate(rows, axis=0), weighted_t, sensors)


def fold_own(out, sensors):
    width = out.shape[1]
    out = jnp.where(own_block(width, sensors), out, 0.0)
    if width < LANES:
        out = jnp.concatenate([out, jnp.zeros((16, LANES - width), jnp.float32)], axis=1)
    return fold(out)


def forward_rows(spectra, kernel_ref, arrived=None):
    sensors = kernel_ref.shape[2]
    rows = []
    for group in range(spectra.shape[0] // 16):
        part = spectra[16 * group : 16 * group + 16]
        if arrived is not None:
            arrived(group)
        re_slab, im_slab = slab(kernel_ref, 0, group), slab(kernel_ref, 1, group)
        out = dot_nt(part.astype(jnp.bfloat16), re_slab) + dot_nt(turned(part), im_slab)
        rows.append(fold_own(out, sensors))
    return jnp.concatenate(rows, axis=0)


def packed_series(rows, weighted_t, sensors):
    times = weighted_t.shape[0]
    series = table_dot(weighted_t, rows)
    left = lax.broadcasted_iota(jnp.int32, (times // 2, LANES), 1) < sensors
    return jnp.where(left, series[: times // 2], series[times // 2 :])


def unpacked(packed, sensors):
    other = pltpu.roll(packed, sensors, 1)
    left = lax.broadcasted_iota(jnp.int32, packed.shape, 1) < sensors
    return jnp.concatenate([jnp.where(left, packed, other), jnp.where(left, other, packed)], axis=0)


def adjoint(residual, kernel_ref, plain_t, weighted, halves):
    freqs, sensors, cells = kernel_ref.shape[1:]
    spectra = table_dot(weighted, residual)
    rows = []
    for group in range(weighted.shape[0] // 16):
        part = spectra[16 * group : 16 * group + 16]
        count = min(GROUP, freqs - group * GROUP)
        width = count * sensors
        re_slab, im_slab = slab(kernel_ref, 0, group), slab(kernel_ref, 1, group)
        wide = jnp.concatenate([part] * (-(-width // LANES)), axis=1)[:, :width]
        wide = jnp.where(own_block(width, sensors), wide, 0.0)
        terms = []
        for _ in range(halves):
            terms.append(wide.astype(jnp.bfloat16))
            wide = wide - terms[-1].astype(jnp.float32)
        left = jnp.concatenate(terms, axis=0)
        swapped = jnp.concatenate([turned(term) for term in terms], axis=0)
        out = dot_nn(left, re_slab) - dot_nn(swapped, im_slab)
        rows.append(tree_sum([out[16 * i : 16 * i + 16] for i in range(halves)]))
    return table_dot(plain_t, jnp.concatenate(rows, axis=0))


def strip(array, row):
    return array[..., row * COLS : (row + 1) * COLS]


def jumps(field, above, below, linked):
    count = field.shape[1] // COLS
    out = []
    for direction in range(4):
        strips = []
        for row in range(count):
            here = strip(field, row)
            if direction == 0:
                there = pltpu.roll(here, COLS - 1, 1)
            elif direction == 1:
                there = pltpu.roll(here, 1, 1)
            elif direction == 2:
                there = above if row == 0 else strip(field, row - 1)
            else:
                there = below if row == count - 1 else strip(field, row + 1)
            strips.append(strip(linked[direction : direction + 1], row) * (there - here))
        out.append(strips)
    return out


def gathered_jumps(values, above, below, linked):
    count = len(values[0])
    out = []
    for row in range(count):
        arriving = (
            pltpu.roll(values[1][row], COLS - 1, 1),
            pltpu.roll(values[0][row], 1, 1),
            above if row == 0 else values[3][row - 1],
            below if row == count - 1 else values[2][row + 1],
        )
        total = None
        for direction in range(4):
            term = strip(linked[direction : direction + 1], row) * (arriving[direction] - values[direction][row])
            total = term if total is None else total + term
        out.append(total)
    return jnp.concatenate(out, axis=1)


def shrunk(shifted, threshold):
    return shifted - jnp.clip(shifted, -threshold, threshold)


def tree_sum(parts):
    parts = list(parts)
    while len(parts) > 1:
        parts = [parts[i] + parts[i + 1] if i + 1 < len(parts) else parts[i] for i in range(0, len(parts), 2)]
    return parts[0]


def total_of(array):
    return jnp.sum(array, axis=(0, 1), keepdims=True)


def square_sum(array):
    return total_of(array * array)


def block_of(scalar, rows=8):
    return jnp.full((rows, LANES), scalar, jnp.float32)


def call(body, out_shapes, *operands, scratch=(), inputs=VMEM, outputs=VMEM):
    single = not isinstance(out_shapes, list)
    shapes = [out_shapes] if single else list(out_shapes)
    shapes = [s if isinstance(s, jax.ShapeDtypeStruct) else jax.ShapeDtypeStruct(s, jnp.float32) for s in shapes]
    out = pl.pallas_call(
        body,
        out_shape=shapes,
        in_specs=[pl.BlockSpec(memory_space=inputs)] * len(operands),
        out_specs=[pl.BlockSpec(memory_space=outputs)] * len(shapes),
        scratch_shapes=list(scratch),
        compiler_params=pltpu.CompilerParams(vmem_limit_bytes=24 * 2**20),
    )(*operands)
    return out[0] if single else out


def summed(parts):
    return tree_sum([part[...] for part in parts])


def is_even():
    return lax.rem(lax.axis_index("cell"), 2) == 0


def edges(head, tail):
    even = is_even()
    return jnp.where(even, tail, head), jnp.where(even, head, tail)


def beside(partner, other):
    even = is_even()
    return jnp.where(even, other, partner), jnp.where(even, partner, other)


def is_odd():
    return lax.rem(lax.axis_index("sensor"), 2) == 1


def spread(rows):
    upper = -(-rows.shape[0] // 16) * 8
    lower = rows[upper:]
    if lower.shape[0] < upper:
        lower = jnp.concatenate([lower, jnp.zeros((upper - lower.shape[0], LANES), rows.dtype)])
    return jnp.concatenate([rows[:upper], lower], axis=1)


def gathered(wide, count):
    return jnp.concatenate([wide[:, :LANES], wide[: count - wide.shape[0], LANES:]])


def rows_of(values):
    row = lax.broadcasted_iota(jnp.int32, (8, LANES), 0)
    out = jnp.zeros((8, LANES), jnp.float32)
    for i, value in enumerate(values):
        if value is not None:
            out = jnp.where(row == i, jnp.broadcast_to(value, (8, LANES)), out)
    return out


def first_forward_body(*refs):
    loaded, (sent, edge, threshold, linked), kept, sems = refs[:10], refs[10:14], refs[14:24], refs[24]
    kernel, kernel_here = loaded[0], kept[0]
    field, multiplier, plain, weighted_t = kept[1:5]
    neighbours, tile_of_cell, tile_weight = kept[7:]
    freqs = kernel.shape[1]
    times, cells = field.shape
    half = times // 2
    copies = []

    def load(source, target):
        copy = pltpu.make_async_copy(source, target, sems.at[len(copies)])
        copy.start()
        copies.append(copy)
        return copy

    early = [load(loaded[i], kept[i]) for i in (1, 3)]
    large = []
    for start in range(0, freqs, CHUNK):
        at = (slice(None), pl.ds(start, min(CHUNK, freqs - start)))
        large.append(load(kernel.at[at], kernel_here.at[at]))
        if start == 0:
            small = [load(loaded[i], kept[i]) for i in (7, 8, 9, 2, 4)]
    late = [load(loaded[i], kept[i]) for i in (5, 6)]
    for copy in early:
        copy.wait()
    spectra = table_dot(plain[...], field[...])
    for copy in small:
        copy.wait()

    cell = lax.broadcasted_iota(jnp.int32, (4, cells), 1) + lax.axis_index("cell") * cells
    linked[0:4, :] = jnp.where(neighbours[...] != cell, 1.0, 0.0)
    linked[4:8, :] = jnp.zeros((4, cells), jnp.float32)
    tile = lax.broadcasted_iota(jnp.int32, (tile_weight.shape[1], cells), 0)
    chosen = jnp.where(tile == tile_of_cell[...], 1.0, 0.0)
    weights = jnp.dot(
        jnp.broadcast_to(tile_weight[...], (8, tile_weight.shape[1])), chosen,
        precision=lax.Precision.HIGHEST, preferred_element_type=jnp.float32,
    )
    limit = SHRINK_SCALE * weights
    threshold[...] = limit
    bottom = cells // COLS - 1
    pairs = (
        (strip(field, 0), strip(field, bottom)),
        (strip(multiplier[2], 0), strip(multiplier[3], bottom)),
        (strip(limit, 0), strip(limit, bottom)),
    )
    for (head, tail), start in zip(pairs, (0, times, 2 * times)):
        one, two = edges(head, tail)
        sent[half + start : half + start + head.shape[0], :] = one
        edge[start : start + head.shape[0], :] = two

    def arrived(group):
        if group * GROUP % CHUNK == 0:
            large[group * GROUP // CHUNK].wait()

    rows = forward_rows(spectra, kernel_here, arrived)
    sent[:half, :] = packed_series(rows, weighted_t[...], kernel.shape[2])
    for copy in late:
        copy.wait()


def turn_body(kernel, came, out):
    freqs, sensors = kernel.shape[1:3]
    for part in range(2):
        for group in range(out.shape[1]):
            width = min(GROUP, freqs - group * GROUP) * sensors
            out[part, group, :, :width] = slab(kernel, part, group).T


def first_adjoint_body(count, *refs):
    observed, two, kernel, plain_t, weighted, _, out = refs[count:]
    times = observed.shape[0]
    predicted = unpacked(summed(refs[:count]), kernel.shape[2])
    residual = predicted - jnp.concatenate([observed[...], observed[...]], axis=1)
    out[:times, :] = adjoint(residual, kernel, plain_t[...], weighted[...], 1)
    out[times:, :] = spread(two[...])


def response_of(field, turned_ref, plain, weighted_t, linked, sent, edge):
    half = field.shape[0] // 2
    rows = field.shape[1] // COLS
    one, two = edges(strip(field, 0), strip(field, rows - 1))
    squares = []
    for row in range(rows):
        here = strip(field, row)
        east = strip(linked[0:1], row) * (pltpu.roll(here, COLS - 1, 1) - here)
        squares.append(east * east)
        if row > 0:
            north = strip(linked[2:3], row) * (strip(field, row - 1) - here)
            squares.append(north * north)
    sensors = turned_ref.shape[3] // GROUP
    sent[:half, :] = forward(field, turned_ref, plain[...], weighted_t[...], sensors)
    sent[half : half + 8, :] = rows_of([square_sum(field), 2.0 * total_of(tree_sum(squares))])
    sent[half + 8 :, :] = one
    edge[...] = two


def merge_body(sent, came, edge, other, linked, out):
    cells = linked.shape[1]
    top = out.shape[0]
    to_partner, to_other = edges(linked[2:3, :COLS], linked[3:4, cells - COLS :])
    across = to_partner * (came[top:, :] - sent[top:, :])
    beyond = to_other * (other[...] - edge[...])
    out[: top - 8, :] = sent[: top - 8, :] + came[: top - 8, :]
    boundary = 2.0 * square_sum(jnp.where(is_odd(), beyond, across))
    out[top - 8 :, :] = sent[top - 8 : top, :] + came[top - 8 : top, :] + rows_of([None, None, boundary])


def start_back_body(start_multiplier, one, two, passed, linked, back, two_out):
    times, cells = back.shape
    half = times // 2
    two = jnp.where(is_odd(), two[...], gathered(passed[times:, :], two.shape[0]))
    two_out[...] = two
    values = [[strip(start_multiplier[k], r) for r in range(cells // COLS)] for k in range(4)]
    above, below = beside(one[half + times : half + 2 * times, :], two[times : 2 * times, :])
    back[...] = gathered_jumps(values, above, below, linked[...])


def first_gradient_body(count, *refs):
    back, linked, kernel, plain, weighted_t, adjoint_out, gradient, sent, edge = refs[count:]
    total = summed(refs[:count])
    field = total + back[...]
    adjoint_out[...] = total
    gradient[...] = field
    response_of(field, kernel, plain, weighted_t, linked[...], sent, edge)


def second_adjoint_body(count, *refs):
    two, kernel, plain_t, weighted, out, norms = refs[count:]
    times = plain_t.shape[0]
    half = times // 2
    total = summed(refs[:count])
    packed, squares = total[:half], total[half : half + 8]
    out[:times, :] = adjoint(unpacked(packed, kernel.shape[2]), kernel, plain_t[...], weighted[...], 2)
    scalars = rows_of([square_sum(packed), squares[2:3, :] * (2.0 / lax.axis_size("sensor"))])
    out[times : times + 8, :] = jnp.concatenate([scalars] * (out.shape[1] // LANES), axis=1)
    out[times + 8 :, :] = spread(two[...])
    norms[...] = squares


def step_of(norms, scalars):
    return norms[0:1, :] / (scalars[0:1, :] + (norms[1:2, :] + scalars[1:2, :]) + TINY)


def both_jumps_body(model, gradient, one, two, grad_one, grad_two, passed, linked, model_jumps, grad_jumps):
    times, cells = model.shape
    half = times // 2
    above, below = beside(one[half : half + times, :], two[:times, :])
    from_other = jnp.where(is_odd(), grad_two[...], gathered(passed[times + 8 :, :], times))
    halos = ((above, below), beside(grad_one[half + 8 :, :], from_other))
    for field, (above, below), out in zip((model, gradient), halos, (model_jumps, grad_jumps)):
        for k, strips in enumerate(jumps(field[...], above, below, linked[...])):
            for r, values in enumerate(strips):
                out[k, :, r * COLS : (r + 1) * COLS] = values


def second_gradient_body(count, *refs):
    (norms, adjoint_in, gradient_in, model, model_jumps, grad_jumps, start_multiplier, threshold, one, two, linked_ref,
     kernel, plain, weighted_t, model_out, jumps_out, multiplier_out, gradient_out, sent, edge) = refs[count:]
    times, cells = model.shape
    half = times // 2
    total = summed(refs[:count])
    step = step_of(norms, total[times:, :LANES])
    linked = linked_ref[...]
    field, gradient = model[...], gradient_in[...]
    rows = cells // COLS
    above, below = beside(one[half:, :], two[...])

    def advance(model_jumps, old_multiplier, limit):
        shifted = model_jumps + old_multiplier
        auxiliary = shrunk(shifted, limit)
        multiplier = shifted - auxiliary
        return multiplier, model_jumps - auxiliary + multiplier

    penalties, new_jumps = [], []
    for k in range(4):
        penalties.append([])
        new_jumps.append([])
        for r in range(rows):
            at = slice(r * COLS, (r + 1) * COLS)
            new = model_jumps[k, :, at] - step * grad_jumps[k, :, at]
            multiplier, penalty = advance(new, strip(start_multiplier[k], r), strip(threshold[0:1], r))
            jumps_out[k, :, at] = new
            multiplier_out[k, :, at] = multiplier
            penalties[k].append(penalty)
            new_jumps[k].append(new)
    _, beside_above = advance(-new_jumps[2][0], above[times : 2 * times], above[2 * times : 2 * times + 1])
    _, beside_below = advance(-new_jumps[3][-1], below[times : 2 * times], below[2 * times : 2 * times + 1])
    back = gathered_jumps(penalties, beside_above, beside_below, linked)
    wide_step = jnp.concatenate([step] * rows, axis=1)
    model_out[...] = field - wide_step * gradient
    new_gradient = adjoint_in[...] - wide_step * total[:times] + back
    gradient_out[...] = new_gradient
    response_of(new_gradient, kernel, plain, weighted_t, linked, sent, edge)


def response_body(count, *refs):
    two, out, passing, norms = refs[count:]
    total = summed(refs[:count])
    packed, squares = total[:-8], total[-8:]
    scalars = rows_of([square_sum(packed), squares[2:3, :] * (2.0 / lax.axis_size("sensor"))])
    out[...] = scalars
    passing[:8, :] = scalars
    passing[8:, :] = two[...]
    norms[...] = squares


def before_finish_body(gradient, model_jumps, multiplier, linked, sum_out, jumps_out):
    field = gradient[...]
    sum_out[...] = model_jumps[...] + multiplier[...]
    nothing = jnp.zeros((field.shape[0], COLS), jnp.float32)
    for k, strips in enumerate(jumps(field, nothing, nothing, linked[...])):
        for r, values in enumerate(strips):
            jumps_out[k, :, r * COLS : (r + 1) * COLS] = values


def finish_body(count, *refs):
    (norms, gradient_in, model, sums, inner_jumps, threshold, grad_one, grad_two, passed, linked,
     estimate_out, auxiliary_out, multiplier_out, estimate_here, auxiliary_here, multiplier_here, sems) = refs[count:]
    step = step_of(norms, tree_sum([part[:8, :] for part in refs[:count]]))
    half = gradient_in.shape[0] // 2
    gradient = gradient_in[...]
    rows = gradient.shape[1] // COLS
    copies = []

    def store(source, target):
        copy = pltpu.make_async_copy(source, target, sems.at[len(copies)])
        copy.start()
        copies.append(copy)

    above, below = beside(grad_one[half + 8 :, :], jnp.where(is_odd(), grad_two[...], passed[8:, :]))
    outer = {
        (2, 0): linked[2:3, :COLS] * (above - strip(gradient, 0)),
        (3, rows - 1): linked[3:4, (rows - 1) * COLS :] * (below - strip(gradient, rows - 1)),
    }
    for k in range(4):
        for r in range(rows):
            at = slice(r * COLS, (r + 1) * COLS)
            shifted = sums[k, :, at] - step * outer.get((k, r), inner_jumps[k, :, at])
            auxiliary = shrunk(shifted, threshold[0:1, at])
            auxiliary_here[k, :, at] = auxiliary
            multiplier_here[k, :, at] = shifted - auxiliary
        store(auxiliary_here.at[k], auxiliary_out.at[k])
        store(multiplier_here.at[k], multiplier_out.at[k])
    estimate_here[...] = model[...] - jnp.concatenate([step] * rows, axis=1) * gradient
    store(estimate_here, estimate_out)
    for copy in copies:
        copy.wait()


def stages_of(count, *radices):
    stages = []
    for radix in radices:
        if count > 1 and count % radix == 0:
            stages.append(radix)
            count //= radix
    while count > 1:
        stages.append(2)
        count //= 2
    return stages


def summing(parts, axis, stride, stages):
    count = lax.axis_size(axis)
    for radix in stages:
        total = tree_sum(parts)
        parts = [total] + [
            lax.ppermute(total, axis, [(i, i ^ (k * stride)) for i in range(count)]) for k in range(1, radix)
        ]
        stride *= radix
    return parts


def sensor_hop(array):
    return lax.ppermute(array, "sensor", [(i, i ^ 1) for i in range(lax.axis_size("sensor"))])


def sensor_parts(array, rows):
    passed = sensor_hop(array)
    total = array[:rows] + passed[:rows]
    return summing([total], "sensor", 2, stages_of(lax.axis_size("sensor") // 2, 2)), passed


def last_sensor_parts(scalars, passing):
    count = lax.axis_size("sensor")
    near, far, across = (
        lax.ppermute(array, "sensor", [(i, i ^ k) for i in range(count)])
        for k, array in ((1, scalars), (2, scalars), (3, passing))
    )
    parts = [scalars, near, far, across]
    if count > 4:
        rows = scalars.shape[0]
        parts = summing([tree_sum([part[:rows] for part in parts])], "sensor", 4, stages_of(count // 4, 4))
    return parts, across


def cell_parts(merged):
    return summing([merged], "cell", 2, stages_of(lax.axis_size("cell") // 2, 4, 4))


def from_partner(array):
    return lax.ppermute(array, "cell", [(i, i ^ 1) for i in range(lax.axis_size("cell"))])


def from_other(array):
    sensors = lax.axis_size("sensor")
    pairs = [
        (i * sensors + s, (i + 1 if i % 2 else i - 1) * sensors + s)
        for i in range(1, lax.axis_size("cell") - 1)
        for s in range(1, sensors, 2)
    ]
    return lax.ppermute(array, ("cell", "sensor"), pairs)


def per_device(kernel, observed, start_model, start_multiplier, neighbours, tile_of_cell, tile_weight):
    times, cells = start_model.shape
    freqs, sensors = kernel.shape[1:3]
    plain, weighted = tables(times, freqs)
    plain, plain_t, weighted, weighted_t = (
        jnp.asarray(table_terms(t)) for t in (plain, plain.T, weighted, weighted.T)
    )
    half = times // 2
    field, row, wide = (times, cells), (times, COLS), (4, times, cells)

    loads = [
        kernel, start_model, start_multiplier, plain, weighted_t, plain_t, weighted,
        neighbours, tile_of_cell[None, :], tile_weight[None, :],
    ]
    sent, edge, threshold, linked, kernel, start_model, start_multiplier, plain, weighted_t, plain_t, weighted = call(
        first_forward_body,
        [(half + 2 * times + 8, LANES), (2 * times + 8, LANES), (8, cells), (8, cells)]
        + [jax.ShapeDtypeStruct(a.shape, a.dtype) for a in loads[:7]],
        *[pltpu.with_memory_space_constraint(a, HBM) for a in loads],
        scratch=[VMEM(a.shape, a.dtype) for a in loads[7:]] + [pltpu.SemaphoreType.DMA((9 + -(-freqs // CHUNK),))],
        inputs=HBM,
    )
    one = from_partner(sent)
    two = from_other(edge)
    parts = cell_parts(sent[:half] + one[:half])
    across = call(
        turn_body, jax.ShapeDtypeStruct((2, plain.shape[0] // 16, cells, GROUP * sensors), kernel.dtype), kernel, one
    )
    message, side, shared = (half + 8 + times, LANES), (times, LANES), (2 * times + 8, LANES)
    back = call(
        functools.partial(first_adjoint_body, len(parts)), (2 * times + 8, cells),
        *parts, observed, two, kernel, plain_t, weighted, across,
    )
    parts, passed = sensor_parts(back, times)
    back, two = call(start_back_body, [field, shared], start_multiplier, one, two, passed, linked)
    adjoint_one, gradient, sent, edge = call(
        functools.partial(first_gradient_body, len(parts)), [field, field, message, side],
        *parts, back, linked, across, plain, weighted_t,
    )
    grad_one, grad_two = from_partner(sent), from_other(edge)
    parts = cell_parts(call(merge_body, (half + 8, LANES), sent, grad_one, edge, grad_two, linked))
    back, norms = call(
        functools.partial(second_adjoint_body, len(parts)), [(times + 8 + half, cells), (8, LANES)],
        *parts, grad_two, kernel, plain_t, weighted,
    )
    parts, passed = sensor_parts(back, times + 8)
    model_jumps, grad_jumps = call(
        both_jumps_body, [wide, wide], start_model, gradient, one, two, grad_one, grad_two, passed, linked
    )
    model, model_jumps, multiplier, gradient, sent, edge = call(
        functools.partial(second_gradient_body, len(parts)), [field, wide, wide, field, message, side],
        *parts, norms, adjoint_one, gradient, start_model, model_jumps, grad_jumps, start_multiplier, threshold,
        one, two, linked, across, plain, weighted_t,
    )
    grad_one, grad_two = from_partner(sent), from_other(edge)
    parts = cell_parts(call(merge_body, (half + 8, LANES), sent, grad_one, edge, grad_two, linked))
    sums, inner_jumps = call(before_finish_body, [wide, wide], gradient, model_jumps, multiplier, linked)
    scalars, passing, norms = call(
        functools.partial(response_body, len(parts)), [(8, LANES), (8 + times, LANES), (8, LANES)], *parts, grad_two
    )
    parts, passed = last_sensor_parts(scalars, passing)
    return tuple(
        call(
            functools.partial(finish_body, len(parts)), [field, wide, wide],
            *parts, norms, gradient, model, sums, inner_jumps, threshold, grad_one, grad_two, passed, linked,
            scratch=[VMEM(shape, jnp.float32) for shape in (field, wide, wide)] + [pltpu.SemaphoreType.DMA((9,))],
            outputs=HBM,
        )
    )


def solution(mesh):
    in_specs = (
        P(None, None, "sensor", "cell"),
        P(None, "sensor"),
        P(None, "cell"),
        P(None, None, "cell"),
        P(None, "cell"),
        P("cell"),
        P(),
    )
    out_specs = (P(None, "cell"), P(None, None, "cell"), P(None, None, "cell"))
    return jax.shard_map(
        per_device, mesh=mesh, in_specs=in_specs, out_specs=out_specs, check_vma=False
    )
```

```python
import functools

import jax
import jax.numpy as jnp
import numpy as np
from jax import lax
from jax.experimental import pallas as pl
from jax.experimental.pallas import tpu as pltpu
from jax.sharding import PartitionSpec as P

COLS = 128
LANES = 128
GROUP = 8
CHUNK = 24
SHRINK_SCALE = 0.4
TINY = 1e-06
VMEM = pltpu.VMEM
HBM = pltpu.HBM


def tables(times, freqs):
    padded = 2 * times
    groups = -(-freqs // GROUP)
    plain = np.zeros((16 * groups, times), np.float64)
    weighted = np.zeros((16 * groups, times), np.float64)
    for f in range(freqs):
        phase = 2.0 * np.pi * ((f * np.arange(times)) % padded) / padded
        weight = (1.0 if f in (0, freqs - 1) else 2.0) / padded
        row = 16 * (f // GROUP) + f % GROUP
        plain[row], plain[row + GROUP] = np.cos(phase), -np.sin(phase)
        weighted[row], weighted[row + GROUP] = weight * np.cos(phase), -weight * np.sin(phase)
    return plain.astype(np.float32), weighted.astype(np.float32)


def table_terms(table):
    high = table.astype(jnp.bfloat16)
    low = (table - high.astype(np.float32)).astype(jnp.bfloat16)
    return np.concatenate([high, high, low], axis=1)


def table_dot(terms, values):
    high = values.astype(jnp.bfloat16)
    low = (values - high.astype(jnp.float32)).astype(jnp.bfloat16)
    return dot_nn(terms, jnp.concatenate([high, low, high], axis=0))


def turned(rows):
    rows = rows.astype(jnp.float32)
    return jnp.concatenate([-rows[GROUP:], rows[:GROUP]], axis=0).astype(jnp.bfloat16)


def dot_nt(left, right):
    return lax.dot_general(left, right, (((1,), (1,)), ((), ())), preferred_element_type=jnp.float32)


def dot_nn(left, right):
    return jnp.dot(left, right, preferred_element_type=jnp.float32)


def slab(kernel_ref, part, group):
    freqs, sensors, cells = kernel_ref.shape[1:]
    count = min(GROUP, freqs - group * GROUP)
    block = kernel_ref[part, group * GROUP : group * GROUP + count]
    return block.reshape(count * sensors, cells)


def own_block(width, sensors):
    row = lax.broadcasted_iota(jnp.int32, (16, width), 0) % GROUP
    lane = lax.broadcasted_iota(jnp.int32, (16, width), 1) // sensors
    return row == lane


def fold(wide):
    total = functools.reduce(
        lambda a, b: a + b, [wide[:, i : i + LANES] for i in range(0, wide.shape[1], LANES)]
    )
    return total + pltpu.roll(total, LANES // 2, 1)


def forward(field, turned_ref, plain, weighted_t, sensors):
    freqs = field.shape[0] + 1
    spectra = table_dot(plain, field)
    rows = []
    for group in range(spectra.shape[0] // 16):
        part = spectra[16 * group : 16 * group + 16]
        width = min(GROUP, freqs - group * GROUP) * sensors
        out = dot_nn(part.astype(jnp.bfloat16), turned_ref[0, group, :, :width])
        out += dot_nn(turned(part), turned_ref[1, group, :, :width])
        rows.append(fold_own(out, sensors))
    return packed_series(jnp.concatenate(rows, axis=0), weighted_t, sensors)


def fold_own(out, sensors):
    width = out.shape[1]
    out = jnp.where(own_block(width, sensors), out, 0.0)
    if width < LANES:
        out = jnp.concatenate([out, jnp.zeros((16, LANES - width), jnp.float32)], axis=1)
    return fold(out)


def forward_rows(spectra, kernel_ref, arrived=None):
    sensors = kernel_ref.shape[2]
    rows = []
    for group in range(spectra.shape[0] // 16):
        part = spectra[16 * group : 16 * group + 16]
        if arrived is not None:
            arrived(group)
        re_slab, im_slab = slab(kernel_ref, 0, group), slab(kernel_ref, 1, group)
        out = dot_nt(part.astype(jnp.bfloat16), re_slab) + dot_nt(turned(part), im_slab)
        rows.append(fold_own(out, sensors))
    return jnp.concatenate(rows, axis=0)


def packed_series(rows, weighted_t, sensors):
    times = weighted_t.shape[0]
    series = table_dot(weighted_t, rows)
    left = lax.broadcasted_iota(jnp.int32, (times // 2, LANES), 1) < sensors
    return jnp.where(left, series[: times // 2], series[times // 2 :])


def unpacked(packed, sensors):
    other = pltpu.roll(packed, sensors, 1)
    left = lax.broadcasted_iota(jnp.int32, packed.shape, 1) < sensors
    return jnp.concatenate([jnp.where(left, packed, other), jnp.where(left, other, packed)], axis=0)


def adjoint(residual, kernel_ref, plain_t, weighted, halves):
    freqs, sensors, cells = kernel_ref.shape[1:]
    spectra = table_dot(weighted, residual)
    rows = []
    for group in range(weighted.shape[0] // 16):
        part = spectra[16 * group : 16 * group + 16]
        count = min(GROUP, freqs - group * GROUP)
        width = count * sensors
        re_slab, im_slab = slab(kernel_ref, 0, group), slab(kernel_ref, 1, group)
        wide = jnp.concatenate([part] * (-(-width // LANES)), axis=1)[:, :width]
        wide = jnp.where(own_block(width, sensors), wide, 0.0)
        terms = []
        for _ in range(halves):
            terms.append(wide.astype(jnp.bfloat16))
            wide = wide - terms[-1].astype(jnp.float32)
        left = jnp.concatenate(terms, axis=0)
        swapped = jnp.concatenate([turned(term) for term in terms], axis=0)
        out = dot_nn(left, re_slab) - dot_nn(swapped, im_slab)
        rows.append(tree_sum([out[16 * i : 16 * i + 16] for i in range(halves)]))
    return table_dot(plain_t, jnp.concatenate(rows, axis=0))


def strip(array, row):
    return array[..., row * COLS : (row + 1) * COLS]


def jumps(field, above, below, linked):
    count = field.shape[1] // COLS
    out = []
    for direction in range(4):
        strips = []
        for row in range(count):
            here = strip(field, row)
            if direction == 0:
                there = pltpu.roll(here, COLS - 1, 1)
            elif direction == 1:
                there = pltpu.roll(here, 1, 1)
            elif direction == 2:
                there = above if row == 0 else strip(field, row - 1)
            else:
                there = below if row == count - 1 else strip(field, row + 1)
            strips.append(strip(linked[direction : direction + 1], row) * (there - here))
        out.append(strips)
    return out


def gathered_jumps(values, above, below, linked):
    count = len(values[0])
    out = []
    for row in range(count):
        arriving = (
            pltpu.roll(values[1][row], COLS - 1, 1),
            pltpu.roll(values[0][row], 1, 1),
            above if row == 0 else values[3][row - 1],
            below if row == count - 1 else values[2][row + 1],
        )
        total = None
        for direction in range(4):
            term = strip(linked[direction : direction + 1], row) * (arriving[direction] - values[direction][row])
            total = term if total is None else total + term
        out.append(total)
    return jnp.concatenate(out, axis=1)


def shrunk(shifted, threshold):
    return shifted - jnp.clip(shifted, -threshold, threshold)


def tree_sum(parts):
    parts = list(parts)
    while len(parts) > 1:
        parts = [parts[i] + parts[i + 1] if i + 1 < len(parts) else parts[i] for i in range(0, len(parts), 2)]
    return parts[0]


def total_of(array):
    return jnp.sum(array, axis=(0, 1), keepdims=True)


def square_sum(array):
    return total_of(array * array)


def block_of(scalar, rows=8):
    return jnp.full((rows, LANES), scalar, jnp.float32)


def call(body, out_shapes, *operands, scratch=(), inputs=VMEM, outputs=VMEM):
    single = not isinstance(out_shapes, list)
    shapes = [out_shapes] if single else list(out_shapes)
    shapes = [s if isinstance(s, jax.ShapeDtypeStruct) else jax.ShapeDtypeStruct(s, jnp.float32) for s in shapes]
    out = pl.pallas_call(
        body,
        out_shape=shapes,
        in_specs=[pl.BlockSpec(memory_space=inputs)] * len(operands),
        out_specs=[pl.BlockSpec(memory_space=outputs)] * len(shapes),
        scratch_shapes=list(scratch),
        compiler_params=pltpu.CompilerParams(vmem_limit_bytes=24 * 2**20),
    )(*operands)
    return out[0] if single else out


def summed(parts):
    return tree_sum([part[...] for part in parts])


def is_even():
    return lax.rem(lax.axis_index("cell"), 2) == 0


def edges(head, tail):
    even = is_even()
    return jnp.where(even, tail, head), jnp.where(even, head, tail)


def beside(partner, other):
    even = is_even()
    return jnp.where(even, other, partner), jnp.where(even, partner, other)


def is_odd():
    return lax.rem(lax.axis_index("sensor"), 2) == 1


def spread(rows):
    upper = -(-rows.shape[0] // 16) * 8
    lower = rows[upper:]
    if lower.shape[0] < upper:
        lower = jnp.concatenate([lower, jnp.zeros((upper - lower.shape[0], LANES), rows.dtype)])
    return jnp.concatenate([rows[:upper], lower], axis=1)


def gathered(wide, count):
    return jnp.concatenate([wide[:, :LANES], wide[: count - wide.shape[0], LANES:]])


def rows_of(values):
    row = lax.broadcasted_iota(jnp.int32, (8, LANES), 0)
    out = jnp.zeros((8, LANES), jnp.float32)
    for i, value in enumerate(values):
        if value is not None:
            out = jnp.where(row == i, jnp.broadcast_to(value, (8, LANES)), out)
    return out


def first_forward_body(*refs):
    loaded, (sent, edge, threshold, linked), kept, sems = refs[:10], refs[10:14], refs[14:24], refs[24]
    kernel, kernel_here = loaded[0], kept[0]
    field, multiplier, plain, weighted_t = kept[1:5]
    neighbours, tile_of_cell, tile_weight = kept[7:]
    freqs = kernel.shape[1]
    times, cells = field.shape
    half = times // 2
    copies = []

    def load(source, target):
        copy = pltpu.make_async_copy(source, target, sems.at[len(copies)])
        copy.start()
        copies.append(copy)
        return copy

    early = [load(loaded[i], kept[i]) for i in (1, 3)]
    large = []
    for start in range(0, freqs, CHUNK):
        at = (slice(None), pl.ds(start, min(CHUNK, freqs - start)))
        large.append(load(kernel.at[at], kernel_here.at[at]))
        if start == 0:
            small = [load(loaded[i], kept[i]) for i in (7, 8, 9, 2, 4)]
    late = [load(loaded[i], kept[i]) for i in (5, 6)]
    for copy in early:
        copy.wait()
    spectra = table_dot(plain[...], field[...])
    for copy in small:
        copy.wait()

    cell = lax.broadcasted_iota(jnp.int32, (4, cells), 1) + lax.axis_index("cell") * cells
    linked[0:4, :] = jnp.where(neighbours[...] != cell, 1.0, 0.0)
    linked[4:8, :] = jnp.zeros((4, cells), jnp.float32)
    tile = lax.broadcasted_iota(jnp.int32, (tile_weight.shape[1], cells), 0)
    chosen = jnp.where(tile == tile_of_cell[...], 1.0, 0.0)
    weights = jnp.dot(
        jnp.broadcast_to(tile_weight[...], (8, tile_weight.shape[1])), chosen,
        precision=lax.Precision.HIGHEST, preferred_element_type=jnp.float32,
    )
    limit = SHRINK_SCALE * weights
    threshold[...] = limit
    bottom = cells // COLS - 1
    pairs = (
        (strip(field, 0), strip(field, bottom)),
        (strip(multiplier[2], 0), strip(multiplier[3], bottom)),
        (strip(limit, 0), strip(limit, bottom)),
    )
    for (head, tail), start in zip(pairs, (0, times, 2 * times)):
        one, two = edges(head, tail)
        sent[half + start : half + start + head.shape[0], :] = one
        edge[start : start + head.shape[0], :] = two

    def arrived(group):
        if group * GROUP % CHUNK == 0:
            large[group * GROUP // CHUNK].wait()

    rows = forward_rows(spectra, kernel_here, arrived)
    sent[:half, :] = packed_series(rows, weighted_t[...], kernel.shape[2])
    for copy in late:
        copy.wait()


def turn_body(kernel, came, out):
    freqs, sensors = kernel.shape[1:3]
    for part in range(2):
        for group in range(out.shape[1]):
            width = min(GROUP, freqs - group * GROUP) * sensors
            out[part, group, :, :width] = slab(kernel, part, group).T


def first_adjoint_body(count, *refs):
    observed, two, kernel, plain_t, weighted, _, out = refs[count:]
    times = observed.shape[0]
    predicted = unpacked(summed(refs[:count]), kernel.shape[2])
    residual = predicted - jnp.concatenate([observed[...], observed[...]], axis=1)
    out[:times, :] = adjoint(residual, kernel, plain_t[...], weighted[...], 1)
    out[times:, :] = spread(two[...])


def response_of(field, turned_ref, plain, weighted_t, linked, sent, edge):
    half = field.shape[0] // 2
    rows = field.shape[1] // COLS
    one, two = edges(strip(field, 0), strip(field, rows - 1))
    squares = []
    for row in range(rows):
        here = strip(field, row)
        east = strip(linked[0:1], row) * (pltpu.roll(here, COLS - 1, 1) - here)
        squares.append(east * east)
        if row > 0:
            north = strip(linked[2:3], row) * (strip(field, row - 1) - here)
            squares.append(north * north)
    sensors = turned_ref.shape[3] // GROUP
    sent[:half, :] = forward(field, turned_ref, plain[...], weighted_t[...], sensors)
    sent[half : half + 8, :] = rows_of([square_sum(field), 2.0 * total_of(tree_sum(squares))])
    sent[half + 8 :, :] = one
    edge[...] = two


def merge_body(sent, came, edge, other, linked, out):
    cells = linked.shape[1]
    top = out.shape[0]
    to_partner, to_other = edges(linked[2:3, :COLS], linked[3:4, cells - COLS :])
    across = to_partner * (came[top:, :] - sent[top:, :])
    beyond = to_other * (other[...] - edge[...])
    out[: top - 8, :] = sent[: top - 8, :] + came[: top - 8, :]
    boundary = 2.0 * square_sum(jnp.where(is_odd(), beyond, across))
    out[top - 8 :, :] = sent[top - 8 : top, :] + came[top - 8 : top, :] + rows_of([None, None, boundary])


def start_back_body(start_multiplier, one, two, passed, linked, back, two_out):
    times, cells = back.shape
    half = times // 2
    two = jnp.where(is_odd(), two[...], gathered(passed[times:, :], two.shape[0]))
    two_out[...] = two
    values = [[strip(start_multiplier[k], r) for r in range(cells // COLS)] for k in range(4)]
    above, below = beside(one[half + times : half + 2 * times, :], two[times : 2 * times, :])
    back[...] = gathered_jumps(values, above, below, linked[...])


def first_gradient_body(count, *refs):
    back, linked, kernel, plain, weighted_t, adjoint_out, gradient, sent, edge = refs[count:]
    total = summed(refs[:count])
    field = total + back[...]
    adjoint_out[...] = total
    gradient[...] = field
    response_of(field, kernel, plain, weighted_t, linked[...], sent, edge)


def second_adjoint_body(count, *refs):
    two, kernel, plain_t, weighted, out, norms = refs[count:]
    times = plain_t.shape[0]
    half = times // 2
    total = summed(refs[:count])
    packed, squares = total[:half], total[half : half + 8]
    out[:times, :] = adjoint(unpacked(packed, kernel.shape[2]), kernel, plain_t[...], weighted[...], 2)
    scalars = rows_of([square_sum(packed), squares[2:3, :] * (2.0 / lax.axis_size("sensor"))])
    out[times : times + 8, :] = jnp.concatenate([scalars] * (out.shape[1] // LANES), axis=1)
    out[times + 8 :, :] = spread(two[...])
    norms[...] = squares


def step_of(norms, scalars):
    return norms[0:1, :] / (scalars[0:1, :] + (norms[1:2, :] + scalars[1:2, :]) + TINY)


def both_jumps_body(model, gradient, one, two, grad_one, grad_two, passed, linked, model_jumps, grad_jumps):
    times, cells = model.shape
    half = times // 2
    above, below = beside(one[half : half + times, :], two[:times, :])
    from_other = jnp.where(is_odd(), grad_two[...], gathered(passed[times + 8 :, :], times))
    halos = ((above, below), beside(grad_one[half + 8 :, :], from_other))
    for field, (above, below), out in zip((model, gradient), halos, (model_jumps, grad_jumps)):
        for k, strips in enumerate(jumps(field[...], above, below, linked[...])):
            for r, values in enumerate(strips):
                out[k, :, r * COLS : (r + 1) * COLS] = values


def second_gradient_body(count, *refs):
    (norms, adjoint_in, gradient_in, model, model_jumps, grad_jumps, start_multiplier, threshold, one, two, linked_ref,
     kernel, plain, weighted_t, model_out, jumps_out, multiplier_out, gradient_out, sent, edge) = refs[count:]
    times, cells = model.shape
    half = times // 2
    total = summed(refs[:count])
    step = step_of(norms, total[times:, :LANES])
    linked = linked_ref[...]
    field, gradient = model[...], gradient_in[...]
    rows = cells // COLS
    above, below = beside(one[half:, :], two[...])

    def advance(model_jumps, old_multiplier, limit):
        shifted = model_jumps + old_multiplier
        auxiliary = shrunk(shifted, limit)
        multiplier = shifted - auxiliary
        return multiplier, model_jumps - auxiliary + multiplier

    penalties, new_jumps = [], []
    for k in range(4):
        penalties.append([])
        new_jumps.append([])
        for r in range(rows):
            at = slice(r * COLS, (r + 1) * COLS)
            new = model_jumps[k, :, at] - step * grad_jumps[k, :, at]
            multiplier, penalty = advance(new, strip(start_multiplier[k], r), strip(threshold[0:1], r))
            jumps_out[k, :, at] = new
            multiplier_out[k, :, at] = multiplier
            penalties[k].append(penalty)
            new_jumps[k].append(new)
    _, beside_above = advance(-new_jumps[2][0], above[times : 2 * times], above[2 * times : 2 * times + 1])
    _, beside_below = advance(-new_jumps[3][-1], below[times : 2 * times], below[2 * times : 2 * times + 1])
    back = gathered_jumps(penalties, beside_above, beside_below, linked)
    wide_step = jnp.concatenate([step] * rows, axis=1)
    model_out[...] = field - wide_step * gradient
    new_gradient = adjoint_in[...] - wide_step * total[:times] + back
    gradient_out[...] = new_gradient
    response_of(new_gradient, kernel, plain, weighted_t, linked, sent, edge)


def response_body(count, *refs):
    two, out, passing, norms = refs[count:]
    total = summed(refs[:count])
    packed, squares = total[:-8], total[-8:]
    scalars = rows_of([square_sum(packed), squares[2:3, :] * (2.0 / lax.axis_size("sensor"))])
    out[...] = scalars
    passing[:8, :] = scalars
    passing[8:, :] = two[...]
    norms[...] = squares


def before_finish_body(gradient, model_jumps, multiplier, linked, sum_out, jumps_out):
    field = gradient[...]
    sum_out[...] = model_jumps[...] + multiplier[...]
    nothing = jnp.zeros((field.shape[0], COLS), jnp.float32)
    for k, strips in enumerate(jumps(field, nothing, nothing, linked[...])):
        for r, values in enumerate(strips):
            jumps_out[k, :, r * COLS : (r + 1) * COLS] = values


def finish_body(count, *refs):
    (norms, gradient_in, model, sums, inner_jumps, threshold, grad_one, grad_two, passed, linked,
     estimate_out, auxiliary_out, multiplier_out, estimate_here, auxiliary_here, multiplier_here, sems) = refs[count:]
    step = step_of(norms, tree_sum([part[:8, :] for part in refs[:count]]))
    half = gradient_in.shape[0] // 2
    gradient = gradient_in[...]
    rows = gradient.shape[1] // COLS
    copies = []

    def store(source, target):
        copy = pltpu.make_async_copy(source, target, sems.at[len(copies)])
        copy.start()
        copies.append(copy)

    above, below = beside(grad_one[half + 8 :, :], jnp.where(is_odd(), grad_two[...], passed[8:, :]))
    outer = {
        (2, 0): linked[2:3, :COLS] * (above - strip(gradient, 0)),
        (3, rows - 1): linked[3:4, (rows - 1) * COLS :] * (below - strip(gradient, rows - 1)),
    }
    for k in range(4):
        for r in range(rows):
            at = slice(r * COLS, (r + 1) * COLS)
            shifted = sums[k, :, at] - step * outer.get((k, r), inner_jumps[k, :, at])
            auxiliary = shrunk(shifted, threshold[0:1, at])
            auxiliary_here[k, :, at] = auxiliary
            multiplier_here[k, :, at] = shifted - auxiliary
        store(auxiliary_here.at[k], auxiliary_out.at[k])
        store(multiplier_here.at[k], multiplier_out.at[k])
    estimate_here[...] = model[...] - jnp.concatenate([step] * rows, axis=1) * gradient
    store(estimate_here, estimate_out)
    for copy in copies:
        copy.wait()


def stages_of(count, *radices):
    stages = []
    for radix in radices:
        if count > 1 and count % radix == 0:
            stages.append(radix)
            count //= radix
    while count > 1:
        stages.append(2)
        count //= 2
    return stages


def summing(parts, axis, stride, stages):
    count = lax.axis_size(axis)
    for radix in stages:
        total = tree_sum(parts)
        parts = [total] + [
            lax.ppermute(total, axis, [(i, i ^ (k * stride)) for i in range(count)]) for k in range(1, radix)
        ]
        stride *= radix
    return parts


def sensor_hop(array):
    return lax.ppermute(array, "sensor", [(i, i ^ 1) for i in range(lax.axis_size("sensor"))])


def sensor_parts(array, rows):
    count = lax.axis_size("sensor")
    own, passed = array[:rows], sensor_hop(array)
    far = [lax.ppermute(own, "sensor", [(i, i ^ k) for i in range(count)]) for k in (2, 3)]
    parts = [own, passed[:rows]] + far
    return summing(parts, "sensor", 4, stages_of(count // 4, 4)), passed


def last_sensor_parts(scalars, passing):
    count = lax.axis_size("sensor")
    near, far, across = (
        lax.ppermute(array, "sensor", [(i, i ^ k) for i in range(count)])
        for k, array in ((1, scalars), (2, scalars), (3, passing))
    )
    parts = [scalars, near, far, across]
    if count > 4:
        rows = scalars.shape[0]
        parts = summing([tree_sum([part[:rows] for part in parts])], "sensor", 4, stages_of(count // 4, 4))
    return parts, across


def cell_parts(merged):
    return summing([merged], "cell", 2, stages_of(lax.axis_size("cell") // 2, 4, 4))


def from_partner(array):
    return lax.ppermute(array, "cell", [(i, i ^ 1) for i in range(lax.axis_size("cell"))])


def from_other(array):
    sensors = lax.axis_size("sensor")
    pairs = [
        (i * sensors + s, (i + 1 if i % 2 else i - 1) * sensors + s)
        for i in range(1, lax.axis_size("cell") - 1)
        for s in range(1, sensors, 2)
    ]
    return lax.ppermute(array, ("cell", "sensor"), pairs)


def per_device(kernel, observed, start_model, start_multiplier, neighbours, tile_of_cell, tile_weight):
    times, cells = start_model.shape
    freqs, sensors = kernel.shape[1:3]
    plain, weighted = tables(times, freqs)
    plain, plain_t, weighted, weighted_t = (
        jnp.asarray(table_terms(t)) for t in (plain, plain.T, weighted, weighted.T)
    )
    half = times // 2
    field, row, wide = (times, cells), (times, COLS), (4, times, cells)

    loads = [
        kernel, start_model, start_multiplier, plain, weighted_t, plain_t, weighted,
        neighbours, tile_of_cell[None, :], tile_weight[None, :],
    ]
    sent, edge, threshold, linked, kernel, start_model, start_multiplier, plain, weighted_t, plain_t, weighted = call(
        first_forward_body,
        [(half + 2 * times + 8, LANES), (2 * times + 8, LANES), (8, cells), (8, cells)]
        + [jax.ShapeDtypeStruct(a.shape, a.dtype) for a in loads[:7]],
        *[pltpu.with_memory_space_constraint(a, HBM) for a in loads],
        scratch=[VMEM(a.shape, a.dtype) for a in loads[7:]] + [pltpu.SemaphoreType.DMA((9 + -(-freqs // CHUNK),))],
        inputs=HBM,
    )
    one = from_partner(sent)
    two = from_other(edge)
    parts = cell_parts(sent[:half] + one[:half])
    across = call(
        turn_body, jax.ShapeDtypeStruct((2, plain.shape[0] // 16, cells, GROUP * sensors), kernel.dtype), kernel, one
    )
    message, side, shared = (half + 8 + times, LANES), (times, LANES), (2 * times + 8, LANES)
    back = call(
        functools.partial(first_adjoint_body, len(parts)), (2 * times + 8, cells),
        *parts, observed, two, kernel, plain_t, weighted, across,
    )
    parts, passed = sensor_parts(back, times)
    back, two = call(start_back_body, [field, shared], start_multiplier, one, two, passed, linked)
    adjoint_one, gradient, sent, edge = call(
        functools.partial(first_gradient_body, len(parts)), [field, field, message, side],
        *parts, back, linked, across, plain, weighted_t,
    )
    grad_one, grad_two = from_partner(sent), from_other(edge)
    parts = cell_parts(call(merge_body, (half + 8, LANES), sent, grad_one, edge, grad_two, linked))
    back, norms = call(
        functools.partial(second_adjoint_body, len(parts)), [(times + 8 + half, cells), (8, LANES)],
        *parts, grad_two, kernel, plain_t, weighted,
    )
    parts, passed = sensor_parts(back, times + 8)
    model_jumps, grad_jumps = call(
        both_jumps_body, [wide, wide], start_model, gradient, one, two, grad_one, grad_two, passed, linked
    )
    model, model_jumps, multiplier, gradient, sent, edge = call(
        functools.partial(second_gradient_body, len(parts)), [field, wide, wide, field, message, side],
        *parts, norms, adjoint_one, gradient, start_model, model_jumps, grad_jumps, start_multiplier, threshold,
        one, two, linked, across, plain, weighted_t,
    )
    grad_one, grad_two = from_partner(sent), from_other(edge)
    parts = cell_parts(call(merge_body, (half + 8, LANES), sent, grad_one, edge, grad_two, linked))
    sums, inner_jumps = call(before_finish_body, [wide, wide], gradient, model_jumps, multiplier, linked)
    scalars, passing, norms = call(
        functools.partial(response_body, len(parts)), [(8, LANES), (8 + times, LANES), (8, LANES)], *parts, grad_two
    )
    parts, passed = last_sensor_parts(scalars, passing)
    return tuple(
        call(
            functools.partial(finish_body, len(parts)), [field, wide, wide],
            *parts, norms, gradient, model, sums, inner_jumps, threshold, grad_one, grad_two, passed, linked,
            scratch=[VMEM(shape, jnp.float32) for shape in (field, wide, wide)] + [pltpu.SemaphoreType.DMA((9,))],
            outputs=HBM,
        )
    )


def solution(mesh):
    in_specs = (
        P(None, None, "sensor", "cell"),
        P(None, "sensor"),
        P(None, "cell"),
        P(None, None, "cell"),
        P(None, "cell"),
        P("cell"),
        P(),
    )
    out_specs = (P(None, "cell"), P(None, None, "cell"), P(None, None, "cell"))
    return jax.shard_map(
        per_device, mesh=mesh, in_specs=in_specs, out_specs=out_specs, check_vma=False
    )
```

```python
import functools

import jax
import jax.numpy as jnp
import numpy as np
from jax import lax
from jax.experimental import pallas as pl
from jax.experimental.pallas import tpu as pltpu
from jax.sharding import PartitionSpec as P

COLS = 128
LANES = 128
GROUP = 8
CHUNK = 40
SHRINK_SCALE = 0.4
TINY = 1e-06
VMEM = pltpu.VMEM
HBM = pltpu.HBM


def tables(times, freqs):
    padded = 2 * times
    groups = -(-freqs // GROUP)
    plain = np.zeros((16 * groups, times), np.float64)
    weighted = np.zeros((16 * groups, times), np.float64)
    for f in range(freqs):
        phase = 2.0 * np.pi * ((f * np.arange(times)) % padded) / padded
        weight = (1.0 if f in (0, freqs - 1) else 2.0) / padded
        row = 16 * (f // GROUP) + f % GROUP
        plain[row], plain[row + GROUP] = np.cos(phase), -np.sin(phase)
        weighted[row], weighted[row + GROUP] = weight * np.cos(phase), -weight * np.sin(phase)
    return plain.astype(np.float32), weighted.astype(np.float32)


def table_terms(table):
    high = table.astype(jnp.bfloat16)
    low = (table - high.astype(np.float32)).astype(jnp.bfloat16)
    return np.concatenate([high, high, low], axis=1)


def table_dot(terms, values):
    high = values.astype(jnp.bfloat16)
    low = (values - high.astype(jnp.float32)).astype(jnp.bfloat16)
    return dot_nn(terms, jnp.concatenate([high, low, high], axis=0))


def turned(rows):
    rows = rows.astype(jnp.float32)
    return jnp.concatenate([-rows[GROUP:], rows[:GROUP]], axis=0).astype(jnp.bfloat16)


def dot_nt(left, right):
    return lax.dot_general(left, right, (((1,), (1,)), ((), ())), preferred_element_type=jnp.float32)


def dot_nn(left, right):
    return jnp.dot(left, right, preferred_element_type=jnp.float32)


def slab(kernel_ref, part, group):
    freqs, sensors, cells = kernel_ref.shape[1:]
    count = min(GROUP, freqs - group * GROUP)
    block = kernel_ref[part, group * GROUP : group * GROUP + count]
    return block.reshape(count * sensors, cells)


def own_block(width, sensors):
    row = lax.broadcasted_iota(jnp.int32, (16, width), 0) % GROUP
    lane = lax.broadcasted_iota(jnp.int32, (16, width), 1) // sensors
    return row == lane


def fold(wide):
    total = functools.reduce(
        lambda a, b: a + b, [wide[:, i : i + LANES] for i in range(0, wide.shape[1], LANES)]
    )
    return total + pltpu.roll(total, LANES // 2, 1)


def forward(field, turned_ref, plain, weighted_t, sensors):
    freqs = field.shape[0] + 1
    spectra = table_dot(plain, field)
    rows = []
    for group in range(spectra.shape[0] // 16):
        part = spectra[16 * group : 16 * group + 16]
        width = min(GROUP, freqs - group * GROUP) * sensors
        out = dot_nn(part.astype(jnp.bfloat16), turned_ref[0, group, :, :width])
        out += dot_nn(turned(part), turned_ref[1, group, :, :width])
        rows.append(fold_own(out, sensors))
    return packed_series(jnp.concatenate(rows, axis=0), weighted_t, sensors)


def fold_own(out, sensors):
    width = out.shape[1]
    out = jnp.where(own_block(width, sensors), out, 0.0)
    if width < LANES:
        out = jnp.concatenate([out, jnp.zeros((16, LANES - width), jnp.float32)], axis=1)
    return fold(out)


def forward_rows(spectra, kernel_ref, arrived=None):
    sensors = kernel_ref.shape[2]
    rows = []
    for group in range(spectra.shape[0] // 16):
        part = spectra[16 * group : 16 * group + 16]
        if arrived is not None:
            arrived(group)
        re_slab, im_slab = slab(kernel_ref, 0, group), slab(kernel_ref, 1, group)
        out = dot_nt(part.astype(jnp.bfloat16), re_slab) + dot_nt(turned(part), im_slab)
        rows.append(fold_own(out, sensors))
    return jnp.concatenate(rows, axis=0)


def packed_series(rows, weighted_t, sensors):
    times = weighted_t.shape[0]
    series = table_dot(weighted_t, rows)
    left = lax.broadcasted_iota(jnp.int32, (times // 2, LANES), 1) < sensors
    return jnp.where(left, series[: times // 2], series[times // 2 :])


def unpacked(packed, sensors):
    other = pltpu.roll(packed, sensors, 1)
    left = lax.broadcasted_iota(jnp.int32, packed.shape, 1) < sensors
    return jnp.concatenate([jnp.where(left, packed, other), jnp.where(left, other, packed)], axis=0)


def adjoint(residual, kernel_ref, plain_t, weighted, halves):
    freqs, sensors, cells = kernel_ref.shape[1:]
    spectra = table_dot(weighted, residual)
    rows = []
    for group in range(weighted.shape[0] // 16):
        part = spectra[16 * group : 16 * group + 16]
        count = min(GROUP, freqs - group * GROUP)
        width = count * sensors
        re_slab, im_slab = slab(kernel_ref, 0, group), slab(kernel_ref, 1, group)
        wide = jnp.concatenate([part] * (-(-width // LANES)), axis=1)[:, :width]
        wide = jnp.where(own_block(width, sensors), wide, 0.0)
        terms = []
        for _ in range(halves):
            terms.append(wide.astype(jnp.bfloat16))
            wide = wide - terms[-1].astype(jnp.float32)
        left = jnp.concatenate(terms, axis=0)
        swapped = jnp.concatenate([turned(term) for term in terms], axis=0)
        out = dot_nn(left, re_slab) - dot_nn(swapped, im_slab)
        rows.append(tree_sum([out[16 * i : 16 * i + 16] for i in range(halves)]))
    return table_dot(plain_t, jnp.concatenate(rows, axis=0))


def strip(array, row):
    return array[..., row * COLS : (row + 1) * COLS]


def jumps(field, above, below, linked):
    count = field.shape[1] // COLS
    out = []
    for direction in range(4):
        strips = []
        for row in range(count):
            here = strip(field, row)
            if direction == 0:
                there = pltpu.roll(here, COLS - 1, 1)
            elif direction == 1:
                there = pltpu.roll(here, 1, 1)
            elif direction == 2:
                there = above if row == 0 else strip(field, row - 1)
            else:
                there = below if row == count - 1 else strip(field, row + 1)
            strips.append(strip(linked[direction : direction + 1], row) * (there - here))
        out.append(strips)
    return out


def gathered_jumps(values, above, below, linked):
    count = len(values[0])
    out = []
    for row in range(count):
        arriving = (
            pltpu.roll(values[1][row], COLS - 1, 1),
            pltpu.roll(values[0][row], 1, 1),
            above if row == 0 else values[3][row - 1],
            below if row == count - 1 else values[2][row + 1],
        )
        total = None
        for direction in range(4):
            term = strip(linked[direction : direction + 1], row) * (arriving[direction] - values[direction][row])
            total = term if total is None else total + term
        out.append(total)
    return jnp.concatenate(out, axis=1)


def shrunk(shifted, threshold):
    return shifted - jnp.clip(shifted, -threshold, threshold)


def tree_sum(parts):
    parts = list(parts)
    while len(parts) > 1:
        parts = [parts[i] + parts[i + 1] if i + 1 < len(parts) else parts[i] for i in range(0, len(parts), 2)]
    return parts[0]


def total_of(array):
    return jnp.sum(array, axis=(0, 1), keepdims=True)


def square_sum(array):
    return total_of(array * array)


def block_of(scalar, rows=8):
    return jnp.full((rows, LANES), scalar, jnp.float32)


def call(body, out_shapes, *operands, scratch=(), inputs=VMEM, outputs=VMEM):
    single = not isinstance(out_shapes, list)
    shapes = [out_shapes] if single else list(out_shapes)
    shapes = [s if isinstance(s, jax.ShapeDtypeStruct) else jax.ShapeDtypeStruct(s, jnp.float32) for s in shapes]
    out = pl.pallas_call(
        body,
        out_shape=shapes,
        in_specs=[pl.BlockSpec(memory_space=inputs)] * len(operands),
        out_specs=[pl.BlockSpec(memory_space=outputs)] * len(shapes),
        scratch_shapes=list(scratch),
        compiler_params=pltpu.CompilerParams(vmem_limit_bytes=24 * 2**20),
    )(*operands)
    return out[0] if single else out


def summed(parts):
    return tree_sum([part[...] for part in parts])


def is_even():
    return lax.rem(lax.axis_index("cell"), 2) == 0


def edges(head, tail):
    even = is_even()
    return jnp.where(even, tail, head), jnp.where(even, head, tail)


def beside(partner, other):
    even = is_even()
    return jnp.where(even, other, partner), jnp.where(even, partner, other)


def is_odd():
    return lax.rem(lax.axis_index("sensor"), 2) == 1


def spread(rows):
    upper = -(-rows.shape[0] // 16) * 8
    lower = rows[upper:]
    if lower.shape[0] < upper:
        lower = jnp.concatenate([lower, jnp.zeros((upper - lower.shape[0], LANES), rows.dtype)])
    return jnp.concatenate([rows[:upper], lower], axis=1)


def gathered(wide, count):
    return jnp.concatenate([wide[:, :LANES], wide[: count - wide.shape[0], LANES:]])


def rows_of(values):
    row = lax.broadcasted_iota(jnp.int32, (8, LANES), 0)
    out = jnp.zeros((8, LANES), jnp.float32)
    for i, value in enumerate(values):
        if value is not None:
            out = jnp.where(row == i, jnp.broadcast_to(value, (8, LANES)), out)
    return out


def first_forward_body(*refs):
    loaded, (sent, edge, threshold, linked), kept, sems = refs[:10], refs[10:14], refs[14:24], refs[24]
    kernel, kernel_here = loaded[0], kept[0]
    field, multiplier, plain, weighted_t = kept[1:5]
    neighbours, tile_of_cell, tile_weight = kept[7:]
    freqs = kernel.shape[1]
    times, cells = field.shape
    half = times // 2
    copies = []

    def load(source, target):
        copy = pltpu.make_async_copy(source, target, sems.at[len(copies)])
        copy.start()
        copies.append(copy)
        return copy

    early = [load(loaded[i], kept[i]) for i in (1, 3)]
    large = []
    for start in range(0, freqs, CHUNK):
        at = (slice(None), pl.ds(start, min(CHUNK, freqs - start)))
        large.append(load(kernel.at[at], kernel_here.at[at]))
        if start == 0:
            small = [load(loaded[i], kept[i]) for i in (7, 8, 9, 2, 4)]
    late = [load(loaded[i], kept[i]) for i in (5, 6)]
    for copy in early:
        copy.wait()
    spectra = table_dot(plain[...], field[...])
    for copy in small:
        copy.wait()

    cell = lax.broadcasted_iota(jnp.int32, (4, cells), 1) + lax.axis_index("cell") * cells
    linked[0:4, :] = jnp.where(neighbours[...] != cell, 1.0, 0.0)
    linked[4:8, :] = jnp.zeros((4, cells), jnp.float32)
    tile = lax.broadcasted_iota(jnp.int32, (tile_weight.shape[1], cells), 0)
    chosen = jnp.where(tile == tile_of_cell[...], 1.0, 0.0)
    weights = jnp.dot(
        jnp.broadcast_to(tile_weight[...], (8, tile_weight.shape[1])), chosen,
        precision=lax.Precision.HIGHEST, preferred_element_type=jnp.float32,
    )
    limit = SHRINK_SCALE * weights
    threshold[...] = limit
    bottom = cells // COLS - 1
    pairs = (
        (strip(field, 0), strip(field, bottom)),
        (strip(multiplier[2], 0), strip(multiplier[3], bottom)),
        (strip(limit, 0), strip(limit, bottom)),
    )
    for (head, tail), start in zip(pairs, (0, times, 2 * times)):
        one, two = edges(head, tail)
        sent[half + start : half + start + head.shape[0], :] = one
        edge[start : start + head.shape[0], :] = two

    def arrived(group):
        if group * GROUP % CHUNK == 0:
            large[group * GROUP // CHUNK].wait()

    rows = forward_rows(spectra, kernel_here, arrived)
    sent[:half, :] = packed_series(rows, weighted_t[...], kernel.shape[2])
    for copy in late:
        copy.wait()


def turn_body(kernel, came, out):
    freqs, sensors = kernel.shape[1:3]
    for part in range(2):
        for group in range(out.shape[1]):
            width = min(GROUP, freqs - group * GROUP) * sensors
            out[part, group, :, :width] = slab(kernel, part, group).T


def first_adjoint_body(count, *refs):
    observed, two, kernel, plain_t, weighted, _, out = refs[count:]
    times = observed.shape[0]
    predicted = unpacked(summed(refs[:count]), kernel.shape[2])
    residual = predicted - jnp.concatenate([observed[...], observed[...]], axis=1)
    out[:times, :] = adjoint(residual, kernel, plain_t[...], weighted[...], 1)
    out[times:, :] = spread(two[...])


def response_of(field, turned_ref, plain, weighted_t, linked, sent, edge):
    half = field.shape[0] // 2
    rows = field.shape[1] // COLS
    one, two = edges(strip(field, 0), strip(field, rows - 1))
    squares = []
    for row in range(rows):
        here = strip(field, row)
        east = strip(linked[0:1], row) * (pltpu.roll(here, COLS - 1, 1) - here)
        squares.append(east * east)
        if row > 0:
            north = strip(linked[2:3], row) * (strip(field, row - 1) - here)
            squares.append(north * north)
    sensors = turned_ref.shape[3] // GROUP
    sent[:half, :] = forward(field, turned_ref, plain[...], weighted_t[...], sensors)
    sent[half : half + 8, :] = rows_of([square_sum(field), 2.0 * total_of(tree_sum(squares))])
    sent[half + 8 :, :] = one
    edge[...] = two


def merge_body(sent, came, edge, other, linked, out):
    cells = linked.shape[1]
    top = out.shape[0]
    to_partner, to_other = edges(linked[2:3, :COLS], linked[3:4, cells - COLS :])
    across = to_partner * (came[top:, :] - sent[top:, :])
    beyond = to_other * (other[...] - edge[...])
    out[: top - 8, :] = sent[: top - 8, :] + came[: top - 8, :]
    boundary = 2.0 * square_sum(jnp.where(is_odd(), beyond, across))
    out[top - 8 :, :] = sent[top - 8 : top, :] + came[top - 8 : top, :] + rows_of([None, None, boundary])


def start_back_body(start_multiplier, one, two, passed, linked, back, two_out):
    times, cells = back.shape
    half = times // 2
    two = jnp.where(is_odd(), two[...], gathered(passed[times:, :], two.shape[0]))
    two_out[...] = two
    values = [[strip(start_multiplier[k], r) for r in range(cells // COLS)] for k in range(4)]
    above, below = beside(one[half + times : half + 2 * times, :], two[times : 2 * times, :])
    back[...] = gathered_jumps(values, above, below, linked[...])


def first_gradient_body(count, *refs):
    back, linked, kernel, plain, weighted_t, adjoint_out, gradient, sent, edge = refs[count:]
    total = summed(refs[:count])
    field = total + back[...]
    adjoint_out[...] = total
    gradient[...] = field
    response_of(field, kernel, plain, weighted_t, linked[...], sent, edge)


def second_adjoint_body(count, *refs):
    two, kernel, plain_t, weighted, out, norms = refs[count:]
    times = plain_t.shape[0]
    half = times // 2
    total = summed(refs[:count])
    packed, squares = total[:half], total[half : half + 8]
    out[:times, :] = adjoint(unpacked(packed, kernel.shape[2]), kernel, plain_t[...], weighted[...], 2)
    scalars = rows_of([square_sum(packed), squares[2:3, :] * (2.0 / lax.axis_size("sensor"))])
    out[times : times + 8, :] = jnp.concatenate([scalars] * (out.shape[1] // LANES), axis=1)
    out[times + 8 :, :] = spread(two[...])
    norms[...] = squares


def step_of(norms, scalars):
    return norms[0:1, :] / (scalars[0:1, :] + (norms[1:2, :] + scalars[1:2, :]) + TINY)


def both_jumps_body(model, gradient, one, two, grad_one, grad_two, passed, linked, model_jumps, grad_jumps):
    times, cells = model.shape
    half = times // 2
    above, below = beside(one[half : half + times, :], two[:times, :])
    from_other = jnp.where(is_odd(), grad_two[...], gathered(passed[times + 8 :, :], times))
    halos = ((above, below), beside(grad_one[half + 8 :, :], from_other))
    for field, (above, below), out in zip((model, gradient), halos, (model_jumps, grad_jumps)):
        for k, strips in enumerate(jumps(field[...], above, below, linked[...])):
            for r, values in enumerate(strips):
                out[k, :, r * COLS : (r + 1) * COLS] = values


def second_gradient_body(count, *refs):
    (norms, adjoint_in, gradient_in, model, model_jumps, grad_jumps, start_multiplier, threshold, one, two, linked_ref,
     kernel, plain, weighted_t, model_out, jumps_out, multiplier_out, gradient_out, sent, edge) = refs[count:]
    times, cells = model.shape
    half = times // 2
    total = summed(refs[:count])
    step = step_of(norms, total[times:, :LANES])
    linked = linked_ref[...]
    field, gradient = model[...], gradient_in[...]
    rows = cells // COLS
    above, below = beside(one[half:, :], two[...])

    def advance(model_jumps, old_multiplier, limit):
        shifted = model_jumps + old_multiplier
        auxiliary = shrunk(shifted, limit)
        multiplier = shifted - auxiliary
        return multiplier, model_jumps - auxiliary + multiplier

    penalties, new_jumps = [], []
    for k in range(4):
        penalties.append([])
        new_jumps.append([])
        for r in range(rows):
            at = slice(r * COLS, (r + 1) * COLS)
            new = model_jumps[k, :, at] - step * grad_jumps[k, :, at]
            multiplier, penalty = advance(new, strip(start_multiplier[k], r), strip(threshold[0:1], r))
            jumps_out[k, :, at] = new
            multiplier_out[k, :, at] = multiplier
            penalties[k].append(penalty)
            new_jumps[k].append(new)
    _, beside_above = advance(-new_jumps[2][0], above[times : 2 * times], above[2 * times : 2 * times + 1])
    _, beside_below = advance(-new_jumps[3][-1], below[times : 2 * times], below[2 * times : 2 * times + 1])
    back = gathered_jumps(penalties, beside_above, beside_below, linked)
    wide_step = jnp.concatenate([step] * rows, axis=1)
    model_out[...] = field - wide_step * gradient
    new_gradient = adjoint_in[...] - wide_step * total[:times] + back
    gradient_out[...] = new_gradient
    response_of(new_gradient, kernel, plain, weighted_t, linked, sent, edge)


def response_body(count, *refs):
    two, out, passing, norms = refs[count:]
    total = summed(refs[:count])
    packed, squares = total[:-8], total[-8:]
    scalars = rows_of([square_sum(packed), squares[2:3, :] * (2.0 / lax.axis_size("sensor"))])
    out[...] = scalars
    passing[:8, :] = scalars
    passing[8:, :] = two[...]
    norms[...] = squares


def before_finish_body(gradient, model_jumps, multiplier, linked, sum_out, jumps_out):
    field = gradient[...]
    sum_out[...] = model_jumps[...] + multiplier[...]
    nothing = jnp.zeros((field.shape[0], COLS), jnp.float32)
    for k, strips in enumerate(jumps(field, nothing, nothing, linked[...])):
        for r, values in enumerate(strips):
            jumps_out[k, :, r * COLS : (r + 1) * COLS] = values


def finish_body(count, *refs):
    (norms, gradient_in, model, sums, inner_jumps, threshold, grad_one, grad_two, passed, linked,
     estimate_out, auxiliary_out, multiplier_out, estimate_here, auxiliary_here, multiplier_here, sems) = refs[count:]
    step = step_of(norms, tree_sum([part[:8, :] for part in refs[:count]]))
    half = gradient_in.shape[0] // 2
    gradient = gradient_in[...]
    rows = gradient.shape[1] // COLS
    copies = []

    def store(source, target):
        copy = pltpu.make_async_copy(source, target, sems.at[len(copies)])
        copy.start()
        copies.append(copy)

    above, below = beside(grad_one[half + 8 :, :], jnp.where(is_odd(), grad_two[...], passed[8:, :]))
    outer = {
        (2, 0): linked[2:3, :COLS] * (above - strip(gradient, 0)),
        (3, rows - 1): linked[3:4, (rows - 1) * COLS :] * (below - strip(gradient, rows - 1)),
    }
    for k in range(4):
        for r in range(rows):
            at = slice(r * COLS, (r + 1) * COLS)
            shifted = sums[k, :, at] - step * outer.get((k, r), inner_jumps[k, :, at])
            auxiliary = shrunk(shifted, threshold[0:1, at])
            auxiliary_here[k, :, at] = auxiliary
            multiplier_here[k, :, at] = shifted - auxiliary
        store(auxiliary_here.at[k], auxiliary_out.at[k])
        store(multiplier_here.at[k], multiplier_out.at[k])
    estimate_here[...] = model[...] - jnp.concatenate([step] * rows, axis=1) * gradient
    store(estimate_here, estimate_out)
    for copy in copies:
        copy.wait()


def stages_of(count, *radices):
    stages = []
    for radix in radices:
        if count > 1 and count % radix == 0:
            stages.append(radix)
            count //= radix
    while count > 1:
        stages.append(2)
        count //= 2
    return stages


def summing(parts, axis, stride, stages):
    count = lax.axis_size(axis)
    for radix in stages:
        total = tree_sum(parts)
        parts = [total] + [
            lax.ppermute(total, axis, [(i, i ^ (k * stride)) for i in range(count)]) for k in range(1, radix)
        ]
        stride *= radix
    return parts


def sensor_hop(array):
    return lax.ppermute(array, "sensor", [(i, i ^ 1) for i in range(lax.axis_size("sensor"))])


def sensor_parts(array, rows):
    passed = sensor_hop(array)
    total = array[:rows] + passed[:rows]
    return summing([total], "sensor", 2, stages_of(lax.axis_size("sensor") // 2, 2)), passed


def last_sensor_parts(scalars, passing):
    count = lax.axis_size("sensor")
    near, far, across = (
        lax.ppermute(array, "sensor", [(i, i ^ k) for i in range(count)])
        for k, array in ((1, scalars), (2, scalars), (3, passing))
    )
    parts = [scalars, near, far, across]
    if count > 4:
        rows = scalars.shape[0]
        parts = summing([tree_sum([part[:rows] for part in parts])], "sensor", 4, stages_of(count // 4, 4))
    return parts, across


def cell_parts(merged):
    return summing([merged], "cell", 2, stages_of(lax.axis_size("cell") // 2, 4, 4))


def from_partner(array):
    return lax.ppermute(array, "cell", [(i, i ^ 1) for i in range(lax.axis_size("cell"))])


def from_other(array):
    sensors = lax.axis_size("sensor")
    pairs = [
        (i * sensors + s, (i + 1 if i % 2 else i - 1) * sensors + s)
        for i in range(1, lax.axis_size("cell") - 1)
        for s in range(1, sensors, 2)
    ]
    return lax.ppermute(array, ("cell", "sensor"), pairs)


def per_device(kernel, observed, start_model, start_multiplier, neighbours, tile_of_cell, tile_weight):
    times, cells = start_model.shape
    freqs, sensors = kernel.shape[1:3]
    plain, weighted = tables(times, freqs)
    plain, plain_t, weighted, weighted_t = (
        jnp.asarray(table_terms(t)) for t in (plain, plain.T, weighted, weighted.T)
    )
    half = times // 2
    field, row, wide = (times, cells), (times, COLS), (4, times, cells)

    loads = [
        kernel, start_model, start_multiplier, plain, weighted_t, plain_t, weighted,
        neighbours, tile_of_cell[None, :], tile_weight[None, :],
    ]
    sent, edge, threshold, linked, kernel, start_model, start_multiplier, plain, weighted_t, plain_t, weighted = call(
        first_forward_body,
        [(half + 2 * times + 8, LANES), (2 * times + 8, LANES), (8, cells), (8, cells)]
        + [jax.ShapeDtypeStruct(a.shape, a.dtype) for a in loads[:7]],
        *[pltpu.with_memory_space_constraint(a, HBM) for a in loads],
        scratch=[VMEM(a.shape, a.dtype) for a in loads[7:]] + [pltpu.SemaphoreType.DMA((9 + -(-freqs // CHUNK),))],
        inputs=HBM,
    )
    one = from_partner(sent)
    two = from_other(edge)
    parts = cell_parts(sent[:half] + one[:half])
    across = call(
        turn_body, jax.ShapeDtypeStruct((2, plain.shape[0] // 16, cells, GROUP * sensors), kernel.dtype), kernel, one
    )
    message, side, shared = (half + 8 + times, LANES), (times, LANES), (2 * times + 8, LANES)
    back = call(
        functools.partial(first_adjoint_body, len(parts)), (2 * times + 8, cells),
        *parts, observed, two, kernel, plain_t, weighted, across,
    )
    parts, passed = sensor_parts(back, times)
    back, two = call(start_back_body, [field, shared], start_multiplier, one, two, passed, linked)
    adjoint_one, gradient, sent, edge = call(
        functools.partial(first_gradient_body, len(parts)), [field, field, message, side],
        *parts, back, linked, across, plain, weighted_t,
    )
    grad_one, grad_two = from_partner(sent), from_other(edge)
    parts = cell_parts(call(merge_body, (half + 8, LANES), sent, grad_one, edge, grad_two, linked))
    back, norms = call(
        functools.partial(second_adjoint_body, len(parts)), [(times + 8 + half, cells), (8, LANES)],
        *parts, grad_two, kernel, plain_t, weighted,
    )
    parts, passed = sensor_parts(back, times + 8)
    model_jumps, grad_jumps = call(
        both_jumps_body, [wide, wide], start_model, gradient, one, two, grad_one, grad_two, passed, linked
    )
    model, model_jumps, multiplier, gradient, sent, edge = call(
        functools.partial(second_gradient_body, len(parts)), [field, wide, wide, field, message, side],
        *parts, norms, adjoint_one, gradient, start_model, model_jumps, grad_jumps, start_multiplier, threshold,
        one, two, linked, across, plain, weighted_t,
    )
    grad_one, grad_two = from_partner(sent), from_other(edge)
    parts = cell_parts(call(merge_body, (half + 8, LANES), sent, grad_one, edge, grad_two, linked))
    sums, inner_jumps = call(before_finish_body, [wide, wide], gradient, model_jumps, multiplier, linked)
    scalars, passing, norms = call(
        functools.partial(response_body, len(parts)), [(8, LANES), (8 + times, LANES), (8, LANES)], *parts, grad_two
    )
    parts, passed = last_sensor_parts(scalars, passing)
    return tuple(
        call(
            functools.partial(finish_body, len(parts)), [field, wide, wide],
            *parts, norms, gradient, model, sums, inner_jumps, threshold, grad_one, grad_two, passed, linked,
            scratch=[VMEM(shape, jnp.float32) for shape in (field, wide, wide)] + [pltpu.SemaphoreType.DMA((9,))],
            outputs=HBM,
        )
    )


def solution(mesh):
    in_specs = (
        P(None, None, "sensor", "cell"),
        P(None, "sensor"),
        P(None, "cell"),
        P(None, None, "cell"),
        P(None, "cell"),
        P("cell"),
        P(),
    )
    out_specs = (P(None, "cell"), P(None, None, "cell"), P(None, None, "cell"))
    return jax.shard_map(
        per_device, mesh=mesh, in_specs=in_specs, out_specs=out_specs, check_vma=False
    )
```

```python
import functools

import jax
import jax.numpy as jnp
import numpy as np
from jax import lax
from jax.experimental import pallas as pl
from jax.experimental.pallas import tpu as pltpu
from jax.sharding import PartitionSpec as P

COLS = 128
LANES = 128
GROUP = 8
CHUNK = 24
SHRINK_SCALE = 0.4
TINY = 1e-06
VMEM = pltpu.VMEM
HBM = pltpu.HBM


def tables(times, freqs):
    padded = 2 * times
    groups = -(-freqs // GROUP)
    plain = np.zeros((16 * groups, times), np.float64)
    weighted = np.zeros((16 * groups, times), np.float64)
    for f in range(freqs):
        phase = 2.0 * np.pi * ((f * np.arange(times)) % padded) / padded
        weight = (1.0 if f in (0, freqs - 1) else 2.0) / padded
        row = 16 * (f // GROUP) + f % GROUP
        plain[row], plain[row + GROUP] = np.cos(phase), -np.sin(phase)
        weighted[row], weighted[row + GROUP] = weight * np.cos(phase), -weight * np.sin(phase)
    return plain.astype(np.float32), weighted.astype(np.float32)


def table_terms(table):
    high = table.astype(jnp.bfloat16)
    low = (table - high.astype(np.float32)).astype(jnp.bfloat16)
    return np.concatenate([high, high, low], axis=1)


def table_dot(terms, values):
    high = values.astype(jnp.bfloat16)
    low = (values - high.astype(jnp.float32)).astype(jnp.bfloat16)
    return dot_nn(terms, jnp.concatenate([high, low, high], axis=0))


def turned(rows):
    rows = rows.astype(jnp.float32)
    return jnp.concatenate([-rows[GROUP:], rows[:GROUP]], axis=0).astype(jnp.bfloat16)


def dot_nt(left, right):
    return lax.dot_general(left, right, (((1,), (1,)), ((), ())), preferred_element_type=jnp.float32)


def dot_nn(left, right):
    return jnp.dot(left, right, preferred_element_type=jnp.float32)


def slab(kernel_ref, part, group):
    freqs, sensors, cells = kernel_ref.shape[1:]
    count = min(GROUP, freqs - group * GROUP)
    block = kernel_ref[part, group * GROUP : group * GROUP + count]
    return block.reshape(count * sensors, cells)


def own_block(width, sensors):
    row = lax.broadcasted_iota(jnp.int32, (16, width), 0) % GROUP
    lane = lax.broadcasted_iota(jnp.int32, (16, width), 1) // sensors
    return row == lane


def fold(wide):
    total = functools.reduce(
        lambda a, b: a + b, [wide[:, i : i + LANES] for i in range(0, wide.shape[1], LANES)]
    )
    return total + pltpu.roll(total, LANES // 2, 1)


def forward(field, turned_ref, plain, weighted_t, sensors):
    freqs = field.shape[0] + 1
    spectra = table_dot(plain, field)
    rows = []
    for group in range(spectra.shape[0] // 16):
        part = spectra[16 * group : 16 * group + 16]
        width = min(GROUP, freqs - group * GROUP) * sensors
        out = dot_nn(part.astype(jnp.bfloat16), turned_ref[0, group, :, :width])
        out += dot_nn(turned(part), turned_ref[1, group, :, :width])
        rows.append(fold_own(out, sensors))
    return packed_series(jnp.concatenate(rows, axis=0), weighted_t, sensors)


def fold_own(out, sensors):
    width = out.shape[1]
    out = jnp.where(own_block(width, sensors), out, 0.0)
    if width < LANES:
        out = jnp.concatenate([out, jnp.zeros((16, LANES - width), jnp.float32)], axis=1)
    return fold(out)


def forward_rows(spectra, kernel_ref, arrived=None):
    sensors = kernel_ref.shape[2]
    rows = []
    for group in range(spectra.shape[0] // 16):
        part = spectra[16 * group : 16 * group + 16]
        if arrived is not None:
            arrived(group)
        re_slab, im_slab = slab(kernel_ref, 0, group), slab(kernel_ref, 1, group)
        out = dot_nt(part.astype(jnp.bfloat16), re_slab) + dot_nt(turned(part), im_slab)
        rows.append(fold_own(out, sensors))
    return jnp.concatenate(rows, axis=0)


def packed_series(rows, weighted_t, sensors):
    times = weighted_t.shape[0]
    series = table_dot(weighted_t, rows)
    left = lax.broadcasted_iota(jnp.int32, (times // 2, LANES), 1) < sensors
    return jnp.where(left, series[: times // 2], series[times // 2 :])


def unpacked(packed, sensors):
    other = pltpu.roll(packed, sensors, 1)
    left = lax.broadcasted_iota(jnp.int32, packed.shape, 1) < sensors
    return jnp.concatenate([jnp.where(left, packed, other), jnp.where(left, other, packed)], axis=0)


def adjoint(residual, kernel_ref, plain_t, weighted, halves):
    freqs, sensors, cells = kernel_ref.shape[1:]
    spectra = table_dot(weighted, residual)
    rows = []
    for group in range(weighted.shape[0] // 16):
        part = spectra[16 * group : 16 * group + 16]
        count = min(GROUP, freqs - group * GROUP)
        width = count * sensors
        re_slab, im_slab = slab(kernel_ref, 0, group), slab(kernel_ref, 1, group)
        wide = jnp.concatenate([part] * (-(-width // LANES)), axis=1)[:, :width]
        wide = jnp.where(own_block(width, sensors), wide, 0.0)
        terms = []
        for _ in range(halves):
            terms.append(wide.astype(jnp.bfloat16))
            wide = wide - terms[-1].astype(jnp.float32)
        left = jnp.concatenate(terms, axis=0)
        swapped = jnp.concatenate([turned(term) for term in terms], axis=0)
        out = dot_nn(left, re_slab) - dot_nn(swapped, im_slab)
        rows.append(tree_sum([out[16 * i : 16 * i + 16] for i in range(halves)]))
    return table_dot(plain_t, jnp.concatenate(rows, axis=0))


def strip(array, row):
    return array[..., row * COLS : (row + 1) * COLS]


def jumps(field, above, below, linked):
    count = field.shape[1] // COLS
    out = []
    for direction in range(4):
        strips = []
        for row in range(count):
            here = strip(field, row)
            if direction == 0:
                there = pltpu.roll(here, COLS - 1, 1)
            elif direction == 1:
                there = pltpu.roll(here, 1, 1)
            elif direction == 2:
                there = above if row == 0 else strip(field, row - 1)
            else:
                there = below if row == count - 1 else strip(field, row + 1)
            strips.append(strip(linked[direction : direction + 1], row) * (there - here))
        out.append(strips)
    return out


def gathered_jumps(values, above, below, linked):
    count = len(values[0])
    out = []
    for row in range(count):
        arriving = (
            pltpu.roll(values[1][row], COLS - 1, 1),
            pltpu.roll(values[0][row], 1, 1),
            above if row == 0 else values[3][row - 1],
            below if row == count - 1 else values[2][row + 1],
        )
        total = None
        for direction in range(4):
            term = strip(linked[direction : direction + 1], row) * (arriving[direction] - values[direction][row])
            total = term if total is None else total + term
        out.append(total)
    return jnp.concatenate(out, axis=1)


def shrunk(shifted, threshold):
    return shifted - jnp.clip(shifted, -threshold, threshold)


def tree_sum(parts):
    parts = list(parts)
    while len(parts) > 1:
        parts = [parts[i] + parts[i + 1] if i + 1 < len(parts) else parts[i] for i in range(0, len(parts), 2)]
    return parts[0]


def total_of(array):
    return jnp.sum(array, axis=(0, 1), keepdims=True)


def square_sum(array):
    return total_of(array * array)


def block_of(scalar, rows=8):
    return jnp.full((rows, LANES), scalar, jnp.float32)


def call(body, out_shapes, *operands, scratch=(), inputs=VMEM, outputs=VMEM):
    single = not isinstance(out_shapes, list)
    shapes = [out_shapes] if single else list(out_shapes)
    shapes = [s if isinstance(s, jax.ShapeDtypeStruct) else jax.ShapeDtypeStruct(s, jnp.float32) for s in shapes]
    out = pl.pallas_call(
        body,
        out_shape=shapes,
        in_specs=[pl.BlockSpec(memory_space=inputs)] * len(operands),
        out_specs=[pl.BlockSpec(memory_space=outputs)] * len(shapes),
        scratch_shapes=list(scratch),
        compiler_params=pltpu.CompilerParams(vmem_limit_bytes=24 * 2**20),
    )(*operands)
    return out[0] if single else out


def summed(parts):
    return tree_sum([part[...] for part in parts])


def is_even():
    return lax.rem(lax.axis_index("cell"), 2) == 0


def edges(head, tail):
    even = is_even()
    return jnp.where(even, tail, head), jnp.where(even, head, tail)


def beside(partner, other):
    even = is_even()
    return jnp.where(even, other, partner), jnp.where(even, partner, other)


def is_odd():
    return lax.rem(lax.axis_index("sensor"), 2) == 1


def spread(rows):
    upper = -(-rows.shape[0] // 16) * 8
    lower = rows[upper:]
    if lower.shape[0] < upper:
        lower = jnp.concatenate([lower, jnp.zeros((upper - lower.shape[0], LANES), rows.dtype)])
    return jnp.concatenate([rows[:upper], lower], axis=1)


def gathered(wide, count):
    return jnp.concatenate([wide[:, :LANES], wide[: count - wide.shape[0], LANES:]])


def rows_of(values):
    row = lax.broadcasted_iota(jnp.int32, (8, LANES), 0)
    out = jnp.zeros((8, LANES), jnp.float32)
    for i, value in enumerate(values):
        if value is not None:
            out = jnp.where(row == i, jnp.broadcast_to(value, (8, LANES)), out)
    return out


def first_forward_body(*refs):
    loaded, (sent, edge, threshold, linked), kept, sems = refs[:10], refs[10:14], refs[14:24], refs[24]
    kernel, kernel_here = loaded[0], kept[0]
    field, multiplier, plain, weighted_t = kept[1:5]
    neighbours, tile_of_cell, tile_weight = kept[7:]
    freqs = kernel.shape[1]
    times, cells = field.shape
    half = times // 2
    copies = []

    def load(source, target):
        copy = pltpu.make_async_copy(source, target, sems.at[len(copies)])
        copy.start()
        copies.append(copy)
        return copy

    early = [load(loaded[i], kept[i]) for i in (1, 3)]
    large = []
    for start in range(0, freqs, CHUNK):
        at = (slice(None), pl.ds(start, min(CHUNK, freqs - start)))
        large.append(load(kernel.at[at], kernel_here.at[at]))
        if start == 0:
            small = [load(loaded[i], kept[i]) for i in (7, 8, 9, 2, 4)]
    late = [load(loaded[i], kept[i]) for i in (5, 6)]
    for copy in early:
        copy.wait()
    spectra = table_dot(plain[...], field[...])
    for copy in small:
        copy.wait()

    cell = lax.broadcasted_iota(jnp.int32, (4, cells), 1) + lax.axis_index("cell") * cells
    linked[0:4, :] = jnp.where(neighbours[...] != cell, 1.0, 0.0)
    linked[4:8, :] = jnp.zeros((4, cells), jnp.float32)
    tile = lax.broadcasted_iota(jnp.int32, (tile_weight.shape[1], cells), 0)
    chosen = jnp.where(tile == tile_of_cell[...], 1.0, 0.0)
    weights = jnp.dot(
        jnp.broadcast_to(tile_weight[...], (8, tile_weight.shape[1])), chosen,
        precision=lax.Precision.HIGHEST, preferred_element_type=jnp.float32,
    )
    limit = SHRINK_SCALE * weights
    threshold[...] = limit
    bottom = cells // COLS - 1
    pairs = (
        (strip(field, 0), strip(field, bottom)),
        (strip(multiplier[2], 0), strip(multiplier[3], bottom)),
        (strip(limit, 0), strip(limit, bottom)),
    )
    for (head, tail), start in zip(pairs, (0, times, 2 * times)):
        one, two = edges(head, tail)
        sent[half + start : half + start + head.shape[0], :] = one
        edge[start : start + head.shape[0], :] = two

    def arrived(group):
        if group * GROUP % CHUNK == 0:
            large[group * GROUP // CHUNK].wait()

    rows = forward_rows(spectra, kernel_here, arrived)
    sent[:half, :] = packed_series(rows, weighted_t[...], kernel.shape[2])
    for copy in late:
        copy.wait()


def turn_body(kernel, came, out):
    freqs, sensors = kernel.shape[1:3]
    for part in range(2):
        for group in range(out.shape[1]):
            width = min(GROUP, freqs - group * GROUP) * sensors
            out[part, group, :, :width] = slab(kernel, part, group).T


def first_adjoint_body(count, *refs):
    observed, two, kernel, plain_t, weighted, _, out = refs[count:]
    times = observed.shape[0]
    predicted = unpacked(summed(refs[:count]), kernel.shape[2])
    residual = predicted - jnp.concatenate([observed[...], observed[...]], axis=1)
    out[:times, :] = adjoint(residual, kernel, plain_t[...], weighted[...], 1)
    out[times:, :] = spread(two[...])


def response_of(field, turned_ref, plain, weighted_t, linked, sent, edge):
    half = field.shape[0] // 2
    rows = field.shape[1] // COLS
    one, two = edges(strip(field, 0), strip(field, rows - 1))
    squares = []
    for row in range(rows):
        here = strip(field, row)
        east = strip(linked[0:1], row) * (pltpu.roll(here, COLS - 1, 1) - here)
        squares.append(east * east)
        if row > 0:
            north = strip(linked[2:3], row) * (strip(field, row - 1) - here)
            squares.append(north * north)
    sensors = turned_ref.shape[3] // GROUP
    sent[:half, :] = forward(field, turned_ref, plain[...], weighted_t[...], sensors)
    sent[half : half + 8, :] = rows_of([square_sum(field), 2.0 * total_of(tree_sum(squares))])
    sent[half + 8 :, :] = one
    edge[...] = two


def merge_body(sent, came, edge, other, linked, out):
    cells = linked.shape[1]
    top = out.shape[0]
    to_partner, to_other = edges(linked[2:3, :COLS], linked[3:4, cells - COLS :])
    across = to_partner * (came[top:, :] - sent[top:, :])
    beyond = to_other * (other[...] - edge[...])
    out[: top - 8, :] = sent[: top - 8, :] + came[: top - 8, :]
    boundary = 2.0 * square_sum(jnp.where(is_odd(), beyond, across))
    out[top - 8 :, :] = sent[top - 8 : top, :] + came[top - 8 : top, :] + rows_of([None, None, boundary])


def start_back_body(start_multiplier, one, two, passed, linked, back, two_out):
    times, cells = back.shape
    half = times // 2
    two = jnp.where(is_odd(), two[...], gathered(passed[times:, :], two.shape[0]))
    two_out[...] = two
    values = [[strip(start_multiplier[k], r) for r in range(cells // COLS)] for k in range(4)]
    above, below = beside(one[half + times : half + 2 * times, :], two[times : 2 * times, :])
    back[...] = gathered_jumps(values, above, below, linked[...])


def first_gradient_body(count, *refs):
    back, linked, kernel, plain, weighted_t, adjoint_out, gradient, sent, edge = refs[count:]
    total = summed(refs[:count])
    field = total + back[...]
    adjoint_out[...] = total
    gradient[...] = field
    response_of(field, kernel, plain, weighted_t, linked[...], sent, edge)


def second_adjoint_body(count, *refs):
    two, kernel, plain_t, weighted, out, norms = refs[count:]
    times = plain_t.shape[0]
    half = times // 2
    total = summed(refs[:count])
    packed, squares = total[:half], total[half : half + 8]
    out[:times, :] = adjoint(unpacked(packed, kernel.shape[2]), kernel, plain_t[...], weighted[...], 2)
    scalars = rows_of([square_sum(packed), squares[2:3, :] * (2.0 / lax.axis_size("sensor"))])
    out[times : times + 8, :] = jnp.concatenate([scalars] * (out.shape[1] // LANES), axis=1)
    out[times + 8 :, :] = spread(two[...])
    norms[...] = squares


def step_of(norms, scalars):
    return norms[0:1, :] / (scalars[0:1, :] + (norms[1:2, :] + scalars[1:2, :]) + TINY)


def both_jumps_body(model, gradient, one, two, grad_one, grad_two, passed, linked, model_jumps, grad_jumps):
    times, cells = model.shape
    half = times // 2
    above, below = beside(one[half : half + times, :], two[:times, :])
    from_other = jnp.where(is_odd(), grad_two[...], gathered(passed[times + 8 :, :], times))
    halos = ((above, below), beside(grad_one[half + 8 :, :], from_other))
    for field, (above, below), out in zip((model, gradient), halos, (model_jumps, grad_jumps)):
        for k, strips in enumerate(jumps(field[...], above, below, linked[...])):
            for r, values in enumerate(strips):
                out[k, :, r * COLS : (r + 1) * COLS] = values


def second_gradient_body(count, *refs):
    (norms, adjoint_in, gradient_in, model, model_jumps, grad_jumps, start_multiplier, threshold, one, two, linked_ref,
     kernel, plain, weighted_t, model_out, sum_out, gradient_out, sent, edge) = refs[count:]
    times, cells = model.shape
    half = times // 2
    total = summed(refs[:count])
    step = step_of(norms, total[times:, :LANES])
    linked = linked_ref[...]
    field, gradient = model[...], gradient_in[...]
    rows = cells // COLS
    above, below = beside(one[half:, :], two[...])

    def advance(model_jumps, old_multiplier, limit):
        shifted = model_jumps + old_multiplier
        auxiliary = shrunk(shifted, limit)
        multiplier = shifted - auxiliary
        return multiplier, model_jumps - auxiliary + multiplier

    penalties, new_jumps = [], []
    for k in range(4):
        penalties.append([])
        new_jumps.append([])
        for r in range(rows):
            at = slice(r * COLS, (r + 1) * COLS)
            new = model_jumps[k, :, at] - step * grad_jumps[k, :, at]
            multiplier, penalty = advance(new, strip(start_multiplier[k], r), strip(threshold[0:1], r))
            sum_out[k, :, at] = new + multiplier
            penalties[k].append(penalty)
            new_jumps[k].append(new)
    _, beside_above = advance(-new_jumps[2][0], above[times : 2 * times], above[2 * times : 2 * times + 1])
    _, beside_below = advance(-new_jumps[3][-1], below[times : 2 * times], below[2 * times : 2 * times + 1])
    back = gathered_jumps(penalties, beside_above, beside_below, linked)
    wide_step = jnp.concatenate([step] * rows, axis=1)
    model_out[...] = field - wide_step * gradient
    new_gradient = adjoint_in[...] - wide_step * total[:times] + back
    gradient_out[...] = new_gradient
    response_of(new_gradient, kernel, plain, weighted_t, linked, sent, edge)


def response_body(count, *refs):
    two, out, passing, norms = refs[count:]
    total = summed(refs[:count])
    packed, squares = total[:-8], total[-8:]
    scalars = rows_of([square_sum(packed), squares[2:3, :] * (2.0 / lax.axis_size("sensor"))])
    out[...] = scalars
    passing[:8, :] = scalars
    passing[8:, :] = two[...]
    norms[...] = squares


def before_finish_body(gradient, linked, jumps_out):
    field = gradient[...]
    nothing = jnp.zeros((field.shape[0], COLS), jnp.float32)
    for k, strips in enumerate(jumps(field, nothing, nothing, linked[...])):
        for r, values in enumerate(strips):
            jumps_out[k, :, r * COLS : (r + 1) * COLS] = values


def finish_body(count, *refs):
    (norms, gradient_in, model, sums, inner_jumps, threshold, grad_one, grad_two, passed, linked,
     estimate_out, auxiliary_out, multiplier_out, estimate_here, auxiliary_here, multiplier_here, sems) = refs[count:]
    step = step_of(norms, tree_sum([part[:8, :] for part in refs[:count]]))
    half = gradient_in.shape[0] // 2
    gradient = gradient_in[...]
    rows = gradient.shape[1] // COLS
    copies = []

    def store(source, target):
        copy = pltpu.make_async_copy(source, target, sems.at[len(copies)])
        copy.start()
        copies.append(copy)

    above, below = beside(grad_one[half + 8 :, :], jnp.where(is_odd(), grad_two[...], passed[8:, :]))
    outer = {
        (2, 0): linked[2:3, :COLS] * (above - strip(gradient, 0)),
        (3, rows - 1): linked[3:4, (rows - 1) * COLS :] * (below - strip(gradient, rows - 1)),
    }
    for k in range(4):
        for r in range(rows):
            at = slice(r * COLS, (r + 1) * COLS)
            shifted = sums[k, :, at] - step * outer.get((k, r), inner_jumps[k, :, at])
            auxiliary = shrunk(shifted, threshold[0:1, at])
            auxiliary_here[k, :, at] = auxiliary
            multiplier_here[k, :, at] = shifted - auxiliary
        store(auxiliary_here.at[k], auxiliary_out.at[k])
        store(multiplier_here.at[k], multiplier_out.at[k])
    estimate_here[...] = model[...] - jnp.concatenate([step] * rows, axis=1) * gradient
    store(estimate_here, estimate_out)
    for copy in copies:
        copy.wait()


def stages_of(count, *radices):
    stages = []
    for radix in radices:
        if count > 1 and count % radix == 0:
            stages.append(radix)
            count //= radix
    while count > 1:
        stages.append(2)
        count //= 2
    return stages


def summing(parts, axis, stride, stages):
    count = lax.axis_size(axis)
    for radix in stages:
        total = tree_sum(parts)
        parts = [total] + [
            lax.ppermute(total, axis, [(i, i ^ (k * stride)) for i in range(count)]) for k in range(1, radix)
        ]
        stride *= radix
    return parts


def sensor_hop(array):
    return lax.ppermute(array, "sensor", [(i, i ^ 1) for i in range(lax.axis_size("sensor"))])


def sensor_parts(array, rows):
    passed = sensor_hop(array)
    total = array[:rows] + passed[:rows]
    return summing([total], "sensor", 2, stages_of(lax.axis_size("sensor") // 2, 2)), passed


def last_sensor_parts(scalars, passing):
    count = lax.axis_size("sensor")
    near, far, across = (
        lax.ppermute(array, "sensor", [(i, i ^ k) for i in range(count)])
        for k, array in ((1, scalars), (2, scalars), (3, passing))
    )
    parts = [scalars, near, far, across]
    if count > 4:
        rows = scalars.shape[0]
        parts = summing([tree_sum([part[:rows] for part in parts])], "sensor", 4, stages_of(count // 4, 4))
    return parts, across


def cell_parts(merged):
    return summing([merged], "cell", 2, stages_of(lax.axis_size("cell") // 2, 4, 4))


def from_partner(array):
    return lax.ppermute(array, "cell", [(i, i ^ 1) for i in range(lax.axis_size("cell"))])


def from_other(array):
    sensors = lax.axis_size("sensor")
    pairs = [
        (i * sensors + s, (i + 1 if i % 2 else i - 1) * sensors + s)
        for i in range(1, lax.axis_size("cell") - 1)
        for s in range(1, sensors, 2)
    ]
    return lax.ppermute(array, ("cell", "sensor"), pairs)


def per_device(kernel, observed, start_model, start_multiplier, neighbours, tile_of_cell, tile_weight):
    times, cells = start_model.shape
    freqs, sensors = kernel.shape[1:3]
    plain, weighted = tables(times, freqs)
    plain, plain_t, weighted, weighted_t = (
        jnp.asarray(table_terms(t)) for t in (plain, plain.T, weighted, weighted.T)
    )
    half = times // 2
    field, row, wide = (times, cells), (times, COLS), (4, times, cells)

    loads = [
        kernel, start_model, start_multiplier, plain, weighted_t, plain_t, weighted,
        neighbours, tile_of_cell[None, :], tile_weight[None, :],
    ]
    sent, edge, threshold, linked, kernel, start_model, start_multiplier, plain, weighted_t, plain_t, weighted = call(
        first_forward_body,
        [(half + 2 * times + 8, LANES), (2 * times + 8, LANES), (8, cells), (8, cells)]
        + [jax.ShapeDtypeStruct(a.shape, a.dtype) for a in loads[:7]],
        *[pltpu.with_memory_space_constraint(a, HBM) for a in loads],
        scratch=[VMEM(a.shape, a.dtype) for a in loads[7:]] + [pltpu.SemaphoreType.DMA((9 + -(-freqs // CHUNK),))],
        inputs=HBM,
    )
    one = from_partner(sent)
    two = from_other(edge)
    parts = cell_parts(sent[:half] + one[:half])
    across = call(
        turn_body, jax.ShapeDtypeStruct((2, plain.shape[0] // 16, cells, GROUP * sensors), kernel.dtype), kernel, one
    )
    message, side, shared = (half + 8 + times, LANES), (times, LANES), (2 * times + 8, LANES)
    back = call(
        functools.partial(first_adjoint_body, len(parts)), (2 * times + 8, cells),
        *parts, observed, two, kernel, plain_t, weighted, across,
    )
    parts, passed = sensor_parts(back, times)
    back, two = call(start_back_body, [field, shared], start_multiplier, one, two, passed, linked)
    adjoint_one, gradient, sent, edge = call(
        functools.partial(first_gradient_body, len(parts)), [field, field, message, side],
        *parts, back, linked, across, plain, weighted_t,
    )
    grad_one, grad_two = from_partner(sent), from_other(edge)
    parts = cell_parts(call(merge_body, (half + 8, LANES), sent, grad_one, edge, grad_two, linked))
    back, norms = call(
        functools.partial(second_adjoint_body, len(parts)), [(times + 8 + half, cells), (8, LANES)],
        *parts, grad_two, kernel, plain_t, weighted,
    )
    parts, passed = sensor_parts(back, times + 8)
    model_jumps, grad_jumps = call(
        both_jumps_body, [wide, wide], start_model, gradient, one, two, grad_one, grad_two, passed, linked
    )
    model, sums, gradient, sent, edge = call(
        functools.partial(second_gradient_body, len(parts)), [field, wide, field, message, side],
        *parts, norms, adjoint_one, gradient, start_model, model_jumps, grad_jumps, start_multiplier, threshold,
        one, two, linked, across, plain, weighted_t,
    )
    grad_one, grad_two = from_partner(sent), from_other(edge)
    parts = cell_parts(call(merge_body, (half + 8, LANES), sent, grad_one, edge, grad_two, linked))
    inner_jumps = call(before_finish_body, wide, gradient, linked)
    scalars, passing, norms = call(
        functools.partial(response_body, len(parts)), [(8, LANES), (8 + times, LANES), (8, LANES)], *parts, grad_two
    )
    parts, passed = last_sensor_parts(scalars, passing)
    return tuple(
        call(
            functools.partial(finish_body, len(parts)), [field, wide, wide],
            *parts, norms, gradient, model, sums, inner_jumps, threshold, grad_one, grad_two, passed, linked,
            scratch=[VMEM(shape, jnp.float32) for shape in (field, wide, wide)] + [pltpu.SemaphoreType.DMA((9,))],
            outputs=HBM,
        )
    )


def solution(mesh):
    in_specs = (
        P(None, None, "sensor", "cell"),
        P(None, "sensor"),
        P(None, "cell"),
        P(None, None, "cell"),
        P(None, "cell"),
        P("cell"),
        P(),
    )
    out_specs = (P(None, "cell"), P(None, None, "cell"), P(None, None, "cell"))
    return jax.shard_map(
        per_device, mesh=mesh, in_specs=in_specs, out_specs=out_specs, check_vma=False
    )
```

```python
import functools

import jax
import jax.numpy as jnp
import numpy as np
from jax import lax
from jax.experimental import pallas as pl
from jax.experimental.pallas import tpu as pltpu
from jax.sharding import PartitionSpec as P

COLS = 128
LANES = 128
GROUP = 8
CHUNK = 24
SHRINK_SCALE = 0.4
TINY = 1e-06
VMEM = pltpu.VMEM
HBM = pltpu.HBM


def tables(times, freqs):
    padded = 2 * times
    groups = -(-freqs // GROUP)
    plain = np.zeros((16 * groups, times), np.float64)
    weighted = np.zeros((16 * groups, times), np.float64)
    for f in range(freqs):
        phase = 2.0 * np.pi * ((f * np.arange(times)) % padded) / padded
        weight = (1.0 if f in (0, freqs - 1) else 2.0) / padded
        row = 16 * (f // GROUP) + f % GROUP
        plain[row], plain[row + GROUP] = np.cos(phase), -np.sin(phase)
        weighted[row], weighted[row + GROUP] = weight * np.cos(phase), -weight * np.sin(phase)
    return plain.astype(np.float32), weighted.astype(np.float32)


def table_terms(table):
    high = table.astype(jnp.bfloat16)
    low = (table - high.astype(np.float32)).astype(jnp.bfloat16)
    return np.concatenate([high, high, low], axis=1)


def table_dot(terms, values):
    high = values.astype(jnp.bfloat16)
    low = (values - high.astype(jnp.float32)).astype(jnp.bfloat16)
    return dot_nn(terms, jnp.concatenate([high, low, high], axis=0))


def turned(rows):
    rows = rows.astype(jnp.float32)
    return jnp.concatenate([-rows[GROUP:], rows[:GROUP]], axis=0).astype(jnp.bfloat16)


def dot_nt(left, right):
    return lax.dot_general(left, right, (((1,), (1,)), ((), ())), preferred_element_type=jnp.float32)


def dot_nn(left, right):
    return jnp.dot(left, right, preferred_element_type=jnp.float32)


def slab(kernel_ref, part, group):
    freqs, sensors, cells = kernel_ref.shape[1:]
    count = min(GROUP, freqs - group * GROUP)
    block = kernel_ref[part, group * GROUP : group * GROUP + count]
    return block.reshape(count * sensors, cells)


def own_block(width, sensors):
    row = lax.broadcasted_iota(jnp.int32, (16, width), 0) % GROUP
    lane = lax.broadcasted_iota(jnp.int32, (16, width), 1) // sensors
    return row == lane


def fold(wide):
    total = functools.reduce(
        lambda a, b: a + b, [wide[:, i : i + LANES] for i in range(0, wide.shape[1], LANES)]
    )
    return total + pltpu.roll(total, LANES // 2, 1)


def forward(field, turned_ref, plain, weighted_t, sensors):
    freqs = field.shape[0] + 1
    spectra = table_dot(plain, field)
    rows = []
    for group in range(spectra.shape[0] // 16):
        part = spectra[16 * group : 16 * group + 16]
        width = min(GROUP, freqs - group * GROUP) * sensors
        out = dot_nn(part.astype(jnp.bfloat16), turned_ref[0, group, :, :width])
        out += dot_nn(turned(part), turned_ref[1, group, :, :width])
        rows.append(fold_own(out, sensors))
    return packed_series(jnp.concatenate(rows, axis=0), weighted_t, sensors)


def fold_own(out, sensors):
    width = out.shape[1]
    out = jnp.where(own_block(width, sensors), out, 0.0)
    if width < LANES:
        out = jnp.concatenate([out, jnp.zeros((16, LANES - width), jnp.float32)], axis=1)
    return fold(out)


def forward_rows(spectra, kernel_ref, arrived=None):
    sensors = kernel_ref.shape[2]
    rows = []
    for group in range(spectra.shape[0] // 16):
        part = spectra[16 * group : 16 * group + 16]
        if arrived is not None:
            arrived(group)
        re_slab, im_slab = slab(kernel_ref, 0, group), slab(kernel_ref, 1, group)
        out = dot_nt(part.astype(jnp.bfloat16), re_slab) + dot_nt(turned(part), im_slab)
        rows.append(fold_own(out, sensors))
    return jnp.concatenate(rows, axis=0)


def packed_series(rows, weighted_t, sensors):
    times = weighted_t.shape[0]
    series = table_dot(weighted_t, rows)
    left = lax.broadcasted_iota(jnp.int32, (times // 2, LANES), 1) < sensors
    return jnp.where(left, series[: times // 2], series[times // 2 :])


def unpacked(packed, sensors):
    other = pltpu.roll(packed, sensors, 1)
    left = lax.broadcasted_iota(jnp.int32, packed.shape, 1) < sensors
    return jnp.concatenate([jnp.where(left, packed, other), jnp.where(left, other, packed)], axis=0)


def adjoint(residual, kernel_ref, plain_t, weighted, halves):
    freqs, sensors, cells = kernel_ref.shape[1:]
    spectra = table_dot(weighted, residual)
    rows = []
    for group in range(weighted.shape[0] // 16):
        part = spectra[16 * group : 16 * group + 16]
        count = min(GROUP, freqs - group * GROUP)
        width = count * sensors
        re_slab, im_slab = slab(kernel_ref, 0, group), slab(kernel_ref, 1, group)
        wide = jnp.concatenate([part] * (-(-width // LANES)), axis=1)[:, :width]
        wide = jnp.where(own_block(width, sensors), wide, 0.0)
        terms = []
        for _ in range(halves):
            terms.append(wide.astype(jnp.bfloat16))
            wide = wide - terms[-1].astype(jnp.float32)
        left = jnp.concatenate(terms, axis=0)
        swapped = jnp.concatenate([turned(term) for term in terms], axis=0)
        out = dot_nn(left, re_slab) - dot_nn(swapped, im_slab)
        rows.append(tree_sum([out[16 * i : 16 * i + 16] for i in range(halves)]))
    return table_dot(plain_t, jnp.concatenate(rows, axis=0))


def strip(array, row):
    return array[..., row * COLS : (row + 1) * COLS]


def jumps(field, above, below, linked):
    count = field.shape[1] // COLS
    out = []
    for direction in range(4):
        strips = []
        for row in range(count):
            here = strip(field, row)
            if direction == 0:
                there = pltpu.roll(here, COLS - 1, 1)
            elif direction == 1:
                there = pltpu.roll(here, 1, 1)
            elif direction == 2:
                there = above if row == 0 else strip(field, row - 1)
            else:
                there = below if row == count - 1 else strip(field, row + 1)
            strips.append(strip(linked[direction : direction + 1], row) * (there - here))
        out.append(strips)
    return out


def gathered_jumps(values, above, below, linked):
    count = len(values[0])
    out = []
    for row in range(count):
        arriving = (
            pltpu.roll(values[1][row], COLS - 1, 1),
            pltpu.roll(values[0][row], 1, 1),
            above if row == 0 else values[3][row - 1],
            below if row == count - 1 else values[2][row + 1],
        )
        total = None
        for direction in range(4):
            term = strip(linked[direction : direction + 1], row) * (arriving[direction] - values[direction][row])
            total = term if total is None else total + term
        out.append(total)
    return jnp.concatenate(out, axis=1)


def shrunk(shifted, threshold):
    return shifted - jnp.clip(shifted, -threshold, threshold)


def tree_sum(parts):
    parts = list(parts)
    while len(parts) > 1:
        parts = [parts[i] + parts[i + 1] if i + 1 < len(parts) else parts[i] for i in range(0, len(parts), 2)]
    return parts[0]


def total_of(array):
    return jnp.sum(array, axis=(0, 1), keepdims=True)


def square_sum(array):
    return total_of(array * array)


def block_of(scalar, rows=8):
    return jnp.full((rows, LANES), scalar, jnp.float32)


def call(body, out_shapes, *operands, scratch=(), inputs=VMEM, outputs=VMEM):
    single = not isinstance(out_shapes, list)
    shapes = [out_shapes] if single else list(out_shapes)
    shapes = [s if isinstance(s, jax.ShapeDtypeStruct) else jax.ShapeDtypeStruct(s, jnp.float32) for s in shapes]
    out = pl.pallas_call(
        body,
        out_shape=shapes,
        in_specs=[pl.BlockSpec(memory_space=inputs)] * len(operands),
        out_specs=[pl.BlockSpec(memory_space=outputs)] * len(shapes),
        scratch_shapes=list(scratch),
        compiler_params=pltpu.CompilerParams(vmem_limit_bytes=24 * 2**20),
    )(*operands)
    return out[0] if single else out


def summed(parts):
    return tree_sum([part[...] for part in parts])


def is_even():
    return lax.rem(lax.axis_index("cell"), 2) == 0


def edges(head, tail):
    even = is_even()
    return jnp.where(even, tail, head), jnp.where(even, head, tail)


def beside(partner, other):
    even = is_even()
    return jnp.where(even, other, partner), jnp.where(even, partner, other)


def is_odd():
    return lax.rem(lax.axis_index("sensor"), 2) == 1


def spread(rows):
    upper = -(-rows.shape[0] // 16) * 8
    lower = rows[upper:]
    if lower.shape[0] < upper:
        lower = jnp.concatenate([lower, jnp.zeros((upper - lower.shape[0], LANES), rows.dtype)])
    return jnp.concatenate([rows[:upper], lower], axis=1)


def gathered(wide, count):
    return jnp.concatenate([wide[:, :LANES], wide[: count - wide.shape[0], LANES:]])


def rows_of(values):
    row = lax.broadcasted_iota(jnp.int32, (8, LANES), 0)
    out = jnp.zeros((8, LANES), jnp.float32)
    for i, value in enumerate(values):
        if value is not None:
            out = jnp.where(row == i, jnp.broadcast_to(value, (8, LANES)), out)
    return out


def first_forward_body(*refs):
    loaded, (sent, edge, threshold, linked), kept, sems = refs[:10], refs[10:14], refs[14:24], refs[24]
    kernel, kernel_here = loaded[0], kept[0]
    field, multiplier, plain, weighted_t = kept[1:5]
    neighbours, tile_of_cell, tile_weight = kept[7:]
    freqs = kernel.shape[1]
    times, cells = field.shape
    half = times // 2
    copies = []

    def load(source, target):
        copy = pltpu.make_async_copy(source, target, sems.at[len(copies)])
        copy.start()
        copies.append(copy)
        return copy

    early = [load(loaded[i], kept[i]) for i in (1, 3)]
    small = [load(loaded[i], kept[i]) for i in (7, 8, 9, 2, 4)]
    large = []
    for start in range(0, freqs, CHUNK):
        at = (slice(None), pl.ds(start, min(CHUNK, freqs - start)))
        large.append(load(kernel.at[at], kernel_here.at[at]))
    late = [load(loaded[i], kept[i]) for i in (5, 6)]
    for copy in early:
        copy.wait()
    spectra = table_dot(plain[...], field[...])
    for copy in small:
        copy.wait()

    cell = lax.broadcasted_iota(jnp.int32, (4, cells), 1) + lax.axis_index("cell") * cells
    linked[0:4, :] = jnp.where(neighbours[...] != cell, 1.0, 0.0)
    linked[4:8, :] = jnp.zeros((4, cells), jnp.float32)
    tile = lax.broadcasted_iota(jnp.int32, (tile_weight.shape[1], cells), 0)
    chosen = jnp.where(tile == tile_of_cell[...], 1.0, 0.0)
    weights = jnp.dot(
        jnp.broadcast_to(tile_weight[...], (8, tile_weight.shape[1])), chosen,
        precision=lax.Precision.HIGHEST, preferred_element_type=jnp.float32,
    )
    limit = SHRINK_SCALE * weights
    threshold[...] = limit
    bottom = cells // COLS - 1
    pairs = (
        (strip(field, 0), strip(field, bottom)),
        (strip(multiplier[2], 0), strip(multiplier[3], bottom)),
        (strip(limit, 0), strip(limit, bottom)),
    )
    for (head, tail), start in zip(pairs, (0, times, 2 * times)):
        one, two = edges(head, tail)
        sent[half + start : half + start + head.shape[0], :] = one
        edge[start : start + head.shape[0], :] = two

    def arrived(group):
        if group * GROUP % CHUNK == 0:
            large[group * GROUP // CHUNK].wait()

    rows = forward_rows(spectra, kernel_here, arrived)
    sent[:half, :] = packed_series(rows, weighted_t[...], kernel.shape[2])
    for copy in late:
        copy.wait()


def turn_body(kernel, came, out):
    freqs, sensors = kernel.shape[1:3]
    for part in range(2):
        for group in range(out.shape[1]):
            width = min(GROUP, freqs - group * GROUP) * sensors
            out[part, group, :, :width] = slab(kernel, part, group).T


def first_adjoint_body(count, *refs):
    observed, two, kernel, plain_t, weighted, _, out = refs[count:]
    times = observed.shape[0]
    predicted = unpacked(summed(refs[:count]), kernel.shape[2])
    residual = predicted - jnp.concatenate([observed[...], observed[...]], axis=1)
    out[:times, :] = adjoint(residual, kernel, plain_t[...], weighted[...], 1)
    out[times:, :] = spread(two[...])


def response_of(field, turned_ref, plain, weighted_t, linked, sent, edge):
    half = field.shape[0] // 2
    rows = field.shape[1] // COLS
    one, two = edges(strip(field, 0), strip(field, rows - 1))
    squares = []
    for row in range(rows):
        here = strip(field, row)
        east = strip(linked[0:1], row) * (pltpu.roll(here, COLS - 1, 1) - here)
        squares.append(east * east)
        if row > 0:
            north = strip(linked[2:3], row) * (strip(field, row - 1) - here)
            squares.append(north * north)
    sensors = turned_ref.shape[3] // GROUP
    sent[:half, :] = forward(field, turned_ref, plain[...], weighted_t[...], sensors)
    sent[half : half + 8, :] = rows_of([square_sum(field), 2.0 * total_of(tree_sum(squares))])
    sent[half + 8 :, :] = one
    edge[...] = two


def merge_body(sent, came, edge, other, linked, out):
    cells = linked.shape[1]
    top = out.shape[0]
    to_partner, to_other = edges(linked[2:3, :COLS], linked[3:4, cells - COLS :])
    across = to_partner * (came[top:, :] - sent[top:, :])
    beyond = to_other * (other[...] - edge[...])
    out[: top - 8, :] = sent[: top - 8, :] + came[: top - 8, :]
    boundary = 2.0 * square_sum(jnp.where(is_odd(), beyond, across))
    out[top - 8 :, :] = sent[top - 8 : top, :] + came[top - 8 : top, :] + rows_of([None, None, boundary])


def start_back_body(start_multiplier, one, two, passed, linked, back, two_out):
    times, cells = back.shape
    half = times // 2
    two = jnp.where(is_odd(), two[...], gathered(passed[times:, :], two.shape[0]))
    two_out[...] = two
    values = [[strip(start_multiplier[k], r) for r in range(cells // COLS)] for k in range(4)]
    above, below = beside(one[half + times : half + 2 * times, :], two[times : 2 * times, :])
    back[...] = gathered_jumps(values, above, below, linked[...])


def first_gradient_body(count, *refs):
    back, linked, kernel, plain, weighted_t, adjoint_out, gradient, sent, edge = refs[count:]
    total = summed(refs[:count])
    field = total + back[...]
    adjoint_out[...] = total
    gradient[...] = field
    response_of(field, kernel, plain, weighted_t, linked[...], sent, edge)


def second_adjoint_body(count, *refs):
    two, kernel, plain_t, weighted, out, norms = refs[count:]
    times = plain_t.shape[0]
    half = times // 2
    total = summed(refs[:count])
    packed, squares = total[:half], total[half : half + 8]
    out[:times, :] = adjoint(unpacked(packed, kernel.shape[2]), kernel, plain_t[...], weighted[...], 2)
    scalars = rows_of([square_sum(packed), squares[2:3, :] * (2.0 / lax.axis_size("sensor"))])
    out[times : times + 8, :] = jnp.concatenate([scalars] * (out.shape[1] // LANES), axis=1)
    out[times + 8 :, :] = spread(two[...])
    norms[...] = squares


def step_of(norms, scalars):
    return norms[0:1, :] / (scalars[0:1, :] + (norms[1:2, :] + scalars[1:2, :]) + TINY)


def both_jumps_body(model, gradient, one, two, grad_one, grad_two, passed, linked, model_jumps, grad_jumps):
    times, cells = model.shape
    half = times // 2
    above, below = beside(one[half : half + times, :], two[:times, :])
    from_other = jnp.where(is_odd(), grad_two[...], gathered(passed[times + 8 :, :], times))
    halos = ((above, below), beside(grad_one[half + 8 :, :], from_other))
    for field, (above, below), out in zip((model, gradient), halos, (model_jumps, grad_jumps)):
        for k, strips in enumerate(jumps(field[...], above, below, linked[...])):
            for r, values in enumerate(strips):
                out[k, :, r * COLS : (r + 1) * COLS] = values


def second_gradient_body(count, *refs):
    (norms, adjoint_in, gradient_in, model, model_jumps, grad_jumps, start_multiplier, threshold, one, two, linked_ref,
     kernel, plain, weighted_t, model_out, sum_out, gradient_out, sent, edge) = refs[count:]
    times, cells = model.shape
    half = times // 2
    total = summed(refs[:count])
    step = step_of(norms, total[times:, :LANES])
    linked = linked_ref[...]
    field, gradient = model[...], gradient_in[...]
    rows = cells // COLS
    above, below = beside(one[half:, :], two[...])

    def advance(model_jumps, old_multiplier, limit):
        shifted = model_jumps + old_multiplier
        auxiliary = shrunk(shifted, limit)
        multiplier = shifted - auxiliary
        return multiplier, model_jumps - auxiliary + multiplier

    penalties, new_jumps = [], []
    for k in range(4):
        penalties.append([])
        new_jumps.append([])
        for r in range(rows):
            at = slice(r * COLS, (r + 1) * COLS)
            new = model_jumps[k, :, at] - step * grad_jumps[k, :, at]
            multiplier, penalty = advance(new, strip(start_multiplier[k], r), strip(threshold[0:1], r))
            sum_out[k, :, at] = new + multiplier
            penalties[k].append(penalty)
            new_jumps[k].append(new)
    _, beside_above = advance(-new_jumps[2][0], above[times : 2 * times], above[2 * times : 2 * times + 1])
    _, beside_below = advance(-new_jumps[3][-1], below[times : 2 * times], below[2 * times : 2 * times + 1])
    back = gathered_jumps(penalties, beside_above, beside_below, linked)
    wide_step = jnp.concatenate([step] * rows, axis=1)
    model_out[...] = field - wide_step * gradient
    new_gradient = adjoint_in[...] - wide_step * total[:times] + back
    gradient_out[...] = new_gradient
    response_of(new_gradient, kernel, plain, weighted_t, linked, sent, edge)


def response_body(count, *refs):
    two, out, passing, norms = refs[count:]
    total = summed(refs[:count])
    packed, squares = total[:-8], total[-8:]
    scalars = rows_of([square_sum(packed), squares[2:3, :] * (2.0 / lax.axis_size("sensor"))])
    out[...] = scalars
    passing[:8, :] = scalars
    passing[8:, :] = two[...]
    norms[...] = squares


def before_finish_body(gradient, linked, jumps_out):
    field = gradient[...]
    nothing = jnp.zeros((field.shape[0], COLS), jnp.float32)
    for k, strips in enumerate(jumps(field, nothing, nothing, linked[...])):
        for r, values in enumerate(strips):
            jumps_out[k, :, r * COLS : (r + 1) * COLS] = values


def finish_body(count, *refs):
    (norms, gradient_in, model, sums, inner_jumps, threshold, grad_one, grad_two, passed, linked,
     estimate_out, auxiliary_out, multiplier_out, estimate_here, auxiliary_here, multiplier_here, sems) = refs[count:]
    step = step_of(norms, tree_sum([part[:8, :] for part in refs[:count]]))
    half = gradient_in.shape[0] // 2
    gradient = gradient_in[...]
    rows = gradient.shape[1] // COLS
    copies = []

    def store(source, target):
        copy = pltpu.make_async_copy(source, target, sems.at[len(copies)])
        copy.start()
        copies.append(copy)

    above, below = beside(grad_one[half + 8 :, :], jnp.where(is_odd(), grad_two[...], passed[8:, :]))
    outer = {
        (2, 0): linked[2:3, :COLS] * (above - strip(gradient, 0)),
        (3, rows - 1): linked[3:4, (rows - 1) * COLS :] * (below - strip(gradient, rows - 1)),
    }
    for k in range(4):
        for r in range(rows):
            at = slice(r * COLS, (r + 1) * COLS)
            shifted = sums[k, :, at] - step * outer.get((k, r), inner_jumps[k, :, at])
            auxiliary = shrunk(shifted, threshold[0:1, at])
            auxiliary_here[k, :, at] = auxiliary
            multiplier_here[k, :, at] = shifted - auxiliary
        store(auxiliary_here.at[k], auxiliary_out.at[k])
        store(multiplier_here.at[k], multiplier_out.at[k])
    estimate_here[...] = model[...] - jnp.concatenate([step] * rows, axis=1) * gradient
    store(estimate_here, estimate_out)
    for copy in copies:
        copy.wait()


def stages_of(count, *radices):
    stages = []
    for radix in radices:
        if count > 1 and count % radix == 0:
            stages.append(radix)
            count //= radix
    while count > 1:
        stages.append(2)
        count //= 2
    return stages


def summing(parts, axis, stride, stages):
    count = lax.axis_size(axis)
    for radix in stages:
        total = tree_sum(parts)
        parts = [total] + [
            lax.ppermute(total, axis, [(i, i ^ (k * stride)) for i in range(count)]) for k in range(1, radix)
        ]
        stride *= radix
    return parts


def sensor_hop(array):
    return lax.ppermute(array, "sensor", [(i, i ^ 1) for i in range(lax.axis_size("sensor"))])


def sensor_parts(array, rows):
    passed = sensor_hop(array)
    total = array[:rows] + passed[:rows]
    return summing([total], "sensor", 2, stages_of(lax.axis_size("sensor") // 2, 2)), passed


def last_sensor_parts(scalars, passing):
    count = lax.axis_size("sensor")
    near, far, across = (
        lax.ppermute(array, "sensor", [(i, i ^ k) for i in range(count)])
        for k, array in ((1, scalars), (2, scalars), (3, passing))
    )
    parts = [scalars, near, far, across]
    if count > 4:
        rows = scalars.shape[0]
        parts = summing([tree_sum([part[:rows] for part in parts])], "sensor", 4, stages_of(count // 4, 4))
    return parts, across


def cell_parts(merged):
    return summing([merged], "cell", 2, stages_of(lax.axis_size("cell") // 2, 4, 4))


def from_partner(array):
    return lax.ppermute(array, "cell", [(i, i ^ 1) for i in range(lax.axis_size("cell"))])


def from_other(array):
    sensors = lax.axis_size("sensor")
    pairs = [
        (i * sensors + s, (i + 1 if i % 2 else i - 1) * sensors + s)
        for i in range(1, lax.axis_size("cell") - 1)
        for s in range(1, sensors, 2)
    ]
    return lax.ppermute(array, ("cell", "sensor"), pairs)


def per_device(kernel, observed, start_model, start_multiplier, neighbours, tile_of_cell, tile_weight):
    times, cells = start_model.shape
    freqs, sensors = kernel.shape[1:3]
    plain, weighted = tables(times, freqs)
    plain, plain_t, weighted, weighted_t = (
        jnp.asarray(table_terms(t)) for t in (plain, plain.T, weighted, weighted.T)
    )
    half = times // 2
    field, row, wide = (times, cells), (times, COLS), (4, times, cells)

    loads = [
        kernel, start_model, start_multiplier, plain, weighted_t, plain_t, weighted,
        neighbours, tile_of_cell[None, :], tile_weight[None, :],
    ]
    sent, edge, threshold, linked, kernel, start_model, start_multiplier, plain, weighted_t, plain_t, weighted = call(
        first_forward_body,
        [(half + 2 * times + 8, LANES), (2 * times + 8, LANES), (8, cells), (8, cells)]
        + [jax.ShapeDtypeStruct(a.shape, a.dtype) for a in loads[:7]],
        *[pltpu.with_memory_space_constraint(a, HBM) for a in loads],
        scratch=[VMEM(a.shape, a.dtype) for a in loads[7:]] + [pltpu.SemaphoreType.DMA((9 + -(-freqs // CHUNK),))],
        inputs=HBM,
    )
    one = from_partner(sent)
    two = from_other(edge)
    parts = cell_parts(sent[:half] + one[:half])
    across = call(
        turn_body, jax.ShapeDtypeStruct((2, plain.shape[0] // 16, cells, GROUP * sensors), kernel.dtype), kernel, one
    )
    message, side, shared = (half + 8 + times, LANES), (times, LANES), (2 * times + 8, LANES)
    back = call(
        functools.partial(first_adjoint_body, len(parts)), (2 * times + 8, cells),
        *parts, observed, two, kernel, plain_t, weighted, across,
    )
    parts, passed = sensor_parts(back, times)
    back, two = call(start_back_body, [field, shared], start_multiplier, one, two, passed, linked)
    adjoint_one, gradient, sent, edge = call(
        functools.partial(first_gradient_body, len(parts)), [field, field, message, side],
        *parts, back, linked, across, plain, weighted_t,
    )
    grad_one, grad_two = from_partner(sent), from_other(edge)
    parts = cell_parts(call(merge_body, (half + 8, LANES), sent, grad_one, edge, grad_two, linked))
    back, norms = call(
        functools.partial(second_adjoint_body, len(parts)), [(times + 8 + half, cells), (8, LANES)],
        *parts, grad_two, kernel, plain_t, weighted,
    )
    parts, passed = sensor_parts(back, times + 8)
    model_jumps, grad_jumps = call(
        both_jumps_body, [wide, wide], start_model, gradient, one, two, grad_one, grad_two, passed, linked
    )
    model, sums, gradient, sent, edge = call(
        functools.partial(second_gradient_body, len(parts)), [field, wide, field, message, side],
        *parts, norms, adjoint_one, gradient, start_model, model_jumps, grad_jumps, start_multiplier, threshold,
        one, two, linked, across, plain, weighted_t,
    )
    grad_one, grad_two = from_partner(sent), from_other(edge)
    parts = cell_parts(call(merge_body, (half + 8, LANES), sent, grad_one, edge, grad_two, linked))
    inner_jumps = call(before_finish_body, wide, gradient, linked)
    scalars, passing, norms = call(
        functools.partial(response_body, len(parts)), [(8, LANES), (8 + times, LANES), (8, LANES)], *parts, grad_two
    )
    parts, passed = last_sensor_parts(scalars, passing)
    return tuple(
        call(
            functools.partial(finish_body, len(parts)), [field, wide, wide],
            *parts, norms, gradient, model, sums, inner_jumps, threshold, grad_one, grad_two, passed, linked,
            scratch=[VMEM(shape, jnp.float32) for shape in (field, wide, wide)] + [pltpu.SemaphoreType.DMA((9,))],
            outputs=HBM,
        )
    )


def solution(mesh):
    in_specs = (
        P(None, None, "sensor", "cell"),
        P(None, "sensor"),
        P(None, "cell"),
        P(None, None, "cell"),
        P(None, "cell"),
        P("cell"),
        P(),
    )
    out_specs = (P(None, "cell"), P(None, None, "cell"), P(None, None, "cell"))
    return jax.shard_map(
        per_device, mesh=mesh, in_specs=in_specs, out_specs=out_specs, check_vma=False
    )
```
